32 devices in a mesh: dp: 8 (over z, y), tensor: 4 (over x, core).
Axes of the slice: x: 2, y: 2, z: 4, core: 2. Of those that a mesh axis runs over, the one named last changes fastest.
Arguments:
- tokens: bfloat16 [16384, 1024], P(('dp', 'tensor')), may hold values from -6 to 6
- segments: int32 [16384], P('dp'), may hold values from 0 to 31, never falling along the last dimension, each value on 1 to 2048 neighbouring positions
- cotangent: bfloat16 [16384, 1024], P(('dp', 'tensor')), may hold values from -12 to 12
- qkv_weight: bfloat16 [1024, 2048], P(None, 'tensor'), may hold values from -0.1875 to 0.1875
- out_weight: bfloat16 [1024, 1024], P('tensor'), may hold values from -1.5 to 1.5
- gate_up_weight: bfloat16 [1024, 2, 4608], P(None, None, 'tensor'), may hold values from -0.1875 to 0.1875
- down_weight: bfloat16 [4608, 1024], P('tensor'), may hold values from -0.09375 to 0.09375
- qkv_master: float32 [1024, 2048], P('dp', 'tensor'), may hold values from -0.1875 to 0.1875
- out_master: float32 [1024, 1024], P('tensor', 'dp'), may hold values from -1.5 to 1.5
- gate_up_master: float32 [1024, 2, 4608], P('dp', None, 'tensor'), may hold values from -0.1875 to 0.1875
- down_master: float32 [4608, 1024], P('tensor', 'dp'), may hold values from -0.09375 to 0.09375
- qkv_mean: float32 [1024, 2048], P('dp', 'tensor'), may hold values from -0.00036621094 to 0.00036621094
- out_mean: float32 [1024, 1024], P('tensor', 'dp'), may hold values from -0.00015258789 to 0.00015258789
- gate_up_mean: float32 [1024, 2, 4608], P('dp', None, 'tensor'), may hold values from -0.00036621094 to 0.00036621094
- down_mean: float32 [4608, 1024], P('tensor', 'dp'), may hold values from -0.00036621094 to 0.00036621094
- qkv_square: float32 [1024, 2048], P('dp', 'tensor'), may hold values from 2.889922e-09 to 1.1559688e-08
- out_square: float32 [1024, 1024], P('tensor', 'dp'), may hold values from 3.4679065e-10 to 1.3871626e-09
- gate_up_square: float32 [1024, 2, 4608], P('dp', None, 'tensor'), may hold values from 2.889922e-09 to 1.1559688e-08
- down_square: float32 [4608, 1024], P('tensor', 'dp'), may hold values from 2.889922e-09 to 1.1559688e-08
- gains: float32 [2176], replicated, may hold values from 0.5 to 9
- gains_mean: float32 [2176], replicated, may hold values from -0.0014648438 to 0.0014648438
- gains_square: float32 [2176], replicated, may hold values from 4.6238753e-08 to 1.8495501e-07
Outputs:
- result: bfloat16 [16384, 1024], P(('dp', 'tensor'))
- input_grad: bfloat16 [16384, 1024], P(('dp', 'tensor'))
- grad_norm: float32 [], replicated
- qkv_new: float32 [1024, 2048], P('dp', 'tensor')
- qkv_copy: bfloat16 [1024, 2048], P('dp', 'tensor')
- qkv_mean_new: float32 [1024, 2048], P('dp', 'tensor')
- qkv_square_new: float32 [1024, 2048], P('dp', 'tensor')
- out_new: float32 [1024, 1024], P('tensor', 'dp')
- out_copy: bfloat16 [1024, 1024], P('tensor', 'dp')
- out_mean_new: float32 [1024, 1024], P('tensor', 'dp')
- out_square_new: float32 [1024, 1024], P('tensor', 'dp')
- gate_up_new: float32 [1024, 2, 4608], P('dp', None, 'tensor')
- gate_up_copy: bfloat16 [1024, 2, 4608], P('dp', None, 'tensor')
- gate_up_mean_new: float32 [1024, 2, 4608], P('dp', None, 'tensor')
- gate_up_square_new: float32 [1024, 2, 4608], P('dp', None, 'tensor')
- down_new: float32 [4608, 1024], P('tensor', 'dp')
- down_copy: bfloat16 [4608, 1024], P('tensor', 'dp')
- down_mean_new: float32 [4608, 1024], P('tensor', 'dp')
- down_square_new: float32 [4608, 1024], P('tensor', 'dp')
- gains_new: float32 [2176], replicated
- gains_mean_new: float32 [2176], replicated
- gains_square_new: float32 [2176], replicated
The draws below stay inside these ranges and needn't reach their ends.
Inputs may be any that keep to these rules, and one draw needn't show every extreme that they name: `segments`: document numbers never fall along the tokens; a document holds 1 to 2048 tokens and one holds exactly 2048.
All inputs are finite; a program needn't handle non-finite values.
Results may differ from the reference program's by a relative error of at most 0.028.
Values may be sent and summed in bfloat16 or wider, within the bound.
No kernel may reach another device: no remote copies, remote signals or barrier semaphores. Data moves between devices by JAX's collectives and lax.ppermute only.
A program may use at most 192 MiB of HBM per device.

```python
import math
import jax
import jax.numpy as jnp
import numpy as np
from jax import lax

D = 1024
QH = 16
KVH = 8
HD = 64
FF = 4608
STEP = 5
SEQ = 2048
TOKENS = 16384
DOCS = 32
QKV = 2048
GAINS = 2176
PARAMS = 17301504
N_DP = 8


def draw_cotangent(key, part):
    key = jax.random.fold_in(key, 7)
    column = jnp.arange(D, dtype=jnp.float32) / D
    noise = jnp.clip(jax.random.normal(key, (TOKENS, D), jnp.float32), -6.0, 6.0)
    values = noise * (0.5 + column)
    return values.astype(jnp.bfloat16)


def draw_gains(key, part):
    key = jax.random.fold_in(key, 11)
    first, second = jax.random.split(key, 2)
    column = jnp.arange(D, dtype=jnp.float32) / D
    ramp = 1.0 + 2.0 * column
    norms = ramp * jax.random.uniform(first, (2, D), jnp.float32, 0.8, 1.2)
    heads = jax.random.uniform(second, (2 * HD,), jnp.float32, 0.8, 1.2)
    return jnp.concatenate([norms.reshape(2 * D), heads])


def steps_of(rng, extent, pieces, low, largest):
    factor_of, own = 1.0, jax.random.fold_in(rng, 6)
    for axis_at, shards_of in pieces:
        steps = jnp.exp(jax.random.uniform(jax.random.fold_in(own, axis_at), (shards_of,), jnp.float32, low / len(pieces), largest / len(pieces)))
        factor_of = factor_of * jnp.repeat(steps, extent[axis_at] // shards_of).reshape([-1 if axis == axis_at else 1 for axis in range(len(extent))])
    return factor_of


def split_up(number_of, total, reach, slope):
    weights = [(1 << 20) // math.isqrt(grade ** slope) + 1 for grade in range(2, number_of + 1)]
    rest, holding = total - reach - (number_of - 1), [1] * (number_of - 1)
    while rest > 0:
        candidates = [i for i in range(number_of - 1) if holding[i] < reach]
        mass, budget = sum([weights[i] for i in candidates]), rest
        for i in candidates:
            extra = min(reach - holding[i], max(1, budget * weights[i] // mass), rest)
            holding[i] = holding[i] + extra
            rest = rest - extra
    return np.array([reach] + holding)


def ragged_sizes(own_key, count, total, bound, slope):
    if count == 2:
        one = jax.random.randint(own_key, (), max(1, total - bound), min(bound, total - 1) + 1)
        return jnp.stack([one, total - one])
    tallies = jnp.asarray(split_up(count, total, bound, slope), jnp.int32)
    pairs = (count - 1) // 2
    source_of, sink = tallies[1:1 + 2 * pairs:2], tallies[2:2 + 2 * pairs:2]
    slack = jnp.minimum(source_of - 1, bound - sink)
    moved = jax.random.randint(jax.random.fold_in(own_key, 1), (pairs,), 0, 1 << 20) % (slack + 1)
    tallies = tallies.at[1:1 + 2 * pairs:2].set(source_of - moved).at[2:2 + 2 * pairs:2].set(sink + moved)
    return tallies[jax.random.permutation(jax.random.fold_in(own_key, 2), count)]


def scatter_about(own_key, dims, width, most, cuts=(), kind=jnp.bfloat16):
    drawn = jax.random.normal(own_key, dims, jnp.float32) * width
    if len(cuts) > 0:
        drawn = steps_of(own_key, dims, cuts, -0.22, 0.18) * drawn
    return jnp.clip(drawn, min=-most, max=most).astype(kind)


def setup_inputs(seed: int = 0) -> dict:
    streams_of = jax.random.split(jax.random.key(seed), 23)
    tokens = scatter_about(streams_of[0], (TOKENS, D), 1.0, 6.0, ((0, 32),))
    segments = jnp.searchsorted(jnp.cumsum(ragged_sizes(streams_of[1], DOCS, TOKENS, SEQ, 2)), jnp.arange(TOKENS), side="right").astype(jnp.int32)
    cotangent = draw_cotangent(jax.random.fold_in(streams_of[22], 71), 0)
    qkv_weight = scatter_about(streams_of[3], (D, QKV), D ** -0.5, 0.1875, ((1, 4),))
    out_weight = scatter_about(streams_of[4], (QH * HD, D), (max(QH * HD * 16 // SEQ, 16)) ** -0.5, 1.5, ((0, 4),))
    gate_up_weight = scatter_about(streams_of[5], (D, 2, FF), D ** -0.5, 0.1875, ((2, 4),))
    down_weight = scatter_about(streams_of[6], (FF, D), FF ** -0.5, 0.09375, ((0, 4),))
    qkv_master = scatter_about(streams_of[7], (D, QKV), D ** -0.5, 0.1875, ((0, 8), (1, 4)), jnp.float32)
    out_master = scatter_about(streams_of[8], (QH * HD, D), (max(QH * HD * 16 // SEQ, 16)) ** -0.5, 1.5, ((0, 4), (1, 8)), jnp.float32)
    gate_up_master = scatter_about(streams_of[9], (D, 2, FF), D ** -0.5, 0.1875, ((0, 8), (2, 4)), jnp.float32)
    down_master = scatter_about(streams_of[10], (FF, D), FF ** -0.5, 0.09375, ((0, 4), (1, 8)), jnp.float32)
    qkv_mean = scatter_about(streams_of[11], (D, QKV), (0.11 / PARAMS ** 0.5), 0.00036621094, ((0, 8), (1, 4)), jnp.float32)
    out_mean = scatter_about(streams_of[12], (QH * HD, D), (0.04 / PARAMS ** 0.5), 0.00015258789, ((0, 4), (1, 8)), jnp.float32)
    gate_up_mean = scatter_about(streams_of[13], (D, 2, FF), (0.11 / PARAMS ** 0.5), 0.00036621094, ((0, 8), (2, 4)), jnp.float32)
    down_mean = scatter_about(streams_of[14], (FF, D), (0.11 / PARAMS ** 0.5), 0.00036621094, ((0, 4), (1, 8)), jnp.float32)
    qkv_square = jnp.clip(jnp.exp(math.log(1.1559688317674954e-08) - 1.3862944 * jax.random.uniform(streams_of[15], (D, QKV), jnp.float32) ** steps_of(streams_of[15], (D, QKV), ((0, 8), (1, 4)), -0.2, 0.2)), 2.8899220794187386e-09, 1.1559688317674954e-08)
    out_square = jnp.clip(jnp.exp(math.log(1.3871626070027787e-09) - 1.3862944 * jax.random.uniform(streams_of[16], (QH * HD, D), jnp.float32) ** steps_of(streams_of[16], (QH * HD, D), ((0, 4), (1, 8)), -0.2, 0.2)), 3.467906517506947e-10, 1.3871626070027787e-09)
    gate_up_square = jnp.clip(jnp.exp(math.log(1.1559688317674954e-08) - 1.3862944 * jax.random.uniform(streams_of[17], (D, 2, FF), jnp.float32) ** steps_of(streams_of[17], (D, 2, FF), ((0, 8), (2, 4)), -0.2, 0.2)), 2.8899220794187386e-09, 1.1559688317674954e-08)
    down_square = jnp.clip(jnp.exp(math.log(1.1559688317674954e-08) - 1.3862944 * jax.random.uniform(streams_of[18], (FF, D), jnp.float32) ** steps_of(streams_of[18], (FF, D), ((0, 4), (1, 8)), -0.2, 0.2)), 2.8899220794187386e-09, 1.1559688317674954e-08)
    gains = draw_gains(jax.random.fold_in(streams_of[22], 71), 0)
    gains_mean = scatter_about(streams_of[20], (GAINS,), (0.44 / PARAMS ** 0.5), 0.0014648438, (), jnp.float32)
    gains_square = jnp.clip(jnp.exp(jax.random.uniform(streams_of[21], (GAINS,), jnp.float32, math.log(4.623875327069982e-08), math.log(1.8495501308279927e-07))), 4.623875327069982e-08, 1.8495501308279927e-07)
    return {"tokens": tokens, "segments": segments, "cotangent": cotangent, "qkv_weight": qkv_weight, "out_weight": out_weight, "gate_up_weight": gate_up_weight, "down_weight": down_weight, "qkv_master": qkv_master, "out_master": out_master, "gate_up_master": gate_up_master, "down_master": down_master, "qkv_mean": qkv_mean, "out_mean": out_mean, "gate_up_mean": gate_up_mean, "down_mean": down_mean, "qkv_square": qkv_square, "out_square": out_square, "gate_up_square": gate_up_square, "down_square": down_square, "gains": gains, "gains_mean": gains_mean, "gains_square": gains_square}


NORM_EPS = 1e-06
ROPE_BASE = 1000000.0
CLIP_NORM = 1.0
BETA_ONE = 0.9
BETA_TWO = 0.95
ADAM_EPS = 1e-08
DECAY = 0.1
RATE_WEIGHT = 0.02
RATE_GAIN = 1.5
MASKED = -1e+30

@jax.custom_vjp
def low(v):
    return lax.optimization_barrier(v.astype(jnp.bfloat16)).astype(jnp.float32)

@jax.custom_vjp
def low_back(v):
    return v

def low_keep(v):
    return (low(v), None)

def low_pass(kept, grad):
    return (grad,)

def back_keep(v):
    return (v, None)

def back_low(kept, grad):
    return (low(grad),)
low.defvjp(low_keep, low_pass)
low_back.defvjp(back_keep, back_low)

def dense(left, right):
    return jnp.dot(left, right, precision=lax.Precision.HIGHEST, preferred_element_type=jnp.float32)

def rms_scale(value):
    return lax.rsqrt(lax.optimization_barrier(jnp.mean(value * value, axis=-1, keepdims=True)) + NORM_EPS)

def positions_of(seg):
    index = jnp.arange(seg.shape[0], dtype=jnp.int32)
    flag = (index == 0) | (seg != jnp.roll(seg, 1))
    starts = lax.cummax(jnp.where(flag, index, 0), axis=0)
    return (index - starts).astype(jnp.float32)

def rotary(position):
    half = HD // 2
    freq = ROPE_BASE ** (-(jnp.arange(half, dtype=jnp.float32) * 2.0 / HD))
    angle = position[:, None] * freq[None, :]
    return (jnp.cos(angle), jnp.sin(angle))

def rotate(value, cos_table, sin_table):
    half = value.shape[-1] // 2
    shape = (value.shape[0],) + (1,) * (value.ndim - 2) + (half,)
    cosine = cos_table.reshape(shape)
    sine = sin_table.reshape(shape)
    first, second = (value[..., :half], value[..., half:])
    return jnp.concatenate([first * cosine - second * sine, second * cosine + first * sine], axis=-1)

def attend(query, key_rot, value, seg):
    length = query.shape[0]
    block = min(512, length)
    count = length // block
    key_index = jnp.arange(length, dtype=jnp.int32)
    scale = HD ** (-0.5)

    def one_block(item):
        query_block, start = item
        row_index = start + jnp.arange(block, dtype=jnp.int32)
        seg_block = lax.dynamic_slice_in_dim(seg, start, block)
        mask = (seg_block[:, None] == seg[None, :]) & (row_index[:, None] >= key_index[None, :])
        raw = low_back(jnp.einsum('bkgd,skd->kgbs', query_block, key_rot, precision=lax.Precision.HIGHEST, preferred_element_type=jnp.float32))
        scores = jnp.where(mask, raw * scale, MASKED)
        top = lax.optimization_barrier(jnp.max(scores, axis=-1, keepdims=True))
        expo = jnp.exp(scores - top)
        probs = expo / lax.optimization_barrier(jnp.sum(expo, axis=-1, keepdims=True))
        return jnp.einsum('kgbs,skd->bkgd', low(probs), value, precision=lax.Precision.HIGHEST, preferred_element_type=jnp.float32)
    blocks = query.reshape((count, block) + query.shape[1:])
    starts = jnp.arange(count, dtype=jnp.int32) * block
    output = lax.map(jax.checkpoint(one_block), (blocks, starts))
    return output.reshape(query.shape)

def layer(inputs, qkv_w, out_w, gate_up_w, down_w, gain_all, seg):
    length = inputs.shape[0]
    ratio = QH // KVH
    attn_gain = gain_all[:D]
    ffn_gain = gain_all[D:2 * D]
    query_gain = gain_all[2 * D:2 * D + HD]
    key_gain = gain_all[2 * D + HD:]
    cos_table, sin_table = rotary(positions_of(seg))
    normed_one = low(inputs * rms_scale(inputs) * attn_gain)
    joint = low_back(dense(normed_one, qkv_w)).reshape(length, KVH, ratio + 2, HD)
    query_raw = joint[:, :, :ratio]
    key_raw = joint[:, :, ratio]
    query = low(rotate(query_raw * rms_scale(query_raw) * query_gain, cos_table, sin_table))
    key_rot = low(rotate(key_raw * rms_scale(key_raw) * key_gain, cos_table, sin_table))
    value = low(joint[:, :, ratio + 1])
    context = low(low_back(attend(query, key_rot, value, seg))).reshape(length, QH * HD)
    middle = inputs + low_back(dense(context, out_w))
    normed_two = low(middle * rms_scale(middle) * ffn_gain)
    gate_up = low_back(dense(normed_two, gate_up_w.reshape(D, 2 * FF))).reshape(length, 2, FF)
    hidden = low(jax.nn.silu(gate_up[:, 0]) * gate_up[:, 1])
    return middle + low_back(dense(hidden, down_w))

def adam(master, mean, square, grad, factor, rate, decay):
    scaled = grad * factor
    mean_new = BETA_ONE * mean + (1.0 - BETA_ONE) * scaled
    square_new = BETA_TWO * square + (1.0 - BETA_TWO) * scaled * scaled
    mean_hat = mean_new / (1.0 - BETA_ONE ** STEP)
    square_hat = square_new / (1.0 - BETA_TWO ** STEP)
    new = master - rate * (mean_hat / (jnp.sqrt(square_hat) + ADAM_EPS) + decay * master)
    return (new, mean_new, square_new)

def reference(tokens, segments, cotangent, qkv_weight, out_weight, gate_up_weight, down_weight, qkv_master, out_master, gate_up_master, down_master, qkv_mean, out_mean, gate_up_mean, down_mean, qkv_square, out_square, gate_up_square, down_square, gains, gains_mean, gains_square):
    weights = (qkv_weight.astype(jnp.float32), out_weight.astype(jnp.float32), gate_up_weight.astype(jnp.float32), down_weight.astype(jnp.float32), gains)
    token_seqs = tokens.reshape(N_DP, SEQ, D)
    grad_seqs = cotangent.reshape(N_DP, SEQ, D)
    seg_seqs = segments.reshape(N_DP, SEQ)

    def one_seq(total, item):
        token_block, grad_block, seg_block = item

        def forward(inputs, qkv_w, out_w, gate_up_w, down_w, gain_all):
            return layer(inputs, qkv_w, out_w, gate_up_w, down_w, gain_all, seg_block)
        output, pull = jax.vjp(forward, token_block.astype(jnp.float32), *weights)
        grads = pull(grad_block.astype(jnp.float32))
        total = jax.tree.map(lambda acc, grad: acc + grad, total, tuple(grads[1:]))
        return (total, (output.astype(jnp.bfloat16), grads[0].astype(jnp.bfloat16)))
    zeros = tuple((jnp.zeros_like(weight) for weight in weights))
    total, (outputs, input_grads) = lax.scan(one_seq, zeros, (token_seqs, grad_seqs, seg_seqs))
    qkv_grad, out_grad, gate_up_grad, down_grad, gain_grad = total
    squares = jnp.sum(qkv_grad * qkv_grad) + jnp.sum(out_grad * out_grad)
    squares = squares + jnp.sum(gate_up_grad * gate_up_grad) + jnp.sum(down_grad * down_grad)
    squares = squares + jnp.sum(gain_grad * gain_grad)
    grad_norm = jnp.sqrt(squares)
    factor = CLIP_NORM / jnp.maximum(grad_norm, CLIP_NORM)
    out_fan = max(QH * HD * 16 // SEQ, 16)
    out_rate = RATE_WEIGHT * (QH * HD / out_fan) ** 0.5
    qkv_new, qkv_mean_new, qkv_square_new = adam(qkv_master, qkv_mean, qkv_square, qkv_grad, factor, RATE_WEIGHT, DECAY)
    out_new, out_mean_new, out_square_new = adam(out_master, out_mean, out_square, out_grad, factor, out_rate, DECAY)
    gate_up_new, gate_up_mean_new, gate_up_square_new = adam(gate_up_master, gate_up_mean, gate_up_square, gate_up_grad, factor, RATE_WEIGHT, DECAY)
    down_new, down_mean_new, down_square_new = adam(down_master, down_mean, down_square, down_grad, factor, RATE_WEIGHT, DECAY)
    gains_new, gains_mean_new, gains_square_new = adam(gains, gains_mean, gains_square, gain_grad, factor, RATE_GAIN, 0.0)
    return (outputs.reshape(TOKENS, D), input_grads.reshape(TOKENS, D), grad_norm, qkv_new, qkv_new.astype(jnp.bfloat16), qkv_mean_new, qkv_square_new, out_new, out_new.astype(jnp.bfloat16), out_mean_new, out_square_new, gate_up_new, gate_up_new.astype(jnp.bfloat16), gate_up_mean_new, gate_up_square_new, down_new, down_new.astype(jnp.bfloat16), down_mean_new, down_square_new, gains_new, gains_mean_new, gains_square_new)
```

```python
import jax
import jax.numpy as jnp
from jax import lax
from jax.experimental import pallas as pl
from jax.experimental.pallas import tpu as pltpu
from jax.sharding import PartitionSpec as P

QH = 16
KVH = 8
HD = 64
STEP = 5


NORM_EPS = 1e-06
ROPE_BASE = 1000000.0
CLIP_NORM = 1.0
BETA_ONE = 0.9
BETA_TWO = 0.95
ADAM_EPS = 1e-08
DECAY = 0.1
RATE_WEIGHT = 0.02
RATE_GAIN = 1.5
MASKED = -1e30

KINDS = QH // KVH + 2
RATIO = QH // KVH
PIECES = 4
HALVES = 2
CORE = 1
ACROSS = 2
MIB = 1024 * 1024


def params(limit=60):
    return pltpu.CompilerParams(vmem_limit_bytes=limit * MIB)


def cost(flops, size):
    return pl.CostEstimate(flops=flops, bytes_accessed=size, transcendentals=0)


def starts_of(seg):
    index = jnp.arange(seg.shape[0], dtype=jnp.int32)
    flag = (index == 0) | (seg != jnp.roll(seg, 1))
    return lax.cummax(jnp.where(flag, index, 0), axis=0)


def rotary(position):
    half = HD // 2
    freq = ROPE_BASE ** (-(jnp.arange(half, dtype=jnp.float32) * 2.0 / HD))
    angle = freq[:, None] * position[None, :]
    return (jnp.cos(angle), jnp.sin(angle))


def dot_nn(left, right):
    return lax.dot_general(
        left, right, (((1,), (0,)), ((), ())), preferred_element_type=jnp.float32
    )


def dot_nt(left, right):
    return lax.dot_general(
        left, right, (((1,), (1,)), ((), ())), preferred_element_type=jnp.float32
    )


def contract_rows(left, right):
    return lax.dot_general(
        left, right, (((0,), (0,)), ((), ())), preferred_element_type=jnp.float32
    )


def rotate(value, cosine, sine):
    half = value.shape[0] // 2
    first, second = (value[:half], value[half:])
    return jnp.concatenate(
        [first * cosine - second * sine, second * cosine + first * sine], axis=0
    )


def rotate_back(grad, cosine, sine):
    half = grad.shape[0] // 2
    first, second = (grad[:half], grad[half:])
    return jnp.concatenate(
        [first * cosine + second * sine, second * cosine - first * sine], axis=0
    )


def row_scale(value):
    return lax.rsqrt(jnp.mean(value * value, axis=-1, keepdims=True) + NORM_EPS)


def head_scale(value):
    return lax.rsqrt(jnp.mean(value * value, axis=0, keepdims=True) + NORM_EPS)


def project_kernel(place_ref, *refs):
    pieces = refs[:2]
    pre_ref, weight_ref, gain_ref, cos_ref, sin_ref = refs[2:7]
    normed_ref, raw_ref, flip_ref, row_ref = refs[-4:]
    step = pl.program_id(0)
    for r in range(2):

        @pl.when(step == r)
        def _(r=r):
            value = pieces[r][...].astype(jnp.float32)
            normed_ref[...] = (value * row_scale(value) * pre_ref[...]).astype(jnp.bfloat16)

    joint = dot_nt(weight_ref[...], normed_ref[...])
    cosine, sine = cos_ref[...], sin_ref[...]
    for slot in range(raw_ref.shape[0]):
        kind = slot % KINDS
        raw = joint[slot * HD : (slot + 1) * HD]
        raw_ref[slot] = raw
        value = raw
        if kind < KINDS - 1:
            gain = gain_ref[:, 1:2] if kind == KINDS - 2 else gain_ref[:, 0:1]
            value = rotate(raw * head_scale(raw) * gain, cosine, sine)
        if kind < KINDS - 2:
            value = value * HD ** (-0.5)
        low = value.astype(jnp.bfloat16)
        flip_ref[slot] = low
        row_ref[slot] = low.T


def project(far, earlier, place, pieces, pre_gain, weight_rows, head_gains, cos_table, sin_table):
    block, width = pieces[0].shape
    length = block * PIECES
    slots = weight_rows.shape[0] // HD
    at = lambda i, p: (i + 2 * far) ^ p[0]
    return pl.pallas_call(
        project_kernel,
        grid_spec=pltpu.PrefetchScalarGridSpec(
            num_scalar_prefetch=1,
            grid=(2,),
            in_specs=[pl.BlockSpec((block, width), lambda i, p: (0, 0))] * 2
            + [
                pl.BlockSpec(pre_gain.shape, lambda i, p: (0, 0)),
                pl.BlockSpec(weight_rows.shape, lambda i, p: (0, 0)),
                pl.BlockSpec(head_gains.shape, lambda i, p: (0, 0)),
                pl.BlockSpec((HD // 2, block), lambda i, p: (0, at(i, p))),
                pl.BlockSpec((HD // 2, block), lambda i, p: (0, at(i, p))),
            ]
            + [pl.BlockSpec(memory_space=pl.ANY)] * len(earlier),
            out_specs=[
                pl.BlockSpec((block, width), lambda i, p: (at(i, p), 0)),
                pl.BlockSpec((slots, HD, block), lambda i, p: (0, 0, at(i, p))),
                pl.BlockSpec((slots, HD, block), lambda i, p: (0, 0, at(i, p))),
                pl.BlockSpec((slots, block, HD), lambda i, p: (0, at(i, p), 0)),
            ],
        ),
        out_shape=[
            jax.ShapeDtypeStruct((length, width), jnp.bfloat16),
            jax.ShapeDtypeStruct((slots, HD, length), jnp.float32),
            jax.ShapeDtypeStruct((slots, HD, length), jnp.bfloat16),
            jax.ShapeDtypeStruct((slots, length, HD), jnp.bfloat16),
        ],
        input_output_aliases={8 + k: k for k in range(len(earlier))},
        compiler_params=params(),
        cost_estimate=cost(length * width * slots * HD, 8 * MIB),
        name="project",
    )(place, *pieces, pre_gain, weight_rows, head_gains, cos_table, sin_table, *earlier)


def mask_of(start_row, first_key, first_query, keys):
    queries = start_row.shape[1]
    key = first_key + lax.broadcasted_iota(jnp.int32, (keys, 1), 0)
    query = first_query + lax.broadcasted_iota(jnp.int32, (1, queries), 1)
    return (key >= start_row) & (key <= query)


def over_keys(one, first, last, at_query, block):
    begin = first // block
    whole = jnp.maximum(begin, jnp.minimum((last + block - 1) // block, at_query))
    pairs = (at_query - whole) // 2
    lax.fori_loop(begin, whole, lambda j, carry: one(True, j * block, block), None)
    lax.fori_loop(
        0, pairs, lambda k, carry: one(False, (whole + 2 * k) * block, 2 * block), None
    )
    lax.fori_loop(
        whole + 2 * pairs, at_query, lambda j, carry: one(False, j * block, block), None
    )
    one(True, at_query * block, block)


def attend_kernel(half, first_ref, last_ref, place_ref, *refs):
    query_ref, key_ref, value_ref, start_ref, weight_ref = refs[:5]
    context_ref, flip_ref, log_ref, send_ref, keep_ref, top_ref, total_ref, sum_ref = refs[-8:]
    groups, ratio = query_ref.shape[:2]
    block = start_ref.shape[1]
    step = pl.program_id(0)
    at_query = HALVES * (step ^ place_ref[0]) + half
    start_row = start_ref[...]
    queries = [
        jnp.concatenate([query_ref[g, h] for h in range(ratio)], axis=1) for g in range(groups)
    ]
    top_ref[...] = jnp.full_like(top_ref, MASKED)
    total_ref[...] = jnp.zeros_like(total_ref)
    sum_ref[...] = jnp.zeros_like(sum_ref)

    def one(masked, at, size):
        at = pl.multiple_of(at, block)
        if masked:
            mask = mask_of(start_row, at, at_query * block, size)
            mask = jnp.concatenate([mask] * ratio, axis=1)
        for g in range(groups):
            scores = dot_nn(key_ref[g, pl.ds(at, size), :], queries[g])
            if masked:
                scores = jnp.where(mask, scores, MASKED)
            top_old = top_ref[g]
            top = jnp.maximum(top_old, jnp.max(scores, axis=0, keepdims=True))
            expo = jnp.exp(scores - top)
            fade = jnp.exp(top_old - top)
            top_ref[g] = top
            total_ref[g] = total_ref[g] * fade + jnp.sum(expo, axis=0, keepdims=True)
            part = dot_nn(value_ref[g, :, pl.ds(at, size)], expo.astype(jnp.bfloat16))
            sum_ref[g] = sum_ref[g] * fade + part

    over_keys(one, first_ref[at_query], last_ref[at_query], at_query, block)
    wide = ratio * HD
    for g in range(groups):
        total = total_ref[g]
        output = sum_ref[g] / total
        both = jnp.concatenate(
            [output[:, h * block : (h + 1) * block] for h in range(ratio)], axis=0
        )
        flip_ref[g * wide : (g + 1) * wide, :] = both.astype(jnp.bfloat16)
        context_ref[:, g * wide : (g + 1) * wide] = both.T.astype(jnp.bfloat16)
        log_total = top_ref[g] + jnp.log(total)
        for h in range(ratio):
            log_ref[g, h] = log_total[:, h * block : (h + 1) * block]
    part = dot_nn(context_ref[...], weight_ref[...]).astype(jnp.bfloat16)

    @pl.when(step % 2 == 1)
    def _():
        send_ref[...] = part

    @pl.when(step % 2 == 0)
    def _():
        keep_ref[...] = part


def attend(half, earlier, place, flipped, rows, starts, weight):
    slots, _, length = flipped.shape
    groups = slots // KINDS
    block = length // PIECES // HALVES
    width = weight.shape[1]
    wide = groups * RATIO * HD
    at = lambda i, p: HALVES * (i ^ p[0]) + half
    flip_four = flipped.reshape(groups, KINDS, HD, length)
    row_four = rows.reshape(groups, KINDS, length, HD)
    out = jax.ShapeDtypeStruct((PIECES // 2, block, width), jnp.bfloat16)
    outs = pl.pallas_call(
        lambda *refs: attend_kernel(half, *refs),
        grid_spec=pltpu.PrefetchScalarGridSpec(
            num_scalar_prefetch=3,
            grid=(PIECES,),
            in_specs=[
                pl.BlockSpec((groups, RATIO, HD, block), lambda i, f, l, p: (0, 0, 0, at(i, p))),
                pl.BlockSpec((groups, None, length, HD), lambda i, f, l, p: (0, RATIO, 0, 0)),
                pl.BlockSpec((groups, None, HD, length), lambda i, f, l, p: (0, RATIO + 1, 0, 0)),
                pl.BlockSpec((1, block), lambda i, f, l, p: (0, at(i, p))),
                pl.BlockSpec(weight.shape, lambda i, f, l, p: (0, 0)),
            ]
            + [pl.BlockSpec(memory_space=pl.ANY)] * len(earlier),
            out_specs=[
                pl.BlockSpec((block, wide), lambda i, f, l, p: (at(i, p), 0)),
                pl.BlockSpec((wide, block), lambda i, f, l, p: (0, at(i, p))),
                pl.BlockSpec((groups, RATIO, 1, block), lambda i, f, l, p: (0, 0, 0, at(i, p))),
                pl.BlockSpec((None, block, width), lambda i, f, l, p: (i // 2, 0, 0)),
                pl.BlockSpec((None, block, width), lambda i, f, l, p: (i // 2, 0, 0)),
            ],
            scratch_shapes=[
                pltpu.VMEM((groups, 1, RATIO * block), jnp.float32),
                pltpu.VMEM((groups, 1, RATIO * block), jnp.float32),
                pltpu.VMEM((groups, HD, RATIO * block), jnp.float32),
            ],
        ),
        out_shape=[
            jax.ShapeDtypeStruct((length, wide), jnp.bfloat16),
            jax.ShapeDtypeStruct((wide, length), jnp.bfloat16),
            jax.ShapeDtypeStruct((groups, RATIO, 1, length), jnp.float32),
            out,
            out,
        ],
        input_output_aliases={8 + k: k for k in range(len(earlier))},
        compiler_params=params(),
        cost_estimate=cost(8 * groups * length * length * 64, 6 * MIB),
        name="attend",
    )(
        starts[::block], starts[block - 1 :: block], place, flip_four, row_four, flip_four,
        starts[None, :], weight, *earlier,
    )
    return (outs[:3], outs[3], outs[4])


def attend_back_kernel(pieces, first_ref, last_ref, place_ref, *refs):
    (query_ref, query_row_ref, key_ref, key_row_ref, value_row_ref, context_ref, log_ref,
     start_ref, weight_ref, raw_ref, raw_key_ref, cos_ref, sin_ref, gain_ref) = refs[:14]
    dh_pieces = refs[14 : 14 + pieces]
    if pieces > 1:
        joint_ref, gain_grad_ref, dh_ref = refs[14 + pieces : 17 + pieces]
    else:
        joint_ref, gain_grad_ref = refs[14 + pieces : 16 + pieces]
        dh_ref = dh_pieces[0]
    query_sum, key_sum, value_sum, query_gain_sum = refs[-4:]
    block = start_ref.shape[1]
    step = pl.program_id(0)
    steps = pl.num_programs(0)
    ratio = query_ref.shape[0]
    wide = ratio * HD

    @pl.when(step == 0)
    def _():
        key_sum[...] = jnp.zeros_like(key_sum)
        value_sum[...] = jnp.zeros_like(value_sum)
        query_gain_sum[...] = jnp.zeros_like(query_gain_sum)

    if pieces > 1:
        source = HALVES * ((step // HALVES) ^ place_ref[0]) + step % HALVES
        for r, piece in enumerate(dh_pieces):

            @pl.when(source == r)
            def _(piece=piece):
                dh_ref[...] = piece[...]

    query = jnp.concatenate([query_ref[h] for h in range(ratio)], axis=1)
    query_row = jnp.concatenate([query_row_ref[h] for h in range(ratio)], axis=0)
    start_row = start_ref[...]
    grad_wide = dot_nt(weight_ref[...], dh_ref[...]).astype(jnp.bfloat16)
    grad_float = grad_wide.astype(jnp.float32)
    products = grad_float * context_ref[...].astype(jnp.float32)
    delta = jnp.concatenate(
        [
            jnp.sum(products[h * HD : (h + 1) * HD], axis=0, keepdims=True)
            for h in range(ratio)
        ],
        axis=1,
    )
    grad = jnp.concatenate([grad_wide[h * HD : (h + 1) * HD] for h in range(ratio)], axis=1)
    turned = grad_float.T.astype(jnp.bfloat16)
    grad_row = jnp.concatenate([turned[:, h * HD : (h + 1) * HD] for h in range(ratio)], axis=0)
    log_total = jnp.concatenate([log_ref[h] for h in range(ratio)], axis=1)
    query_sum[...] = jnp.zeros_like(query_sum)

    def one(masked, at, size):
        at = pl.multiple_of(at, block)
        here = pl.ds(at, size)
        probs = jnp.exp(dot_nn(key_row_ref[here, :], query) - log_total)
        if masked:
            mask = mask_of(start_row, at, step * block, size)
            probs = jnp.where(jnp.concatenate([mask] * ratio, axis=1), probs, 0.0)
        prob_grad = dot_nn(value_row_ref[here, :], grad)
        score_grad = (probs * (prob_grad - delta)).astype(jnp.bfloat16)
        value_sum[here, :] += dot_nn(probs.astype(jnp.bfloat16), grad_row)
        key_sum[here, :] += dot_nn(score_grad, query_row)
        query_sum[...] += dot_nn(key_ref[:, here], score_grad)

    over_keys(one, first_ref[step], last_ref[step], step, block)

    def unwind(part, raw, cosine, sine, gain):
        inverse = head_scale(raw)
        back = rotate_back(part, cosine, sine)
        scaled = back * gain
        lean = jnp.mean(scaled * raw, axis=0, keepdims=True)
        return (back * raw * inverse, inverse * scaled - raw * inverse**3 * lean)

    at = pl.multiple_of(step * block, block)
    here = pl.ds(at, block)
    outs = []
    for h in range(ratio):
        part = query_sum[:, h * block : (h + 1) * block] * HD ** (-0.5)
        gain_part, out = unwind(
            part, raw_ref[h], cos_ref[:, here], sin_ref[:, here], gain_ref[:, 0:1]
        )
        query_gain_sum[...] += gain_part
        outs.append(out)
    joint_ref[here, :wide] = jnp.concatenate(outs, axis=0).T.astype(jnp.bfloat16)

    @pl.when(step == steps - 1)
    def _():
        def one_key(j, total):
            at = pl.multiple_of(j * block, block)
            here = pl.ds(at, block)
            pair = jnp.concatenate([key_sum[here, :], value_sum[here, :]], axis=1).T
            gain_part, out = unwind(
                pair[:HD], raw_key_ref[:, here], cos_ref[:, here], sin_ref[:, here],
                gain_ref[:, 1:2],
            )
            both = jnp.concatenate([out, pair[HD:]], axis=0)
            joint_ref[here, wide:] = both.T.astype(jnp.bfloat16)
            return total + gain_part

        key_gain_sum = lax.fori_loop(
            0, steps, one_key, jnp.zeros(query_gain_sum.shape, jnp.float32)
        )
        both = jnp.concatenate([query_gain_sum[...], key_gain_sum], axis=0).T
        gain_grad_ref[...] = jnp.sum(both, axis=0, keepdims=True)


def attend_back(
    g, place, flipped, rows, context_flip, log_total, starts, dh, weight, raw, tables, head_gains
):
    slots, _, length = flipped.shape
    groups = slots // KINDS
    ratio = RATIO
    block = length // PIECES // HALVES
    wide = ratio * HD
    width = weight.shape[1]
    pieces = len(dh)
    flip_four = flipped.reshape(groups, KINDS, HD, length)
    row_four = rows.reshape(groups, KINDS, length, HD)
    raw_four = raw.reshape(groups, KINDS, HD, length)
    by_step = pl.BlockSpec((block, width), lambda i, f, l, p: (i, 0))
    whole = pl.BlockSpec((block, width), lambda i, f, l, p: (0, 0))
    outs = pl.pallas_call(
        lambda *refs: attend_back_kernel(pieces, *refs),
        grid_spec=pltpu.PrefetchScalarGridSpec(
            num_scalar_prefetch=3,
            grid=(length // block,),
            in_specs=[
                pl.BlockSpec((None, ratio, HD, block), lambda i, f, l, p: (g, 0, 0, i)),
                pl.BlockSpec((None, ratio, block, HD), lambda i, f, l, p: (g, 0, i, 0)),
                pl.BlockSpec((None, None, HD, length), lambda i, f, l, p: (g, ratio, 0, 0)),
                pl.BlockSpec((None, None, length, HD), lambda i, f, l, p: (g, ratio, 0, 0)),
                pl.BlockSpec((None, None, length, HD), lambda i, f, l, p: (g, ratio + 1, 0, 0)),
                pl.BlockSpec((wide, block), lambda i, f, l, p: (g, i)),
                pl.BlockSpec((None, ratio, 1, block), lambda i, f, l, p: (g, 0, 0, i)),
                pl.BlockSpec((1, block), lambda i, f, l, p: (0, i)),
                pl.BlockSpec((wide, width), lambda i, f, l, p: (g, 0)),
                pl.BlockSpec((None, ratio, HD, block), lambda i, f, l, p: (g, 0, 0, i)),
                pl.BlockSpec((None, None, HD, length), lambda i, f, l, p: (g, ratio, 0, 0)),
                pl.BlockSpec((HD // 2, length), lambda i, f, l, p: (0, 0)),
                pl.BlockSpec((HD // 2, length), lambda i, f, l, p: (0, 0)),
                pl.BlockSpec(head_gains.shape, lambda i, f, l, p: (0, 0)),
            ]
            + [whole if pieces > 1 else by_step] * pieces,
            out_specs=[
                pl.BlockSpec((length, wide + 2 * HD), lambda i, f, l, p: (0, 0)),
                pl.BlockSpec((1, 2 * HD), lambda i, f, l, p: (0, 0)),
            ]
            + [by_step] * (pieces > 1),
            scratch_shapes=[
                pltpu.VMEM((HD, ratio * block), jnp.float32),
                pltpu.VMEM((length, HD), jnp.float32),
                pltpu.VMEM((length, HD), jnp.float32),
                pltpu.VMEM((HD, block), jnp.float32),
            ],
        ),
        out_shape=[
            jax.ShapeDtypeStruct((length, wide + 2 * HD), jnp.bfloat16),
            jax.ShapeDtypeStruct((1, 2 * HD), jnp.float32),
        ]
        + [jax.ShapeDtypeStruct((length, width), jnp.bfloat16)] * (pieces > 1),
        compiler_params=params(),
        cost_estimate=cost(20 * length * length * 128, 12 * MIB),
        name="attend_back",
    )(
        starts[::block], starts[block - 1 :: block], place, flip_four, row_four, flip_four, row_four, row_four, context_flip,
        log_total, starts[None, :], weight, raw_four, raw_four, tables[0], tables[1],
        head_gains, *dh,
    )
    return outs


def spread_kernel(groups, place_ref, *refs):
    send_rows, keep_rows = refs[:groups], refs[groups : 2 * groups]
    weight_ref, send_out, keep_out = refs[2 * groups :]
    depth = weight_ref.shape[0] // groups
    for rows, out in ((send_rows, send_out), (keep_rows, keep_out)):
        joined = jnp.concatenate([row[...] for row in rows], axis=1)
        out[...] = dot_nn(joined, weight_ref[...]).astype(jnp.bfloat16)


def spread(place, rows, weight):
    groups = len(rows)
    length, depth = rows[0].shape
    width = weight.shape[1]
    block = length // PIECES
    out = jax.ShapeDtypeStruct((PIECES // 2, block, width), jnp.bfloat16)
    return pl.pallas_call(
        lambda *refs: spread_kernel(groups, *refs),
        grid_spec=pltpu.PrefetchScalarGridSpec(
            num_scalar_prefetch=1,
            grid=(PIECES // 2,),
            in_specs=[pl.BlockSpec((block, depth), lambda i, p: ((2 * i + 1) ^ p[0], 0))] * groups
            + [pl.BlockSpec((block, depth), lambda i, p: ((2 * i) ^ p[0], 0))] * groups
            + [pl.BlockSpec(weight.shape, lambda i, p: (0, 0))],
            out_specs=[pl.BlockSpec((None, block, width), lambda i, p: (i, 0, 0))] * 2,
        ),
        out_shape=[out, out],
        compiler_params=params(),
        cost_estimate=cost(2 * length * width * depth * groups, 6 * MIB),
        name="spread",
    )(place, *rows, *rows, weight)


def feed_kernel(*refs):
    xs, grads, joint_ref, down_ref = refs[:2], refs[2:4], refs[4], refs[5]
    x_ref, grad_ref, hidden_ref, low_ref, out_keep, out_send, back_keep, back_send = refs[-8:]
    hidden_width = down_ref.shape[0]
    block = xs[0].shape[0]
    for r in range(2):
        x_ref[r * block : (r + 1) * block, :] = xs[r][...]
        grad_ref[r * block : (r + 1) * block, :] = grads[r][...]
    both = dot_nn(x_ref[...], joint_ref[...])
    gate, up = (both[:, :hidden_width], both[:, hidden_width:])
    sigmoid = 1.0 / (1.0 + jnp.exp(-gate))
    swish = gate * sigmoid
    hidden = (swish * up).astype(jnp.bfloat16)
    hidden_ref[...] = hidden
    hidden_grad = dot_nt(grad_ref[...], down_ref[...])
    low_ref[:, :hidden_width] = (
        hidden_grad * up * sigmoid * (1.0 + gate * (1.0 - sigmoid))
    ).astype(jnp.bfloat16)
    low_ref[:, hidden_width:] = (hidden_grad * swish).astype(jnp.bfloat16)
    out = dot_nn(hidden, down_ref[...]).astype(jnp.bfloat16)
    out_keep[...] = out[:block]
    out_send[...] = out[block:]
    back = dot_nt(low_ref[...], joint_ref[...]).astype(jnp.bfloat16)
    back_keep[...] = back[:block]
    back_send[...] = back[block:]


def feed(call, half, earlier, normed, grads, joint_weight, down_weight):
    block, width = normed[0].shape
    hidden_width = down_weight.shape[0]
    length = block * PIECES * HALVES
    once = pl.Buffered(1)
    row = lambda columns: pl.BlockSpec((2 * block, columns), lambda i: (call, 0))
    whole = lambda value: pl.BlockSpec(value.shape, lambda i: (0, 0), pipeline_mode=once)
    pair = pl.BlockSpec((block, width), lambda i: (0, 0))
    full = lambda columns: jax.ShapeDtypeStruct((length, columns), jnp.bfloat16)
    outs = pl.pallas_call(
        feed_kernel,
        grid=(1,),
        in_specs=[pl.BlockSpec((block, width), lambda i: (0, 0), pipeline_mode=once)] * 2
        + [pl.BlockSpec((block, width), lambda i: (half, 0), pipeline_mode=once)] * 2
        + [whole(joint_weight), whole(down_weight)]
        + [pl.BlockSpec(memory_space=pl.ANY)] * len(earlier),
        out_specs=[row(width), row(width), row(hidden_width), row(2 * hidden_width)] + [pair] * 4,
        out_shape=[full(width), full(width), full(hidden_width), full(2 * hidden_width)]
        + [jax.ShapeDtypeStruct((block, width), jnp.bfloat16)] * 4,
        input_output_aliases={6 + k: k for k in range(len(earlier))},
        compiler_params=params(),
        cost_estimate=cost(3 * length * width * hidden_width, 16 * MIB),
        name="feed",
    )(*normed, *grads, joint_weight, down_weight, *earlier)
    return (outs[:4], outs[4:6], outs[6:8])


def norm_kernel(x_ref, keep_ref, near_ref, far_ref, gain_ref, middle_ref, normed_ref):
    f32 = jnp.float32
    middle = x_ref[...].astype(f32) + (
        keep_ref[...].astype(f32) + near_ref[...].astype(f32) + far_ref[...].astype(f32)
    )
    middle_ref[...] = middle
    normed_ref[...] = (middle * row_scale(middle) * gain_ref[...]).astype(jnp.bfloat16)


def first_of(value, rows, width):
    if value.ndim == 3:
        return pl.BlockSpec((None, rows, width), lambda i: (0, i, 0))
    return pl.BlockSpec((rows, width), lambda i: (i, 0))


def norm(half, tokens, keep, near, far, gain):
    length, width = far.shape
    steps = 2
    rows = length // steps
    flat = pl.BlockSpec((rows, width), lambda i: (i, 0))
    return pl.pallas_call(
        norm_kernel,
        grid=(steps,),
        in_specs=[
            pl.BlockSpec((rows, width), lambda i: (half * steps + i, 0)),
            first_of(keep, rows, width),
            first_of(near, rows, width),
            flat,
            pl.BlockSpec(gain.shape, lambda i: (0, 0)),
        ],
        out_specs=[flat, flat],
        out_shape=[
            jax.ShapeDtypeStruct((length, width), jnp.float32),
            jax.ShapeDtypeStruct((length, width), jnp.bfloat16),
        ],
        compiler_params=params(),
        cost_estimate=cost(0, 4 * MIB),
        name="norm",
    )(tokens, keep, near, far, gain)


def norm_back_of(value, skip, grad, gain):
    inverse = row_scale(value)
    scaled = grad * gain
    lean = jnp.mean(scaled * value, axis=-1, keepdims=True)
    total = skip + (inverse * scaled - value * (inverse**3 * lean))
    return total, jnp.sum(grad * value * inverse, axis=0, keepdims=True)


def norm_back_kernel(
    value_ref, skip_ref, keep_ref, near_ref, far_ref, gain_ref, low_ref, part_ref
):
    f32 = jnp.float32
    grad = keep_ref[...].astype(f32) + near_ref[...].astype(f32) + far_ref[...].astype(f32)
    total, part = norm_back_of(value_ref[...], skip_ref[...].astype(f32), grad, gain_ref[...])
    low_ref[...] = total.astype(jnp.bfloat16)

    @pl.when(pl.program_id(0) == 0)
    def _():
        part_ref[...] = jnp.zeros_like(part_ref)

    part_ref[...] += part


def norm_back(half, value, skip, keep, near, far, gain):
    length, width = far.shape
    steps = 2
    rows = length // steps
    flat = pl.BlockSpec((rows, width), lambda i: (i, 0))
    return pl.pallas_call(
        norm_back_kernel,
        grid=(steps,),
        in_specs=[
            flat,
            pl.BlockSpec((rows, width), lambda i: (half * steps + i, 0)),
            first_of(keep, rows, width),
            first_of(near, rows, width),
            flat,
            pl.BlockSpec(gain.shape, lambda i: (0, 0)),
        ],
        out_specs=[flat, pl.BlockSpec((1, width), lambda i: (0, 0))],
        out_shape=[
            jax.ShapeDtypeStruct((length, width), jnp.bfloat16),
            jax.ShapeDtypeStruct((1, width), jnp.float32),
        ],
        compiler_params=params(),
        cost_estimate=cost(0, 6 * MIB),
        name="norm_back",
    )(value, skip, keep, near, far, gain)


def row_kernel(counts, *refs):
    row_ref, scatter_ref = refs[-1], refs[-2]
    parts, heads, squares = refs[: counts[0]], refs[counts[0] : counts[1]], refs[counts[1] : -2]
    width = parts[0].shape[1]
    total = lambda items: sum([item[...] for item in items[1:]], items[0][...])
    row_ref[:, :width] = jnp.zeros((1, width), jnp.float32)
    row_ref[:, width : 2 * width] = total(parts)
    row_ref[:, 2 * width : 2 * width + 2 * HD] = total(heads)
    scattered = scatter_ref[...].astype(jnp.float32)
    over = jnp.sum(scattered * scattered, axis=0, keepdims=True)
    square = jnp.sum(over, axis=1, keepdims=True) + total(squares)
    lane = lax.broadcasted_iota(jnp.int32, (1, 2 * HD), 1)
    row_ref[:, 2 * width + 2 * HD :] = jnp.where(lane == 0, square, 0.0)


def row_of(parts, heads, squares, scattered):
    counts = (len(parts), len(parts) + len(heads))
    return pl.pallas_call(
        lambda *refs: row_kernel(counts, *refs),
        out_shape=jax.ShapeDtypeStruct((1, 2 * parts[0].shape[1] + 4 * HD), jnp.float32),
        compiler_params=params(24),
        cost_estimate=cost(0, MIB),
        name="row",
    )(*parts, *heads, *squares, scattered)


def finish_kernel(
    x_ref, near_skip, far_skip, keep_ref, near_ref, far_ref, gain_ref, begin_ref,
    input_grad_ref, row_ref,
):
    f32 = jnp.float32
    step = pl.program_id(0)
    width = x_ref.shape[1]
    grad = keep_ref[...].astype(f32) + near_ref[...].astype(f32) + far_ref[...].astype(f32)
    skip = jnp.where(step < pl.num_programs(0) // HALVES, near_skip[...], far_skip[...])
    total, part = norm_back_of(
        x_ref[...].astype(f32), skip.astype(f32), grad, gain_ref[...]
    )
    input_grad_ref[...] = total.astype(jnp.bfloat16)

    @pl.when(step == 0)
    def _():
        row_ref[...] = begin_ref[...]

    row_ref[:, :width] += part


def finish(tokens, skips, keep, near, far, gain, row):
    length, width = far.shape
    each = 1
    rows = length // HALVES // each
    flat = pl.BlockSpec((rows, width), lambda i: (i, 0))
    whole = lambda value: pl.BlockSpec(value.shape, lambda i: (0, 0))
    return pl.pallas_call(
        finish_kernel,
        grid=(HALVES * each,),
        in_specs=[
            flat,
            pl.BlockSpec((rows, width), lambda i: (jnp.minimum(i, each - 1), 0)),
            pl.BlockSpec((rows, width), lambda i: (jnp.maximum(i - each, 0), 0)),
            first_of(keep, rows, width),
            first_of(near, rows, width),
            flat,
            whole(gain),
            whole(row),
        ],
        out_specs=[flat, whole(row)],
        out_shape=[
            jax.ShapeDtypeStruct((length, width), jnp.bfloat16),
            jax.ShapeDtypeStruct(row.shape, jnp.float32),
        ],
        compiler_params=params(),
        cost_estimate=cost(0, 6 * MIB),
        name="finish",
    )(tokens, *skips, keep, near, far, gain, row)


def exchange(value, axis, bit):
    size = lax.axis_size(axis)
    return lax.ppermute(value, axis, [(i, i ^ bit) for i in range(size)])


def after(value, *others):
    return lax.optimization_barrier((value, *others))[0]


def power_of_two(count):
    return count & (count - 1) == 0


class ScatterSum:
    def __init__(self, grads, flipped):
        size = lax.axis_size("dp")
        rows = grads[0].shape[0] // size
        self.left = [1 << k for k in reversed(range(size.bit_length() - 1))]
        self.order = self.left[::-1]
        self.flipped = flipped
        self.sources = [grad.reshape(size, rows, grad.shape[1]) for grad in grads]
        self.columns = sum(grad.shape[1] for grad in grads)
        self.joined = True
        self.total = None


def advance_kernel(plans, here_ref, *refs):
    count = sum(plan[0] for plan in plans)
    ins, outs = refs[:count], refs[count:]
    squares = jnp.zeros((1, 1), jnp.float32)
    for sources, joined, stride, shift, flipped in plans:
        parts, ins = ins[:sources], ins[sources:]

        def value(at, parts=parts, joined=joined):
            if joined:
                return jnp.concatenate([part[at] for part in parts], axis=1)
            return parts[0][at].astype(jnp.float32) + parts[1][at].astype(jnp.float32)

        if stride is None:
            total = value(0).astype(jnp.float32)
            over = jnp.sum(total * total, axis=0, keepdims=True)
            squares += jnp.sum(over, axis=1, keepdims=True)
            at = 0
            for columns, turned in flipped:
                part = total[:, at : at + columns]
                outs[0][...] = part.T if turned else part
                at, outs = at + columns, outs[1:]
            continue
        sent, kept, outs = outs[0], outs[1], outs[2:]
        own = (here_ref[0] >> shift) & 1
        for k in range(sent.shape[0]):
            base = k // stride * 2 * stride + k % stride
            sent[k] = value(base + (1 - own) * stride).astype(sent.dtype)
            kept[k] = value(base + own * stride).astype(kept.dtype)
    outs[0][...] = squares


def advance(here, items, *gates):
    plans, ins, shapes = [], [], []
    for item in items:
        rows, columns = item.sources[0].shape[1], item.columns
        if item.order:
            bit = item.order[0]
            at = item.left.index(bit)
            stride = 1 << (len(item.left) - 1 - at)
            plans.append((len(item.sources), item.joined, stride, bit.bit_length() - 1, ()))
            half = (item.sources[0].shape[0] // 2, rows, columns)
            shapes += [jax.ShapeDtypeStruct(half, jnp.bfloat16)] * 2
        else:
            plans.append((len(item.sources), item.joined, None, 0, item.flipped))
            for part, turned in item.flipped:
                shape = (part, rows) if turned else (rows, part)
                shapes.append(jax.ShapeDtypeStruct(shape, jnp.float32))
        ins += item.sources
    shapes.append(jax.ShapeDtypeStruct((1, 1), jnp.float32))
    if gates:
        ins[-1] = after(ins[-1], *gates)
    vmem = pl.BlockSpec(memory_space=pltpu.VMEM)
    outs = list(pl.pallas_call(
        lambda *refs: advance_kernel(plans, *refs),
        in_specs=[pl.BlockSpec(memory_space=pltpu.SMEM)] + [vmem] * len(ins),
        out_specs=[vmem] * len(shapes),
        out_shape=shapes,
        compiler_params=params(24),
        cost_estimate=cost(0, 6 * MIB),
        name="advance",
    )(here, *ins))
    sent_all = []
    for item in items:
        if item.order:
            bit = item.order.pop(0)
            item.left.remove(bit)
            sent, kept = outs.pop(0), outs.pop(0)
            item.sources, item.joined = [kept, exchange(sent, "dp", bit)], False
            sent_all.append(sent)
        else:
            item.total = [outs.pop(0) for _ in item.flipped]
    return sent_all, outs[0]


def sum_all(value):
    for axis in ("tensor", "dp"):
        size = lax.axis_size(axis)
        if not power_of_two(size):
            value = lax.psum(value, axis)
            continue
        bit = 1
        while bit < size:
            if 2 * bit < size:
                one, two, three = [exchange(value, axis, bit * k) for k in (1, 2, 3)]
                value = (value + one) + (two + three)
                bit *= 4
            else:
                value = value + exchange(value, axis, bit)
                bit *= 2
    return value


def adam(master, mean, square, grad, factor, rate, decay):
    scaled = grad * factor
    mean_new = BETA_ONE * mean + (1.0 - BETA_ONE) * scaled
    square_new = BETA_TWO * square + (1.0 - BETA_TWO) * scaled * scaled
    mean_hat = mean_new / (1.0 - BETA_ONE**STEP)
    square_hat = square_new / (1.0 - BETA_TWO**STEP)
    new = master - rate * (mean_hat / (jnp.sqrt(square_hat) + ADAM_EPS) + decay * master)
    return (new, mean_new, square_new)


def adam_kernel(
    out_rate, entries, sum_ref, out_sum, early_ref, late_ref, joint_ref, down_sum, *refs
):
    gain_sum = sum_ref[:, :entries]
    squares = sum_ref[:, entries : entries + 1]
    norm = jnp.sqrt(squares + jnp.sum(gain_sum * gain_sum, axis=1, keepdims=True))
    factor = CLIP_NORM / jnp.maximum(norm, CLIP_NORM)
    states = [refs[3 * k : 3 * k + 3] for k in range(4)]
    results = [refs[12 + 4 * k : 16 + 4 * k] for k in range(4)]
    refs[28][...] = norm

    def update(state, result, at, grad, rate):
        new, mean, square = adam(
            state[0][at], state[1][at], state[2][at], grad.astype(jnp.float32), factor, rate,
            DECAY,
        )
        result[0][at] = new
        result[1][at] = new.astype(jnp.bfloat16)
        result[2][at] = mean
        result[3][at] = square

    rows = slice(None)
    early = early_ref.shape[1]
    half = joint_ref.shape[1] // 2
    update(states[1], results[1], (rows, rows), out_sum[...], out_rate)
    update(states[0], results[0], (rows, slice(0, early)), early_ref[...], RATE_WEIGHT)
    update(states[0], results[0], (rows, slice(early, None)), late_ref[...], RATE_WEIGHT)
    update(states[2], results[2], (rows, 0, rows), joint_ref[:, :half], RATE_WEIGHT)
    update(states[2], results[2], (rows, 1, rows), joint_ref[:, half:], RATE_WEIGHT)
    update(states[3], results[3], (rows, rows), down_sum[...], RATE_WEIGHT)


def adam_all(entries, summed, sums, states, out_rate):
    steps = max(1, states[0][0].shape[0] // 32)

    def block(array):
        rows = array.shape[0] // steps
        rest = array.shape[1:]
        return pl.BlockSpec((rows,) + rest, lambda i: (i,) + (0,) * len(rest))

    shapes = []
    for state in states:
        shapes += [
            jax.ShapeDtypeStruct(state[0].shape, dtype)
            for dtype in (jnp.float32, jnp.bfloat16, jnp.float32, jnp.float32)
        ]
    arrays = [*sums]
    for state in states:
        arrays += state
    small = lambda shape: pl.BlockSpec(shape, lambda i: (0, 0))
    return pl.pallas_call(
        lambda *refs: adam_kernel(out_rate, entries, *refs),
        grid=(steps,),
        in_specs=[small(summed.shape)] + [block(array) for array in arrays],
        out_specs=[block(shape) for shape in shapes] + [small((1, 1))],
        out_shape=shapes + [jax.ShapeDtypeStruct((1, 1), jnp.float32)],
        compiler_params=params(),
        cost_estimate=cost(0, 16 * MIB),
        name="adam",
    )(summed, *arrays)


def shards(
    tokens,
    segments,
    cotangent,
    qkv_weight,
    out_weight,
    gate_up_weight,
    down_weight,
    qkv_master,
    out_master,
    gate_up_master,
    down_master,
    qkv_mean,
    out_mean,
    gate_up_mean,
    down_mean,
    qkv_square,
    out_square,
    gate_up_square,
    down_square,
    gains,
    gains_mean,
    gains_square,
):
    width = tokens.shape[1]
    length = segments.shape[0]
    groups = qkv_weight.shape[1] // (KINDS * HD)
    hidden_width = down_weight.shape[0]
    block = length // PIECES // HALVES
    attn_gain = gains[None, :width]
    ffn_gain = gains[None, width : 2 * width]
    head_gains = jnp.stack([gains[2 * width : 2 * width + HD], gains[2 * width + HD :]], axis=1)
    place = lax.axis_index("tensor").astype(jnp.int32).reshape(1)
    here = lax.axis_index("dp").astype(jnp.int32).reshape(1)

    across = exchange(tokens, "tensor", ACROSS)
    beside = exchange(tokens, "tensor", CORE)
    starts = starts_of(segments)
    tables = rotary((jnp.arange(length, dtype=jnp.int32) - starts).astype(jnp.float32))
    weight_rows = qkv_weight.T
    inner = (attn_gain, weight_rows, head_gains, *tables)
    near_part = project(0, [], place, [tokens, beside], *inner)
    flat_weight = after(gate_up_weight, near_part[2]).reshape(width, 2 * hidden_width)
    across = after(across, near_part[2], flat_weight)
    corner = exchange(across, "tensor", CORE)
    normed_one, raw, flipped, rows = project(1, near_part, place, [across, corner], *inner)

    grad_across = exchange(after(cotangent, across), "tensor", ACROSS)
    grad_pieces = [
        cotangent,
        exchange(after(cotangent, across), "tensor", CORE),
        grad_across,
        exchange(grad_across, "tensor", CORE),
    ]

    def added(left, right):
        return (left.astype(jnp.float32) + right.astype(jnp.float32)).astype(jnp.bfloat16)

    def halfway(send, keep):
        near = exchange(send, "tensor", CORE)
        return (keep, near, added(keep[1], near[1]))

    def across_of(passed):
        keep, near, passed = passed
        return (keep, near, exchange(passed, "tensor", ACROSS))

    attended, send, keep = attend(0, [], place, flipped, rows, starts, out_weight)
    passed = halfway(after(send, grad_across), keep)
    shares = across_of(passed)
    flipped_late = after(flipped, passed[2])
    attended, send, keep = attend(1, attended, place, flipped_late, rows, starts, out_weight)
    context, context_flip, log_total = attended

    weights = (flat_weight, down_weight)
    middle, normed = norm(0, tokens, *shares, ffn_gain)
    middles = [middle]
    beside, across = exchange(normed, "tensor", CORE), exchange(normed, "tensor", ACROSS)
    passed = halfway(after(send, shares[2]), keep)
    shares = across_of(passed)
    full, out_near, back_near = feed(
        0, 0, [], [after(normed, passed[2]), beside], grad_pieces[:2], *weights
    )
    across = after(across, out_near[0])
    corner = exchange(across, "tensor", CORE)
    full, out_far, back_far = feed(1, 0, full, [across, corner], grad_pieces[2:], *weights)
    outs, backs = [(*out_near, *out_far)], [(*back_near, *back_far)]

    keep, near, far = shares
    middle, normed = norm(1, tokens, keep, near, after(far, out_far[0]), ffn_gain)
    middles.append(middle)
    beside, across = exchange(normed, "tensor", CORE), exchange(normed, "tensor", ACROSS)
    full, out_near, back_near = feed(2, 1, full, [normed, beside], grad_pieces[:2], *weights)

    def share_of(pieces, *gates):
        third = exchange(pieces[3], "tensor", CORE)
        third = after(third, *gates) if gates else third
        return (pieces[0], exchange(pieces[1], "tensor", CORE), added(pieces[2], third))

    passed = share_of(backs[0], out_near[0])
    sums = [across_of(passed)]
    across = after(across, out_near[0])
    corner = exchange(across, "tensor", CORE)
    across = after(across, passed[2])
    full, out_far, back_far = feed(3, 1, full, [across, corner], grad_pieces[2:], *weights)
    outs.append((*out_near, *out_far))
    backs.append((*back_near, *back_far))
    normed_two, grad_full, hidden, flat_low = full

    def dh_of(half, keep, near, far):
        low, part = norm_back(half, middles[half], cotangent, keep, near, far, ffn_gain)
        across = exchange(low, "tensor", ACROSS)
        pieces = [low, exchange(low, "tensor", CORE), across, exchange(across, "tensor", CORE)]
        return pieces, part

    keep, near, far = sums[0]
    first_dh = dh_of(0, keep, near, after(far, out_far[0]))
    passed = share_of(after(tuple(backs[1]), far))
    sums.append(across_of(passed))
    normed_two = after(normed_two, passed[2], first_dh[0][0])
    joint_grad = contract_rows(normed_two, flat_low).astype(jnp.bfloat16)
    out_sums = [share_of(after(tuple(out), passed[2])) for out in outs]
    keep, near, far = sums[1]
    second_dh = dh_of(1, keep, near, after(far, joint_grad))
    pieces_dh, ffn_parts = zip(first_dh, second_dh)
    joint_sum = lax.psum_scatter(
        after(joint_grad, pieces_dh[1][2]), "dp", scatter_dimension=0, tiled=True
    )
    down_grad = contract_rows(after(grad_full, pieces_dh[1][0]), hidden).astype(jnp.bfloat16)
    down = ScatterSum([down_grad], [(hidden_width, True)])
    sent, _ = advance(here, [down], pieces_dh[1][2])

    dh = [pieces_dh[half][r] for r in range(PIECES) for half in range(HALVES)]
    dh[0] = after(dh[0], *sent, *[item[2] for item in out_sums])
    out_fars = [
        exchange(after(item[2], pieces_dh[1][2]), "tensor", ACROSS) for item in out_sums
    ]

    joints, head_parts, mixed, early = [], [], [], []
    for g in range(groups):
        outs_back = attend_back(
            g, place, flipped, rows, context_flip, log_total, starts, dh, out_weight, raw, tables,
            head_gains,
        )
        joints.append(outs_back[0])
        head_parts.append(outs_back[1])
        if g == 0:
            dh_full = outs_back[2]
            early = ScatterSum(
                [
                    contract_rows(dh_full, context).astype(jnp.bfloat16),
                    contract_rows(normed_one, outs_back[0]).astype(jnp.bfloat16),
                ],
                [(context.shape[1], True), (joints[0].shape[1], False)],
            )
            sent, _ = advance(here, [down, early], outs_back[1])
            dh = [after(dh_full, *sent, *out_fars)]
        else:
            dh = [dh_full]
    sent, square = advance(here, [down, early], joints[-1])
    joints[0] = after(joints[0], *sent)
    send, keep = spread(place, joints, weight_rows)
    late = [
        contract_rows(normed_one, after(joints[g], keep)).astype(jnp.bfloat16)
        for g in range(1, groups)
    ]
    near = exchange(send, "tensor", CORE)
    third = after(near, down.sources[1], early.sources[1])
    passed = (keep, near, added(keep[1], third[1]))
    keep, near, far = across_of(passed)
    late = ScatterSum(late, [(joints[0].shape[1] * (groups - 1), False)])
    pending = [down, early, late]
    squares = [square]
    gates = [passed[2]]
    while pending:
        pending = [item for item in pending if item.total is None]
        _, square = advance(here, pending, *gates)
        squares.append(square)
        pending = [item for item in pending if item.total is None]
        gates = []

    results = []
    for half in range(HALVES):
        keep_out, near_out, _ = out_sums[half]
        total = keep_out.astype(jnp.float32) + near_out.astype(jnp.float32)
        results.append(middles[half] + (total + out_fars[half].astype(jnp.float32)))
    result = jnp.concatenate(results, axis=0).astype(jnp.bfloat16)

    row = row_of(ffn_parts, head_parts, squares, joint_sum)
    skips = [pieces[0] for pieces in pieces_dh]
    input_grad, row = finish(tokens, skips, keep, near, far, attn_gain, row)
    summed = sum_all(row)
    entries = gains.shape[0]
    out_fan = max(QH * HD * 16 // length, 16)
    out_rate = RATE_WEIGHT * (QH * HD / out_fan) ** 0.5
    updated = adam_all(
        entries, summed, [*early.total, *late.total, joint_sum, *down.total],
        [
            (qkv_master, qkv_mean, qkv_square),
            (out_master, out_mean, out_square),
            (gate_up_master, gate_up_mean, gate_up_square),
            (down_master, down_mean, down_square),
        ],
        out_rate,
    )
    grad_norm = updated[16][0, 0]
    factor = CLIP_NORM / jnp.maximum(grad_norm, CLIP_NORM)
    gain_results = adam(
        gains, gains_mean, gains_square, summed[0, :entries], factor, RATE_GAIN, 0.0
    )
    return (result, input_grad, grad_norm, *updated[:16], *gain_results)


def solution(mesh):
    in_specs = (
        P(("dp", "tensor"), None),
        P("dp"),
        P(("dp", "tensor"), None),
        P(None, "tensor"),
        P("tensor", None),
        P(None, None, "tensor"),
        P("tensor", None),
        P("dp", "tensor"),
        P("tensor", "dp"),
        P("dp", None, "tensor"),
        P("tensor", "dp"),
        P("dp", "tensor"),
        P("tensor", "dp"),
        P("dp", None, "tensor"),
        P("tensor", "dp"),
        P("dp", "tensor"),
        P("tensor", "dp"),
        P("dp", None, "tensor"),
        P("tensor", "dp"),
        P(),
        P(),
        P(),
    )
    out_specs = (
        P(("dp", "tensor"), None),
        P(("dp", "tensor"), None),
        P(),
        P("dp", "tensor"),
        P("dp", "tensor"),
        P("dp", "tensor"),
        P("dp", "tensor"),
        P("tensor", "dp"),
        P("tensor", "dp"),
        P("tensor", "dp"),
        P("tensor", "dp"),
        P("dp", None, "tensor"),
        P("dp", None, "tensor"),
        P("dp", None, "tensor"),
        P("dp", None, "tensor"),
        P("tensor", "dp"),
        P("tensor", "dp"),
        P("tensor", "dp"),
        P("tensor", "dp"),
        P(),
        P(),
        P(),
    )
    return jax.shard_map(shards, mesh=mesh, in_specs=in_specs, out_specs=out_specs, check_vma=False)
```

```python
import jax
import jax.numpy as jnp
from jax import lax
from jax.experimental import pallas as pl
from jax.experimental.pallas import tpu as pltpu
from jax.sharding import PartitionSpec as P

QH = 16
KVH = 8
HD = 64
STEP = 5


NORM_EPS = 1e-06
ROPE_BASE = 1000000.0
CLIP_NORM = 1.0
BETA_ONE = 0.9
BETA_TWO = 0.95
ADAM_EPS = 1e-08
DECAY = 0.1
RATE_WEIGHT = 0.02
RATE_GAIN = 1.5
MASKED = -1e30

KINDS = QH // KVH + 2
RATIO = QH // KVH
ONES = 16
PARTS = 2
PIECES = 4
HALVES = 2
CORE = 1
ACROSS = 2
MIB = 1024 * 1024


def params(limit=60):
    return pltpu.CompilerParams(vmem_limit_bytes=limit * MIB)


def cost(flops, size):
    return pl.CostEstimate(flops=flops, bytes_accessed=size, transcendentals=0)


def starts_of(seg):
    index = jnp.arange(seg.shape[0], dtype=jnp.int32)
    flag = (index == 0) | (seg != jnp.roll(seg, 1))
    return lax.cummax(jnp.where(flag, index, 0), axis=0)


def rotary(position):
    half = HD // 2
    freq = ROPE_BASE ** (-(jnp.arange(half, dtype=jnp.float32) * 2.0 / HD))
    angle = freq[:, None] * position[None, :]
    return (jnp.cos(angle), jnp.sin(angle))


def dot_nn(left, right):
    return lax.dot_general(
        left, right, (((1,), (0,)), ((), ())), preferred_element_type=jnp.float32
    )


def dot_nt(left, right):
    return lax.dot_general(
        left, right, (((1,), (1,)), ((), ())), preferred_element_type=jnp.float32
    )


def contract_rows(left, right):
    return lax.dot_general(
        left, right, (((0,), (0,)), ((), ())), preferred_element_type=jnp.float32
    )


def rotate(value, cosine, sine):
    half = value.shape[0] // 2
    first, second = (value[:half], value[half:])
    return jnp.concatenate(
        [first * cosine - second * sine, second * cosine + first * sine], axis=0
    )


def rotate_back(grad, cosine, sine):
    half = grad.shape[0] // 2
    first, second = (grad[:half], grad[half:])
    return jnp.concatenate(
        [first * cosine + second * sine, second * cosine - first * sine], axis=0
    )


def row_scale(value):
    return lax.rsqrt(jnp.mean(value * value, axis=-1, keepdims=True) + NORM_EPS)


def head_scale(value):
    return lax.rsqrt(jnp.mean(value * value, axis=0, keepdims=True) + NORM_EPS)


def project_kernel(place_ref, *refs):
    pieces = refs[:2]
    pre_ref, weight_ref, gain_ref, cos_ref, sin_ref = refs[2:7]
    normed_ref, raw_ref, flip_ref, row_ref = refs[-4:]
    step = pl.program_id(0)
    for r in range(2):

        @pl.when(step // PARTS == r)
        def _(r=r):
            value = pieces[r][...].astype(jnp.float32)
            normed_ref[...] = (value * row_scale(value) * pre_ref[...]).astype(jnp.bfloat16)

    joint = dot_nt(weight_ref[...], normed_ref[...])
    cosine, sine = cos_ref[...], sin_ref[...]
    for slot in range(raw_ref.shape[0]):
        kind = slot % KINDS
        raw = joint[slot * HD : (slot + 1) * HD]
        raw_ref[slot] = raw
        value = raw
        if kind < KINDS - 1:
            gain = gain_ref[:, 1:2] if kind == KINDS - 2 else gain_ref[:, 0:1]
            value = rotate(raw * head_scale(raw) * gain, cosine, sine)
        if kind < KINDS - 2:
            value = value * HD ** (-0.5)
        low = value.astype(jnp.bfloat16)
        flip_ref[slot] = low
        row_ref[slot] = low.T


def project(far, earlier, place, pieces, pre_gain, weight_rows, head_gains, cos_table, sin_table):
    rows, width = pieces[0].shape
    length = rows * PIECES
    block = rows // PARTS
    slots = weight_rows.shape[0] // HD
    at = lambda i, p: PARTS * ((i // PARTS + 2 * far) ^ p[0]) + i % PARTS

    def piece(r):
        return pl.BlockSpec(
            (block, width), lambda i, p: (jnp.clip(i - PARTS * r, 0, PARTS - 1), 0)
        )

    return pl.pallas_call(
        project_kernel,
        grid_spec=pltpu.PrefetchScalarGridSpec(
            num_scalar_prefetch=1,
            grid=(2 * PARTS,),
            in_specs=[piece(0), piece(1)]
            + [
                pl.BlockSpec(pre_gain.shape, lambda i, p: (0, 0)),
                pl.BlockSpec(weight_rows.shape, lambda i, p: (0, 0)),
                pl.BlockSpec(head_gains.shape, lambda i, p: (0, 0)),
                pl.BlockSpec((HD // 2, block), lambda i, p: (0, at(i, p))),
                pl.BlockSpec((HD // 2, block), lambda i, p: (0, at(i, p))),
            ]
            + [pl.BlockSpec(memory_space=pl.ANY)] * len(earlier),
            out_specs=[
                pl.BlockSpec((block, width), lambda i, p: (at(i, p), 0)),
                pl.BlockSpec((slots, HD, block), lambda i, p: (0, 0, at(i, p))),
                pl.BlockSpec((slots, HD, block), lambda i, p: (0, 0, at(i, p))),
                pl.BlockSpec((slots, block, HD), lambda i, p: (0, at(i, p), 0)),
            ],
        ),
        out_shape=[
            jax.ShapeDtypeStruct((length, width), jnp.bfloat16),
            jax.ShapeDtypeStruct((slots, HD, length), jnp.float32),
            jax.ShapeDtypeStruct((slots, HD, length), jnp.bfloat16),
            jax.ShapeDtypeStruct((slots, length, HD), jnp.bfloat16),
        ],
        input_output_aliases={8 + k: k for k in range(len(earlier))},
        compiler_params=params(),
        cost_estimate=cost(length * width * slots * HD, 8 * MIB),
        name="project",
    )(place, *pieces, pre_gain, weight_rows, head_gains, cos_table, sin_table, *earlier)


def mask_of(start_row, first_key, first_query, keys):
    queries = start_row.shape[1]
    key = first_key + lax.broadcasted_iota(jnp.int32, (keys, 1), 0)
    query = first_query + lax.broadcasted_iota(jnp.int32, (1, queries), 1)
    return (key >= start_row) & (key <= query)


def over_keys(one, first, last, at_query, block):
    begin = first // block
    whole = jnp.maximum(begin, jnp.minimum((last + block - 1) // block, at_query))
    pairs = (at_query - whole) // 2
    lax.fori_loop(begin, whole, lambda j, carry: one(True, j * block, block), None)
    lax.fori_loop(
        0, pairs, lambda k, carry: one(False, (whole + 2 * k) * block, 2 * block), None
    )
    lax.fori_loop(
        whole + 2 * pairs, at_query, lambda j, carry: one(False, j * block, block), None
    )
    one(True, at_query * block, block)


def attend_kernel(half, first_ref, last_ref, place_ref, *refs):
    query_ref, key_ref, value_ref, start_ref, weight_ref = refs[:5]
    context_ref, flip_ref, log_ref, send_ref, keep_ref, top_ref, sum_ref = refs[-7:]
    groups, ratio = query_ref.shape[:2]
    block = start_ref.shape[1]
    step = pl.program_id(0)
    at_query = HALVES * (step ^ place_ref[0]) + half
    start_row = start_ref[...]
    queries = [
        jnp.concatenate([query_ref[g, h] for h in range(ratio)], axis=1) for g in range(groups)
    ]
    ones = jnp.ones((ONES, 2 * block), jnp.bfloat16)
    top_ref[...] = jnp.full_like(top_ref, MASKED)
    sum_ref[...] = jnp.zeros_like(sum_ref)

    def one(masked, at, size):
        at = pl.multiple_of(at, block)
        if masked:
            mask = mask_of(start_row, at, at_query * block, size)
            mask = jnp.concatenate([mask] * ratio, axis=1)
        for g in range(groups):
            scores = dot_nn(key_ref[g, pl.ds(at, size), :], queries[g])
            if masked:
                scores = jnp.where(mask, scores, MASKED)
            top_old = top_ref[g]
            top = jnp.maximum(top_old, jnp.max(scores, axis=0, keepdims=True))
            expo = jnp.exp((scores - top).astype(jnp.bfloat16))
            top_ref[g] = top
            value = jnp.concatenate([value_ref[g, :, pl.ds(at, size)], ones[:, :size]], axis=0)
            sum_ref[g] = sum_ref[g] * jnp.exp(top_old - top) + dot_nn(value, expo)

    over_keys(one, first_ref[at_query], last_ref[at_query], at_query, block)
    wide = ratio * HD
    for g in range(groups):
        total = sum_ref[g, HD : HD + 1]
        output = sum_ref[g, :HD] / total
        both = jnp.concatenate(
            [output[:, h * block : (h + 1) * block] for h in range(ratio)], axis=0
        )
        flip_ref[g * wide : (g + 1) * wide, :] = both.astype(jnp.bfloat16)
        context_ref[:, g * wide : (g + 1) * wide] = both.T.astype(jnp.bfloat16)
        log_total = top_ref[g] + jnp.log(total)
        for h in range(ratio):
            log_ref[g, h] = log_total[:, h * block : (h + 1) * block]
    part = dot_nn(context_ref[...], weight_ref[...]).astype(jnp.bfloat16)

    @pl.when(step % 2 == 1)
    def _():
        send_ref[...] = part

    @pl.when(step % 2 == 0)
    def _():
        keep_ref[...] = part


def attend(half, earlier, place, flipped, rows, starts, weight):
    slots, _, length = flipped.shape
    groups = slots // KINDS
    block = length // PIECES // HALVES
    width = weight.shape[1]
    wide = groups * RATIO * HD
    at = lambda i, p: HALVES * (i ^ p[0]) + half
    flip_four = flipped.reshape(groups, KINDS, HD, length)
    row_four = rows.reshape(groups, KINDS, length, HD)
    out = jax.ShapeDtypeStruct((PIECES // 2, block, width), jnp.bfloat16)
    outs = pl.pallas_call(
        lambda *refs: attend_kernel(half, *refs),
        grid_spec=pltpu.PrefetchScalarGridSpec(
            num_scalar_prefetch=3,
            grid=(PIECES,),
            in_specs=[
                pl.BlockSpec((groups, RATIO, HD, block), lambda i, f, l, p: (0, 0, 0, at(i, p))),
                pl.BlockSpec((groups, None, length, HD), lambda i, f, l, p: (0, RATIO, 0, 0)),
                pl.BlockSpec((groups, None, HD, length), lambda i, f, l, p: (0, RATIO + 1, 0, 0)),
                pl.BlockSpec((1, block), lambda i, f, l, p: (0, at(i, p))),
                pl.BlockSpec(weight.shape, lambda i, f, l, p: (0, 0)),
            ]
            + [pl.BlockSpec(memory_space=pl.ANY)] * len(earlier),
            out_specs=[
                pl.BlockSpec((block, wide), lambda i, f, l, p: (at(i, p), 0)),
                pl.BlockSpec((wide, block), lambda i, f, l, p: (0, at(i, p))),
                pl.BlockSpec((groups, RATIO, 1, block), lambda i, f, l, p: (0, 0, 0, at(i, p))),
                pl.BlockSpec((None, block, width), lambda i, f, l, p: (i // 2, 0, 0)),
                pl.BlockSpec((None, block, width), lambda i, f, l, p: (i // 2, 0, 0)),
            ],
            scratch_shapes=[
                pltpu.VMEM((groups, 1, RATIO * block), jnp.float32),
                pltpu.VMEM((groups, HD + ONES, RATIO * block), jnp.float32),
            ],
        ),
        out_shape=[
            jax.ShapeDtypeStruct((length, wide), jnp.bfloat16),
            jax.ShapeDtypeStruct((wide, length), jnp.bfloat16),
            jax.ShapeDtypeStruct((groups, RATIO, 1, length), jnp.float32),
            out,
            out,
        ],
        input_output_aliases={8 + k: k for k in range(len(earlier))},
        compiler_params=params(),
        cost_estimate=cost(8 * groups * length * length * 64, 6 * MIB),
        name="attend",
    )(
        starts[::block], starts[block - 1 :: block], place, flip_four, row_four, flip_four,
        starts[None, :], weight, *earlier,
    )
    return (outs[:3], outs[3], outs[4])


def attend_back_kernel(pieces, first_ref, last_ref, place_ref, *refs):
    (query_ref, query_row_ref, key_ref, key_row_ref, value_row_ref, context_ref, log_ref,
     start_ref, weight_ref, raw_ref, raw_key_ref, cos_ref, sin_ref, gain_ref) = refs[:14]
    dh_pieces = refs[14 : 14 + pieces]
    if pieces > 1:
        joint_ref, gain_grad_ref, dh_ref = refs[14 + pieces : 17 + pieces]
    else:
        joint_ref, gain_grad_ref = refs[14 + pieces : 16 + pieces]
        dh_ref = dh_pieces[0]
    query_sum, key_sum, value_sum, query_gain_sum = refs[-4:]
    block = start_ref.shape[1]
    step = pl.program_id(0)
    steps = pl.num_programs(0)
    ratio = query_ref.shape[0]
    wide = ratio * HD

    @pl.when(step == 0)
    def _():
        key_sum[...] = jnp.zeros_like(key_sum)
        value_sum[...] = jnp.zeros_like(value_sum)
        query_gain_sum[...] = jnp.zeros_like(query_gain_sum)

    if pieces > 1:
        source = HALVES * ((step // HALVES) ^ place_ref[0]) + step % HALVES
        for r, piece in enumerate(dh_pieces):

            @pl.when(source == r)
            def _(piece=piece):
                dh_ref[...] = piece[...]

    query = jnp.concatenate([query_ref[h] for h in range(ratio)], axis=1)
    query_row = jnp.concatenate([query_row_ref[h] for h in range(ratio)], axis=0)
    start_row = start_ref[...]
    grad_wide = dot_nt(weight_ref[...], dh_ref[...]).astype(jnp.bfloat16)
    grad_float = grad_wide.astype(jnp.float32)
    products = grad_float * context_ref[...].astype(jnp.float32)
    delta = jnp.concatenate(
        [
            jnp.sum(products[h * HD : (h + 1) * HD], axis=0, keepdims=True)
            for h in range(ratio)
        ],
        axis=1,
    )
    grad = jnp.concatenate([grad_wide[h * HD : (h + 1) * HD] for h in range(ratio)], axis=1)
    turned = grad_float.T.astype(jnp.bfloat16)
    grad_row = jnp.concatenate([turned[:, h * HD : (h + 1) * HD] for h in range(ratio)], axis=0)
    log_total = jnp.concatenate([log_ref[h] for h in range(ratio)], axis=1)
    query_sum[...] = jnp.zeros_like(query_sum)

    def one(masked, at, size):
        at = pl.multiple_of(at, block)
        here = pl.ds(at, size)
        power = dot_nn(key_row_ref[here, :], query) - log_total
        if masked:
            mask = mask_of(start_row, at, step * block, size)
            power = jnp.where(jnp.concatenate([mask] * ratio, axis=1), power, MASKED)
        probs = jnp.exp(power.astype(jnp.bfloat16))
        prob_grad = dot_nn(value_row_ref[here, :], grad)
        score_grad = probs * (prob_grad - delta).astype(jnp.bfloat16)
        value_sum[here, :] += dot_nn(probs, grad_row)
        key_sum[here, :] += dot_nn(score_grad, query_row)
        query_sum[...] += dot_nn(key_ref[:, here], score_grad)

    over_keys(one, first_ref[step], last_ref[step], step, block)

    def unwind(part, raw, cosine, sine, gain):
        inverse = head_scale(raw)
        back = rotate_back(part, cosine, sine)
        scaled = back * gain
        lean = jnp.mean(scaled * raw, axis=0, keepdims=True)
        return (back * raw * inverse, inverse * scaled - raw * inverse**3 * lean)

    at = pl.multiple_of(step * block, block)
    here = pl.ds(at, block)
    outs = []
    for h in range(ratio):
        part = query_sum[:, h * block : (h + 1) * block] * HD ** (-0.5)
        gain_part, out = unwind(
            part, raw_ref[h], cos_ref[:, here], sin_ref[:, here], gain_ref[:, 0:1]
        )
        query_gain_sum[...] += gain_part
        outs.append(out)
    joint_ref[here, :wide] = jnp.concatenate(outs, axis=0).T.astype(jnp.bfloat16)

    @pl.when(step == steps - 1)
    def _():
        def one_key(j, total):
            at = pl.multiple_of(j * block, block)
            here = pl.ds(at, block)
            pair = jnp.concatenate([key_sum[here, :], value_sum[here, :]], axis=1).T
            gain_part, out = unwind(
                pair[:HD], raw_key_ref[:, here], cos_ref[:, here], sin_ref[:, here],
                gain_ref[:, 1:2],
            )
            both = jnp.concatenate([out, pair[HD:]], axis=0)
            joint_ref[here, wide:] = both.T.astype(jnp.bfloat16)
            return total + gain_part

        key_gain_sum = lax.fori_loop(
            0, steps, one_key, jnp.zeros(query_gain_sum.shape, jnp.float32)
        )
        both = jnp.concatenate([query_gain_sum[...], key_gain_sum], axis=0).T
        gain_grad_ref[...] = jnp.sum(both, axis=0, keepdims=True)


def attend_back(
    g, place, flipped, rows, context_flip, log_total, starts, dh, weight, raw, tables, head_gains
):
    slots, _, length = flipped.shape
    groups = slots // KINDS
    ratio = RATIO
    block = length // PIECES // HALVES
    wide = ratio * HD
    width = weight.shape[1]
    pieces = len(dh)
    flip_four = flipped.reshape(groups, KINDS, HD, length)
    row_four = rows.reshape(groups, KINDS, length, HD)
    raw_four = raw.reshape(groups, KINDS, HD, length)
    by_step = pl.BlockSpec((block, width), lambda i, f, l, p: (i, 0))
    whole = pl.BlockSpec((block, width), lambda i, f, l, p: (0, 0))
    outs = pl.pallas_call(
        lambda *refs: attend_back_kernel(pieces, *refs),
        grid_spec=pltpu.PrefetchScalarGridSpec(
            num_scalar_prefetch=3,
            grid=(length // block,),
            in_specs=[
                pl.BlockSpec((None, ratio, HD, block), lambda i, f, l, p: (g, 0, 0, i)),
                pl.BlockSpec((None, ratio, block, HD), lambda i, f, l, p: (g, 0, i, 0)),
                pl.BlockSpec((None, None, HD, length), lambda i, f, l, p: (g, ratio, 0, 0)),
                pl.BlockSpec((None, None, length, HD), lambda i, f, l, p: (g, ratio, 0, 0)),
                pl.BlockSpec((None, None, length, HD), lambda i, f, l, p: (g, ratio + 1, 0, 0)),
                pl.BlockSpec((wide, block), lambda i, f, l, p: (g, i)),
                pl.BlockSpec((None, ratio, 1, block), lambda i, f, l, p: (g, 0, 0, i)),
                pl.BlockSpec((1, block), lambda i, f, l, p: (0, i)),
                pl.BlockSpec((wide, width), lambda i, f, l, p: (g, 0)),
                pl.BlockSpec((None, ratio, HD, block), lambda i, f, l, p: (g, 0, 0, i)),
                pl.BlockSpec((None, None, HD, length), lambda i, f, l, p: (g, ratio, 0, 0)),
                pl.BlockSpec((HD // 2, length), lambda i, f, l, p: (0, 0)),
                pl.BlockSpec((HD // 2, length), lambda i, f, l, p: (0, 0)),
                pl.BlockSpec(head_gains.shape, lambda i, f, l, p: (0, 0)),
            ]
            + [whole if pieces > 1 else by_step] * pieces,
            out_specs=[
                pl.BlockSpec((length, wide + 2 * HD), lambda i, f, l, p: (0, 0)),
                pl.BlockSpec((1, 2 * HD), lambda i, f, l, p: (0, 0)),
            ]
            + [by_step] * (pieces > 1),
            scratch_shapes=[
                pltpu.VMEM((HD, ratio * block), jnp.float32),
                pltpu.VMEM((length, HD), jnp.float32),
                pltpu.VMEM((length, HD), jnp.float32),
                pltpu.VMEM((HD, block), jnp.float32),
            ],
        ),
        out_shape=[
            jax.ShapeDtypeStruct((length, wide + 2 * HD), jnp.bfloat16),
            jax.ShapeDtypeStruct((1, 2 * HD), jnp.float32),
        ]
        + [jax.ShapeDtypeStruct((length, width), jnp.bfloat16)] * (pieces > 1),
        compiler_params=params(),
        cost_estimate=cost(20 * length * length * 128, 12 * MIB),
        name="attend_back",
    )(
        starts[::block], starts[block - 1 :: block], place, flip_four, row_four, flip_four, row_four, row_four, context_flip,
        log_total, starts[None, :], weight, raw_four, raw_four, tables[0], tables[1],
        head_gains, *dh,
    )
    return outs


def spread_kernel(groups, place_ref, *refs):
    send_rows, keep_rows = refs[:groups], refs[groups : 2 * groups]
    weight_ref, send_out, keep_out = refs[2 * groups :]
    depth = weight_ref.shape[0] // groups
    for rows, out in ((send_rows, send_out), (keep_rows, keep_out)):
        joined = jnp.concatenate([row[...] for row in rows], axis=1)
        out[...] = dot_nn(joined, weight_ref[...]).astype(jnp.bfloat16)


def spread(place, rows, weight):
    groups = len(rows)
    length, depth = rows[0].shape
    width = weight.shape[1]
    block = length // PIECES
    out = jax.ShapeDtypeStruct((PIECES // 2, block, width), jnp.bfloat16)
    return pl.pallas_call(
        lambda *refs: spread_kernel(groups, *refs),
        grid_spec=pltpu.PrefetchScalarGridSpec(
            num_scalar_prefetch=1,
            grid=(PIECES // 2,),
            in_specs=[pl.BlockSpec((block, depth), lambda i, p: ((2 * i + 1) ^ p[0], 0))] * groups
            + [pl.BlockSpec((block, depth), lambda i, p: ((2 * i) ^ p[0], 0))] * groups
            + [pl.BlockSpec(weight.shape, lambda i, p: (0, 0))],
            out_specs=[pl.BlockSpec((None, block, width), lambda i, p: (i, 0, 0))] * 2,
        ),
        out_shape=[out, out],
        compiler_params=params(),
        cost_estimate=cost(2 * length * width * depth * groups, 6 * MIB),
        name="spread",
    )(place, *rows, *rows, weight)


def feed_kernel(*refs):
    xs, grads, joint_ref, down_ref = refs[:2], refs[2:4], refs[4], refs[5]
    x_ref, grad_ref, hidden_ref, low_ref, out_keep, out_send, back_keep, back_send = refs[-8:]
    hidden_width = down_ref.shape[0]
    block = xs[0].shape[0]
    for r in range(2):
        x_ref[r * block : (r + 1) * block, :] = xs[r][...]
        grad_ref[r * block : (r + 1) * block, :] = grads[r][...]
    both = dot_nn(x_ref[...], joint_ref[...])
    gate, up = (both[:, :hidden_width], both[:, hidden_width:])
    sigmoid = 1.0 / (1.0 + jnp.exp(-gate))
    swish = gate * sigmoid
    hidden = (swish * up).astype(jnp.bfloat16)
    hidden_ref[...] = hidden
    hidden_grad = dot_nt(grad_ref[...], down_ref[...])
    low_ref[:, :hidden_width] = (
        hidden_grad * up * sigmoid * (1.0 + gate * (1.0 - sigmoid))
    ).astype(jnp.bfloat16)
    low_ref[:, hidden_width:] = (hidden_grad * swish).astype(jnp.bfloat16)
    out = dot_nn(hidden, down_ref[...]).astype(jnp.bfloat16)
    out_keep[...] = out[:block]
    out_send[...] = out[block:]
    back = dot_nt(low_ref[...], joint_ref[...]).astype(jnp.bfloat16)
    back_keep[...] = back[:block]
    back_send[...] = back[block:]


def feed(call, half, earlier, normed, grads, joint_weight, down_weight):
    block, width = normed[0].shape
    hidden_width = down_weight.shape[0]
    length = block * PIECES * HALVES
    once = pl.Buffered(1)
    row = lambda columns: pl.BlockSpec((2 * block, columns), lambda i: (call, 0))
    whole = lambda value: pl.BlockSpec(value.shape, lambda i: (0, 0), pipeline_mode=once)
    pair = pl.BlockSpec((block, width), lambda i: (0, 0))
    full = lambda columns: jax.ShapeDtypeStruct((length, columns), jnp.bfloat16)
    outs = pl.pallas_call(
        feed_kernel,
        grid=(1,),
        in_specs=[pl.BlockSpec((block, width), lambda i: (0, 0), pipeline_mode=once)] * 2
        + [pl.BlockSpec((block, width), lambda i: (half, 0), pipeline_mode=once)] * 2
        + [whole(joint_weight), whole(down_weight)]
        + [pl.BlockSpec(memory_space=pl.ANY)] * len(earlier),
        out_specs=[row(width), row(width), row(hidden_width), row(2 * hidden_width)] + [pair] * 4,
        out_shape=[full(width), full(width), full(hidden_width), full(2 * hidden_width)]
        + [jax.ShapeDtypeStruct((block, width), jnp.bfloat16)] * 4,
        input_output_aliases={6 + k: k for k in range(len(earlier))},
        compiler_params=params(),
        cost_estimate=cost(3 * length * width * hidden_width, 16 * MIB),
        name="feed",
    )(*normed, *grads, joint_weight, down_weight, *earlier)
    return (outs[:4], outs[4:6], outs[6:8])


def norm_kernel(x_ref, keep_ref, near_ref, far_ref, gain_ref, middle_ref, normed_ref):
    f32 = jnp.float32
    middle = x_ref[...].astype(f32) + (
        keep_ref[...].astype(f32) + near_ref[...].astype(f32) + far_ref[...].astype(f32)
    )
    middle_ref[...] = middle
    normed_ref[...] = (middle * row_scale(middle) * gain_ref[...]).astype(jnp.bfloat16)


def first_of(value, rows, width):
    if value.ndim == 3:
        return pl.BlockSpec((None, rows, width), lambda i: (0, i, 0))
    return pl.BlockSpec((rows, width), lambda i: (i, 0))


def norm(half, tokens, keep, near, far, gain):
    length, width = far.shape
    steps = 2
    rows = length // steps
    flat = pl.BlockSpec((rows, width), lambda i: (i, 0))
    return pl.pallas_call(
        norm_kernel,
        grid=(steps,),
        in_specs=[
            pl.BlockSpec((rows, width), lambda i: (half * steps + i, 0)),
            first_of(keep, rows, width),
            first_of(near, rows, width),
            flat,
            pl.BlockSpec(gain.shape, lambda i: (0, 0)),
        ],
        out_specs=[flat, flat],
        out_shape=[
            jax.ShapeDtypeStruct((length, width), jnp.float32),
            jax.ShapeDtypeStruct((length, width), jnp.bfloat16),
        ],
        compiler_params=params(),
        cost_estimate=cost(0, 4 * MIB),
        name="norm",
    )(tokens, keep, near, far, gain)


def norm_back_of(value, skip, grad, gain):
    inverse = row_scale(value)
    scaled = grad * gain
    lean = jnp.mean(scaled * value, axis=-1, keepdims=True)
    total = skip + (inverse * scaled - value * (inverse**3 * lean))
    return total, jnp.sum(grad * value * inverse, axis=0, keepdims=True)


def norm_back_kernel(
    value_ref, skip_ref, keep_ref, near_ref, far_ref, gain_ref, low_ref, part_ref
):
    f32 = jnp.float32
    grad = keep_ref[...].astype(f32) + near_ref[...].astype(f32) + far_ref[...].astype(f32)
    total, part = norm_back_of(value_ref[...], skip_ref[...].astype(f32), grad, gain_ref[...])
    low_ref[...] = total.astype(jnp.bfloat16)

    @pl.when(pl.program_id(0) == 0)
    def _():
        part_ref[...] = jnp.zeros_like(part_ref)

    part_ref[...] += part


def norm_back(half, value, skip, keep, near, far, gain):
    length, width = far.shape
    steps = 2
    rows = length // steps
    flat = pl.BlockSpec((rows, width), lambda i: (i, 0))
    return pl.pallas_call(
        norm_back_kernel,
        grid=(steps,),
        in_specs=[
            flat,
            pl.BlockSpec((rows, width), lambda i: (half * steps + i, 0)),
            first_of(keep, rows, width),
            first_of(near, rows, width),
            flat,
            pl.BlockSpec(gain.shape, lambda i: (0, 0)),
        ],
        out_specs=[flat, pl.BlockSpec((1, width), lambda i: (0, 0))],
        out_shape=[
            jax.ShapeDtypeStruct((length, width), jnp.bfloat16),
            jax.ShapeDtypeStruct((1, width), jnp.float32),
        ],
        compiler_params=params(),
        cost_estimate=cost(0, 6 * MIB),
        name="norm_back",
    )(value, skip, keep, near, far, gain)


def row_kernel(counts, *refs):
    row_ref, scatter_ref = refs[-1], refs[-2]
    parts, heads, squares = refs[: counts[0]], refs[counts[0] : counts[1]], refs[counts[1] : -2]
    width = parts[0].shape[1]
    total = lambda items: sum([item[...] for item in items[1:]], items[0][...])
    row_ref[:, :width] = jnp.zeros((1, width), jnp.float32)
    row_ref[:, width : 2 * width] = total(parts)
    row_ref[:, 2 * width : 2 * width + 2 * HD] = total(heads)
    scattered = scatter_ref[...].astype(jnp.float32)
    over = jnp.sum(scattered * scattered, axis=0, keepdims=True)
    square = jnp.sum(over, axis=1, keepdims=True) + total(squares)
    lane = lax.broadcasted_iota(jnp.int32, (1, 2 * HD), 1)
    row_ref[:, 2 * width + 2 * HD :] = jnp.where(lane == 0, square, 0.0)


def row_of(parts, heads, squares, scattered):
    counts = (len(parts), len(parts) + len(heads))
    return pl.pallas_call(
        lambda *refs: row_kernel(counts, *refs),
        out_shape=jax.ShapeDtypeStruct((1, 2 * parts[0].shape[1] + 4 * HD), jnp.float32),
        compiler_params=params(24),
        cost_estimate=cost(0, MIB),
        name="row",
    )(*parts, *heads, *squares, scattered)


def finish_kernel(
    x_ref, near_skip, far_skip, keep_ref, near_ref, far_ref, gain_ref, begin_ref, square_ref,
    input_grad_ref, row_ref,
):
    f32 = jnp.float32
    step = pl.program_id(0)
    width = x_ref.shape[1]
    grad = keep_ref[...].astype(f32) + near_ref[...].astype(f32) + far_ref[...].astype(f32)
    skip = jnp.where(step < pl.num_programs(0) // HALVES, near_skip[...], far_skip[...])
    total, part = norm_back_of(
        x_ref[...].astype(f32), skip.astype(f32), grad, gain_ref[...]
    )
    input_grad_ref[...] = total.astype(jnp.bfloat16)

    @pl.when(step == 0)
    def _():
        lane = lax.broadcasted_iota(jnp.int32, row_ref.shape, 1)
        last = jnp.where(lane == 2 * width + 2 * HD, square_ref[...], 0.0)
        row_ref[...] = begin_ref[...] + last

    row_ref[:, :width] += part


def finish(tokens, skips, keep, near, far, gain, row, square):
    length, width = far.shape
    each = 1
    rows = length // HALVES // each
    flat = pl.BlockSpec((rows, width), lambda i: (i, 0))
    whole = lambda value: pl.BlockSpec(value.shape, lambda i: (0, 0))
    return pl.pallas_call(
        finish_kernel,
        grid=(HALVES * each,),
        in_specs=[
            flat,
            pl.BlockSpec((rows, width), lambda i: (jnp.minimum(i, each - 1), 0)),
            pl.BlockSpec((rows, width), lambda i: (jnp.maximum(i - each, 0), 0)),
            first_of(keep, rows, width),
            first_of(near, rows, width),
            flat,
            whole(gain),
            whole(row),
            whole(square),
        ],
        out_specs=[flat, whole(row)],
        out_shape=[
            jax.ShapeDtypeStruct((length, width), jnp.bfloat16),
            jax.ShapeDtypeStruct(row.shape, jnp.float32),
        ],
        compiler_params=params(),
        cost_estimate=cost(0, 6 * MIB),
        name="finish",
    )(tokens, *skips, keep, near, far, gain, row, square)


def exchange(value, axis, bit):
    size = lax.axis_size(axis)
    return lax.ppermute(value, axis, [(i, i ^ bit) for i in range(size)])


def after(value, *others):
    return lax.optimization_barrier((value, *others))[0]


def power_of_two(count):
    return count & (count - 1) == 0


class ScatterSum:
    def __init__(self, grads, flipped):
        size = lax.axis_size("dp")
        rows = grads[0].shape[0] // size
        self.left = [1 << k for k in reversed(range(size.bit_length() - 1))]
        self.order = self.left[::-1]
        self.flipped = flipped
        self.sources = [grad.reshape(size, rows, grad.shape[1]) for grad in grads]
        self.columns = sum(grad.shape[1] for grad in grads)
        self.joined = True
        self.total = None


def advance_kernel(plans, here_ref, *refs):
    count = sum(plan[0] for plan in plans)
    ins, outs = refs[:count], refs[count:]
    squares = jnp.zeros((1, 1), jnp.float32)
    for sources, joined, stride, shift, flipped in plans:
        parts, ins = ins[:sources], ins[sources:]

        def value(at, parts=parts, joined=joined):
            if joined:
                return jnp.concatenate([part[at] for part in parts], axis=1)
            return parts[0][at].astype(jnp.float32) + parts[1][at].astype(jnp.float32)

        if stride is None:
            total = value(0).astype(jnp.float32)
            over = jnp.sum(total * total, axis=0, keepdims=True)
            squares += jnp.sum(over, axis=1, keepdims=True)
            at = 0
            for columns, turned in flipped:
                part = total[:, at : at + columns]
                outs[0][...] = part.T if turned else part
                at, outs = at + columns, outs[1:]
            continue
        sent, kept, outs = outs[0], outs[1], outs[2:]
        own = (here_ref[0] >> shift) & 1
        for k in range(sent.shape[0]):
            base = k // stride * 2 * stride + k % stride
            sent[k] = value(base + (1 - own) * stride).astype(sent.dtype)
            kept[k] = value(base + own * stride).astype(kept.dtype)
    outs[0][...] = squares


def advance(here, items, *gates):
    plans, ins, shapes = [], [], []
    for item in items:
        rows, columns = item.sources[0].shape[1], item.columns
        if item.order:
            bit = item.order[0]
            at = item.left.index(bit)
            stride = 1 << (len(item.left) - 1 - at)
            plans.append((len(item.sources), item.joined, stride, bit.bit_length() - 1, ()))
            half = (item.sources[0].shape[0] // 2, rows, columns)
            shapes += [jax.ShapeDtypeStruct(half, jnp.bfloat16)] * 2
        else:
            plans.append((len(item.sources), item.joined, None, 0, item.flipped))
            for part, turned in item.flipped:
                shape = (part, rows) if turned else (rows, part)
                shapes.append(jax.ShapeDtypeStruct(shape, jnp.float32))
        ins += item.sources
    shapes.append(jax.ShapeDtypeStruct((1, 1), jnp.float32))
    if gates:
        ins[-1] = after(ins[-1], *gates)
    vmem = pl.BlockSpec(memory_space=pltpu.VMEM)
    outs = list(pl.pallas_call(
        lambda *refs: advance_kernel(plans, *refs),
        in_specs=[pl.BlockSpec(memory_space=pltpu.SMEM)] + [vmem] * len(ins),
        out_specs=[vmem] * len(shapes),
        out_shape=shapes,
        compiler_params=params(24),
        cost_estimate=cost(0, 6 * MIB),
        name="advance",
    )(here, *ins))
    sent_all = []
    for item in items:
        if item.order:
            bit = item.order.pop(0)
            item.left.remove(bit)
            sent, kept = outs.pop(0), outs.pop(0)
            item.sources, item.joined = [kept, exchange(sent, "dp", bit)], False
            sent_all.append(sent)
        else:
            item.total = [outs.pop(0) for _ in item.flipped]
    return sent_all, outs[0]


def sum_all(value):
    for axis in ("tensor", "dp"):
        size = lax.axis_size(axis)
        if not power_of_two(size):
            value = lax.psum(value, axis)
            continue
        bit = 1
        while bit < size:
            if 2 * bit < size:
                one, two, three = [exchange(value, axis, bit * k) for k in (1, 2, 3)]
                value = (value + one) + (two + three)
                bit *= 4
            else:
                value = value + exchange(value, axis, bit)
                bit *= 2
    return value


def adam(master, mean, square, grad, factor, rate, decay):
    scaled = grad * factor
    mean_new = BETA_ONE * mean + (1.0 - BETA_ONE) * scaled
    square_new = BETA_TWO * square + (1.0 - BETA_TWO) * scaled * scaled
    mean_hat = mean_new / (1.0 - BETA_ONE**STEP)
    square_hat = square_new / (1.0 - BETA_TWO**STEP)
    new = master - rate * (mean_hat / (jnp.sqrt(square_hat) + ADAM_EPS) + decay * master)
    return (new, mean_new, square_new)


def adam_kernel(
    out_rate, entries, sum_ref, out_sum, early_ref, late_ref, joint_ref, down_sum, *refs
):
    gain_sum = sum_ref[:, :entries]
    squares = sum_ref[:, entries : entries + 1]
    norm = jnp.sqrt(squares + jnp.sum(gain_sum * gain_sum, axis=1, keepdims=True))
    factor = CLIP_NORM / jnp.maximum(norm, CLIP_NORM)
    states = [refs[3 * k : 3 * k + 3] for k in range(4)]
    results = [refs[12 + 4 * k : 16 + 4 * k] for k in range(4)]
    refs[28][...] = norm

    def update(state, result, at, grad, rate):
        new, mean, square = adam(
            state[0][at], state[1][at], state[2][at], grad.astype(jnp.float32), factor, rate,
            DECAY,
        )
        result[0][at] = new
        result[1][at] = new.astype(jnp.bfloat16)
        result[2][at] = mean
        result[3][at] = square

    rows = slice(None)
    early = early_ref.shape[1]
    half = joint_ref.shape[1] // 2
    update(states[1], results[1], (rows, rows), out_sum[...], out_rate)
    update(states[0], results[0], (rows, slice(0, early)), early_ref[...], RATE_WEIGHT)
    update(states[0], results[0], (rows, slice(early, None)), late_ref[...], RATE_WEIGHT)
    update(states[2], results[2], (rows, 0, rows), joint_ref[:, :half], RATE_WEIGHT)
    update(states[2], results[2], (rows, 1, rows), joint_ref[:, half:], RATE_WEIGHT)
    update(states[3], results[3], (rows, rows), down_sum[...], RATE_WEIGHT)


def adam_all(entries, summed, sums, states, out_rate):
    steps = max(1, states[0][0].shape[0] // 32)

    def block(array):
        rows = array.shape[0] // steps
        rest = array.shape[1:]
        return pl.BlockSpec((rows,) + rest, lambda i: (i,) + (0,) * len(rest))

    shapes = []
    for state in states:
        shapes += [
            jax.ShapeDtypeStruct(state[0].shape, dtype)
            for dtype in (jnp.float32, jnp.bfloat16, jnp.float32, jnp.float32)
        ]
    arrays = [*sums]
    for state in states:
        arrays += state
    small = lambda shape: pl.BlockSpec(shape, lambda i: (0, 0))
    return pl.pallas_call(
        lambda *refs: adam_kernel(out_rate, entries, *refs),
        grid=(steps,),
        in_specs=[small(summed.shape)] + [block(array) for array in arrays],
        out_specs=[block(shape) for shape in shapes] + [small((1, 1))],
        out_shape=shapes + [jax.ShapeDtypeStruct((1, 1), jnp.float32)],
        compiler_params=params(),
        cost_estimate=cost(0, 16 * MIB),
        name="adam",
    )(summed, *arrays)


def shards(
    tokens,
    segments,
    cotangent,
    qkv_weight,
    out_weight,
    gate_up_weight,
    down_weight,
    qkv_master,
    out_master,
    gate_up_master,
    down_master,
    qkv_mean,
    out_mean,
    gate_up_mean,
    down_mean,
    qkv_square,
    out_square,
    gate_up_square,
    down_square,
    gains,
    gains_mean,
    gains_square,
):
    width = tokens.shape[1]
    length = segments.shape[0]
    groups = qkv_weight.shape[1] // (KINDS * HD)
    hidden_width = down_weight.shape[0]
    block = length // PIECES // HALVES
    attn_gain = gains[None, :width]
    ffn_gain = gains[None, width : 2 * width]
    head_gains = jnp.stack([gains[2 * width : 2 * width + HD], gains[2 * width + HD :]], axis=1)
    place = lax.axis_index("tensor").astype(jnp.int32).reshape(1)
    here = lax.axis_index("dp").astype(jnp.int32).reshape(1)

    across = exchange(tokens, "tensor", ACROSS)
    beside = exchange(tokens, "tensor", CORE)
    starts = starts_of(segments)
    tables = rotary((jnp.arange(length, dtype=jnp.int32) - starts).astype(jnp.float32))
    weight_rows = qkv_weight.T
    inner = (attn_gain, weight_rows, head_gains, *tables)
    near_part = project(0, [], place, [tokens, beside], *inner)
    flat_weight = after(gate_up_weight, near_part[2]).reshape(width, 2 * hidden_width)
    across = after(across, near_part[2], flat_weight)
    corner = exchange(across, "tensor", CORE)
    normed_one, raw, flipped, rows = project(1, near_part, place, [across, corner], *inner)

    grad_across = exchange(after(cotangent, across), "tensor", ACROSS)
    grad_pieces = [
        cotangent,
        exchange(after(cotangent, across), "tensor", CORE),
        grad_across,
        exchange(grad_across, "tensor", CORE),
    ]

    def added(left, right):
        return (left.astype(jnp.float32) + right.astype(jnp.float32)).astype(jnp.bfloat16)

    def halfway(send, keep):
        near = exchange(send, "tensor", CORE)
        return (keep, near, added(keep[1], near[1]))

    def across_of(passed):
        keep, near, passed = passed
        return (keep, near, exchange(passed, "tensor", ACROSS))

    attended, send, keep = attend(0, [], place, flipped, rows, starts, out_weight)
    passed = halfway(after(send, grad_across), keep)
    shares = across_of(passed)
    flipped_late = after(flipped, passed[2])
    attended, send, keep = attend(1, attended, place, flipped_late, rows, starts, out_weight)
    context, context_flip, log_total = attended

    weights = (flat_weight, down_weight)
    middle, normed = norm(0, tokens, *shares, ffn_gain)
    middles = [middle]
    beside, across = exchange(normed, "tensor", CORE), exchange(normed, "tensor", ACROSS)
    passed = halfway(after(send, shares[2]), keep)
    shares = across_of(passed)
    full, out_near, back_near = feed(
        0, 0, [], [after(normed, passed[2]), beside], grad_pieces[:2], *weights
    )
    across = after(across, out_near[0])
    corner = exchange(across, "tensor", CORE)
    full, out_far, back_far = feed(1, 0, full, [across, corner], grad_pieces[2:], *weights)
    outs, backs = [(*out_near, *out_far)], [(*back_near, *back_far)]

    keep, near, far = shares
    middle, normed = norm(1, tokens, keep, near, after(far, out_far[0]), ffn_gain)
    middles.append(middle)
    beside, across = exchange(normed, "tensor", CORE), exchange(normed, "tensor", ACROSS)
    full, out_near, back_near = feed(2, 1, full, [normed, beside], grad_pieces[:2], *weights)

    def share_of(pieces, *gates):
        third = exchange(pieces[3], "tensor", CORE)
        third = after(third, *gates) if gates else third
        return (pieces[0], exchange(pieces[1], "tensor", CORE), added(pieces[2], third))

    passed = share_of(backs[0], out_near[0])
    sums = [across_of(passed)]
    across = after(across, out_near[0])
    corner = exchange(across, "tensor", CORE)
    across = after(across, passed[2])
    full, out_far, back_far = feed(3, 1, full, [across, corner], grad_pieces[2:], *weights)
    outs.append((*out_near, *out_far))
    backs.append((*back_near, *back_far))
    normed_two, grad_full, hidden, flat_low = full

    def dh_of(half, keep, near, far):
        low, part = norm_back(half, middles[half], cotangent, keep, near, far, ffn_gain)
        across = exchange(low, "tensor", ACROSS)
        pieces = [low, exchange(low, "tensor", CORE), across, exchange(across, "tensor", CORE)]
        return pieces, part

    keep, near, far = sums[0]
    first_dh = dh_of(0, keep, near, after(far, out_far[0]))
    passed = share_of(after(tuple(backs[1]), far))
    sums.append(across_of(passed))
    normed_two = after(normed_two, passed[2], first_dh[0][0])
    joint_grad = contract_rows(normed_two, flat_low).astype(jnp.bfloat16)
    out_sums = [share_of(after(tuple(out), passed[2])) for out in outs]
    keep, near, far = sums[1]
    far_late = after(far, joint_grad, first_dh[0][2])
    second_dh = dh_of(1, keep, near, far_late)
    pieces_dh, ffn_parts = zip(first_dh, second_dh)
    joint_sum = lax.psum_scatter(
        after(joint_grad, far_late), "dp", scatter_dimension=0, tiled=True
    )
    down_grad = contract_rows(after(grad_full, pieces_dh[1][0]), hidden).astype(jnp.bfloat16)
    down = ScatterSum([down_grad], [(hidden_width, True)])
    sent, _ = advance(here, [down], pieces_dh[1][2])

    dh = [pieces_dh[half][r] for r in range(PIECES) for half in range(HALVES)]
    dh[0] = after(dh[0], *sent, *[item[2] for item in out_sums])
    out_fars = [
        exchange(after(item[2], pieces_dh[1][2]), "tensor", ACROSS) for item in out_sums
    ]

    joints, head_parts, mixed, early = [], [], [], []
    for g in range(groups):
        outs_back = attend_back(
            g, place, flipped, rows, context_flip, log_total, starts, dh, out_weight, raw, tables,
            head_gains,
        )
        joints.append(outs_back[0])
        head_parts.append(outs_back[1])
        if g == 0:
            dh_full = outs_back[2]
            early = ScatterSum(
                [
                    contract_rows(dh_full, context).astype(jnp.bfloat16),
                    contract_rows(normed_one, outs_back[0]).astype(jnp.bfloat16),
                ],
                [(context.shape[1], True), (joints[0].shape[1], False)],
            )
            sent, _ = advance(here, [down, early], outs_back[1])
            dh = [after(dh_full, *sent, *out_fars)]
        else:
            dh = [dh_full]
    sent, square = advance(here, [down, early], joints[-1])
    joints[0] = after(joints[0], *sent)
    send, keep = spread(place, joints, weight_rows)
    late = [
        contract_rows(normed_one, after(joints[g], keep)).astype(jnp.bfloat16)
        for g in range(1, groups)
    ]
    near = exchange(send, "tensor", CORE)
    third = after(near, down.sources[1], early.sources[1])
    passed = (keep, near, added(keep[1], third[1]))
    keep, near, far = across_of(passed)
    late = ScatterSum(late, [(joints[0].shape[1] * (groups - 1), False)])
    pending = [down, early, late]
    squares = [square]
    gates = [passed[2]]
    while pending:
        pending = [item for item in pending if item.total is None]
        _, square = advance(here, pending, *gates)
        squares.append(square)
        pending = [item for item in pending if item.total is None]
        gates = []

    results = []
    for half in range(HALVES):
        keep_out, near_out, _ = out_sums[half]
        total = keep_out.astype(jnp.float32) + near_out.astype(jnp.float32)
        results.append(middles[half] + (total + out_fars[half].astype(jnp.float32)))
    result = jnp.concatenate(results, axis=0).astype(jnp.bfloat16)

    ffn_parts = [after(ffn_parts[0], result), *ffn_parts[1:]]
    row = row_of(ffn_parts, head_parts, squares[:-1], joint_sum)
    skips = [pieces[0] for pieces in pieces_dh]
    input_grad, row = finish(tokens, skips, keep, near, far, attn_gain, row, squares[-1])
    summed = sum_all(row)
    entries = gains.shape[0]
    out_fan = max(QH * HD * 16 // length, 16)
    out_rate = RATE_WEIGHT * (QH * HD / out_fan) ** 0.5
    updated = adam_all(
        entries, summed, [*early.total, *late.total, joint_sum, *down.total],
        [
            (qkv_master, qkv_mean, qkv_square),
            (out_master, out_mean, out_square),
            (gate_up_master, gate_up_mean, gate_up_square),
            (down_master, down_mean, down_square),
        ],
        out_rate,
    )
    grad_norm = updated[16][0, 0]
    factor = CLIP_NORM / jnp.maximum(grad_norm, CLIP_NORM)
    gain_results = adam(
        gains, gains_mean, gains_square, summed[0, :entries], factor, RATE_GAIN, 0.0
    )
    return (result, input_grad, grad_norm, *updated[:16], *gain_results)


def solution(mesh):
    in_specs = (
        P(("dp", "tensor"), None),
        P("dp"),
        P(("dp", "tensor"), None),
        P(None, "tensor"),
        P("tensor", None),
        P(None, None, "tensor"),
        P("tensor", None),
        P("dp", "tensor"),
        P("tensor", "dp"),
        P("dp", None, "tensor"),
        P("tensor", "dp"),
        P("dp", "tensor"),
        P("tensor", "dp"),
        P("dp", None, "tensor"),
        P("tensor", "dp"),
        P("dp", "tensor"),
        P("tensor", "dp"),
        P("dp", None, "tensor"),
        P("tensor", "dp"),
        P(),
        P(),
        P(),
    )
    out_specs = (
        P(("dp", "tensor"), None),
        P(("dp", "tensor"), None),
        P(),
        P("dp", "tensor"),
        P("dp", "tensor"),
        P("dp", "tensor"),
        P("dp", "tensor"),
        P("tensor", "dp"),
        P("tensor", "dp"),
        P("tensor", "dp"),
        P("tensor", "dp"),
        P("dp", None, "tensor"),
        P("dp", None, "tensor"),
        P("dp", None, "tensor"),
        P("dp", None, "tensor"),
        P("tensor", "dp"),
        P("tensor", "dp"),
        P("tensor", "dp"),
        P("tensor", "dp"),
        P(),
        P(),
        P(),
    )
    return jax.shard_map(shards, mesh=mesh, in_specs=in_specs, out_specs=out_specs, check_vma=False)
```

```python
import jax
import jax.numpy as jnp
from jax import lax
from jax.experimental import pallas as pl
from jax.experimental.pallas import tpu as pltpu
from jax.sharding import PartitionSpec as P

QH = 16
KVH = 8
HD = 64
STEP = 5


NORM_EPS = 1e-06
ROPE_BASE = 1000000.0
CLIP_NORM = 1.0
BETA_ONE = 0.9
BETA_TWO = 0.95
ADAM_EPS = 1e-08
DECAY = 0.1
RATE_WEIGHT = 0.02
RATE_GAIN = 1.5
MASKED = -1e30

KINDS = QH // KVH + 2
RATIO = QH // KVH
PARTS = 2
PIECES = 4
HALVES = 2
CORE = 1
ACROSS = 2
MIB = 1024 * 1024


def params(limit=60):
    return pltpu.CompilerParams(vmem_limit_bytes=limit * MIB)


def cost(flops, size):
    return pl.CostEstimate(flops=flops // 8, bytes_accessed=size // 8, transcendentals=0)


def starts_of(seg):
    index = jnp.arange(seg.shape[0], dtype=jnp.int32)
    flag = (index == 0) | (seg != jnp.roll(seg, 1))
    return lax.cummax(jnp.where(flag, index, 0), axis=0)


def rotary(position):
    half = HD // 2
    freq = ROPE_BASE ** (-(jnp.arange(half, dtype=jnp.float32) * 2.0 / HD))
    angle = freq[:, None] * position[None, :]
    return (jnp.cos(angle), jnp.sin(angle))


def dot_nn(left, right):
    return lax.dot_general(
        left, right, (((1,), (0,)), ((), ())), preferred_element_type=jnp.float32
    )


def dot_nt(left, right):
    return lax.dot_general(
        left, right, (((1,), (1,)), ((), ())), preferred_element_type=jnp.float32
    )


def contract_rows(left, right):
    return lax.dot_general(
        left, right, (((0,), (0,)), ((), ())), preferred_element_type=jnp.float32
    )


def rotate(value, cosine, sine):
    half = value.shape[0] // 2
    first, second = (value[:half], value[half:])
    return jnp.concatenate(
        [first * cosine - second * sine, second * cosine + first * sine], axis=0
    )


def rotate_back(grad, cosine, sine):
    half = grad.shape[0] // 2
    first, second = (grad[:half], grad[half:])
    return jnp.concatenate(
        [first * cosine + second * sine, second * cosine - first * sine], axis=0
    )


def row_scale(value):
    return lax.rsqrt(jnp.mean(value * value, axis=-1, keepdims=True) + NORM_EPS)


def head_scale(value):
    return lax.rsqrt(jnp.mean(value * value, axis=0, keepdims=True) + NORM_EPS)


def project_kernel(place_ref, *refs):
    pieces = refs[:2]
    pre_ref, weight_ref, gain_ref, cos_ref, sin_ref = refs[2:7]
    normed_ref, raw_ref, flip_ref, row_ref = refs[-4:]
    step = pl.program_id(0)
    for r in range(2):

        @pl.when(step // PARTS == r)
        def _(r=r):
            value = pieces[r][...].astype(jnp.float32)
            normed_ref[...] = (value * row_scale(value) * pre_ref[...]).astype(jnp.bfloat16)

    joint = dot_nt(weight_ref[...], normed_ref[...])
    cosine, sine = cos_ref[...], sin_ref[...]
    for slot in range(raw_ref.shape[0]):
        kind = slot % KINDS
        raw = joint[slot * HD : (slot + 1) * HD]
        raw_ref[slot] = raw
        value = raw
        if kind < KINDS - 1:
            gain = gain_ref[:, 1:2] if kind == KINDS - 2 else gain_ref[:, 0:1]
            value = rotate(raw * head_scale(raw) * gain, cosine, sine)
        if kind < KINDS - 2:
            value = value * HD ** (-0.5)
        low = value.astype(jnp.bfloat16)
        flip_ref[slot] = low
        row_ref[slot] = low.T


def project(far, earlier, place, pieces, pre_gain, weight_rows, head_gains, cos_table, sin_table):
    rows, width = pieces[0].shape
    length = rows * PIECES
    block = rows // PARTS
    slots = weight_rows.shape[0] // HD
    at = lambda i, p: PARTS * ((i // PARTS + 2 * far) ^ p[0]) + i % PARTS

    def piece(r):
        return pl.BlockSpec(
            (block, width), lambda i, p: (jnp.clip(i - PARTS * r, 0, PARTS - 1), 0)
        )

    return pl.pallas_call(
        project_kernel,
        grid_spec=pltpu.PrefetchScalarGridSpec(
            num_scalar_prefetch=1,
            grid=(2 * PARTS,),
            in_specs=[piece(0), piece(1)]
            + [
                pl.BlockSpec(pre_gain.shape, lambda i, p: (0, 0)),
                pl.BlockSpec(weight_rows.shape, lambda i, p: (0, 0)),
                pl.BlockSpec(head_gains.shape, lambda i, p: (0, 0)),
                pl.BlockSpec((HD // 2, block), lambda i, p: (0, at(i, p))),
                pl.BlockSpec((HD // 2, block), lambda i, p: (0, at(i, p))),
            ]
            + [pl.BlockSpec(memory_space=pl.ANY)] * len(earlier),
            out_specs=[
                pl.BlockSpec((block, width), lambda i, p: (at(i, p), 0)),
                pl.BlockSpec((slots, HD, block), lambda i, p: (0, 0, at(i, p))),
                pl.BlockSpec((slots, HD, block), lambda i, p: (0, 0, at(i, p))),
                pl.BlockSpec((slots, block, HD), lambda i, p: (0, at(i, p), 0)),
            ],
        ),
        out_shape=[
            jax.ShapeDtypeStruct((length, width), jnp.bfloat16),
            jax.ShapeDtypeStruct((slots, HD, length), jnp.float32),
            jax.ShapeDtypeStruct((slots, HD, length), jnp.bfloat16),
            jax.ShapeDtypeStruct((slots, length, HD), jnp.bfloat16),
        ],
        input_output_aliases={8 + k: k for k in range(len(earlier))},
        compiler_params=params(),
        cost_estimate=cost(length * width * slots * HD, 8 * MIB),
        name="project",
    )(place, *pieces, pre_gain, weight_rows, head_gains, cos_table, sin_table, *earlier)


def mask_of(start_row, first_key, first_query, keys):
    queries = start_row.shape[1]
    key = first_key + lax.broadcasted_iota(jnp.int32, (keys, 1), 0)
    query = first_query + lax.broadcasted_iota(jnp.int32, (1, queries), 1)
    return (key >= start_row) & (key <= query)


def over_keys(one, first, last, at_query, block):
    begin = first // block
    whole = jnp.maximum(begin, jnp.minimum((last + block - 1) // block, at_query))
    pairs = (at_query - whole) // 2
    lax.fori_loop(begin, whole, lambda j, carry: one(True, j * block, block), None)
    lax.fori_loop(
        0, pairs, lambda k, carry: one(False, (whole + 2 * k) * block, 2 * block), None
    )
    lax.fori_loop(
        whole + 2 * pairs, at_query, lambda j, carry: one(False, j * block, block), None
    )
    one(True, at_query * block, block)


def attend_kernel(half, first_ref, last_ref, place_ref, *refs):
    query_ref, key_ref, value_ref, start_ref, weight_ref = refs[:5]
    context_ref, flip_ref, log_ref, send_ref, keep_ref, top_ref, total_ref, sum_ref = refs[-8:]
    groups, ratio = query_ref.shape[:2]
    block = start_ref.shape[1]
    step = pl.program_id(0)
    at_query = HALVES * (step ^ place_ref[0]) + half
    start_row = start_ref[...]
    queries = [
        jnp.concatenate([query_ref[g, h] for h in range(ratio)], axis=1) for g in range(groups)
    ]
    top_ref[...] = jnp.full_like(top_ref, MASKED)
    total_ref[...] = jnp.zeros_like(total_ref)
    sum_ref[...] = jnp.zeros_like(sum_ref)

    def one(masked, at, size):
        at = pl.multiple_of(at, block)
        if masked:
            mask = mask_of(start_row, at, at_query * block, size)
            mask = jnp.concatenate([mask] * ratio, axis=1)
        for g in range(groups):
            scores = dot_nn(key_ref[g, pl.ds(at, size), :], queries[g])
            if masked:
                scores = jnp.where(mask, scores, MASKED)
            top_old = top_ref[g]
            top = jnp.maximum(top_old, jnp.max(scores, axis=0, keepdims=True))
            expo = jnp.exp(scores - top)
            fade = jnp.exp(top_old - top)
            top_ref[g] = top
            total_ref[g] = total_ref[g] * fade + jnp.sum(expo, axis=0, keepdims=True)
            part = dot_nn(value_ref[g, :, pl.ds(at, size)], expo.astype(jnp.bfloat16))
            sum_ref[g] = sum_ref[g] * fade + part

    over_keys(one, first_ref[at_query], last_ref[at_query], at_query, block)
    wide = ratio * HD
    for g in range(groups):
        total = total_ref[g]
        output = sum_ref[g] / total
        both = jnp.concatenate(
            [output[:, h * block : (h + 1) * block] for h in range(ratio)], axis=0
        )
        flip_ref[g * wide : (g + 1) * wide, :] = both.astype(jnp.bfloat16)
        context_ref[:, g * wide : (g + 1) * wide] = both.T.astype(jnp.bfloat16)
        log_total = top_ref[g] + jnp.log(total)
        for h in range(ratio):
            log_ref[g, h] = log_total[:, h * block : (h + 1) * block]
    part = dot_nn(context_ref[...], weight_ref[...]).astype(jnp.bfloat16)

    @pl.when(step % 2 == 1)
    def _():
        send_ref[...] = part

    @pl.when(step % 2 == 0)
    def _():
        keep_ref[...] = part


def attend(half, earlier, place, flipped, rows, starts, weight):
    slots, _, length = flipped.shape
    groups = slots // KINDS
    block = length // PIECES // HALVES
    width = weight.shape[1]
    wide = groups * RATIO * HD
    at = lambda i, p: HALVES * (i ^ p[0]) + half
    flip_four = flipped.reshape(groups, KINDS, HD, length)
    row_four = rows.reshape(groups, KINDS, length, HD)
    out = jax.ShapeDtypeStruct((PIECES // 2, block, width), jnp.bfloat16)
    outs = pl.pallas_call(
        lambda *refs: attend_kernel(half, *refs),
        grid_spec=pltpu.PrefetchScalarGridSpec(
            num_scalar_prefetch=3,
            grid=(PIECES,),
            in_specs=[
                pl.BlockSpec((groups, RATIO, HD, block), lambda i, f, l, p: (0, 0, 0, at(i, p))),
                pl.BlockSpec((groups, None, length, HD), lambda i, f, l, p: (0, RATIO, 0, 0)),
                pl.BlockSpec((groups, None, HD, length), lambda i, f, l, p: (0, RATIO + 1, 0, 0)),
                pl.BlockSpec((1, block), lambda i, f, l, p: (0, at(i, p))),
                pl.BlockSpec(weight.shape, lambda i, f, l, p: (0, 0)),
            ]
            + [pl.BlockSpec(memory_space=pl.ANY)] * len(earlier),
            out_specs=[
                pl.BlockSpec((block, wide), lambda i, f, l, p: (at(i, p), 0)),
                pl.BlockSpec((wide, block), lambda i, f, l, p: (0, at(i, p))),
                pl.BlockSpec((groups, RATIO, 1, block), lambda i, f, l, p: (0, 0, 0, at(i, p))),
                pl.BlockSpec((None, block, width), lambda i, f, l, p: (i // 2, 0, 0)),
                pl.BlockSpec((None, block, width), lambda i, f, l, p: (i // 2, 0, 0)),
            ],
            scratch_shapes=[
                pltpu.VMEM((groups, 1, RATIO * block), jnp.float32),
                pltpu.VMEM((groups, 1, RATIO * block), jnp.float32),
                pltpu.VMEM((groups, HD, RATIO * block), jnp.float32),
            ],
        ),
        out_shape=[
            jax.ShapeDtypeStruct((length, wide), jnp.bfloat16),
            jax.ShapeDtypeStruct((wide, length), jnp.bfloat16),
            jax.ShapeDtypeStruct((groups, RATIO, 1, length), jnp.float32),
            out,
            out,
        ],
        input_output_aliases={8 + k: k for k in range(len(earlier))},
        compiler_params=params(),
        cost_estimate=cost(8 * groups * length * length * 64, 6 * MIB),
        name="attend",
    )(
        starts[::block], starts[block - 1 :: block], place, flip_four, row_four, flip_four,
        starts[None, :], weight, *earlier,
    )
    return (outs[:3], outs[3], outs[4])


def attend_back_kernel(pieces, first_ref, last_ref, place_ref, *refs):
    (query_ref, query_row_ref, key_ref, key_row_ref, value_row_ref, context_ref, log_ref,
     start_ref, weight_ref, raw_ref, raw_key_ref, cos_ref, sin_ref, gain_ref) = refs[:14]
    dh_pieces = refs[14 : 14 + pieces]
    if pieces > 1:
        joint_ref, gain_grad_ref, dh_ref = refs[14 + pieces : 17 + pieces]
    else:
        joint_ref, gain_grad_ref = refs[14 + pieces : 16 + pieces]
        dh_ref = dh_pieces[0]
    query_sum, key_sum, value_sum, query_gain_sum = refs[-4:]
    block = start_ref.shape[1]
    step = pl.program_id(0)
    steps = pl.num_programs(0)
    ratio = query_ref.shape[0]
    wide = ratio * HD

    @pl.when(step == 0)
    def _():
        key_sum[...] = jnp.zeros_like(key_sum)
        value_sum[...] = jnp.zeros_like(value_sum)
        query_gain_sum[...] = jnp.zeros_like(query_gain_sum)

    if pieces > 1:
        source = HALVES * ((step // HALVES) ^ place_ref[0]) + step % HALVES
        for r, piece in enumerate(dh_pieces):

            @pl.when(source == r)
            def _(piece=piece):
                dh_ref[...] = piece[...]

    query = jnp.concatenate([query_ref[h] for h in range(ratio)], axis=1)
    query_row = jnp.concatenate([query_row_ref[h] for h in range(ratio)], axis=0)
    start_row = start_ref[...]
    grad_wide = dot_nt(weight_ref[...], dh_ref[...]).astype(jnp.bfloat16)
    grad_float = grad_wide.astype(jnp.float32)
    products = grad_float * context_ref[...].astype(jnp.float32)
    delta = jnp.concatenate(
        [
            jnp.sum(products[h * HD : (h + 1) * HD], axis=0, keepdims=True)
            for h in range(ratio)
        ],
        axis=1,
    )
    grad = jnp.concatenate([grad_wide[h * HD : (h + 1) * HD] for h in range(ratio)], axis=1)
    turned = grad_float.T.astype(jnp.bfloat16)
    grad_row = jnp.concatenate([turned[:, h * HD : (h + 1) * HD] for h in range(ratio)], axis=0)
    log_total = jnp.concatenate([log_ref[h] for h in range(ratio)], axis=1)
    query_sum[...] = jnp.zeros_like(query_sum)

    def one(masked, at, size):
        at = pl.multiple_of(at, block)
        here = pl.ds(at, size)
        probs = jnp.exp(dot_nn(key_row_ref[here, :], query) - log_total)
        if masked:
            mask = mask_of(start_row, at, step * block, size)
            probs = jnp.where(jnp.concatenate([mask] * ratio, axis=1), probs, 0.0)
        prob_grad = dot_nn(value_row_ref[here, :], grad)
        score_grad = (probs * (prob_grad - delta)).astype(jnp.bfloat16)
        value_sum[here, :] += dot_nn(probs.astype(jnp.bfloat16), grad_row)
        key_sum[here, :] += dot_nn(score_grad, query_row)
        query_sum[...] += dot_nn(key_ref[:, here], score_grad)

    over_keys(one, first_ref[step], last_ref[step], step, block)

    def unwind(part, raw, cosine, sine, gain):
        inverse = head_scale(raw)
        back = rotate_back(part, cosine, sine)
        scaled = back * gain
        lean = jnp.mean(scaled * raw, axis=0, keepdims=True)
        return (back * raw * inverse, inverse * scaled - raw * inverse**3 * lean)

    at = pl.multiple_of(step * block, block)
    here = pl.ds(at, block)
    outs = []
    for h in range(ratio):
        part = query_sum[:, h * block : (h + 1) * block] * HD ** (-0.5)
        gain_part, out = unwind(
            part, raw_ref[h], cos_ref[:, here], sin_ref[:, here], gain_ref[:, 0:1]
        )
        query_gain_sum[...] += gain_part
        outs.append(out)
    joint_ref[here, :wide] = jnp.concatenate(outs, axis=0).T.astype(jnp.bfloat16)

    @pl.when(step == steps - 1)
    def _():
        def one_key(j, total):
            at = pl.multiple_of(j * block, block)
            here = pl.ds(at, block)
            pair = jnp.concatenate([key_sum[here, :], value_sum[here, :]], axis=1).T
            gain_part, out = unwind(
                pair[:HD], raw_key_ref[:, here], cos_ref[:, here], sin_ref[:, here],
                gain_ref[:, 1:2],
            )
            both = jnp.concatenate([out, pair[HD:]], axis=0)
            joint_ref[here, wide:] = both.T.astype(jnp.bfloat16)
            return total + gain_part

        key_gain_sum = lax.fori_loop(
            0, steps, one_key, jnp.zeros(query_gain_sum.shape, jnp.float32)
        )
        both = jnp.concatenate([query_gain_sum[...], key_gain_sum], axis=0).T
        gain_grad_ref[...] = jnp.sum(both, axis=0, keepdims=True)


def attend_back(
    g, place, flipped, rows, context_flip, log_total, starts, dh, weight, raw, tables, head_gains
):
    slots, _, length = flipped.shape
    groups = slots // KINDS
    ratio = RATIO
    block = length // PIECES // HALVES
    wide = ratio * HD
    width = weight.shape[1]
    pieces = len(dh)
    flip_four = flipped.reshape(groups, KINDS, HD, length)
    row_four = rows.reshape(groups, KINDS, length, HD)
    raw_four = raw.reshape(groups, KINDS, HD, length)
    by_step = pl.BlockSpec((block, width), lambda i, f, l, p: (i, 0))
    whole = pl.BlockSpec((block, width), lambda i, f, l, p: (0, 0))
    outs = pl.pallas_call(
        lambda *refs: attend_back_kernel(pieces, *refs),
        grid_spec=pltpu.PrefetchScalarGridSpec(
            num_scalar_prefetch=3,
            grid=(length // block,),
            in_specs=[
                pl.BlockSpec((None, ratio, HD, block), lambda i, f, l, p: (g, 0, 0, i)),
                pl.BlockSpec((None, ratio, block, HD), lambda i, f, l, p: (g, 0, i, 0)),
                pl.BlockSpec((None, None, HD, length), lambda i, f, l, p: (g, ratio, 0, 0)),
                pl.BlockSpec((None, None, length, HD), lambda i, f, l, p: (g, ratio, 0, 0)),
                pl.BlockSpec((None, None, length, HD), lambda i, f, l, p: (g, ratio + 1, 0, 0)),
                pl.BlockSpec((wide, block), lambda i, f, l, p: (g, i)),
                pl.BlockSpec((None, ratio, 1, block), lambda i, f, l, p: (g, 0, 0, i)),
                pl.BlockSpec((1, block), lambda i, f, l, p: (0, i)),
                pl.BlockSpec((wide, width), lambda i, f, l, p: (g, 0)),
                pl.BlockSpec((None, ratio, HD, block), lambda i, f, l, p: (g, 0, 0, i)),
                pl.BlockSpec((None, None, HD, length), lambda i, f, l, p: (g, ratio, 0, 0)),
                pl.BlockSpec((HD // 2, length), lambda i, f, l, p: (0, 0)),
                pl.BlockSpec((HD // 2, length), lambda i, f, l, p: (0, 0)),
                pl.BlockSpec(head_gains.shape, lambda i, f, l, p: (0, 0)),
            ]
            + [whole if pieces > 1 else by_step] * pieces,
            out_specs=[
                pl.BlockSpec((length, wide + 2 * HD), lambda i, f, l, p: (0, 0)),
                pl.BlockSpec((1, 2 * HD), lambda i, f, l, p: (0, 0)),
            ]
            + [by_step] * (pieces > 1),
            scratch_shapes=[
                pltpu.VMEM((HD, ratio * block), jnp.float32),
                pltpu.VMEM((length, HD), jnp.float32),
                pltpu.VMEM((length, HD), jnp.float32),
                pltpu.VMEM((HD, block), jnp.float32),
            ],
        ),
        out_shape=[
            jax.ShapeDtypeStruct((length, wide + 2 * HD), jnp.bfloat16),
            jax.ShapeDtypeStruct((1, 2 * HD), jnp.float32),
        ]
        + [jax.ShapeDtypeStruct((length, width), jnp.bfloat16)] * (pieces > 1),
        compiler_params=params(),
        cost_estimate=cost(20 * length * length * 128, 12 * MIB),
        name="attend_back",
    )(
        starts[::block], starts[block - 1 :: block], place, flip_four, row_four, flip_four, row_four, row_four, context_flip,
        log_total, starts[None, :], weight, raw_four, raw_four, tables[0], tables[1],
        head_gains, *dh,
    )
    return outs


def spread_kernel(groups, place_ref, *refs):
    send_rows, keep_rows = refs[:groups], refs[groups : 2 * groups]
    weight_ref, send_out, keep_out = refs[2 * groups :]
    depth = weight_ref.shape[0] // groups
    for rows, out in ((send_rows, send_out), (keep_rows, keep_out)):
        joined = jnp.concatenate([row[...] for row in rows], axis=1)
        out[...] = dot_nn(joined, weight_ref[...]).astype(jnp.bfloat16)


def spread(place, rows, weight):
    groups = len(rows)
    length, depth = rows[0].shape
    width = weight.shape[1]
    block = length // PIECES
    out = jax.ShapeDtypeStruct((PIECES // 2, block, width), jnp.bfloat16)
    return pl.pallas_call(
        lambda *refs: spread_kernel(groups, *refs),
        grid_spec=pltpu.PrefetchScalarGridSpec(
            num_scalar_prefetch=1,
            grid=(PIECES // 2,),
            in_specs=[pl.BlockSpec((block, depth), lambda i, p: ((2 * i + 1) ^ p[0], 0))] * groups
            + [pl.BlockSpec((block, depth), lambda i, p: ((2 * i) ^ p[0], 0))] * groups
            + [pl.BlockSpec(weight.shape, lambda i, p: (0, 0))],
            out_specs=[pl.BlockSpec((None, block, width), lambda i, p: (i, 0, 0))] * 2,
        ),
        out_shape=[out, out],
        compiler_params=params(),
        cost_estimate=cost(2 * length * width * depth * groups, 6 * MIB),
        name="spread",
    )(place, *rows, *rows, weight)


def feed_kernel(*refs):
    xs, grads, joint_ref, down_ref = refs[:2], refs[2:4], refs[4], refs[5]
    x_ref, grad_ref, hidden_ref, low_ref, out_keep, out_send, back_keep, back_send = refs[-8:]
    hidden_width = down_ref.shape[0]
    block = xs[0].shape[0]
    for r in range(2):
        x_ref[r * block : (r + 1) * block, :] = xs[r][...]
        grad_ref[r * block : (r + 1) * block, :] = grads[r][...]
    both = dot_nn(x_ref[...], joint_ref[...])
    gate, up = (both[:, :hidden_width], both[:, hidden_width:])
    sigmoid = 1.0 / (1.0 + jnp.exp(-gate))
    swish = gate * sigmoid
    hidden = (swish * up).astype(jnp.bfloat16)
    hidden_ref[...] = hidden
    hidden_grad = dot_nt(grad_ref[...], down_ref[...])
    low_ref[:, :hidden_width] = (
        hidden_grad * up * sigmoid * (1.0 + gate * (1.0 - sigmoid))
    ).astype(jnp.bfloat16)
    low_ref[:, hidden_width:] = (hidden_grad * swish).astype(jnp.bfloat16)
    out = dot_nn(hidden, down_ref[...]).astype(jnp.bfloat16)
    out_keep[...] = out[:block]
    out_send[...] = out[block:]
    back = dot_nt(low_ref[...], joint_ref[...]).astype(jnp.bfloat16)
    back_keep[...] = back[:block]
    back_send[...] = back[block:]


def feed(call, half, earlier, normed, grads, joint_weight, down_weight):
    block, width = normed[0].shape
    hidden_width = down_weight.shape[0]
    length = block * PIECES * HALVES
    once = pl.Buffered(1)
    row = lambda columns: pl.BlockSpec((2 * block, columns), lambda i: (call, 0))
    whole = lambda value: pl.BlockSpec(value.shape, lambda i: (0, 0), pipeline_mode=once)
    pair = pl.BlockSpec((block, width), lambda i: (0, 0))
    full = lambda columns: jax.ShapeDtypeStruct((length, columns), jnp.bfloat16)
    outs = pl.pallas_call(
        feed_kernel,
        grid=(1,),
        in_specs=[pl.BlockSpec((block, width), lambda i: (0, 0), pipeline_mode=once)] * 2
        + [pl.BlockSpec((block, width), lambda i: (half, 0), pipeline_mode=once)] * 2
        + [whole(joint_weight), whole(down_weight)]
        + [pl.BlockSpec(memory_space=pl.ANY)] * len(earlier),
        out_specs=[row(width), row(width), row(hidden_width), row(2 * hidden_width)] + [pair] * 4,
        out_shape=[full(width), full(width), full(hidden_width), full(2 * hidden_width)]
        + [jax.ShapeDtypeStruct((block, width), jnp.bfloat16)] * 4,
        input_output_aliases={6 + k: k for k in range(len(earlier))},
        compiler_params=params(),
        cost_estimate=cost(3 * length * width * hidden_width, 16 * MIB),
        name="feed",
    )(*normed, *grads, joint_weight, down_weight, *earlier)
    return (outs[:4], outs[4:6], outs[6:8])


def norm_kernel(x_ref, keep_ref, near_ref, far_ref, gain_ref, middle_ref, normed_ref):
    f32 = jnp.float32
    middle = x_ref[...].astype(f32) + (
        keep_ref[...].astype(f32) + near_ref[...].astype(f32) + far_ref[...].astype(f32)
    )
    middle_ref[...] = middle
    normed_ref[...] = (middle * row_scale(middle) * gain_ref[...]).astype(jnp.bfloat16)


def first_of(value, rows, width):
    if value.ndim == 3:
        return pl.BlockSpec((None, rows, width), lambda i: (0, i, 0))
    return pl.BlockSpec((rows, width), lambda i: (i, 0))


def norm(half, tokens, keep, near, far, gain):
    length, width = far.shape
    steps = 2
    rows = length // steps
    flat = pl.BlockSpec((rows, width), lambda i: (i, 0))
    return pl.pallas_call(
        norm_kernel,
        grid=(steps,),
        in_specs=[
            pl.BlockSpec((rows, width), lambda i: (half * steps + i, 0)),
            first_of(keep, rows, width),
            first_of(near, rows, width),
            flat,
            pl.BlockSpec(gain.shape, lambda i: (0, 0)),
        ],
        out_specs=[flat, flat],
        out_shape=[
            jax.ShapeDtypeStruct((length, width), jnp.float32),
            jax.ShapeDtypeStruct((length, width), jnp.bfloat16),
        ],
        compiler_params=params(),
        cost_estimate=cost(0, 4 * MIB),
        name="norm",
    )(tokens, keep, near, far, gain)


def norm_back_of(value, skip, grad, gain):
    inverse = row_scale(value)
    scaled = grad * gain
    lean = jnp.mean(scaled * value, axis=-1, keepdims=True)
    total = skip + (inverse * scaled - value * (inverse**3 * lean))
    return total, jnp.sum(grad * value * inverse, axis=0, keepdims=True)


def norm_back_kernel(
    value_ref, skip_ref, keep_ref, near_ref, far_ref, gain_ref, low_ref, part_ref
):
    f32 = jnp.float32
    grad = keep_ref[...].astype(f32) + near_ref[...].astype(f32) + far_ref[...].astype(f32)
    total, part = norm_back_of(value_ref[...], skip_ref[...].astype(f32), grad, gain_ref[...])
    low_ref[...] = total.astype(jnp.bfloat16)

    @pl.when(pl.program_id(0) == 0)
    def _():
        part_ref[...] = jnp.zeros_like(part_ref)

    part_ref[...] += part


def norm_back(half, value, skip, keep, near, far, gain):
    length, width = far.shape
    steps = 2
    rows = length // steps
    flat = pl.BlockSpec((rows, width), lambda i: (i, 0))
    return pl.pallas_call(
        norm_back_kernel,
        grid=(steps,),
        in_specs=[
            flat,
            pl.BlockSpec((rows, width), lambda i: (half * steps + i, 0)),
            first_of(keep, rows, width),
            first_of(near, rows, width),
            flat,
            pl.BlockSpec(gain.shape, lambda i: (0, 0)),
        ],
        out_specs=[flat, pl.BlockSpec((1, width), lambda i: (0, 0))],
        out_shape=[
            jax.ShapeDtypeStruct((length, width), jnp.bfloat16),
            jax.ShapeDtypeStruct((1, width), jnp.float32),
        ],
        compiler_params=params(),
        cost_estimate=cost(0, 6 * MIB),
        name="norm_back",
    )(value, skip, keep, near, far, gain)


def row_kernel(counts, *refs):
    scatter_ref, row_ref, turned_ref = refs[-3:]
    parts, heads, squares = refs[: counts[0]], refs[counts[0] : counts[1]], refs[counts[1] : -3]
    width = parts[0].shape[1]
    total = lambda items: sum([item[...] for item in items[1:]], items[0][...])
    row_ref[:, :width] = jnp.zeros((1, width), jnp.float32)
    row_ref[:, width : 2 * width] = total(parts)
    row_ref[:, 2 * width : 2 * width + 2 * HD] = total(heads)
    scattered = scatter_ref[...].astype(jnp.float32)
    turned_ref[...] = scattered.T
    over = jnp.sum(scattered * scattered, axis=0, keepdims=True)
    square = jnp.sum(over, axis=1, keepdims=True) + total(squares)
    lane = lax.broadcasted_iota(jnp.int32, (1, 2 * HD), 1)
    row_ref[:, 2 * width + 2 * HD :] = jnp.where(lane == 0, square, 0.0)


def row_of(parts, heads, squares, scattered):
    counts = (len(parts), len(parts) + len(heads))
    return pl.pallas_call(
        lambda *refs: row_kernel(counts, *refs),
        out_shape=[
            jax.ShapeDtypeStruct((1, 2 * parts[0].shape[1] + 4 * HD), jnp.float32),
            jax.ShapeDtypeStruct(scattered.shape[::-1], jnp.float32),
        ],
        compiler_params=params(24),
        cost_estimate=cost(0, MIB),
        name="row",
    )(*parts, *heads, *squares, scattered)


def finish_kernel(
    x_ref, near_skip, far_skip, keep_ref, near_ref, far_ref, gain_ref, begin_ref, square_ref,
    input_grad_ref, row_ref,
):
    f32 = jnp.float32
    step = pl.program_id(0)
    width = x_ref.shape[1]
    grad = keep_ref[...].astype(f32) + near_ref[...].astype(f32) + far_ref[...].astype(f32)
    skip = jnp.where(step < pl.num_programs(0) // HALVES, near_skip[...], far_skip[...])
    total, part = norm_back_of(
        x_ref[...].astype(f32), skip.astype(f32), grad, gain_ref[...]
    )
    input_grad_ref[...] = total.astype(jnp.bfloat16)

    @pl.when(step == 0)
    def _():
        lane = lax.broadcasted_iota(jnp.int32, row_ref.shape, 1)
        last = jnp.where(lane == 2 * width + 2 * HD, square_ref[...], 0.0)
        row_ref[...] = begin_ref[...] + last

    row_ref[:, :width] += part


def finish(tokens, skips, keep, near, far, gain, row, square):
    length, width = far.shape
    each = 1
    rows = length // HALVES // each
    flat = pl.BlockSpec((rows, width), lambda i: (i, 0))
    whole = lambda value: pl.BlockSpec(value.shape, lambda i: (0, 0))
    return pl.pallas_call(
        finish_kernel,
        grid=(HALVES * each,),
        in_specs=[
            flat,
            pl.BlockSpec((rows, width), lambda i: (jnp.minimum(i, each - 1), 0)),
            pl.BlockSpec((rows, width), lambda i: (jnp.maximum(i - each, 0), 0)),
            first_of(keep, rows, width),
            first_of(near, rows, width),
            flat,
            whole(gain),
            whole(row),
            whole(square),
        ],
        out_specs=[flat, whole(row)],
        out_shape=[
            jax.ShapeDtypeStruct((length, width), jnp.bfloat16),
            jax.ShapeDtypeStruct(row.shape, jnp.float32),
        ],
        compiler_params=params(),
        cost_estimate=cost(0, 6 * MIB),
        name="finish",
    )(tokens, *skips, keep, near, far, gain, row, square)


def exchange(value, axis, bit):
    size = lax.axis_size(axis)
    return lax.ppermute(value, axis, [(i, i ^ bit) for i in range(size)])


def after(value, *others):
    return lax.optimization_barrier((value, *others))[0]


def power_of_two(count):
    return count & (count - 1) == 0


class ScatterSum:
    def __init__(self, grads, flipped, second_first=False):
        size = lax.axis_size("dp")
        rows = grads[0].shape[0] // size
        self.left = [1 << k for k in reversed(range(size.bit_length() - 1))]
        self.order = self.left[::-1]
        if second_first:
            self.order[:2] = self.order[1::-1]
        self.flipped = flipped
        self.sources = [grad.reshape(size, rows, grad.shape[1]) for grad in grads]
        self.columns = sum(grad.shape[1] for grad in grads)
        self.joined = True
        self.total = None


def advance_kernel(plans, here_ref, *refs):
    count = sum(plan[0] for plan in plans)
    ins, outs = refs[:count], refs[count:]
    squares = jnp.zeros((1, 1), jnp.float32)
    for sources, joined, stride, shift, flipped in plans:
        parts, ins = ins[:sources], ins[sources:]

        def value(at, parts=parts, joined=joined):
            if joined:
                return jnp.concatenate([part[at] for part in parts], axis=1)
            return parts[0][at].astype(jnp.float32) + parts[1][at].astype(jnp.float32)

        if stride is None:
            total = value(0).astype(jnp.float32)
            over = jnp.sum(total * total, axis=0, keepdims=True)
            squares += jnp.sum(over, axis=1, keepdims=True)
            at = 0
            for columns, turned in flipped:
                part = total[:, at : at + columns]
                outs[0][...] = part.T if turned else part
                at, outs = at + columns, outs[1:]
            continue
        sent, kept, outs = outs[0], outs[1], outs[2:]
        own = (here_ref[0] >> shift) & 1
        for k in range(sent.shape[0]):
            base = k // stride * 2 * stride + k % stride
            sent[k] = value(base + (1 - own) * stride).astype(sent.dtype)
            kept[k] = value(base + own * stride).astype(kept.dtype)
    outs[0][...] = squares


def advance(here, items, *gates):
    plans, ins, shapes = [], [], []
    for item in items:
        rows, columns = item.sources[0].shape[1], item.columns
        if item.order:
            bit = item.order[0]
            at = item.left.index(bit)
            stride = 1 << (len(item.left) - 1 - at)
            plans.append((len(item.sources), item.joined, stride, bit.bit_length() - 1, ()))
            half = (item.sources[0].shape[0] // 2, rows, columns)
            shapes += [jax.ShapeDtypeStruct(half, jnp.bfloat16)] * 2
        else:
            plans.append((len(item.sources), item.joined, None, 0, item.flipped))
            for part, turned in item.flipped:
                shape = (part, rows) if turned else (rows, part)
                shapes.append(jax.ShapeDtypeStruct(shape, jnp.float32))
        ins += item.sources
    shapes.append(jax.ShapeDtypeStruct((1, 1), jnp.float32))
    if gates:
        ins[-1] = after(ins[-1], *gates)
    vmem = pl.BlockSpec(memory_space=pltpu.VMEM)
    outs = list(pl.pallas_call(
        lambda *refs: advance_kernel(plans, *refs),
        in_specs=[pl.BlockSpec(memory_space=pltpu.SMEM)] + [vmem] * len(ins),
        out_specs=[vmem] * len(shapes),
        out_shape=shapes,
        compiler_params=params(24),
        cost_estimate=cost(0, 6 * MIB),
        name="advance",
    )(here, *ins))
    sent_all = []
    for item in items:
        if item.order:
            bit = item.order.pop(0)
            item.left.remove(bit)
            sent, kept = outs.pop(0), outs.pop(0)
            item.sources, item.joined = [kept, exchange(sent, "dp", bit)], False
            sent_all.append(sent)
        else:
            item.total = [outs.pop(0) for _ in item.flipped]
    return sent_all, outs[0]


def sum_all(value):
    for axis in ("tensor", "dp"):
        size = lax.axis_size(axis)
        if not power_of_two(size):
            value = lax.psum(value, axis)
            continue
        bit = 1
        while bit < size:
            if 2 * bit < size:
                one, two, three = [exchange(value, axis, bit * k) for k in (1, 2, 3)]
                value = (value + one) + (two + three)
                bit *= 4
            else:
                value = value + exchange(value, axis, bit)
                bit *= 2
    return value


def adam(master, mean, square, grad, factor, rate, decay):
    scaled = grad * factor
    mean_new = BETA_ONE * mean + (1.0 - BETA_ONE) * scaled
    square_new = BETA_TWO * square + (1.0 - BETA_TWO) * scaled * scaled
    mean_hat = mean_new / (1.0 - BETA_ONE**STEP)
    square_hat = square_new / (1.0 - BETA_TWO**STEP)
    new = master - rate * (mean_hat / (jnp.sqrt(square_hat) + ADAM_EPS) + decay * master)
    return (new, mean_new, square_new)


def adam_kernel(
    out_rate, entries, sum_ref, out_sum, early_ref, late_ref, gate_ref, up_ref, down_sum, *refs
):
    gain_sum = sum_ref[:, :entries]
    squares = sum_ref[:, entries : entries + 1]
    norm = jnp.sqrt(squares + jnp.sum(gain_sum * gain_sum, axis=1, keepdims=True))
    factor = CLIP_NORM / jnp.maximum(norm, CLIP_NORM)
    states = [refs[3 * k : 3 * k + 3] for k in range(4)]
    results = [refs[12 + 4 * k : 16 + 4 * k] for k in range(4)]
    refs[28][...] = norm

    def update(state, result, at, grad, rate):
        new, mean, square = adam(
            state[0][at], state[1][at], state[2][at], grad.astype(jnp.float32), factor, rate,
            DECAY,
        )
        result[0][at] = new
        result[1][at] = new.astype(jnp.bfloat16)
        result[2][at] = mean
        result[3][at] = square

    rows = slice(None)
    early = early_ref.shape[1]
    update(states[1], results[1], (rows, rows), out_sum[...], out_rate)
    update(states[0], results[0], (rows, slice(0, early)), early_ref[...], RATE_WEIGHT)
    update(states[0], results[0], (rows, slice(early, None)), late_ref[...], RATE_WEIGHT)
    update(states[2], results[2], (rows, 0, rows), gate_ref[...], RATE_WEIGHT)
    update(states[2], results[2], (rows, 1, rows), up_ref[...], RATE_WEIGHT)
    update(states[3], results[3], (rows, rows), down_sum[...], RATE_WEIGHT)


def adam_all(entries, summed, sums, states, out_rate):
    steps = max(1, states[0][0].shape[0] // 32)

    def block(array):
        rows = array.shape[0] // steps
        rest = array.shape[1:]
        return pl.BlockSpec((rows,) + rest, lambda i: (i,) + (0,) * len(rest))

    shapes = []
    for state in states:
        shapes += [
            jax.ShapeDtypeStruct(state[0].shape, dtype)
            for dtype in (jnp.float32, jnp.bfloat16, jnp.float32, jnp.float32)
        ]
    arrays = [*sums]
    for state in states:
        arrays += state
    small = lambda shape: pl.BlockSpec(shape, lambda i: (0, 0))
    return pl.pallas_call(
        lambda *refs: adam_kernel(out_rate, entries, *refs),
        grid=(steps,),
        in_specs=[small(summed.shape)] + [block(array) for array in arrays],
        out_specs=[block(shape) for shape in shapes] + [small((1, 1))],
        out_shape=shapes + [jax.ShapeDtypeStruct((1, 1), jnp.float32)],
        compiler_params=params(),
        cost_estimate=cost(0, 16 * MIB),
        name="adam",
    )(summed, *arrays)


def shards(
    tokens,
    segments,
    cotangent,
    qkv_weight,
    out_weight,
    gate_up_weight,
    down_weight,
    qkv_master,
    out_master,
    gate_up_master,
    down_master,
    qkv_mean,
    out_mean,
    gate_up_mean,
    down_mean,
    qkv_square,
    out_square,
    gate_up_square,
    down_square,
    gains,
    gains_mean,
    gains_square,
):
    width = tokens.shape[1]
    length = segments.shape[0]
    groups = qkv_weight.shape[1] // (KINDS * HD)
    hidden_width = down_weight.shape[0]
    block = length // PIECES // HALVES
    attn_gain = gains[None, :width]
    ffn_gain = gains[None, width : 2 * width]
    head_gains = jnp.stack([gains[2 * width : 2 * width + HD], gains[2 * width + HD :]], axis=1)
    place = lax.axis_index("tensor").astype(jnp.int32).reshape(1)
    here = lax.axis_index("dp").astype(jnp.int32).reshape(1)

    across = exchange(tokens, "tensor", ACROSS)
    beside = exchange(tokens, "tensor", CORE)
    starts = starts_of(segments)
    tables = rotary((jnp.arange(length, dtype=jnp.int32) - starts).astype(jnp.float32))
    weight_rows = qkv_weight.T
    inner = (attn_gain, weight_rows, head_gains, *tables)
    near_part = project(0, [], place, [tokens, beside], *inner)
    flat_weight = after(gate_up_weight, near_part[2]).reshape(width, 2 * hidden_width)
    across = after(across, near_part[2], flat_weight)
    corner = exchange(across, "tensor", CORE)
    normed_one, raw, flipped, rows = project(1, near_part, place, [across, corner], *inner)

    grad_across = exchange(after(cotangent, across), "tensor", ACROSS)
    grad_pieces = [
        cotangent,
        exchange(after(cotangent, across), "tensor", CORE),
        grad_across,
        exchange(grad_across, "tensor", CORE),
    ]

    def added(left, right):
        return (left.astype(jnp.float32) + right.astype(jnp.float32)).astype(jnp.bfloat16)

    def halfway(send, keep):
        near = exchange(send, "tensor", CORE)
        return (keep, near, added(keep[1], near[1]))

    def across_of(passed):
        keep, near, passed = passed
        return (keep, near, exchange(passed, "tensor", ACROSS))

    attended, send, keep = attend(0, [], place, flipped, rows, starts, out_weight)
    passed = halfway(after(send, grad_across), keep)
    shares = across_of(passed)
    flipped_late = after(flipped, passed[2])
    attended, send, keep = attend(1, attended, place, flipped_late, rows, starts, out_weight)
    context, context_flip, log_total = attended

    weights = (flat_weight, down_weight)
    middle, normed = norm(0, tokens, *shares, ffn_gain)
    middles = [middle]
    beside, across = exchange(normed, "tensor", CORE), exchange(normed, "tensor", ACROSS)
    passed = halfway(after(send, shares[2]), keep)
    shares = across_of(passed)
    full, out_near, back_near = feed(
        0, 0, [], [after(normed, passed[2]), beside], grad_pieces[:2], *weights
    )
    across = after(across, out_near[0])
    corner = exchange(across, "tensor", CORE)
    full, out_far, back_far = feed(1, 0, full, [across, corner], grad_pieces[2:], *weights)
    outs, backs = [(*out_near, *out_far)], [(*back_near, *back_far)]

    keep, near, far = shares
    middle, normed = norm(1, tokens, keep, near, after(far, out_far[0]), ffn_gain)
    middles.append(middle)
    beside, across = exchange(normed, "tensor", CORE), exchange(normed, "tensor", ACROSS)
    full, out_near, back_near = feed(2, 1, full, [normed, beside], grad_pieces[:2], *weights)

    def share_of(pieces, *gates):
        third = exchange(pieces[3], "tensor", CORE)
        third = after(third, *gates) if gates else third
        return (pieces[0], exchange(pieces[1], "tensor", CORE), added(pieces[2], third))

    passed = share_of(backs[0], out_near[0])
    sums = [across_of(passed)]
    across = after(across, out_near[0])
    corner = exchange(across, "tensor", CORE)
    across = after(across, passed[2])
    full, out_far, back_far = feed(3, 1, full, [across, corner], grad_pieces[2:], *weights)
    outs.append((*out_near, *out_far))
    backs.append((*back_near, *back_far))
    normed_two, grad_full, hidden, flat_low = full

    def dh_of(half, keep, near, far):
        low, part = norm_back(half, middles[half], cotangent, keep, near, far, ffn_gain)
        across = exchange(low, "tensor", ACROSS)
        pieces = [low, exchange(low, "tensor", CORE), across, exchange(across, "tensor", CORE)]
        return pieces, part

    keep, near, far = sums[0]
    first_dh = dh_of(0, keep, near, after(far, out_far[0]))
    passed = share_of(after(tuple(backs[1]), far))
    sums.append(across_of(passed))
    sent = after(grad_full, passed[2], first_dh[0][0])
    down_grad = contract_rows(sent, hidden).astype(jnp.bfloat16)
    gate_grad = contract_rows(after(normed_two, down_grad), flat_low[:, :hidden_width])
    gate = ScatterSum([gate_grad.astype(jnp.bfloat16)], [(hidden_width, False)])
    sent, square = advance(here, [gate])
    squares = [square]
    out_sums = [share_of(after(tuple(out), passed[2])) for out in outs]
    keep, near, far = sums[1]
    far_late = after(far, sent[0], first_dh[0][2])
    second_dh = dh_of(1, keep, near, far_late)
    pieces_dh, ffn_parts = zip(first_dh, second_dh)
    down_sum = lax.psum_scatter(
        after(down_grad, far_late), "dp", scatter_dimension=0, tiled=True
    )
    normed_two = after(normed_two, pieces_dh[1][0])
    up_grad = contract_rows(normed_two, flat_low[:, hidden_width:])
    up = ScatterSum([up_grad.astype(jnp.bfloat16)], [(hidden_width, False)], True)
    advance(here, [up], pieces_dh[1][2])
    sent, _ = advance(here, [gate], up.sources[0])

    dh = [pieces_dh[half][r] for r in range(PIECES) for half in range(HALVES)]
    dh[0] = after(dh[0], *sent, *[item[2] for item in out_sums])
    out_fars = [
        exchange(after(item[2], pieces_dh[1][2]), "tensor", ACROSS) for item in out_sums
    ]

    joints, head_parts, mixed, early = [], [], [], []
    for g in range(groups):
        outs_back = attend_back(
            g, place, flipped, rows, context_flip, log_total, starts, dh, out_weight, raw, tables,
            head_gains,
        )
        joints.append(outs_back[0])
        head_parts.append(outs_back[1])
        if g == 0:
            dh_full = outs_back[2]
            early = ScatterSum(
                [
                    contract_rows(dh_full, context).astype(jnp.bfloat16),
                    contract_rows(normed_one, outs_back[0]).astype(jnp.bfloat16),
                ],
                [(context.shape[1], True), (joints[0].shape[1], False)],
            )
            sent, _ = advance(here, [gate, up, early], outs_back[1])
            dh = [after(dh_full, *sent, *out_fars)]
        else:
            dh = [dh_full]
    sent, square = advance(here, [gate, up, early], joints[-1], down_sum)
    squares.append(square)
    joints[0] = after(joints[0], *sent)
    send, keep = spread(place, joints, weight_rows)
    late = [
        contract_rows(normed_one, after(joints[g], keep)).astype(jnp.bfloat16)
        for g in range(1, groups)
    ]
    near = exchange(send, "tensor", CORE)
    passed = (keep, near, added(keep[1], near[1]))
    keep, near, far = across_of(passed)
    late = ScatterSum(late, [(joints[0].shape[1] * (groups - 1), False)])
    pending = [gate, up, early, late]
    gates = [passed[2]]
    while pending:
        pending = [item for item in pending if item.total is None]
        _, square = advance(here, pending, *gates)
        squares.append(square)
        pending = [item for item in pending if item.total is None]
        gates = []

    results = []
    for half in range(HALVES):
        keep_out, near_out, _ = out_sums[half]
        total = keep_out.astype(jnp.float32) + near_out.astype(jnp.float32)
        results.append(middles[half] + (total + out_fars[half].astype(jnp.float32)))
    result = jnp.concatenate(results, axis=0).astype(jnp.bfloat16)

    ffn_parts = [after(ffn_parts[0], result), *ffn_parts[1:]]
    row, down_total = row_of(ffn_parts, head_parts, squares[1:-1], down_sum)
    skips = [pieces[0] for pieces in pieces_dh]
    input_grad, row = finish(tokens, skips, keep, near, far, attn_gain, row, squares[-1])
    summed = sum_all(row)
    entries = gains.shape[0]
    out_fan = max(QH * HD * 16 // length, 16)
    out_rate = RATE_WEIGHT * (QH * HD / out_fan) ** 0.5
    updated = adam_all(
        entries, summed, [*early.total, *late.total, *gate.total, *up.total, down_total],
        [
            (qkv_master, qkv_mean, qkv_square),
            (out_master, out_mean, out_square),
            (gate_up_master, gate_up_mean, gate_up_square),
            (down_master, down_mean, down_square),
        ],
        out_rate,
    )
    grad_norm = updated[16][0, 0]
    factor = CLIP_NORM / jnp.maximum(grad_norm, CLIP_NORM)
    gain_results = adam(
        gains, gains_mean, gains_square, summed[0, :entries], factor, RATE_GAIN, 0.0
    )
    return (result, input_grad, grad_norm, *updated[:16], *gain_results)


def solution(mesh):
    in_specs = (
        P(("dp", "tensor"), None),
        P("dp"),
        P(("dp", "tensor"), None),
        P(None, "tensor"),
        P("tensor", None),
        P(None, None, "tensor"),
        P("tensor", None),
        P("dp", "tensor"),
        P("tensor", "dp"),
        P("dp", None, "tensor"),
        P("tensor", "dp"),
        P("dp", "tensor"),
        P("tensor", "dp"),
        P("dp", None, "tensor"),
        P("tensor", "dp"),
        P("dp", "tensor"),
        P("tensor", "dp"),
        P("dp", None, "tensor"),
        P("tensor", "dp"),
        P(),
        P(),
        P(),
    )
    out_specs = (
        P(("dp", "tensor"), None),
        P(("dp", "tensor"), None),
        P(),
        P("dp", "tensor"),
        P("dp", "tensor"),
        P("dp", "tensor"),
        P("dp", "tensor"),
        P("tensor", "dp"),
        P("tensor", "dp"),
        P("tensor", "dp"),
        P("tensor", "dp"),
        P("dp", None, "tensor"),
        P("dp", None, "tensor"),
        P("dp", None, "tensor"),
        P("dp", None, "tensor"),
        P("tensor", "dp"),
        P("tensor", "dp"),
        P("tensor", "dp"),
        P("tensor", "dp"),
        P(),
        P(),
        P(),
    )
    return jax.shard_map(shards, mesh=mesh, in_specs=in_specs, out_specs=out_specs, check_vma=False)
```

```python
import jax
import jax.numpy as jnp
from jax import lax
from jax.experimental import pallas as pl
from jax.experimental.pallas import tpu as pltpu
from jax.sharding import PartitionSpec as P

QH = 16
KVH = 8
HD = 64
STEP = 5


NORM_EPS = 1e-06
ROPE_BASE = 1000000.0
CLIP_NORM = 1.0
BETA_ONE = 0.9
BETA_TWO = 0.95
ADAM_EPS = 1e-08
DECAY = 0.1
RATE_WEIGHT = 0.02
RATE_GAIN = 1.5
MASKED = -1e30

KINDS = QH // KVH + 2
RATIO = QH // KVH
PARTS = 2
PIECES = 4
HALVES = 2
CORE = 1
ACROSS = 2
MIB = 1024 * 1024


def params(limit=60):
    return pltpu.CompilerParams(vmem_limit_bytes=limit * MIB)


def cost(flops, size):
    return pl.CostEstimate(flops=flops // 8, bytes_accessed=size // 8, transcendentals=0)


def starts_of(seg):
    index = jnp.arange(seg.shape[0], dtype=jnp.int32)
    flag = (index == 0) | (seg != jnp.roll(seg, 1))
    return lax.cummax(jnp.where(flag, index, 0), axis=0)


def rotary(position):
    half = HD // 2
    freq = ROPE_BASE ** (-(jnp.arange(half, dtype=jnp.float32) * 2.0 / HD))
    angle = freq[:, None] * position[None, :]
    return (jnp.cos(angle), jnp.sin(angle))


def dot_nn(left, right):
    return lax.dot_general(
        left, right, (((1,), (0,)), ((), ())), preferred_element_type=jnp.float32
    )


def dot_nt(left, right):
    return lax.dot_general(
        left, right, (((1,), (1,)), ((), ())), preferred_element_type=jnp.float32
    )


def contract_rows(left, right):
    return lax.dot_general(
        left, right, (((0,), (0,)), ((), ())), preferred_element_type=jnp.float32
    )


def rotate(value, cosine, sine):
    half = value.shape[0] // 2
    first, second = (value[:half], value[half:])
    return jnp.concatenate(
        [first * cosine - second * sine, second * cosine + first * sine], axis=0
    )


def rotate_back(grad, cosine, sine):
    half = grad.shape[0] // 2
    first, second = (grad[:half], grad[half:])
    return jnp.concatenate(
        [first * cosine + second * sine, second * cosine - first * sine], axis=0
    )


def row_scale(value):
    return lax.rsqrt(jnp.mean(value * value, axis=-1, keepdims=True) + NORM_EPS)


def head_scale(value):
    return lax.rsqrt(jnp.mean(value * value, axis=0, keepdims=True) + NORM_EPS)


def project_kernel(place_ref, *refs):
    pieces = refs[:2]
    pre_ref, weight_ref, gain_ref, cos_ref, sin_ref = refs[2:7]
    normed_ref, raw_ref, flip_ref, row_ref = refs[-4:]
    step = pl.program_id(0)
    for r in range(2):

        @pl.when(step // PARTS == r)
        def _(r=r):
            value = pieces[r][...].astype(jnp.float32)
            normed_ref[...] = (value * row_scale(value) * pre_ref[...]).astype(jnp.bfloat16)

    joint = dot_nt(weight_ref[...], normed_ref[...])
    cosine, sine = cos_ref[...], sin_ref[...]
    for slot in range(raw_ref.shape[0]):
        kind = slot % KINDS
        raw = joint[slot * HD : (slot + 1) * HD]
        raw_ref[slot] = raw
        value = raw
        if kind < KINDS - 1:
            gain = gain_ref[:, 1:2] if kind == KINDS - 2 else gain_ref[:, 0:1]
            value = rotate(raw * head_scale(raw) * gain, cosine, sine)
        if kind < KINDS - 2:
            value = value * HD ** (-0.5)
        low = value.astype(jnp.bfloat16)
        flip_ref[slot] = low
        row_ref[slot] = low.T


def project(far, earlier, place, pieces, pre_gain, weight_rows, head_gains, cos_table, sin_table):
    rows, width = pieces[0].shape
    length = rows * PIECES
    block = rows // PARTS
    slots = weight_rows.shape[0] // HD
    at = lambda i, p: PARTS * ((i // PARTS + 2 * far) ^ p[0]) + i % PARTS

    def piece(r):
        return pl.BlockSpec(
            (block, width), lambda i, p: (jnp.clip(i - PARTS * r, 0, PARTS - 1), 0)
        )

    return pl.pallas_call(
        project_kernel,
        grid_spec=pltpu.PrefetchScalarGridSpec(
            num_scalar_prefetch=1,
            grid=(2 * PARTS,),
            in_specs=[piece(0), piece(1)]
            + [
                pl.BlockSpec(pre_gain.shape, lambda i, p: (0, 0)),
                pl.BlockSpec(weight_rows.shape, lambda i, p: (0, 0)),
                pl.BlockSpec(head_gains.shape, lambda i, p: (0, 0)),
                pl.BlockSpec((HD // 2, block), lambda i, p: (0, at(i, p))),
                pl.BlockSpec((HD // 2, block), lambda i, p: (0, at(i, p))),
            ]
            + [pl.BlockSpec(memory_space=pl.ANY)] * len(earlier),
            out_specs=[
                pl.BlockSpec((block, width), lambda i, p: (at(i, p), 0)),
                pl.BlockSpec((slots, HD, block), lambda i, p: (0, 0, at(i, p))),
                pl.BlockSpec((slots, HD, block), lambda i, p: (0, 0, at(i, p))),
                pl.BlockSpec((slots, block, HD), lambda i, p: (0, at(i, p), 0)),
            ],
        ),
        out_shape=[
            jax.ShapeDtypeStruct((length, width), jnp.bfloat16),
            jax.ShapeDtypeStruct((slots, HD, length), jnp.float32),
            jax.ShapeDtypeStruct((slots, HD, length), jnp.bfloat16),
            jax.ShapeDtypeStruct((slots, length, HD), jnp.bfloat16),
        ],
        input_output_aliases={8 + k: k for k in range(len(earlier))},
        compiler_params=params(),
        cost_estimate=cost(length * width * slots * HD, 8 * MIB),
        name="project",
    )(place, *pieces, pre_gain, weight_rows, head_gains, cos_table, sin_table, *earlier)


def mask_of(start_row, first_key, first_query, keys):
    queries = start_row.shape[1]
    key = first_key + lax.broadcasted_iota(jnp.int32, (keys, 1), 0)
    query = first_query + lax.broadcasted_iota(jnp.int32, (1, queries), 1)
    return (key >= start_row) & (key <= query)


def over_keys(one, first, last, at_query, block):
    begin = first // block
    whole = jnp.maximum(begin, jnp.minimum((last + block - 1) // block, at_query))
    pairs = (at_query - whole) // 2
    lax.fori_loop(begin, whole, lambda j, carry: one(True, j * block, block), None)
    lax.fori_loop(
        0, pairs, lambda k, carry: one(False, (whole + 2 * k) * block, 2 * block), None
    )
    lax.fori_loop(
        whole + 2 * pairs, at_query, lambda j, carry: one(False, j * block, block), None
    )
    one(True, at_query * block, block)


def attend_kernel(half, first_ref, last_ref, place_ref, *refs):
    query_ref, key_ref, value_ref, start_ref, weight_ref = refs[:5]
    context_ref, flip_ref, log_ref, send_ref, keep_ref, top_ref, total_ref, sum_ref = refs[-8:]
    groups, ratio = query_ref.shape[:2]
    block = start_ref.shape[1]
    step = pl.program_id(0)
    at_query = HALVES * (step ^ place_ref[0]) + half
    start_row = start_ref[...]
    queries = [
        jnp.concatenate([query_ref[g, h] for h in range(ratio)], axis=1) for g in range(groups)
    ]
    top_ref[...] = jnp.full_like(top_ref, MASKED)
    total_ref[...] = jnp.zeros_like(total_ref)
    sum_ref[...] = jnp.zeros_like(sum_ref)

    def one(masked, at, size):
        at = pl.multiple_of(at, block)
        if masked:
            mask = mask_of(start_row, at, at_query * block, size)
            mask = jnp.concatenate([mask] * ratio, axis=1)
        for g in range(groups):
            scores = dot_nn(key_ref[g, pl.ds(at, size), :], queries[g])
            if masked:
                scores = jnp.where(mask, scores, MASKED)
            top_old = top_ref[g]
            top = jnp.maximum(top_old, jnp.max(scores, axis=0, keepdims=True))
            expo = jnp.exp(scores - top)
            fade = jnp.exp(top_old - top)
            top_ref[g] = top
            total_ref[g] = total_ref[g] * fade + jnp.sum(expo, axis=0, keepdims=True)
            part = dot_nn(value_ref[g, :, pl.ds(at, size)], expo.astype(jnp.bfloat16))
            sum_ref[g] = sum_ref[g] * fade + part

    over_keys(one, first_ref[at_query], last_ref[at_query], at_query, block)
    wide = ratio * HD
    for g in range(groups):
        total = total_ref[g]
        output = sum_ref[g] / total
        both = jnp.concatenate(
            [output[:, h * block : (h + 1) * block] for h in range(ratio)], axis=0
        )
        flip_ref[g * wide : (g + 1) * wide, :] = both.astype(jnp.bfloat16)
        context_ref[:, g * wide : (g + 1) * wide] = both.T.astype(jnp.bfloat16)
        log_total = top_ref[g] + jnp.log(total)
        for h in range(ratio):
            log_ref[g, h] = log_total[:, h * block : (h + 1) * block]
    part = dot_nn(context_ref[...], weight_ref[...]).astype(jnp.bfloat16)

    @pl.when(step % 2 == 1)
    def _():
        send_ref[...] = part

    @pl.when(step % 2 == 0)
    def _():
        keep_ref[...] = part


def attend(half, earlier, place, flipped, rows, starts, weight):
    slots, _, length = flipped.shape
    groups = slots // KINDS
    block = length // PIECES // HALVES
    width = weight.shape[1]
    wide = groups * RATIO * HD
    at = lambda i, p: HALVES * (i ^ p[0]) + half
    flip_four = flipped.reshape(groups, KINDS, HD, length)
    row_four = rows.reshape(groups, KINDS, length, HD)
    out = jax.ShapeDtypeStruct((PIECES // 2, block, width), jnp.bfloat16)
    outs = pl.pallas_call(
        lambda *refs: attend_kernel(half, *refs),
        grid_spec=pltpu.PrefetchScalarGridSpec(
            num_scalar_prefetch=3,
            grid=(PIECES,),
            in_specs=[
                pl.BlockSpec((groups, RATIO, HD, block), lambda i, f, l, p: (0, 0, 0, at(i, p))),
                pl.BlockSpec((groups, None, length, HD), lambda i, f, l, p: (0, RATIO, 0, 0)),
                pl.BlockSpec((groups, None, HD, length), lambda i, f, l, p: (0, RATIO + 1, 0, 0)),
                pl.BlockSpec((1, block), lambda i, f, l, p: (0, at(i, p))),
                pl.BlockSpec(weight.shape, lambda i, f, l, p: (0, 0)),
            ]
            + [pl.BlockSpec(memory_space=pl.ANY)] * len(earlier),
            out_specs=[
                pl.BlockSpec((block, wide), lambda i, f, l, p: (at(i, p), 0)),
                pl.BlockSpec((wide, block), lambda i, f, l, p: (0, at(i, p))),
                pl.BlockSpec((groups, RATIO, 1, block), lambda i, f, l, p: (0, 0, 0, at(i, p))),
                pl.BlockSpec((None, block, width), lambda i, f, l, p: (i // 2, 0, 0)),
                pl.BlockSpec((None, block, width), lambda i, f, l, p: (i // 2, 0, 0)),
            ],
            scratch_shapes=[
                pltpu.VMEM((groups, 1, RATIO * block), jnp.float32),
                pltpu.VMEM((groups, 1, RATIO * block), jnp.float32),
                pltpu.VMEM((groups, HD, RATIO * block), jnp.float32),
            ],
        ),
        out_shape=[
            jax.ShapeDtypeStruct((length, wide), jnp.bfloat16),
            jax.ShapeDtypeStruct((wide, length), jnp.bfloat16),
            jax.ShapeDtypeStruct((groups, RATIO, 1, length), jnp.float32),
            out,
            out,
        ],
        input_output_aliases={8 + k: k for k in range(len(earlier))},
        compiler_params=params(),
        cost_estimate=cost(8 * groups * length * length * 64, 6 * MIB),
        name="attend",
    )(
        starts[::block], starts[block - 1 :: block], place, flip_four, row_four, flip_four,
        starts[None, :], weight, *earlier,
    )
    return (outs[:3], outs[3], outs[4])


def attend_back_kernel(pieces, first_ref, last_ref, place_ref, *refs):
    (query_ref, query_row_ref, key_ref, key_row_ref, value_row_ref, context_ref, log_ref,
     start_ref, weight_ref, raw_ref, raw_key_ref, cos_ref, sin_ref, gain_ref) = refs[:14]
    dh_pieces = refs[14 : 14 + pieces]
    if pieces > 1:
        joint_ref, gain_grad_ref, dh_ref = refs[14 + pieces : 17 + pieces]
    else:
        joint_ref, gain_grad_ref = refs[14 + pieces : 16 + pieces]
        dh_ref = dh_pieces[0]
    query_sum, key_sum, value_sum, query_gain_sum = refs[-4:]
    block = start_ref.shape[1]
    step = pl.program_id(0)
    steps = pl.num_programs(0)
    ratio = query_ref.shape[0]
    wide = ratio * HD

    @pl.when(step == 0)
    def _():
        key_sum[...] = jnp.zeros_like(key_sum)
        value_sum[...] = jnp.zeros_like(value_sum)
        query_gain_sum[...] = jnp.zeros_like(query_gain_sum)

    if pieces > 1:
        source = HALVES * ((step // HALVES) ^ place_ref[0]) + step % HALVES
        for r, piece in enumerate(dh_pieces):

            @pl.when(source == r)
            def _(piece=piece):
                dh_ref[...] = piece[...]

    query = jnp.concatenate([query_ref[h] for h in range(ratio)], axis=1)
    query_row = jnp.concatenate([query_row_ref[h] for h in range(ratio)], axis=0)
    start_row = start_ref[...]
    grad_wide = dot_nt(weight_ref[...], dh_ref[...]).astype(jnp.bfloat16)
    grad_float = grad_wide.astype(jnp.float32)
    products = grad_float * context_ref[...].astype(jnp.float32)
    delta = jnp.concatenate(
        [
            jnp.sum(products[h * HD : (h + 1) * HD], axis=0, keepdims=True)
            for h in range(ratio)
        ],
        axis=1,
    )
    grad = jnp.concatenate([grad_wide[h * HD : (h + 1) * HD] for h in range(ratio)], axis=1)
    turned = grad_float.T.astype(jnp.bfloat16)
    grad_row = jnp.concatenate([turned[:, h * HD : (h + 1) * HD] for h in range(ratio)], axis=0)
    log_total = jnp.concatenate([log_ref[h] for h in range(ratio)], axis=1)
    query_sum[...] = jnp.zeros_like(query_sum)

    def one(masked, at, size):
        at = pl.multiple_of(at, block)
        here = pl.ds(at, size)
        probs = jnp.exp(dot_nn(key_row_ref[here, :], query) - log_total)
        if masked:
            mask = mask_of(start_row, at, step * block, size)
            probs = jnp.where(jnp.concatenate([mask] * ratio, axis=1), probs, 0.0)
        prob_grad = dot_nn(value_row_ref[here, :], grad)
        score_grad = (probs * (prob_grad - delta)).astype(jnp.bfloat16)
        value_sum[here, :] += dot_nn(probs.astype(jnp.bfloat16), grad_row)
        key_sum[here, :] += dot_nn(score_grad, query_row)
        query_sum[...] += dot_nn(key_ref[:, here], score_grad)

    over_keys(one, first_ref[step], last_ref[step], step, block)

    def unwind(part, raw, cosine, sine, gain):
        inverse = head_scale(raw)
        back = rotate_back(part, cosine, sine)
        scaled = back * gain
        lean = jnp.mean(scaled * raw, axis=0, keepdims=True)
        return (back * raw * inverse, inverse * scaled - raw * inverse**3 * lean)

    at = pl.multiple_of(step * block, block)
    here = pl.ds(at, block)
    outs = []
    for h in range(ratio):
        part = query_sum[:, h * block : (h + 1) * block] * HD ** (-0.5)
        gain_part, out = unwind(
            part, raw_ref[h], cos_ref[:, here], sin_ref[:, here], gain_ref[:, 0:1]
        )
        query_gain_sum[...] += gain_part
        outs.append(out)
    joint_ref[here, :wide] = jnp.concatenate(outs, axis=0).T.astype(jnp.bfloat16)

    @pl.when(step == steps - 1)
    def _():
        def one_key(j, total):
            at = pl.multiple_of(j * block, block)
            here = pl.ds(at, block)
            pair = jnp.concatenate([key_sum[here, :], value_sum[here, :]], axis=1).T
            gain_part, out = unwind(
                pair[:HD], raw_key_ref[:, here], cos_ref[:, here], sin_ref[:, here],
                gain_ref[:, 1:2],
            )
            both = jnp.concatenate([out, pair[HD:]], axis=0)
            joint_ref[here, wide:] = both.T.astype(jnp.bfloat16)
            return total + gain_part

        key_gain_sum = lax.fori_loop(
            0, steps, one_key, jnp.zeros(query_gain_sum.shape, jnp.float32)
        )
        both = jnp.concatenate([query_gain_sum[...], key_gain_sum], axis=0).T
        gain_grad_ref[...] = jnp.sum(both, axis=0, keepdims=True)


def attend_back(
    g, place, flipped, rows, context_flip, log_total, starts, dh, weight, raw, tables, head_gains
):
    slots, _, length = flipped.shape
    groups = slots // KINDS
    ratio = RATIO
    block = length // PIECES // HALVES
    wide = ratio * HD
    width = weight.shape[1]
    pieces = len(dh)
    flip_four = flipped.reshape(groups, KINDS, HD, length)
    row_four = rows.reshape(groups, KINDS, length, HD)
    raw_four = raw.reshape(groups, KINDS, HD, length)
    by_step = pl.BlockSpec((block, width), lambda i, f, l, p: (i, 0))
    whole = pl.BlockSpec((block, width), lambda i, f, l, p: (0, 0))
    outs = pl.pallas_call(
        lambda *refs: attend_back_kernel(pieces, *refs),
        grid_spec=pltpu.PrefetchScalarGridSpec(
            num_scalar_prefetch=3,
            grid=(length // block,),
            in_specs=[
                pl.BlockSpec((None, ratio, HD, block), lambda i, f, l, p: (g, 0, 0, i)),
                pl.BlockSpec((None, ratio, block, HD), lambda i, f, l, p: (g, 0, i, 0)),
                pl.BlockSpec((None, None, HD, length), lambda i, f, l, p: (g, ratio, 0, 0)),
                pl.BlockSpec((None, None, length, HD), lambda i, f, l, p: (g, ratio, 0, 0)),
                pl.BlockSpec((None, None, length, HD), lambda i, f, l, p: (g, ratio + 1, 0, 0)),
                pl.BlockSpec((wide, block), lambda i, f, l, p: (g, i)),
                pl.BlockSpec((None, ratio, 1, block), lambda i, f, l, p: (g, 0, 0, i)),
                pl.BlockSpec((1, block), lambda i, f, l, p: (0, i)),
                pl.BlockSpec((wide, width), lambda i, f, l, p: (g, 0)),
                pl.BlockSpec((None, ratio, HD, block), lambda i, f, l, p: (g, 0, 0, i)),
                pl.BlockSpec((None, None, HD, length), lambda i, f, l, p: (g, ratio, 0, 0)),
                pl.BlockSpec((HD // 2, length), lambda i, f, l, p: (0, 0)),
                pl.BlockSpec((HD // 2, length), lambda i, f, l, p: (0, 0)),
                pl.BlockSpec(head_gains.shape, lambda i, f, l, p: (0, 0)),
            ]
            + [whole if pieces > 1 else by_step] * pieces,
            out_specs=[
                pl.BlockSpec((length, wide + 2 * HD), lambda i, f, l, p: (0, 0)),
                pl.BlockSpec((1, 2 * HD), lambda i, f, l, p: (0, 0)),
            ]
            + [by_step] * (pieces > 1),
            scratch_shapes=[
                pltpu.VMEM((HD, ratio * block), jnp.float32),
                pltpu.VMEM((length, HD), jnp.float32),
                pltpu.VMEM((length, HD), jnp.float32),
                pltpu.VMEM((HD, block), jnp.float32),
            ],
        ),
        out_shape=[
            jax.ShapeDtypeStruct((length, wide + 2 * HD), jnp.bfloat16),
            jax.ShapeDtypeStruct((1, 2 * HD), jnp.float32),
        ]
        + [jax.ShapeDtypeStruct((length, width), jnp.bfloat16)] * (pieces > 1),
        compiler_params=params(),
        cost_estimate=cost(20 * length * length * 128, 12 * MIB),
        name="attend_back",
    )(
        starts[::block], starts[block - 1 :: block], place, flip_four, row_four, flip_four, row_four, row_four, context_flip,
        log_total, starts[None, :], weight, raw_four, raw_four, tables[0], tables[1],
        head_gains, *dh,
    )
    return outs


def spread_kernel(groups, place_ref, *refs):
    send_rows, keep_rows = refs[:groups], refs[groups : 2 * groups]
    weight_ref, send_out, keep_out = refs[2 * groups :]
    depth = weight_ref.shape[0] // groups
    for rows, out in ((send_rows, send_out), (keep_rows, keep_out)):
        joined = jnp.concatenate([row[...] for row in rows], axis=1)
        out[...] = dot_nn(joined, weight_ref[...]).astype(jnp.bfloat16)


def spread(place, rows, weight):
    groups = len(rows)
    length, depth = rows[0].shape
    width = weight.shape[1]
    block = length // PIECES
    out = jax.ShapeDtypeStruct((PIECES // 2, block, width), jnp.bfloat16)
    return pl.pallas_call(
        lambda *refs: spread_kernel(groups, *refs),
        grid_spec=pltpu.PrefetchScalarGridSpec(
            num_scalar_prefetch=1,
            grid=(PIECES // 2,),
            in_specs=[pl.BlockSpec((block, depth), lambda i, p: ((2 * i + 1) ^ p[0], 0))] * groups
            + [pl.BlockSpec((block, depth), lambda i, p: ((2 * i) ^ p[0], 0))] * groups
            + [pl.BlockSpec(weight.shape, lambda i, p: (0, 0))],
            out_specs=[pl.BlockSpec((None, block, width), lambda i, p: (i, 0, 0))] * 2,
        ),
        out_shape=[out, out],
        compiler_params=params(),
        cost_estimate=cost(2 * length * width * depth * groups, 6 * MIB),
        name="spread",
    )(place, *rows, *rows, weight)


def feed_kernel(call, *refs):
    xs, grads, joint_hbm, down_hbm = refs[:2], refs[2:4], refs[4], refs[5]
    (x_full, grad_full, hidden_full, low_full, out_keep, out_send, back_keep, back_send,
     x_ref, grad_ref, hidden_ref, low_ref, joint_ref, down_ref, sems) = refs[-15:]
    hidden_width = down_ref.shape[0]
    block = xs[0].shape[0]
    cut = (hidden_width + 255) // 256 * 256
    rows = pl.ds(call * 2 * block, 2 * block)

    def copy(source, target, k):
        item = pltpu.make_async_copy(source, target, sems.at[k])
        item.start()
        return item

    first = copy(joint_hbm.at[:, :cut], joint_ref.at[:, :cut], 0)
    second = copy(joint_hbm.at[:, cut:], joint_ref.at[:, cut:], 1)
    third = copy(down_hbm, down_ref, 2)
    for r in range(2):
        x_ref[r * block : (r + 1) * block, :] = xs[r][...]
        grad_ref[r * block : (r + 1) * block, :] = grads[r][...]
    stores = [copy(x_ref, x_full.at[rows, :], 3), copy(grad_ref, grad_full.at[rows, :], 4)]
    first.wait()
    left = dot_nn(x_ref[...], joint_ref[:, :cut])
    second.wait()
    right = dot_nn(x_ref[...], joint_ref[:, cut:])
    gate = left[:, :hidden_width]
    up = jnp.concatenate([left[:, hidden_width:], right], axis=1)
    sigmoid = 1.0 / (1.0 + jnp.exp(-gate))
    swish = gate * sigmoid
    hidden_ref[...] = (swish * up).astype(jnp.bfloat16)
    stores.append(copy(hidden_ref, hidden_full.at[rows, :], 5))
    third.wait()
    hidden_grad = dot_nt(grad_ref[...], down_ref[...])
    low_ref[:, :hidden_width] = (
        hidden_grad * up * sigmoid * (1.0 + gate * (1.0 - sigmoid))
    ).astype(jnp.bfloat16)
    low_ref[:, hidden_width:] = (hidden_grad * swish).astype(jnp.bfloat16)
    stores.append(copy(low_ref, low_full.at[rows, :], 6))
    out = dot_nn(hidden_ref[...], down_ref[...]).astype(jnp.bfloat16)
    out_keep[...] = out[:block]
    out_send[...] = out[block:]
    back = dot_nt(low_ref[...], joint_ref[...]).astype(jnp.bfloat16)
    back_keep[...] = back[:block]
    back_send[...] = back[block:]
    for item in stores:
        item.wait()


def feed(call, half, earlier, normed, grads, joint_weight, down_weight):
    block, width = normed[0].shape
    hidden_width = down_weight.shape[0]
    length = block * PIECES * HALVES
    once = pl.Buffered(1)
    pair = pl.BlockSpec((block, width), lambda i: (0, 0))
    full = lambda columns: jax.ShapeDtypeStruct((length, columns), jnp.bfloat16)
    any_space = pl.BlockSpec(memory_space=pl.ANY)
    rows = lambda columns: pltpu.VMEM((2 * block, columns), jnp.bfloat16)
    outs = pl.pallas_call(
        lambda *refs: feed_kernel(call, *refs),
        grid=(1,),
        in_specs=[pl.BlockSpec((block, width), lambda i: (0, 0), pipeline_mode=once)] * 2
        + [pl.BlockSpec((block, width), lambda i: (half, 0), pipeline_mode=once)] * 2
        + [any_space] * (2 + len(earlier)),
        out_specs=[any_space] * 4 + [pair] * 4,
        out_shape=[full(width), full(width), full(hidden_width), full(2 * hidden_width)]
        + [jax.ShapeDtypeStruct((block, width), jnp.bfloat16)] * 4,
        scratch_shapes=[
            rows(width), rows(width), rows(hidden_width), rows(2 * hidden_width),
            pltpu.VMEM(joint_weight.shape, jnp.bfloat16),
            pltpu.VMEM(down_weight.shape, jnp.bfloat16),
            pltpu.SemaphoreType.DMA((7,)),
        ],
        input_output_aliases={6 + k: k for k in range(len(earlier))},
        compiler_params=params(),
        cost_estimate=cost(3 * length * width * hidden_width, 16 * MIB),
        name="feed",
    )(*normed, *grads, joint_weight, down_weight, *earlier)
    return (outs[:4], outs[4:6], outs[6:8])


def norm_kernel(x_ref, keep_ref, near_ref, far_ref, gain_ref, middle_ref, normed_ref):
    f32 = jnp.float32
    middle = x_ref[...].astype(f32) + (
        keep_ref[...].astype(f32) + near_ref[...].astype(f32) + far_ref[...].astype(f32)
    )
    middle_ref[...] = middle
    normed_ref[...] = (middle * row_scale(middle) * gain_ref[...]).astype(jnp.bfloat16)


def first_of(value, rows, width):
    if value.ndim == 3:
        return pl.BlockSpec((None, rows, width), lambda i: (0, i, 0))
    return pl.BlockSpec((rows, width), lambda i: (i, 0))


def norm(half, tokens, keep, near, far, gain):
    length, width = far.shape
    steps = 2
    rows = length // steps
    flat = pl.BlockSpec((rows, width), lambda i: (i, 0))
    return pl.pallas_call(
        norm_kernel,
        grid=(steps,),
        in_specs=[
            pl.BlockSpec((rows, width), lambda i: (half * steps + i, 0)),
            first_of(keep, rows, width),
            first_of(near, rows, width),
            flat,
            pl.BlockSpec(gain.shape, lambda i: (0, 0)),
        ],
        out_specs=[flat, flat],
        out_shape=[
            jax.ShapeDtypeStruct((length, width), jnp.float32),
            jax.ShapeDtypeStruct((length, width), jnp.bfloat16),
        ],
        compiler_params=params(),
        cost_estimate=cost(0, 4 * MIB),
        name="norm",
    )(tokens, keep, near, far, gain)


def norm_back_of(value, skip, grad, gain):
    inverse = row_scale(value)
    scaled = grad * gain
    lean = jnp.mean(scaled * value, axis=-1, keepdims=True)
    total = skip + (inverse * scaled - value * (inverse**3 * lean))
    return total, jnp.sum(grad * value * inverse, axis=0, keepdims=True)


def norm_back_kernel(
    value_ref, skip_ref, keep_ref, near_ref, far_ref, gain_ref, low_ref, part_ref
):
    f32 = jnp.float32
    grad = keep_ref[...].astype(f32) + near_ref[...].astype(f32) + far_ref[...].astype(f32)
    total, part = norm_back_of(value_ref[...], skip_ref[...].astype(f32), grad, gain_ref[...])
    low_ref[...] = total.astype(jnp.bfloat16)

    @pl.when(pl.program_id(0) == 0)
    def _():
        part_ref[...] = jnp.zeros_like(part_ref)

    part_ref[...] += part


def norm_back(half, value, skip, keep, near, far, gain):
    length, width = far.shape
    steps = 2
    rows = length // steps
    flat = pl.BlockSpec((rows, width), lambda i: (i, 0))
    return pl.pallas_call(
        norm_back_kernel,
        grid=(steps,),
        in_specs=[
            flat,
            pl.BlockSpec((rows, width), lambda i: (half * steps + i, 0)),
            first_of(keep, rows, width),
            first_of(near, rows, width),
            flat,
            pl.BlockSpec(gain.shape, lambda i: (0, 0)),
        ],
        out_specs=[flat, pl.BlockSpec((1, width), lambda i: (0, 0))],
        out_shape=[
            jax.ShapeDtypeStruct((length, width), jnp.bfloat16),
            jax.ShapeDtypeStruct((1, width), jnp.float32),
        ],
        compiler_params=params(),
        cost_estimate=cost(0, 6 * MIB),
        name="norm_back",
    )(value, skip, keep, near, far, gain)


def row_kernel(counts, *refs):
    scatter_ref, row_ref, turned_ref = refs[-3:]
    parts, heads, squares = refs[: counts[0]], refs[counts[0] : counts[1]], refs[counts[1] : -3]
    width = parts[0].shape[1]
    total = lambda items: sum([item[...] for item in items[1:]], items[0][...])
    row_ref[:, :width] = jnp.zeros((1, width), jnp.float32)
    row_ref[:, width : 2 * width] = total(parts)
    row_ref[:, 2 * width : 2 * width + 2 * HD] = total(heads)
    scattered = scatter_ref[...].astype(jnp.float32)
    turned_ref[...] = scattered.T
    over = jnp.sum(scattered * scattered, axis=0, keepdims=True)
    square = jnp.sum(over, axis=1, keepdims=True) + total(squares)
    lane = lax.broadcasted_iota(jnp.int32, (1, 2 * HD), 1)
    row_ref[:, 2 * width + 2 * HD :] = jnp.where(lane == 0, square, 0.0)


def row_of(parts, heads, squares, scattered):
    counts = (len(parts), len(parts) + len(heads))
    return pl.pallas_call(
        lambda *refs: row_kernel(counts, *refs),
        out_shape=[
            jax.ShapeDtypeStruct((1, 2 * parts[0].shape[1] + 4 * HD), jnp.float32),
            jax.ShapeDtypeStruct(scattered.shape[::-1], jnp.float32),
        ],
        compiler_params=params(24),
        cost_estimate=cost(0, MIB),
        name="row",
    )(*parts, *heads, *squares, scattered)


def finish_kernel(
    x_ref, near_skip, far_skip, keep_ref, near_ref, far_ref, gain_ref, begin_ref, square_ref,
    input_grad_ref, row_ref,
):
    f32 = jnp.float32
    step = pl.program_id(0)
    width = x_ref.shape[1]
    grad = keep_ref[...].astype(f32) + near_ref[...].astype(f32) + far_ref[...].astype(f32)
    skip = jnp.where(step < pl.num_programs(0) // HALVES, near_skip[...], far_skip[...])
    total, part = norm_back_of(
        x_ref[...].astype(f32), skip.astype(f32), grad, gain_ref[...]
    )
    input_grad_ref[...] = total.astype(jnp.bfloat16)

    @pl.when(step == 0)
    def _():
        lane = lax.broadcasted_iota(jnp.int32, row_ref.shape, 1)
        last = jnp.where(lane == 2 * width + 2 * HD, square_ref[...], 0.0)
        row_ref[...] = begin_ref[...] + last

    row_ref[:, :width] += part


def finish(tokens, skips, keep, near, far, gain, row, square):
    length, width = far.shape
    each = 1
    rows = length // HALVES // each
    flat = pl.BlockSpec((rows, width), lambda i: (i, 0))
    whole = lambda value: pl.BlockSpec(value.shape, lambda i: (0, 0))
    return pl.pallas_call(
        finish_kernel,
        grid=(HALVES * each,),
        in_specs=[
            flat,
            pl.BlockSpec((rows, width), lambda i: (jnp.minimum(i, each - 1), 0)),
            pl.BlockSpec((rows, width), lambda i: (jnp.maximum(i - each, 0), 0)),
            first_of(keep, rows, width),
            first_of(near, rows, width),
            flat,
            whole(gain),
            whole(row),
            whole(square),
        ],
        out_specs=[flat, whole(row)],
        out_shape=[
            jax.ShapeDtypeStruct((length, width), jnp.bfloat16),
            jax.ShapeDtypeStruct(row.shape, jnp.float32),
        ],
        compiler_params=params(),
        cost_estimate=cost(0, 6 * MIB),
        name="finish",
    )(tokens, *skips, keep, near, far, gain, row, square)


def exchange(value, axis, bit):
    size = lax.axis_size(axis)
    return lax.ppermute(value, axis, [(i, i ^ bit) for i in range(size)])


def after(value, *others):
    return lax.optimization_barrier((value, *others))[0]


def power_of_two(count):
    return count & (count - 1) == 0


class ScatterSum:
    def __init__(self, grads, flipped, second_first=False):
        size = lax.axis_size("dp")
        rows = grads[0].shape[0] // size
        self.left = [1 << k for k in reversed(range(size.bit_length() - 1))]
        self.order = self.left[::-1]
        if second_first:
            self.order[:2] = self.order[1::-1]
        self.flipped = flipped
        self.sources = [grad.reshape(size, rows, grad.shape[1]) for grad in grads]
        self.columns = sum(grad.shape[1] for grad in grads)
        self.joined = True
        self.total = None


def advance_kernel(plans, here_ref, *refs):
    count = sum(plan[0] for plan in plans)
    ins, outs = refs[:count], refs[count:]
    squares = jnp.zeros((1, 1), jnp.float32)
    for sources, joined, stride, shift, flipped in plans:
        parts, ins = ins[:sources], ins[sources:]

        def value(at, parts=parts, joined=joined):
            if joined:
                return jnp.concatenate([part[at] for part in parts], axis=1)
            return parts[0][at].astype(jnp.float32) + parts[1][at].astype(jnp.float32)

        if stride is None:
            total = value(0).astype(jnp.float32)
            over = jnp.sum(total * total, axis=0, keepdims=True)
            squares += jnp.sum(over, axis=1, keepdims=True)
            at = 0
            for columns, turned in flipped:
                part = total[:, at : at + columns]
                outs[0][...] = part.T if turned else part
                at, outs = at + columns, outs[1:]
            continue
        sent, kept, outs = outs[0], outs[1], outs[2:]
        own = (here_ref[0] >> shift) & 1
        for k in range(sent.shape[0]):
            base = k // stride * 2 * stride + k % stride
            sent[k] = value(base + (1 - own) * stride).astype(sent.dtype)
            kept[k] = value(base + own * stride).astype(kept.dtype)
    outs[0][...] = squares


def advance(here, items, *gates):
    plans, ins, shapes = [], [], []
    for item in items:
        rows, columns = item.sources[0].shape[1], item.columns
        if item.order:
            bit = item.order[0]
            at = item.left.index(bit)
            stride = 1 << (len(item.left) - 1 - at)
            plans.append((len(item.sources), item.joined, stride, bit.bit_length() - 1, ()))
            half = (item.sources[0].shape[0] // 2, rows, columns)
            shapes += [jax.ShapeDtypeStruct(half, jnp.bfloat16)] * 2
        else:
            plans.append((len(item.sources), item.joined, None, 0, item.flipped))
            for part, turned in item.flipped:
                shape = (part, rows) if turned else (rows, part)
                shapes.append(jax.ShapeDtypeStruct(shape, jnp.float32))
        ins += item.sources
    shapes.append(jax.ShapeDtypeStruct((1, 1), jnp.float32))
    if gates:
        ins[-1] = after(ins[-1], *gates)
    vmem = pl.BlockSpec(memory_space=pltpu.VMEM)
    outs = list(pl.pallas_call(
        lambda *refs: advance_kernel(plans, *refs),
        in_specs=[pl.BlockSpec(memory_space=pltpu.SMEM)] + [vmem] * len(ins),
        out_specs=[vmem] * len(shapes),
        out_shape=shapes,
        compiler_params=params(24),
        cost_estimate=cost(0, 6 * MIB),
        name="advance",
    )(here, *ins))
    sent_all = []
    for item in items:
        if item.order:
            bit = item.order.pop(0)
            item.left.remove(bit)
            sent, kept = outs.pop(0), outs.pop(0)
            item.sources, item.joined = [kept, exchange(sent, "dp", bit)], False
            sent_all.append(sent)
        else:
            item.total = [outs.pop(0) for _ in item.flipped]
    return sent_all, outs[0]


def sum_all(value):
    for axis in ("tensor", "dp"):
        size = lax.axis_size(axis)
        if not power_of_two(size):
            value = lax.psum(value, axis)
            continue
        bit = 1
        while bit < size:
            if 2 * bit < size:
                one, two, three = [exchange(value, axis, bit * k) for k in (1, 2, 3)]
                value = (value + one) + (two + three)
                bit *= 4
            else:
                value = value + exchange(value, axis, bit)
                bit *= 2
    return value


def adam(master, mean, square, grad, factor, rate, decay):
    scaled = grad * factor
    mean_new = BETA_ONE * mean + (1.0 - BETA_ONE) * scaled
    square_new = BETA_TWO * square + (1.0 - BETA_TWO) * scaled * scaled
    mean_hat = mean_new / (1.0 - BETA_ONE**STEP)
    square_hat = square_new / (1.0 - BETA_TWO**STEP)
    new = master - rate * (mean_hat / (jnp.sqrt(square_hat) + ADAM_EPS) + decay * master)
    return (new, mean_new, square_new)


def adam_kernel(
    out_rate, entries, sum_ref, out_sum, early_ref, late_ref, gate_ref, up_ref, down_sum, *refs
):
    gain_sum = sum_ref[:, :entries]
    squares = sum_ref[:, entries : entries + 1]
    norm = jnp.sqrt(squares + jnp.sum(gain_sum * gain_sum, axis=1, keepdims=True))
    factor = CLIP_NORM / jnp.maximum(norm, CLIP_NORM)
    states = [refs[3 * k : 3 * k + 3] for k in range(4)]
    results = [refs[12 + 4 * k : 16 + 4 * k] for k in range(4)]
    refs[28][...] = norm

    def update(state, result, at, grad, rate):
        new, mean, square = adam(
            state[0][at], state[1][at], state[2][at], grad.astype(jnp.float32), factor, rate,
            DECAY,
        )
        result[0][at] = new
        result[1][at] = new.astype(jnp.bfloat16)
        result[2][at] = mean
        result[3][at] = square

    rows = slice(None)
    early = early_ref.shape[1]
    update(states[1], results[1], (rows, rows), out_sum[...], out_rate)
    update(states[0], results[0], (rows, slice(0, early)), early_ref[...], RATE_WEIGHT)
    update(states[0], results[0], (rows, slice(early, None)), late_ref[...], RATE_WEIGHT)
    update(states[2], results[2], (rows, 0, rows), gate_ref[...], RATE_WEIGHT)
    update(states[2], results[2], (rows, 1, rows), up_ref[...], RATE_WEIGHT)
    update(states[3], results[3], (rows, rows), down_sum[...], RATE_WEIGHT)


def adam_all(entries, summed, sums, states, out_rate):
    steps = max(1, states[0][0].shape[0] // 32)

    def block(array):
        rows = array.shape[0] // steps
        rest = array.shape[1:]
        return pl.BlockSpec((rows,) + rest, lambda i: (i,) + (0,) * len(rest))

    shapes = []
    for state in states:
        shapes += [
            jax.ShapeDtypeStruct(state[0].shape, dtype)
            for dtype in (jnp.float32, jnp.bfloat16, jnp.float32, jnp.float32)
        ]
    arrays = [*sums]
    for state in states:
        arrays += state
    small = lambda shape: pl.BlockSpec(shape, lambda i: (0, 0))
    return pl.pallas_call(
        lambda *refs: adam_kernel(out_rate, entries, *refs),
        grid=(steps,),
        in_specs=[small(summed.shape)] + [block(array) for array in arrays],
        out_specs=[block(shape) for shape in shapes] + [small((1, 1))],
        out_shape=shapes + [jax.ShapeDtypeStruct((1, 1), jnp.float32)],
        compiler_params=params(),
        cost_estimate=cost(0, 16 * MIB),
        name="adam",
    )(summed, *arrays)


def shards(
    tokens,
    segments,
    cotangent,
    qkv_weight,
    out_weight,
    gate_up_weight,
    down_weight,
    qkv_master,
    out_master,
    gate_up_master,
    down_master,
    qkv_mean,
    out_mean,
    gate_up_mean,
    down_mean,
    qkv_square,
    out_square,
    gate_up_square,
    down_square,
    gains,
    gains_mean,
    gains_square,
):
    width = tokens.shape[1]
    length = segments.shape[0]
    groups = qkv_weight.shape[1] // (KINDS * HD)
    hidden_width = down_weight.shape[0]
    block = length // PIECES // HALVES
    attn_gain = gains[None, :width]
    ffn_gain = gains[None, width : 2 * width]
    head_gains = jnp.stack([gains[2 * width : 2 * width + HD], gains[2 * width + HD :]], axis=1)
    place = lax.axis_index("tensor").astype(jnp.int32).reshape(1)
    here = lax.axis_index("dp").astype(jnp.int32).reshape(1)

    across = exchange(tokens, "tensor", ACROSS)
    beside = exchange(tokens, "tensor", CORE)
    starts = starts_of(segments)
    tables = rotary((jnp.arange(length, dtype=jnp.int32) - starts).astype(jnp.float32))
    weight_rows = qkv_weight.T
    inner = (attn_gain, weight_rows, head_gains, *tables)
    near_part = project(0, [], place, [tokens, beside], *inner)
    flat_weight = after(gate_up_weight, near_part[2]).reshape(width, 2 * hidden_width)
    across = after(across, near_part[2], flat_weight)
    corner = exchange(across, "tensor", CORE)
    normed_one, raw, flipped, rows = project(1, near_part, place, [across, corner], *inner)

    grad_across = exchange(after(cotangent, across), "tensor", ACROSS)
    grad_pieces = [
        cotangent,
        exchange(after(cotangent, across), "tensor", CORE),
        grad_across,
        exchange(grad_across, "tensor", CORE),
    ]

    def added(left, right):
        return (left.astype(jnp.float32) + right.astype(jnp.float32)).astype(jnp.bfloat16)

    def halfway(send, keep):
        near = exchange(send, "tensor", CORE)
        return (keep, near, added(keep[1], near[1]))

    def across_of(passed):
        keep, near, passed = passed
        return (keep, near, exchange(passed, "tensor", ACROSS))

    attended, send, keep = attend(0, [], place, flipped, rows, starts, out_weight)
    passed = halfway(after(send, grad_across), keep)
    shares = across_of(passed)
    flipped_late = after(flipped, passed[2])
    attended, send, keep = attend(1, attended, place, flipped_late, rows, starts, out_weight)
    context, context_flip, log_total = attended

    weights = (flat_weight, down_weight)
    middle, normed = norm(0, tokens, *shares, ffn_gain)
    middles = [middle]
    beside, across = exchange(normed, "tensor", CORE), exchange(normed, "tensor", ACROSS)
    passed = halfway(after(send, shares[2]), keep)
    shares = across_of(passed)
    full, out_near, back_near = feed(
        0, 0, [], [after(normed, passed[2]), beside], grad_pieces[:2], *weights
    )
    across = after(across, out_near[0])
    corner = exchange(across, "tensor", CORE)
    full, out_far, back_far = feed(1, 0, full, [across, corner], grad_pieces[2:], *weights)
    outs, backs = [(*out_near, *out_far)], [(*back_near, *back_far)]

    keep, near, far = shares
    middle, normed = norm(1, tokens, keep, near, after(far, out_far[0]), ffn_gain)
    middles.append(middle)
    beside, across = exchange(normed, "tensor", CORE), exchange(normed, "tensor", ACROSS)
    full, out_near, back_near = feed(2, 1, full, [normed, beside], grad_pieces[:2], *weights)

    def share_of(pieces, *gates):
        third = exchange(pieces[3], "tensor", CORE)
        third = after(third, *gates) if gates else third
        return (pieces[0], exchange(pieces[1], "tensor", CORE), added(pieces[2], third))

    passed = share_of(backs[0], out_near[0])
    sums = [across_of(passed)]
    across = after(across, out_near[0])
    corner = exchange(across, "tensor", CORE)
    across = after(across, passed[2])
    full, out_far, back_far = feed(3, 1, full, [across, corner], grad_pieces[2:], *weights)
    outs.append((*out_near, *out_far))
    backs.append((*back_near, *back_far))
    normed_two, grad_full, hidden, flat_low = full

    def dh_of(half, keep, near, far):
        low, part = norm_back(half, middles[half], cotangent, keep, near, far, ffn_gain)
        across = exchange(low, "tensor", ACROSS)
        pieces = [low, exchange(low, "tensor", CORE), across, exchange(across, "tensor", CORE)]
        return pieces, part

    keep, near, far = sums[0]
    first_dh = dh_of(0, keep, near, after(far, out_far[0]))
    passed = share_of(after(tuple(backs[1]), far))
    sums.append(across_of(passed))
    sent = after(grad_full, passed[2], first_dh[0][0])
    down_grad = contract_rows(sent, hidden).astype(jnp.bfloat16)
    gate_grad = contract_rows(after(normed_two, down_grad), flat_low[:, :hidden_width])
    gate = ScatterSum([gate_grad.astype(jnp.bfloat16)], [(hidden_width, False)])
    sent, square = advance(here, [gate])
    squares = [square]
    out_sums = [share_of(after(tuple(out), passed[2])) for out in outs]
    keep, near, far = sums[1]
    far_late = after(far, sent[0], first_dh[0][2])
    second_dh = dh_of(1, keep, near, far_late)
    pieces_dh, ffn_parts = zip(first_dh, second_dh)
    down_sum = lax.psum_scatter(
        after(down_grad, far_late), "dp", scatter_dimension=0, tiled=True
    )
    normed_two = after(normed_two, pieces_dh[1][0])
    up_grad = contract_rows(normed_two, flat_low[:, hidden_width:])
    up = ScatterSum([up_grad.astype(jnp.bfloat16)], [(hidden_width, False)], True)
    sent, _ = advance(here, [up], pieces_dh[1][2])

    dh = [pieces_dh[half][r] for r in range(PIECES) for half in range(HALVES)]
    dh[0] = after(dh[0], *sent, *[item[2] for item in out_sums])
    out_fars = [
        exchange(after(item[2], pieces_dh[1][2]), "tensor", ACROSS) for item in out_sums
    ]

    joints, head_parts, mixed, early = [], [], [], []
    for g in range(groups):
        outs_back = attend_back(
            g, place, flipped, rows, context_flip, log_total, starts, dh, out_weight, raw, tables,
            head_gains,
        )
        joints.append(outs_back[0])
        head_parts.append(outs_back[1])
        if g == 0:
            dh_full = outs_back[2]
            early = ScatterSum(
                [
                    contract_rows(dh_full, context).astype(jnp.bfloat16),
                    contract_rows(normed_one, outs_back[0]).astype(jnp.bfloat16),
                ],
                [(context.shape[1], True), (joints[0].shape[1], False)],
            )
            sent, _ = advance(here, [gate, up, early], outs_back[1])
            dh = [after(dh_full, *sent, *out_fars)]
        else:
            dh = [dh_full]
    sent, square = advance(here, [gate, up, early], joints[-1], down_sum)
    squares.append(square)
    joints[0] = after(joints[0], *sent)
    send, keep = spread(place, joints, weight_rows)
    late = [
        contract_rows(normed_one, after(joints[g], keep)).astype(jnp.bfloat16)
        for g in range(1, groups)
    ]
    near = exchange(send, "tensor", CORE)
    passed = (keep, near, added(keep[1], near[1]))
    keep, near, far = across_of(passed)
    late = ScatterSum(late, [(joints[0].shape[1] * (groups - 1), False)])
    advance(here, [late], passed[2])
    pending = [early, late]
    while pending != [late]:
        _, square = advance(here, pending)
        squares.append(square)
        pending = [item for item in (gate, up, early, late) if item.total is None]

    results = []
    for half in range(HALVES):
        keep_out, near_out, _ = out_sums[half]
        total = keep_out.astype(jnp.float32) + near_out.astype(jnp.float32)
        results.append(middles[half] + (total + out_fars[half].astype(jnp.float32)))
    result = jnp.concatenate(results, axis=0).astype(jnp.bfloat16)

    ffn_parts = [after(ffn_parts[0], result), *ffn_parts[1:]]
    row, down_total = row_of(ffn_parts, head_parts, squares, down_sum)
    gates = [row]
    while late.total is None:
        _, square = advance(here, [late], *gates)
        gates = []
    skips = [pieces[0] for pieces in pieces_dh]
    input_grad, row = finish(tokens, skips, keep, near, far, attn_gain, row, square)
    summed = sum_all(row)
    entries = gains.shape[0]
    out_fan = max(QH * HD * 16 // length, 16)
    out_rate = RATE_WEIGHT * (QH * HD / out_fan) ** 0.5
    updated = adam_all(
        entries, summed, [*early.total, *late.total, *gate.total, *up.total, down_total],
        [
            (qkv_master, qkv_mean, qkv_square),
            (out_master, out_mean, out_square),
            (gate_up_master, gate_up_mean, gate_up_square),
            (down_master, down_mean, down_square),
        ],
        out_rate,
    )
    grad_norm = updated[16][0, 0]
    factor = CLIP_NORM / jnp.maximum(grad_norm, CLIP_NORM)
    gain_results = adam(
        gains, gains_mean, gains_square, summed[0, :entries], factor, RATE_GAIN, 0.0
    )
    return (result, input_grad, grad_norm, *updated[:16], *gain_results)


def solution(mesh):
    in_specs = (
        P(("dp", "tensor"), None),
        P("dp"),
        P(("dp", "tensor"), None),
        P(None, "tensor"),
        P("tensor", None),
        P(None, None, "tensor"),
        P("tensor", None),
        P("dp", "tensor"),
        P("tensor", "dp"),
        P("dp", None, "tensor"),
        P("tensor", "dp"),
        P("dp", "tensor"),
        P("tensor", "dp"),
        P("dp", None, "tensor"),
        P("tensor", "dp"),
        P("dp", "tensor"),
        P("tensor", "dp"),
        P("dp", None, "tensor"),
        P("tensor", "dp"),
        P(),
        P(),
        P(),
    )
    out_specs = (
        P(("dp", "tensor"), None),
        P(("dp", "tensor"), None),
        P(),
        P("dp", "tensor"),
        P("dp", "tensor"),
        P("dp", "tensor"),
        P("dp", "tensor"),
        P("tensor", "dp"),
        P("tensor", "dp"),
        P("tensor", "dp"),
        P("tensor", "dp"),
        P("dp", None, "tensor"),
        P("dp", None, "tensor"),
        P("dp", None, "tensor"),
        P("dp", None, "tensor"),
        P("tensor", "dp"),
        P("tensor", "dp"),
        P("tensor", "dp"),
        P("tensor", "dp"),
        P(),
        P(),
        P(),
    )
    return jax.shard_map(shards, mesh=mesh, in_specs=in_specs, out_specs=out_specs, check_vma=False)
```

```python
import jax
import jax.numpy as jnp
from jax import lax
from jax.experimental import pallas as pl
from jax.experimental.pallas import tpu as pltpu
from jax.sharding import PartitionSpec as P

QH = 16
KVH = 8
HD = 64
STEP = 5


NORM_EPS = 1e-06
ROPE_BASE = 1000000.0
CLIP_NORM = 1.0
BETA_ONE = 0.9
BETA_TWO = 0.95
ADAM_EPS = 1e-08
DECAY = 0.1
RATE_WEIGHT = 0.02
RATE_GAIN = 1.5
MASKED = -1e30

KINDS = QH // KVH + 2
RATIO = QH // KVH
PARTS = 2
PIECES = 4
HALVES = 2
CORE = 1
ACROSS = 2
MIB = 1024 * 1024


def params(limit=60):
    return pltpu.CompilerParams(vmem_limit_bytes=limit * MIB)


def cost(flops, size):
    return pl.CostEstimate(flops=flops // 8, bytes_accessed=size // 8, transcendentals=0)


def starts_of(seg):
    index = jnp.arange(seg.shape[0], dtype=jnp.int32)
    flag = (index == 0) | (seg != jnp.roll(seg, 1))
    return lax.cummax(jnp.where(flag, index, 0), axis=0)


def rotary(position):
    half = HD // 2
    freq = ROPE_BASE ** (-(jnp.arange(half, dtype=jnp.float32) * 2.0 / HD))
    angle = freq[:, None] * position[None, :]
    return (jnp.cos(angle), jnp.sin(angle))


def dot_nn(left, right):
    return lax.dot_general(
        left, right, (((1,), (0,)), ((), ())), preferred_element_type=jnp.float32
    )


def dot_nt(left, right):
    return lax.dot_general(
        left, right, (((1,), (1,)), ((), ())), preferred_element_type=jnp.float32
    )


def contract_rows(left, right):
    return lax.dot_general(
        left, right, (((0,), (0,)), ((), ())), preferred_element_type=jnp.float32
    )


def rotate(value, cosine, sine):
    half = value.shape[0] // 2
    first, second = (value[:half], value[half:])
    return jnp.concatenate(
        [first * cosine - second * sine, second * cosine + first * sine], axis=0
    )


def rotate_back(grad, cosine, sine):
    half = grad.shape[0] // 2
    first, second = (grad[:half], grad[half:])
    return jnp.concatenate(
        [first * cosine + second * sine, second * cosine - first * sine], axis=0
    )


def row_scale(value):
    return lax.rsqrt(jnp.mean(value * value, axis=-1, keepdims=True) + NORM_EPS)


def head_scale(value):
    return lax.rsqrt(jnp.mean(value * value, axis=0, keepdims=True) + NORM_EPS)


def project_kernel(place_ref, *refs):
    pieces = refs[:2]
    pre_ref, weight_ref, gain_ref, cos_ref, sin_ref = refs[2:7]
    normed_ref, raw_ref, flip_ref, row_ref = refs[-4:]
    step = pl.program_id(0)
    for r in range(2):

        @pl.when(step // PARTS == r)
        def _(r=r):
            value = pieces[r][...].astype(jnp.float32)
            normed_ref[...] = (value * row_scale(value) * pre_ref[...]).astype(jnp.bfloat16)

    joint = dot_nt(weight_ref[...], normed_ref[...])
    cosine, sine = cos_ref[...], sin_ref[...]
    for slot in range(raw_ref.shape[0]):
        kind = slot % KINDS
        raw = joint[slot * HD : (slot + 1) * HD]
        raw_ref[slot] = raw
        value = raw
        if kind < KINDS - 1:
            gain = gain_ref[:, 1:2] if kind == KINDS - 2 else gain_ref[:, 0:1]
            value = rotate(raw * head_scale(raw) * gain, cosine, sine)
        if kind < KINDS - 2:
            value = value * HD ** (-0.5)
        low = value.astype(jnp.bfloat16)
        flip_ref[slot] = low
        row_ref[slot] = low.T


def project(far, earlier, place, pieces, pre_gain, weight_rows, head_gains, cos_table, sin_table):
    rows, width = pieces[0].shape
    length = rows * PIECES
    block = rows // PARTS
    slots = weight_rows.shape[0] // HD
    at = lambda i, p: PARTS * ((i // PARTS + 2 * far) ^ p[0]) + i % PARTS

    def piece(r):
        return pl.BlockSpec(
            (block, width), lambda i, p: (jnp.clip(i - PARTS * r, 0, PARTS - 1), 0)
        )

    return pl.pallas_call(
        project_kernel,
        grid_spec=pltpu.PrefetchScalarGridSpec(
            num_scalar_prefetch=1,
            grid=(2 * PARTS,),
            in_specs=[piece(0), piece(1)]
            + [
                pl.BlockSpec(pre_gain.shape, lambda i, p: (0, 0)),
                pl.BlockSpec(weight_rows.shape, lambda i, p: (0, 0)),
                pl.BlockSpec(head_gains.shape, lambda i, p: (0, 0)),
                pl.BlockSpec((HD // 2, block), lambda i, p: (0, at(i, p))),
                pl.BlockSpec((HD // 2, block), lambda i, p: (0, at(i, p))),
            ]
            + [pl.BlockSpec(memory_space=pl.ANY)] * len(earlier),
            out_specs=[
                pl.BlockSpec((block, width), lambda i, p: (at(i, p), 0)),
                pl.BlockSpec((slots, HD, block), lambda i, p: (0, 0, at(i, p))),
                pl.BlockSpec((slots, HD, block), lambda i, p: (0, 0, at(i, p))),
                pl.BlockSpec((slots, block, HD), lambda i, p: (0, at(i, p), 0)),
            ],
        ),
        out_shape=[
            jax.ShapeDtypeStruct((length, width), jnp.bfloat16),
            jax.ShapeDtypeStruct((slots, HD, length), jnp.float32),
            jax.ShapeDtypeStruct((slots, HD, length), jnp.bfloat16),
            jax.ShapeDtypeStruct((slots, length, HD), jnp.bfloat16),
        ],
        input_output_aliases={8 + k: k for k in range(len(earlier))},
        compiler_params=params(),
        cost_estimate=cost(length * width * slots * HD, 8 * MIB),
        name="project",
    )(place, *pieces, pre_gain, weight_rows, head_gains, cos_table, sin_table, *earlier)


def mask_of(start_row, first_key, first_query, keys):
    queries = start_row.shape[1]
    key = first_key + lax.broadcasted_iota(jnp.int32, (keys, 1), 0)
    query = first_query + lax.broadcasted_iota(jnp.int32, (1, queries), 1)
    return (key >= start_row) & (key <= query)


def over_keys(one, first, last, at_query, block):
    begin = first // block
    whole = jnp.maximum(begin, jnp.minimum((last + block - 1) // block, at_query))
    pairs = (at_query - whole) // 2
    lax.fori_loop(begin, whole, lambda j, carry: one(True, j * block, block), None)
    lax.fori_loop(
        0, pairs, lambda k, carry: one(False, (whole + 2 * k) * block, 2 * block), None
    )
    lax.fori_loop(
        whole + 2 * pairs, at_query, lambda j, carry: one(False, j * block, block), None
    )
    one(True, at_query * block, block)


def attend_kernel(half, first_ref, last_ref, place_ref, *refs):
    query_ref, key_ref, value_ref, start_ref, weight_ref = refs[:5]
    context_ref, flip_ref, log_ref, send_ref, keep_ref, top_ref, total_ref, sum_ref = refs[-8:]
    groups, ratio = query_ref.shape[:2]
    block = start_ref.shape[1]
    step = pl.program_id(0)
    at_query = HALVES * (step ^ place_ref[0]) + half
    start_row = start_ref[...]
    queries = [
        jnp.concatenate([query_ref[g, h] for h in range(ratio)], axis=1) for g in range(groups)
    ]
    top_ref[...] = jnp.full_like(top_ref, MASKED)
    total_ref[...] = jnp.zeros_like(total_ref)
    sum_ref[...] = jnp.zeros_like(sum_ref)

    def one(masked, at, size):
        at = pl.multiple_of(at, block)
        if masked:
            mask = mask_of(start_row, at, at_query * block, size)
            mask = jnp.concatenate([mask] * ratio, axis=1)
        for g in range(groups):
            scores = dot_nn(key_ref[g, pl.ds(at, size), :], queries[g])
            if masked:
                scores = jnp.where(mask, scores, MASKED)
            top_old = top_ref[g]
            top = jnp.maximum(top_old, jnp.max(scores, axis=0, keepdims=True))
            expo = jnp.exp(scores - top)
            fade = jnp.exp(top_old - top)
            top_ref[g] = top
            total_ref[g] = total_ref[g] * fade + jnp.sum(expo, axis=0, keepdims=True)
            part = dot_nn(value_ref[g, :, pl.ds(at, size)], expo.astype(jnp.bfloat16))
            sum_ref[g] = sum_ref[g] * fade + part

    over_keys(one, first_ref[at_query], last_ref[at_query], at_query, block)
    wide = ratio * HD
    for g in range(groups):
        total = total_ref[g]
        output = sum_ref[g] / total
        both = jnp.concatenate(
            [output[:, h * block : (h + 1) * block] for h in range(ratio)], axis=0
        )
        flip_ref[g * wide : (g + 1) * wide, :] = both.astype(jnp.bfloat16)
        context_ref[:, g * wide : (g + 1) * wide] = both.T.astype(jnp.bfloat16)
        log_total = top_ref[g] + jnp.log(total)
        for h in range(ratio):
            log_ref[g, h] = log_total[:, h * block : (h + 1) * block]
    part = dot_nn(context_ref[...], weight_ref[...]).astype(jnp.bfloat16)

    @pl.when(step % 2 == 1)
    def _():
        send_ref[...] = part

    @pl.when(step % 2 == 0)
    def _():
        keep_ref[...] = part


def attend(half, earlier, place, flipped, rows, starts, weight):
    slots, _, length = flipped.shape
    groups = slots // KINDS
    block = length // PIECES // HALVES
    width = weight.shape[1]
    wide = groups * RATIO * HD
    at = lambda i, p: HALVES * (i ^ p[0]) + half
    flip_four = flipped.reshape(groups, KINDS, HD, length)
    row_four = rows.reshape(groups, KINDS, length, HD)
    out = jax.ShapeDtypeStruct((PIECES // 2, block, width), jnp.bfloat16)
    outs = pl.pallas_call(
        lambda *refs: attend_kernel(half, *refs),
        grid_spec=pltpu.PrefetchScalarGridSpec(
            num_scalar_prefetch=3,
            grid=(PIECES,),
            in_specs=[
                pl.BlockSpec((groups, RATIO, HD, block), lambda i, f, l, p: (0, 0, 0, at(i, p))),
                pl.BlockSpec((groups, None, length, HD), lambda i, f, l, p: (0, RATIO, 0, 0)),
                pl.BlockSpec((groups, None, HD, length), lambda i, f, l, p: (0, RATIO + 1, 0, 0)),
                pl.BlockSpec((1, block), lambda i, f, l, p: (0, at(i, p))),
                pl.BlockSpec(weight.shape, lambda i, f, l, p: (0, 0)),
            ]
            + [pl.BlockSpec(memory_space=pl.ANY)] * len(earlier),
            out_specs=[
                pl.BlockSpec((block, wide), lambda i, f, l, p: (at(i, p), 0)),
                pl.BlockSpec((wide, block), lambda i, f, l, p: (0, at(i, p))),
                pl.BlockSpec((groups, RATIO, 1, block), lambda i, f, l, p: (0, 0, 0, at(i, p))),
                pl.BlockSpec((None, block, width), lambda i, f, l, p: (i // 2, 0, 0)),
                pl.BlockSpec((None, block, width), lambda i, f, l, p: (i // 2, 0, 0)),
            ],
            scratch_shapes=[
                pltpu.VMEM((groups, 1, RATIO * block), jnp.float32),
                pltpu.VMEM((groups, 1, RATIO * block), jnp.float32),
                pltpu.VMEM((groups, HD, RATIO * block), jnp.float32),
            ],
        ),
        out_shape=[
            jax.ShapeDtypeStruct((length, wide), jnp.bfloat16),
            jax.ShapeDtypeStruct((wide, length), jnp.bfloat16),
            jax.ShapeDtypeStruct((groups, RATIO, 1, length), jnp.float32),
            out,
            out,
        ],
        input_output_aliases={8 + k: k for k in range(len(earlier))},
        compiler_params=params(),
        cost_estimate=cost(8 * groups * length * length * 64, 6 * MIB),
        name="attend",
    )(
        starts[::block], starts[block - 1 :: block], place, flip_four, row_four, flip_four,
        starts[None, :], weight, *earlier,
    )
    return (outs[:3], outs[3], outs[4])


def attend_back_kernel(pieces, first_ref, last_ref, place_ref, *refs):
    (query_ref, query_row_ref, key_ref, key_row_ref, value_row_ref, context_ref, log_ref,
     start_ref, weight_ref, raw_ref, raw_key_ref, cos_ref, sin_ref, gain_ref) = refs[:14]
    dh_pieces = refs[14 : 14 + pieces]
    if pieces > 1:
        joint_ref, gain_grad_ref, dh_ref = refs[14 + pieces : 17 + pieces]
    else:
        joint_ref, gain_grad_ref = refs[14 + pieces : 16 + pieces]
        dh_ref = dh_pieces[0]
    query_sum, key_sum, value_sum, query_gain_sum = refs[-4:]
    block = start_ref.shape[1]
    step = pl.program_id(0)
    steps = pl.num_programs(0)
    ratio = query_ref.shape[0]
    wide = ratio * HD

    @pl.when(step == 0)
    def _():
        key_sum[...] = jnp.zeros_like(key_sum)
        value_sum[...] = jnp.zeros_like(value_sum)
        query_gain_sum[...] = jnp.zeros_like(query_gain_sum)

    if pieces > 1:
        source = HALVES * ((step // HALVES) ^ place_ref[0]) + step % HALVES
        for r, piece in enumerate(dh_pieces):

            @pl.when(source == r)
            def _(piece=piece):
                dh_ref[...] = piece[...]

    query = jnp.concatenate([query_ref[h] for h in range(ratio)], axis=1)
    query_row = jnp.concatenate([query_row_ref[h] for h in range(ratio)], axis=0)
    start_row = start_ref[...]
    grad_wide = dot_nt(weight_ref[...], dh_ref[...]).astype(jnp.bfloat16)
    grad_float = grad_wide.astype(jnp.float32)
    products = grad_float * context_ref[...].astype(jnp.float32)
    delta = jnp.concatenate(
        [
            jnp.sum(products[h * HD : (h + 1) * HD], axis=0, keepdims=True)
            for h in range(ratio)
        ],
        axis=1,
    )
    grad = jnp.concatenate([grad_wide[h * HD : (h + 1) * HD] for h in range(ratio)], axis=1)
    turned = grad_float.T.astype(jnp.bfloat16)
    grad_row = jnp.concatenate([turned[:, h * HD : (h + 1) * HD] for h in range(ratio)], axis=0)
    log_total = jnp.concatenate([log_ref[h] for h in range(ratio)], axis=1)
    query_sum[...] = jnp.zeros_like(query_sum)

    def one(masked, at, size):
        at = pl.multiple_of(at, block)
        here = pl.ds(at, size)
        probs = jnp.exp(dot_nn(key_row_ref[here, :], query) - log_total)
        if masked:
            mask = mask_of(start_row, at, step * block, size)
            probs = jnp.where(jnp.concatenate([mask] * ratio, axis=1), probs, 0.0)
        prob_grad = dot_nn(value_row_ref[here, :], grad)
        score_grad = (probs * (prob_grad - delta)).astype(jnp.bfloat16)
        value_sum[here, :] += dot_nn(probs.astype(jnp.bfloat16), grad_row)
        key_sum[here, :] += dot_nn(score_grad, query_row)
        query_sum[...] += dot_nn(key_ref[:, here], score_grad)

    over_keys(one, first_ref[step], last_ref[step], step, block)

    def unwind(part, raw, cosine, sine, gain):
        inverse = head_scale(raw)
        back = rotate_back(part, cosine, sine)
        scaled = back * gain
        lean = jnp.mean(scaled * raw, axis=0, keepdims=True)
        return (back * raw * inverse, inverse * scaled - raw * inverse**3 * lean)

    at = pl.multiple_of(step * block, block)
    here = pl.ds(at, block)
    outs = []
    for h in range(ratio):
        part = query_sum[:, h * block : (h + 1) * block] * HD ** (-0.5)
        gain_part, out = unwind(
            part, raw_ref[h], cos_ref[:, here], sin_ref[:, here], gain_ref[:, 0:1]
        )
        query_gain_sum[...] += gain_part
        outs.append(out)
    joint_ref[here, :wide] = jnp.concatenate(outs, axis=0).T.astype(jnp.bfloat16)

    @pl.when(step == steps - 1)
    def _():
        def one_key(j, total):
            at = pl.multiple_of(j * block, block)
            here = pl.ds(at, block)
            pair = jnp.concatenate([key_sum[here, :], value_sum[here, :]], axis=1).T
            gain_part, out = unwind(
                pair[:HD], raw_key_ref[:, here], cos_ref[:, here], sin_ref[:, here],
                gain_ref[:, 1:2],
            )
            both = jnp.concatenate([out, pair[HD:]], axis=0)
            joint_ref[here, wide:] = both.T.astype(jnp.bfloat16)
            return total + gain_part

        key_gain_sum = lax.fori_loop(
            0, steps, one_key, jnp.zeros(query_gain_sum.shape, jnp.float32)
        )
        both = jnp.concatenate([query_gain_sum[...], key_gain_sum], axis=0).T
        gain_grad_ref[...] = jnp.sum(both, axis=0, keepdims=True)


def attend_back(
    g, place, flipped, rows, context_flip, log_total, starts, dh, weight, raw, tables, head_gains
):
    slots, _, length = flipped.shape
    groups = slots // KINDS
    ratio = RATIO
    block = length // PIECES // HALVES
    wide = ratio * HD
    width = weight.shape[1]
    pieces = len(dh)
    flip_four = flipped.reshape(groups, KINDS, HD, length)
    row_four = rows.reshape(groups, KINDS, length, HD)
    raw_four = raw.reshape(groups, KINDS, HD, length)
    by_step = pl.BlockSpec((block, width), lambda i, f, l, p: (i, 0))
    whole = pl.BlockSpec((block, width), lambda i, f, l, p: (0, 0))
    outs = pl.pallas_call(
        lambda *refs: attend_back_kernel(pieces, *refs),
        grid_spec=pltpu.PrefetchScalarGridSpec(
            num_scalar_prefetch=3,
            grid=(length // block,),
            in_specs=[
                pl.BlockSpec((None, ratio, HD, block), lambda i, f, l, p: (g, 0, 0, i)),
                pl.BlockSpec((None, ratio, block, HD), lambda i, f, l, p: (g, 0, i, 0)),
                pl.BlockSpec((None, None, HD, length), lambda i, f, l, p: (g, ratio, 0, 0)),
                pl.BlockSpec((None, None, length, HD), lambda i, f, l, p: (g, ratio, 0, 0)),
                pl.BlockSpec((None, None, length, HD), lambda i, f, l, p: (g, ratio + 1, 0, 0)),
                pl.BlockSpec((wide, block), lambda i, f, l, p: (g, i)),
                pl.BlockSpec((None, ratio, 1, block), lambda i, f, l, p: (g, 0, 0, i)),
                pl.BlockSpec((1, block), lambda i, f, l, p: (0, i)),
                pl.BlockSpec((wide, width), lambda i, f, l, p: (g, 0)),
                pl.BlockSpec((None, ratio, HD, block), lambda i, f, l, p: (g, 0, 0, i)),
                pl.BlockSpec((None, None, HD, length), lambda i, f, l, p: (g, ratio, 0, 0)),
                pl.BlockSpec((HD // 2, length), lambda i, f, l, p: (0, 0)),
                pl.BlockSpec((HD // 2, length), lambda i, f, l, p: (0, 0)),
                pl.BlockSpec(head_gains.shape, lambda i, f, l, p: (0, 0)),
            ]
            + [whole if pieces > 1 else by_step] * pieces,
            out_specs=[
                pl.BlockSpec((length, wide + 2 * HD), lambda i, f, l, p: (0, 0)),
                pl.BlockSpec((1, 2 * HD), lambda i, f, l, p: (0, 0)),
            ]
            + [by_step] * (pieces > 1),
            scratch_shapes=[
                pltpu.VMEM((HD, ratio * block), jnp.float32),
                pltpu.VMEM((length, HD), jnp.float32),
                pltpu.VMEM((length, HD), jnp.float32),
                pltpu.VMEM((HD, block), jnp.float32),
            ],
        ),
        out_shape=[
            jax.ShapeDtypeStruct((length, wide + 2 * HD), jnp.bfloat16),
            jax.ShapeDtypeStruct((1, 2 * HD), jnp.float32),
        ]
        + [jax.ShapeDtypeStruct((length, width), jnp.bfloat16)] * (pieces > 1),
        compiler_params=params(),
        cost_estimate=cost(20 * length * length * 128, 12 * MIB),
        name="attend_back",
    )(
        starts[::block], starts[block - 1 :: block], place, flip_four, row_four, flip_four, row_four, row_four, context_flip,
        log_total, starts[None, :], weight, raw_four, raw_four, tables[0], tables[1],
        head_gains, *dh,
    )
    return outs


def spread_kernel(groups, place_ref, *refs):
    send_rows, keep_rows = refs[:groups], refs[groups : 2 * groups]
    weight_ref, send_out, keep_out = refs[2 * groups :]
    depth = weight_ref.shape[0] // groups
    for rows, out in ((send_rows, send_out), (keep_rows, keep_out)):
        joined = jnp.concatenate([row[...] for row in rows], axis=1)
        out[...] = dot_nn(joined, weight_ref[...]).astype(jnp.bfloat16)


def spread(place, rows, weight):
    groups = len(rows)
    length, depth = rows[0].shape
    width = weight.shape[1]
    block = length // PIECES
    out = jax.ShapeDtypeStruct((PIECES // 2, block, width), jnp.bfloat16)
    return pl.pallas_call(
        lambda *refs: spread_kernel(groups, *refs),
        grid_spec=pltpu.PrefetchScalarGridSpec(
            num_scalar_prefetch=1,
            grid=(PIECES // 2,),
            in_specs=[pl.BlockSpec((block, depth), lambda i, p: ((2 * i + 1) ^ p[0], 0))] * groups
            + [pl.BlockSpec((block, depth), lambda i, p: ((2 * i) ^ p[0], 0))] * groups
            + [pl.BlockSpec(weight.shape, lambda i, p: (0, 0))],
            out_specs=[pl.BlockSpec((None, block, width), lambda i, p: (i, 0, 0))] * 2,
        ),
        out_shape=[out, out],
        compiler_params=params(),
        cost_estimate=cost(2 * length * width * depth * groups, 6 * MIB),
        name="spread",
    )(place, *rows, *rows, weight)


def feed_kernel(*refs):
    xs, grads, joint_ref, down_ref = refs[:2], refs[2:4], refs[4], refs[5]
    x_ref, grad_ref, hidden_ref, low_ref, out_keep, out_send, back_keep, back_send = refs[-8:]
    hidden_width = down_ref.shape[0]
    block = xs[0].shape[0]
    for r in range(2):
        x_ref[r * block : (r + 1) * block, :] = xs[r][...]
        grad_ref[r * block : (r + 1) * block, :] = grads[r][...]
    both = dot_nn(x_ref[...], joint_ref[...])
    gate, up = (both[:, :hidden_width], both[:, hidden_width:])
    sigmoid = 1.0 / (1.0 + jnp.exp(-gate))
    swish = gate * sigmoid
    hidden = (swish * up).astype(jnp.bfloat16)
    hidden_ref[...] = hidden
    hidden_grad = dot_nt(grad_ref[...], down_ref[...])
    low_ref[:, :hidden_width] = (
        hidden_grad * up * sigmoid * (1.0 + gate * (1.0 - sigmoid))
    ).astype(jnp.bfloat16)
    low_ref[:, hidden_width:] = (hidden_grad * swish).astype(jnp.bfloat16)
    out = dot_nn(hidden, down_ref[...]).astype(jnp.bfloat16)
    out_keep[...] = out[:block]
    out_send[...] = out[block:]
    back = dot_nt(low_ref[...], joint_ref[...]).astype(jnp.bfloat16)
    back_keep[...] = back[:block]
    back_send[...] = back[block:]


def feed(call, half, earlier, normed, grads, joint_weight, down_weight):
    block, width = normed[0].shape
    hidden_width = down_weight.shape[0]
    length = block * PIECES * HALVES
    once = pl.Buffered(1)
    row = lambda columns: pl.BlockSpec((2 * block, columns), lambda i: (call, 0))
    whole = lambda value: pl.BlockSpec(value.shape, lambda i: (0, 0), pipeline_mode=once)
    pair = pl.BlockSpec((block, width), lambda i: (0, 0))
    full = lambda columns: jax.ShapeDtypeStruct((length, columns), jnp.bfloat16)
    outs = pl.pallas_call(
        feed_kernel,
        grid=(1,),
        in_specs=[pl.BlockSpec((block, width), lambda i: (0, 0), pipeline_mode=once)] * 2
        + [pl.BlockSpec((block, width), lambda i: (half, 0), pipeline_mode=once)] * 2
        + [whole(joint_weight), whole(down_weight)]
        + [pl.BlockSpec(memory_space=pl.ANY)] * len(earlier),
        out_specs=[row(width), row(width), row(hidden_width), row(2 * hidden_width)] + [pair] * 4,
        out_shape=[full(width), full(width), full(hidden_width), full(2 * hidden_width)]
        + [jax.ShapeDtypeStruct((block, width), jnp.bfloat16)] * 4,
        input_output_aliases={6 + k: k for k in range(len(earlier))},
        compiler_params=params(),
        cost_estimate=cost(3 * length * width * hidden_width, 16 * MIB),
        name="feed",
    )(*normed, *grads, joint_weight, down_weight, *earlier)
    return (outs[:4], outs[4:6], outs[6:8])


def norm_kernel(x_ref, keep_ref, near_ref, far_ref, gain_ref, middle_ref, normed_ref):
    f32 = jnp.float32
    middle = x_ref[...].astype(f32) + (
        keep_ref[...].astype(f32) + near_ref[...].astype(f32) + far_ref[...].astype(f32)
    )
    middle_ref[...] = middle
    normed_ref[...] = (middle * row_scale(middle) * gain_ref[...]).astype(jnp.bfloat16)


def first_of(value, rows, width):
    if value.ndim == 3:
        return pl.BlockSpec((None, rows, width), lambda i: (0, i, 0))
    return pl.BlockSpec((rows, width), lambda i: (i, 0))


def norm(half, tokens, keep, near, far, gain):
    length, width = far.shape
    steps = 2
    rows = length // steps
    flat = pl.BlockSpec((rows, width), lambda i: (i, 0))
    return pl.pallas_call(
        norm_kernel,
        grid=(steps,),
        in_specs=[
            pl.BlockSpec((rows, width), lambda i: (half * steps + i, 0)),
            first_of(keep, rows, width),
            first_of(near, rows, width),
            flat,
            pl.BlockSpec(gain.shape, lambda i: (0, 0)),
        ],
        out_specs=[flat, flat],
        out_shape=[
            jax.ShapeDtypeStruct((length, width), jnp.float32),
            jax.ShapeDtypeStruct((length, width), jnp.bfloat16),
        ],
        compiler_params=params(),
        cost_estimate=cost(0, 4 * MIB),
        name="norm",
    )(tokens, keep, near, far, gain)


def norm_back_of(value, skip, grad, gain):
    inverse = row_scale(value)
    scaled = grad * gain
    lean = jnp.mean(scaled * value, axis=-1, keepdims=True)
    total = skip + (inverse * scaled - value * (inverse**3 * lean))
    return total, jnp.sum(grad * value * inverse, axis=0, keepdims=True)


def norm_back_kernel(
    value_ref, skip_ref, keep_ref, near_ref, far_ref, gain_ref, low_ref, part_ref
):
    f32 = jnp.float32
    grad = keep_ref[...].astype(f32) + near_ref[...].astype(f32) + far_ref[...].astype(f32)
    total, part = norm_back_of(value_ref[...], skip_ref[...].astype(f32), grad, gain_ref[...])
    low_ref[...] = total.astype(jnp.bfloat16)

    @pl.when(pl.program_id(0) == 0)
    def _():
        part_ref[...] = jnp.zeros_like(part_ref)

    part_ref[...] += part


def norm_back(half, value, skip, keep, near, far, gain):
    length, width = far.shape
    steps = 2
    rows = length // steps
    flat = pl.BlockSpec((rows, width), lambda i: (i, 0))
    return pl.pallas_call(
        norm_back_kernel,
        grid=(steps,),
        in_specs=[
            flat,
            pl.BlockSpec((rows, width), lambda i: (half * steps + i, 0)),
            first_of(keep, rows, width),
            first_of(near, rows, width),
            flat,
            pl.BlockSpec(gain.shape, lambda i: (0, 0)),
        ],
        out_specs=[flat, pl.BlockSpec((1, width), lambda i: (0, 0))],
        out_shape=[
            jax.ShapeDtypeStruct((length, width), jnp.bfloat16),
            jax.ShapeDtypeStruct((1, width), jnp.float32),
        ],
        compiler_params=params(),
        cost_estimate=cost(0, 6 * MIB),
        name="norm_back",
    )(value, skip, keep, near, far, gain)


def row_kernel(counts, *refs):
    row_ref = refs[-1]
    parts, heads, squares = refs[: counts[0]], refs[counts[0] : counts[1]], refs[counts[1] : -1]
    width = parts[0].shape[1]
    total = lambda items: sum([item[...] for item in items[1:]], items[0][...])
    row_ref[:, :width] = jnp.zeros((1, width), jnp.float32)
    row_ref[:, width : 2 * width] = total(parts)
    row_ref[:, 2 * width : 2 * width + 2 * HD] = total(heads)
    lane = lax.broadcasted_iota(jnp.int32, (1, 2 * HD), 1)
    row_ref[:, 2 * width + 2 * HD :] = jnp.where(lane == 0, total(squares), 0.0)


def row_of(parts, heads, squares):
    counts = (len(parts), len(parts) + len(heads))
    return pl.pallas_call(
        lambda *refs: row_kernel(counts, *refs),
        out_shape=jax.ShapeDtypeStruct((1, 2 * parts[0].shape[1] + 4 * HD), jnp.float32),
        compiler_params=params(24),
        cost_estimate=cost(0, MIB),
        name="row",
    )(*parts, *heads, *squares)


def finish_kernel(
    x_ref, near_skip, far_skip, keep_ref, near_ref, far_ref, gain_ref, begin_ref, square_ref,
    input_grad_ref, row_ref,
):
    f32 = jnp.float32
    step = pl.program_id(0)
    width = x_ref.shape[1]
    grad = keep_ref[...].astype(f32) + near_ref[...].astype(f32) + far_ref[...].astype(f32)
    skip = jnp.where(step < pl.num_programs(0) // HALVES, near_skip[...], far_skip[...])
    total, part = norm_back_of(
        x_ref[...].astype(f32), skip.astype(f32), grad, gain_ref[...]
    )
    input_grad_ref[...] = total.astype(jnp.bfloat16)

    @pl.when(step == 0)
    def _():
        lane = lax.broadcasted_iota(jnp.int32, row_ref.shape, 1)
        last = jnp.where(lane == 2 * width + 2 * HD, square_ref[...], 0.0)
        row_ref[...] = begin_ref[...] + last

    row_ref[:, :width] += part


def finish(tokens, skips, keep, near, far, gain, row, square):
    length, width = far.shape
    each = 1
    rows = length // HALVES // each
    flat = pl.BlockSpec((rows, width), lambda i: (i, 0))
    whole = lambda value: pl.BlockSpec(value.shape, lambda i: (0, 0))
    return pl.pallas_call(
        finish_kernel,
        grid=(HALVES * each,),
        in_specs=[
            flat,
            pl.BlockSpec((rows, width), lambda i: (jnp.minimum(i, each - 1), 0)),
            pl.BlockSpec((rows, width), lambda i: (jnp.maximum(i - each, 0), 0)),
            first_of(keep, rows, width),
            first_of(near, rows, width),
            flat,
            whole(gain),
            whole(row),
            whole(square),
        ],
        out_specs=[flat, whole(row)],
        out_shape=[
            jax.ShapeDtypeStruct((length, width), jnp.bfloat16),
            jax.ShapeDtypeStruct(row.shape, jnp.float32),
        ],
        compiler_params=params(),
        cost_estimate=cost(0, 6 * MIB),
        name="finish",
    )(tokens, *skips, keep, near, far, gain, row, square)


def exchange(value, axis, bit):
    size = lax.axis_size(axis)
    return lax.ppermute(value, axis, [(i, i ^ bit) for i in range(size)])


def after(value, *others):
    return lax.optimization_barrier((value, *others))[0]


def power_of_two(count):
    return count & (count - 1) == 0


class ScatterSum:
    def __init__(self, grads, flipped, second_first=False):
        size = lax.axis_size("dp")
        rows = grads[0].shape[0] // size
        self.left = [1 << k for k in reversed(range(size.bit_length() - 1))]
        self.order = self.left[::-1]
        if second_first:
            self.order[:2] = self.order[1::-1]
        self.flipped = flipped
        self.sources = [grad.reshape(size, rows, grad.shape[1]) for grad in grads]
        self.columns = sum(grad.shape[1] for grad in grads)
        self.joined = True
        self.total = None


def advance_kernel(plans, here_ref, *refs):
    count = sum(plan[0] for plan in plans)
    ins, outs = refs[:count], refs[count:]
    squares = jnp.zeros((1, 1), jnp.float32)
    for sources, joined, stride, shift, flipped in plans:
        parts, ins = ins[:sources], ins[sources:]

        def value(at, parts=parts, joined=joined):
            if joined:
                return jnp.concatenate([part[at] for part in parts], axis=1)
            return parts[0][at].astype(jnp.float32) + parts[1][at].astype(jnp.float32)

        if stride is None:
            total = value(0).astype(jnp.float32)
            over = jnp.sum(total * total, axis=0, keepdims=True)
            squares += jnp.sum(over, axis=1, keepdims=True)
            at = 0
            for columns, turned in flipped:
                part = total[:, at : at + columns]
                outs[0][...] = part.T if turned else part
                at, outs = at + columns, outs[1:]
            continue
        sent, kept, outs = outs[0], outs[1], outs[2:]
        own = (here_ref[0] >> shift) & 1
        for k in range(sent.shape[0]):
            base = k // stride * 2 * stride + k % stride
            sent[k] = value(base + (1 - own) * stride).astype(sent.dtype)
            kept[k] = value(base + own * stride).astype(kept.dtype)
    outs[0][...] = squares


def advance(here, items, *gates):
    plans, ins, shapes = [], [], []
    for item in items:
        rows, columns = item.sources[0].shape[1], item.columns
        if item.order:
            bit = item.order[0]
            at = item.left.index(bit)
            stride = 1 << (len(item.left) - 1 - at)
            plans.append((len(item.sources), item.joined, stride, bit.bit_length() - 1, ()))
            half = (item.sources[0].shape[0] // 2, rows, columns)
            shapes += [jax.ShapeDtypeStruct(half, jnp.bfloat16)] * 2
        else:
            plans.append((len(item.sources), item.joined, None, 0, item.flipped))
            for part, turned in item.flipped:
                shape = (part, rows) if turned else (rows, part)
                shapes.append(jax.ShapeDtypeStruct(shape, jnp.float32))
        ins += item.sources
    shapes.append(jax.ShapeDtypeStruct((1, 1), jnp.float32))
    if gates:
        ins[-1] = after(ins[-1], *gates)
    vmem = pl.BlockSpec(memory_space=pltpu.VMEM)
    outs = list(pl.pallas_call(
        lambda *refs: advance_kernel(plans, *refs),
        in_specs=[pl.BlockSpec(memory_space=pltpu.SMEM)] + [vmem] * len(ins),
        out_specs=[vmem] * len(shapes),
        out_shape=shapes,
        compiler_params=params(24),
        cost_estimate=cost(0, 6 * MIB),
        name="advance",
    )(here, *ins))
    sent_all = []
    for item in items:
        if item.order:
            bit = item.order.pop(0)
            item.left.remove(bit)
            sent, kept = outs.pop(0), outs.pop(0)
            item.sources, item.joined = [kept, exchange(sent, "dp", bit)], False
            sent_all.append(sent)
        else:
            item.total = [outs.pop(0) for _ in item.flipped]
    return sent_all, outs[0]


def sum_all(value):
    for axis in ("tensor", "dp"):
        size = lax.axis_size(axis)
        if not power_of_two(size):
            value = lax.psum(value, axis)
            continue
        bit = 1
        while bit < size:
            if 2 * bit < size:
                one, two, three = [exchange(value, axis, bit * k) for k in (1, 2, 3)]
                value = (value + one) + (two + three)
                bit *= 4
            else:
                value = value + exchange(value, axis, bit)
                bit *= 2
    return value


def adam(master, mean, square, grad, factor, rate, decay):
    scaled = grad * factor
    mean_new = BETA_ONE * mean + (1.0 - BETA_ONE) * scaled
    square_new = BETA_TWO * square + (1.0 - BETA_TWO) * scaled * scaled
    mean_hat = mean_new / (1.0 - BETA_ONE**STEP)
    square_hat = square_new / (1.0 - BETA_TWO**STEP)
    new = master - rate * (mean_hat / (jnp.sqrt(square_hat) + ADAM_EPS) + decay * master)
    return (new, mean_new, square_new)


def adam_kernel(
    out_rate, entries, sum_ref, out_sum, early_ref, late_ref, gate_ref, up_ref, down_sum, *refs
):
    gain_sum = sum_ref[:, :entries]
    squares = sum_ref[:, entries : entries + 1]
    norm = jnp.sqrt(squares + jnp.sum(gain_sum * gain_sum, axis=1, keepdims=True))
    factor = CLIP_NORM / jnp.maximum(norm, CLIP_NORM)
    states = [refs[3 * k : 3 * k + 3] for k in range(4)]
    results = [refs[12 + 4 * k : 16 + 4 * k] for k in range(4)]
    refs[28][...] = norm

    def update(state, result, at, grad, rate):
        new, mean, square = adam(
            state[0][at], state[1][at], state[2][at], grad.astype(jnp.float32), factor, rate,
            DECAY,
        )
        result[0][at] = new
        result[1][at] = new.astype(jnp.bfloat16)
        result[2][at] = mean
        result[3][at] = square

    rows = slice(None)
    early = early_ref.shape[1]
    update(states[1], results[1], (rows, rows), out_sum[...], out_rate)
    update(states[0], results[0], (rows, slice(0, early)), early_ref[...], RATE_WEIGHT)
    update(states[0], results[0], (rows, slice(early, None)), late_ref[...], RATE_WEIGHT)
    update(states[2], results[2], (rows, 0, rows), gate_ref[...], RATE_WEIGHT)
    update(states[2], results[2], (rows, 1, rows), up_ref[...], RATE_WEIGHT)
    update(states[3], results[3], (rows, rows), down_sum[...], RATE_WEIGHT)


def adam_all(entries, summed, sums, states, out_rate):
    steps = max(1, states[0][0].shape[0] // 32)

    def block(array):
        rows = array.shape[0] // steps
        rest = array.shape[1:]
        return pl.BlockSpec((rows,) + rest, lambda i: (i,) + (0,) * len(rest))

    shapes = []
    for state in states:
        shapes += [
            jax.ShapeDtypeStruct(state[0].shape, dtype)
            for dtype in (jnp.float32, jnp.bfloat16, jnp.float32, jnp.float32)
        ]
    arrays = [*sums]
    for state in states:
        arrays += state
    small = lambda shape: pl.BlockSpec(shape, lambda i: (0, 0))
    return pl.pallas_call(
        lambda *refs: adam_kernel(out_rate, entries, *refs),
        grid=(steps,),
        in_specs=[small(summed.shape)] + [block(array) for array in arrays],
        out_specs=[block(shape) for shape in shapes] + [small((1, 1))],
        out_shape=shapes + [jax.ShapeDtypeStruct((1, 1), jnp.float32)],
        compiler_params=params(),
        cost_estimate=cost(0, 16 * MIB),
        name="adam",
    )(summed, *arrays)


def shards(
    tokens,
    segments,
    cotangent,
    qkv_weight,
    out_weight,
    gate_up_weight,
    down_weight,
    qkv_master,
    out_master,
    gate_up_master,
    down_master,
    qkv_mean,
    out_mean,
    gate_up_mean,
    down_mean,
    qkv_square,
    out_square,
    gate_up_square,
    down_square,
    gains,
    gains_mean,
    gains_square,
):
    width = tokens.shape[1]
    length = segments.shape[0]
    groups = qkv_weight.shape[1] // (KINDS * HD)
    hidden_width = down_weight.shape[0]
    block = length // PIECES // HALVES
    attn_gain = gains[None, :width]
    ffn_gain = gains[None, width : 2 * width]
    head_gains = jnp.stack([gains[2 * width : 2 * width + HD], gains[2 * width + HD :]], axis=1)
    place = lax.axis_index("tensor").astype(jnp.int32).reshape(1)
    here = lax.axis_index("dp").astype(jnp.int32).reshape(1)

    across = exchange(tokens, "tensor", ACROSS)
    beside = exchange(tokens, "tensor", CORE)
    starts = starts_of(segments)
    tables = rotary((jnp.arange(length, dtype=jnp.int32) - starts).astype(jnp.float32))
    weight_rows = qkv_weight.T
    inner = (attn_gain, weight_rows, head_gains, *tables)
    near_part = project(0, [], place, [tokens, beside], *inner)
    flat_weight = after(gate_up_weight, near_part[2]).reshape(width, 2 * hidden_width)
    across = after(across, near_part[2], flat_weight)
    corner = exchange(across, "tensor", CORE)
    normed_one, raw, flipped, rows = project(1, near_part, place, [across, corner], *inner)

    grad_across = exchange(after(cotangent, across), "tensor", ACROSS)
    grad_pieces = [
        cotangent,
        exchange(after(cotangent, across), "tensor", CORE),
        grad_across,
        exchange(grad_across, "tensor", CORE),
    ]

    def added(left, right):
        return (left.astype(jnp.float32) + right.astype(jnp.float32)).astype(jnp.bfloat16)

    def halfway(send, keep):
        near = exchange(send, "tensor", CORE)
        return (keep, near, added(keep[1], near[1]))

    def across_of(passed):
        keep, near, passed = passed
        return (keep, near, exchange(passed, "tensor", ACROSS))

    attended, send, keep = attend(0, [], place, flipped, rows, starts, out_weight)
    passed = halfway(after(send, grad_across), keep)
    shares = across_of(passed)
    flipped_late = after(flipped, passed[2])
    attended, send, keep = attend(1, attended, place, flipped_late, rows, starts, out_weight)
    context, context_flip, log_total = attended

    weights = (flat_weight, down_weight)
    middle, normed = norm(0, tokens, *shares, ffn_gain)
    middles = [middle]
    beside, across = exchange(normed, "tensor", CORE), exchange(normed, "tensor", ACROSS)
    passed = halfway(after(send, shares[2]), keep)
    shares = across_of(passed)
    full, out_near, back_near = feed(
        0, 0, [], [after(normed, passed[2]), beside], grad_pieces[:2], *weights
    )
    across = after(across, out_near[0])
    corner = exchange(across, "tensor", CORE)
    full, out_far, back_far = feed(1, 0, full, [across, corner], grad_pieces[2:], *weights)
    outs, backs = [(*out_near, *out_far)], [(*back_near, *back_far)]

    keep, near, far = shares
    middle, normed = norm(1, tokens, keep, near, after(far, out_far[0]), ffn_gain)
    middles.append(middle)
    beside, across = exchange(normed, "tensor", CORE), exchange(normed, "tensor", ACROSS)
    full, out_near, back_near = feed(2, 1, full, [normed, beside], grad_pieces[:2], *weights)

    def share_of(pieces, *gates):
        third = exchange(pieces[3], "tensor", CORE)
        third = after(third, *gates) if gates else third
        return (pieces[0], exchange(pieces[1], "tensor", CORE), added(pieces[2], third))

    passed = share_of(backs[0], out_near[0])
    sums = [across_of(passed)]
    across = after(across, out_near[0])
    corner = exchange(across, "tensor", CORE)
    across = after(across, passed[2])
    full, out_far, back_far = feed(3, 1, full, [across, corner], grad_pieces[2:], *weights)
    outs.append((*out_near, *out_far))
    backs.append((*back_near, *back_far))
    normed_two, grad_full, hidden, flat_low = full

    def dh_of(half, keep, near, far):
        low, part = norm_back(half, middles[half], cotangent, keep, near, far, ffn_gain)
        across = exchange(low, "tensor", ACROSS)
        pieces = [low, exchange(low, "tensor", CORE), across, exchange(across, "tensor", CORE)]
        return pieces, part

    keep, near, far = sums[0]
    first_dh = dh_of(0, keep, near, after(far, out_far[0]))
    passed = share_of(after(tuple(backs[1]), far))
    sums.append(across_of(passed))
    normed_two = after(normed_two, passed[2], first_dh[0][0])
    gate_grad = contract_rows(normed_two, flat_low[:, :hidden_width])
    gate = ScatterSum([gate_grad.astype(jnp.bfloat16)], [(hidden_width, False)])
    sent, square = advance(here, [gate])
    squares = [square]
    up_grad = contract_rows(after(normed_two, sent[0]), flat_low[:, hidden_width:])
    up = ScatterSum([up_grad.astype(jnp.bfloat16)], [(hidden_width, False)], True)
    sent, _ = advance(here, [up])
    out_sums = [share_of(after(tuple(out), passed[2])) for out in outs]
    keep, near, far = sums[1]
    second_dh = dh_of(1, keep, near, after(far, sent[0], first_dh[0][2]))
    pieces_dh, ffn_parts = zip(first_dh, second_dh)
    down_grad = contract_rows(after(grad_full, pieces_dh[1][0]), hidden).astype(jnp.bfloat16)
    down = ScatterSum([down_grad], [(hidden_width, True)])
    sent, _ = advance(here, [down])
    sent, _ = advance(here, [gate], sent[0])

    dh = [pieces_dh[half][r] for r in range(PIECES) for half in range(HALVES)]
    dh[0] = after(dh[0], *sent, *[item[2] for item in out_sums])
    out_fars = [
        exchange(after(item[2], pieces_dh[1][2]), "tensor", ACROSS) for item in out_sums
    ]

    joints, head_parts, mixed, early = [], [], [], []
    for g in range(groups):
        outs_back = attend_back(
            g, place, flipped, rows, context_flip, log_total, starts, dh, out_weight, raw, tables,
            head_gains,
        )
        joints.append(outs_back[0])
        head_parts.append(outs_back[1])
        if g == 0:
            dh_full = outs_back[2]
            early = ScatterSum(
                [
                    contract_rows(dh_full, context).astype(jnp.bfloat16),
                    contract_rows(normed_one, outs_back[0]).astype(jnp.bfloat16),
                ],
                [(context.shape[1], True), (joints[0].shape[1], False)],
            )
            sent, _ = advance(here, [gate, up, down, early], outs_back[1])
            dh = [after(dh_full, *sent, *out_fars)]
        else:
            dh = [dh_full]
    sent, square = advance(here, [gate, up, down, early], joints[-1])
    squares.append(square)
    joints[0] = after(joints[0], *sent)
    send, keep = spread(place, joints, weight_rows)
    late = [
        contract_rows(normed_one, after(joints[g], keep)).astype(jnp.bfloat16)
        for g in range(1, groups)
    ]
    near = exchange(send, "tensor", CORE)
    passed = (keep, near, added(keep[1], near[1]))
    keep, near, far = across_of(passed)
    late = ScatterSum(late, [(joints[0].shape[1] * (groups - 1), False)])
    advance(here, [late], passed[2])
    pending = [item for item in (gate, up, down, early, late) if item.total is None]
    while pending != [late]:
        _, square = advance(here, pending)
        squares.append(square)
        pending = [item for item in (gate, up, down, early, late) if item.total is None]

    results = []
    for half in range(HALVES):
        keep_out, near_out, _ = out_sums[half]
        total = keep_out.astype(jnp.float32) + near_out.astype(jnp.float32)
        results.append(middles[half] + (total + out_fars[half].astype(jnp.float32)))
    result = jnp.concatenate(results, axis=0).astype(jnp.bfloat16)

    ffn_parts = [after(ffn_parts[0], result), *ffn_parts[1:]]
    row = row_of(ffn_parts, head_parts, squares)
    gates = [row]
    while late.total is None:
        _, square = advance(here, [late], *gates)
        gates = []
    skips = [pieces[0] for pieces in pieces_dh]
    input_grad, row = finish(tokens, skips, keep, near, far, attn_gain, row, square)
    summed = sum_all(row)
    entries = gains.shape[0]
    out_fan = max(QH * HD * 16 // length, 16)
    out_rate = RATE_WEIGHT * (QH * HD / out_fan) ** 0.5
    updated = adam_all(
        entries, summed, [*early.total, *late.total, *gate.total, *up.total, *down.total],
        [
            (qkv_master, qkv_mean, qkv_square),
            (out_master, out_mean, out_square),
            (gate_up_master, gate_up_mean, gate_up_square),
            (down_master, down_mean, down_square),
        ],
        out_rate,
    )
    grad_norm = updated[16][0, 0]
    factor = CLIP_NORM / jnp.maximum(grad_norm, CLIP_NORM)
    gain_results = adam(
        gains, gains_mean, gains_square, summed[0, :entries], factor, RATE_GAIN, 0.0
    )
    return (result, input_grad, grad_norm, *updated[:16], *gain_results)


def solution(mesh):
    in_specs = (
        P(("dp", "tensor"), None),
        P("dp"),
        P(("dp", "tensor"), None),
        P(None, "tensor"),
        P("tensor", None),
        P(None, None, "tensor"),
        P("tensor", None),
        P("dp", "tensor"),
        P("tensor", "dp"),
        P("dp", None, "tensor"),
        P("tensor", "dp"),
        P("dp", "tensor"),
        P("tensor", "dp"),
        P("dp", None, "tensor"),
        P("tensor", "dp"),
        P("dp", "tensor"),
        P("tensor", "dp"),
        P("dp", None, "tensor"),
        P("tensor", "dp"),
        P(),
        P(),
        P(),
    )
    out_specs = (
        P(("dp", "tensor"), None),
        P(("dp", "tensor"), None),
        P(),
        P("dp", "tensor"),
        P("dp", "tensor"),
        P("dp", "tensor"),
        P("dp", "tensor"),
        P("tensor", "dp"),
        P("tensor", "dp"),
        P("tensor", "dp"),
        P("tensor", "dp"),
        P("dp", None, "tensor"),
        P("dp", None, "tensor"),
        P("dp", None, "tensor"),
        P("dp", None, "tensor"),
        P("tensor", "dp"),
        P("tensor", "dp"),
        P("tensor", "dp"),
        P("tensor", "dp"),
        P(),
        P(),
        P(),
    )
    return jax.shard_map(shards, mesh=mesh, in_specs=in_specs, out_specs=out_specs, check_vma=False)
```

```python
import jax
import jax.numpy as jnp
from jax import lax
from jax.experimental import pallas as pl
from jax.experimental.pallas import tpu as pltpu
from jax.sharding import PartitionSpec as P

QH = 16
KVH = 8
HD = 64
STEP = 5


NORM_EPS = 1e-06
ROPE_BASE = 1000000.0
CLIP_NORM = 1.0
BETA_ONE = 0.9
BETA_TWO = 0.95
ADAM_EPS = 1e-08
DECAY = 0.1
RATE_WEIGHT = 0.02
RATE_GAIN = 1.5
MASKED = -1e30

KINDS = QH // KVH + 2
RATIO = QH // KVH
PARTS = 1
PIECES = 4
HALVES = 2
CORE = 1
ACROSS = 2
MIB = 1024 * 1024


def params(limit=60):
    return pltpu.CompilerParams(vmem_limit_bytes=limit * MIB)


def cost(flops, size):
    return pl.CostEstimate(flops=flops // 8, bytes_accessed=size // 8, transcendentals=0)


def starts_of(seg):
    index = jnp.arange(seg.shape[0], dtype=jnp.int32)
    flag = (index == 0) | (seg != jnp.roll(seg, 1))
    return lax.cummax(jnp.where(flag, index, 0), axis=0)


def rotary(position):
    half = HD // 2
    freq = ROPE_BASE ** (-(jnp.arange(half, dtype=jnp.float32) * 2.0 / HD))
    angle = freq[:, None] * position[None, :]
    return (jnp.cos(angle), jnp.sin(angle))


def dot_nn(left, right):
    return lax.dot_general(
        left, right, (((1,), (0,)), ((), ())), preferred_element_type=jnp.float32
    )


def dot_nt(left, right):
    return lax.dot_general(
        left, right, (((1,), (1,)), ((), ())), preferred_element_type=jnp.float32
    )


def contract_rows(left, right):
    return lax.dot_general(
        left, right, (((0,), (0,)), ((), ())), preferred_element_type=jnp.float32
    )


def rotate(value, cosine, sine):
    half = value.shape[0] // 2
    first, second = (value[:half], value[half:])
    return jnp.concatenate(
        [first * cosine - second * sine, second * cosine + first * sine], axis=0
    )


def rotate_back(grad, cosine, sine):
    half = grad.shape[0] // 2
    first, second = (grad[:half], grad[half:])
    return jnp.concatenate(
        [first * cosine + second * sine, second * cosine - first * sine], axis=0
    )


def row_scale(value):
    return lax.rsqrt(jnp.mean(value * value, axis=-1, keepdims=True) + NORM_EPS)


def head_scale(value):
    return lax.rsqrt(jnp.mean(value * value, axis=0, keepdims=True) + NORM_EPS)


def project_kernel(place_ref, *refs):
    pieces = refs[:2]
    pre_ref, weight_ref, gain_ref, cos_ref, sin_ref = refs[2:7]
    normed_ref, raw_ref, flip_ref, row_ref = refs[-4:]
    step = pl.program_id(0)
    for r in range(2):

        @pl.when(step // PARTS == r)
        def _(r=r):
            value = pieces[r][...].astype(jnp.float32)
            normed_ref[...] = (value * row_scale(value) * pre_ref[...]).astype(jnp.bfloat16)

    joint = dot_nt(weight_ref[...], normed_ref[...])
    cosine, sine = cos_ref[...], sin_ref[...]
    for slot in range(raw_ref.shape[0]):
        kind = slot % KINDS
        raw = joint[slot * HD : (slot + 1) * HD]
        raw_ref[slot] = raw
        value = raw
        if kind < KINDS - 1:
            gain = gain_ref[:, 1:2] if kind == KINDS - 2 else gain_ref[:, 0:1]
            value = rotate(raw * head_scale(raw) * gain, cosine, sine)
        if kind < KINDS - 2:
            value = value * HD ** (-0.5)
        low = value.astype(jnp.bfloat16)
        flip_ref[slot] = low
        row_ref[slot] = low.T


def project(far, earlier, place, pieces, pre_gain, weight_rows, head_gains, cos_table, sin_table):
    rows, width = pieces[0].shape
    length = rows * PIECES
    block = rows // PARTS
    slots = weight_rows.shape[0] // HD
    at = lambda i, p: PARTS * ((i // PARTS + 2 * far) ^ p[0]) + i % PARTS

    def piece(r):
        return pl.BlockSpec(
            (block, width), lambda i, p: (jnp.clip(i - PARTS * r, 0, PARTS - 1), 0)
        )

    return pl.pallas_call(
        project_kernel,
        grid_spec=pltpu.PrefetchScalarGridSpec(
            num_scalar_prefetch=1,
            grid=(2 * PARTS,),
            in_specs=[piece(0), piece(1)]
            + [
                pl.BlockSpec(pre_gain.shape, lambda i, p: (0, 0)),
                pl.BlockSpec(weight_rows.shape, lambda i, p: (0, 0)),
                pl.BlockSpec(head_gains.shape, lambda i, p: (0, 0)),
                pl.BlockSpec((HD // 2, block), lambda i, p: (0, at(i, p))),
                pl.BlockSpec((HD // 2, block), lambda i, p: (0, at(i, p))),
            ]
            + [pl.BlockSpec(memory_space=pl.ANY)] * len(earlier),
            out_specs=[
                pl.BlockSpec((block, width), lambda i, p: (at(i, p), 0)),
                pl.BlockSpec((slots, HD, block), lambda i, p: (0, 0, at(i, p))),
                pl.BlockSpec((slots, HD, block), lambda i, p: (0, 0, at(i, p))),
                pl.BlockSpec((slots, block, HD), lambda i, p: (0, at(i, p), 0)),
            ],
        ),
        out_shape=[
            jax.ShapeDtypeStruct((length, width), jnp.bfloat16),
            jax.ShapeDtypeStruct((slots, HD, length), jnp.float32),
            jax.ShapeDtypeStruct((slots, HD, length), jnp.bfloat16),
            jax.ShapeDtypeStruct((slots, length, HD), jnp.bfloat16),
        ],
        input_output_aliases={8 + k: k for k in range(len(earlier))},
        compiler_params=params(),
        cost_estimate=cost(length * width * slots * HD, 8 * MIB),
        name="project",
    )(place, *pieces, pre_gain, weight_rows, head_gains, cos_table, sin_table, *earlier)


def mask_of(start_row, first_key, first_query, keys):
    queries = start_row.shape[1]
    key = first_key + lax.broadcasted_iota(jnp.int32, (keys, 1), 0)
    query = first_query + lax.broadcasted_iota(jnp.int32, (1, queries), 1)
    return (key >= start_row) & (key <= query)


def over_keys(one, first, last, at_query, block):
    begin = first // block
    whole = jnp.maximum(begin, jnp.minimum((last + block - 1) // block, at_query))
    pairs = (at_query - whole) // 2
    lax.fori_loop(begin, whole, lambda j, carry: one(True, j * block, block), None)
    lax.fori_loop(
        0, pairs, lambda k, carry: one(False, (whole + 2 * k) * block, 2 * block), None
    )
    lax.fori_loop(
        whole + 2 * pairs, at_query, lambda j, carry: one(False, j * block, block), None
    )
    one(True, at_query * block, block)


def attend_kernel(half, first_ref, last_ref, place_ref, *refs):
    query_ref, key_ref, value_ref, start_ref, weight_ref = refs[:5]
    context_ref, flip_ref, log_ref, send_ref, keep_ref, top_ref, total_ref, sum_ref = refs[-8:]
    groups, ratio = query_ref.shape[:2]
    block = start_ref.shape[1]
    step = pl.program_id(0)
    at_query = HALVES * (step ^ place_ref[0]) + half
    start_row = start_ref[...]
    queries = [
        jnp.concatenate([query_ref[g, h] for h in range(ratio)], axis=1) for g in range(groups)
    ]
    top_ref[...] = jnp.full_like(top_ref, MASKED)
    total_ref[...] = jnp.zeros_like(total_ref)
    sum_ref[...] = jnp.zeros_like(sum_ref)

    def one(masked, at, size):
        at = pl.multiple_of(at, block)
        if masked:
            mask = mask_of(start_row, at, at_query * block, size)
            mask = jnp.concatenate([mask] * ratio, axis=1)
        for g in range(groups):
            scores = dot_nn(key_ref[g, pl.ds(at, size), :], queries[g])
            if masked:
                scores = jnp.where(mask, scores, MASKED)
            top_old = top_ref[g]
            top = jnp.maximum(top_old, jnp.max(scores, axis=0, keepdims=True))
            expo = jnp.exp(scores - top)
            fade = jnp.exp(top_old - top)
            top_ref[g] = top
            total_ref[g] = total_ref[g] * fade + jnp.sum(expo, axis=0, keepdims=True)
            part = dot_nn(value_ref[g, :, pl.ds(at, size)], expo.astype(jnp.bfloat16))
            sum_ref[g] = sum_ref[g] * fade + part

    over_keys(one, first_ref[at_query], last_ref[at_query], at_query, block)
    wide = ratio * HD
    for g in range(groups):
        total = total_ref[g]
        output = sum_ref[g] / total
        both = jnp.concatenate(
            [output[:, h * block : (h + 1) * block] for h in range(ratio)], axis=0
        )
        flip_ref[g * wide : (g + 1) * wide, :] = both.astype(jnp.bfloat16)
        context_ref[:, g * wide : (g + 1) * wide] = both.T.astype(jnp.bfloat16)
        log_total = top_ref[g] + jnp.log(total)
        for h in range(ratio):
            log_ref[g, h] = log_total[:, h * block : (h + 1) * block]
    part = dot_nn(context_ref[...], weight_ref[...]).astype(jnp.bfloat16)

    @pl.when(step % 2 == 1)
    def _():
        send_ref[...] = part

    @pl.when(step % 2 == 0)
    def _():
        keep_ref[...] = part


def attend(half, earlier, place, flipped, rows, starts, weight):
    slots, _, length = flipped.shape
    groups = slots // KINDS
    block = length // PIECES // HALVES
    width = weight.shape[1]
    wide = groups * RATIO * HD
    at = lambda i, p: HALVES * (i ^ p[0]) + half
    flip_four = flipped.reshape(groups, KINDS, HD, length)
    row_four = rows.reshape(groups, KINDS, length, HD)
    out = jax.ShapeDtypeStruct((PIECES // 2, block, width), jnp.bfloat16)
    outs = pl.pallas_call(
        lambda *refs: attend_kernel(half, *refs),
        grid_spec=pltpu.PrefetchScalarGridSpec(
            num_scalar_prefetch=3,
            grid=(PIECES,),
            in_specs=[
                pl.BlockSpec((groups, RATIO, HD, block), lambda i, f, l, p: (0, 0, 0, at(i, p))),
                pl.BlockSpec((groups, None, length, HD), lambda i, f, l, p: (0, RATIO, 0, 0)),
                pl.BlockSpec((groups, None, HD, length), lambda i, f, l, p: (0, RATIO + 1, 0, 0)),
                pl.BlockSpec((1, block), lambda i, f, l, p: (0, at(i, p))),
                pl.BlockSpec(weight.shape, lambda i, f, l, p: (0, 0)),
            ]
            + [pl.BlockSpec(memory_space=pl.ANY)] * len(earlier),
            out_specs=[
                pl.BlockSpec((block, wide), lambda i, f, l, p: (at(i, p), 0)),
                pl.BlockSpec((wide, block), lambda i, f, l, p: (0, at(i, p))),
                pl.BlockSpec((groups, RATIO, 1, block), lambda i, f, l, p: (0, 0, 0, at(i, p))),
                pl.BlockSpec((None, block, width), lambda i, f, l, p: (i // 2, 0, 0)),
                pl.BlockSpec((None, block, width), lambda i, f, l, p: (i // 2, 0, 0)),
            ],
            scratch_shapes=[
                pltpu.VMEM((groups, 1, RATIO * block), jnp.float32),
                pltpu.VMEM((groups, 1, RATIO * block), jnp.float32),
                pltpu.VMEM((groups, HD, RATIO * block), jnp.float32),
            ],
        ),
        out_shape=[
            jax.ShapeDtypeStruct((length, wide), jnp.bfloat16),
            jax.ShapeDtypeStruct((wide, length), jnp.bfloat16),
            jax.ShapeDtypeStruct((groups, RATIO, 1, length), jnp.float32),
            out,
            out,
        ],
        input_output_aliases={8 + k: k for k in range(len(earlier))},
        compiler_params=params(),
        cost_estimate=cost(8 * groups * length * length * 64, 6 * MIB),
        name="attend",
    )(
        starts[::block], starts[block - 1 :: block], place, flip_four, row_four, flip_four,
        starts[None, :], weight, *earlier,
    )
    return (outs[:3], outs[3], outs[4])


def attend_back_kernel(pieces, first_ref, last_ref, place_ref, *refs):
    (query_ref, query_row_ref, key_ref, key_row_ref, value_row_ref, context_ref, log_ref,
     start_ref, weight_ref, raw_ref, raw_key_ref, cos_ref, sin_ref, gain_ref) = refs[:14]
    dh_pieces = refs[14 : 14 + pieces]
    if pieces > 1:
        joint_ref, gain_grad_ref, dh_ref = refs[14 + pieces : 17 + pieces]
    else:
        joint_ref, gain_grad_ref = refs[14 + pieces : 16 + pieces]
        dh_ref = dh_pieces[0]
    query_sum, key_sum, value_sum, query_gain_sum = refs[-4:]
    block = start_ref.shape[1]
    step = pl.program_id(0)
    steps = pl.num_programs(0)
    ratio = query_ref.shape[0]
    wide = ratio * HD

    @pl.when(step == 0)
    def _():
        key_sum[...] = jnp.zeros_like(key_sum)
        value_sum[...] = jnp.zeros_like(value_sum)
        query_gain_sum[...] = jnp.zeros_like(query_gain_sum)

    if pieces > 1:
        source = HALVES * ((step // HALVES) ^ place_ref[0]) + step % HALVES
        for r, piece in enumerate(dh_pieces):

            @pl.when(source == r)
            def _(piece=piece):
                dh_ref[...] = piece[...]

    query = jnp.concatenate([query_ref[h] for h in range(ratio)], axis=1)
    query_row = jnp.concatenate([query_row_ref[h] for h in range(ratio)], axis=0)
    start_row = start_ref[...]
    grad_wide = dot_nt(weight_ref[...], dh_ref[...]).astype(jnp.bfloat16)
    grad_float = grad_wide.astype(jnp.float32)
    products = grad_float * context_ref[...].astype(jnp.float32)
    delta = jnp.concatenate(
        [
            jnp.sum(products[h * HD : (h + 1) * HD], axis=0, keepdims=True)
            for h in range(ratio)
        ],
        axis=1,
    )
    grad = jnp.concatenate([grad_wide[h * HD : (h + 1) * HD] for h in range(ratio)], axis=1)
    turned = grad_float.T.astype(jnp.bfloat16)
    grad_row = jnp.concatenate([turned[:, h * HD : (h + 1) * HD] for h in range(ratio)], axis=0)
    log_total = jnp.concatenate([log_ref[h] for h in range(ratio)], axis=1)
    query_sum[...] = jnp.zeros_like(query_sum)

    def one(masked, at, size):
        at = pl.multiple_of(at, block)
        here = pl.ds(at, size)
        probs = jnp.exp(dot_nn(key_row_ref[here, :], query) - log_total)
        if masked:
            mask = mask_of(start_row, at, step * block, size)
            probs = jnp.where(jnp.concatenate([mask] * ratio, axis=1), probs, 0.0)
        prob_grad = dot_nn(value_row_ref[here, :], grad)
        score_grad = (probs * (prob_grad - delta)).astype(jnp.bfloat16)
        value_sum[here, :] += dot_nn(probs.astype(jnp.bfloat16), grad_row)
        key_sum[here, :] += dot_nn(score_grad, query_row)
        query_sum[...] += dot_nn(key_ref[:, here], score_grad)

    over_keys(one, first_ref[step], last_ref[step], step, block)

    def unwind(part, raw, cosine, sine, gain):
        inverse = head_scale(raw)
        back = rotate_back(part, cosine, sine)
        scaled = back * gain
        lean = jnp.mean(scaled * raw, axis=0, keepdims=True)
        return (back * raw * inverse, inverse * scaled - raw * inverse**3 * lean)

    at = pl.multiple_of(step * block, block)
    here = pl.ds(at, block)
    outs = []
    for h in range(ratio):
        part = query_sum[:, h * block : (h + 1) * block] * HD ** (-0.5)
        gain_part, out = unwind(
            part, raw_ref[h], cos_ref[:, here], sin_ref[:, here], gain_ref[:, 0:1]
        )
        query_gain_sum[...] += gain_part
        outs.append(out)
    joint_ref[here, :wide] = jnp.concatenate(outs, axis=0).T.astype(jnp.bfloat16)

    @pl.when(step == steps - 1)
    def _():
        def one_key(j, total):
            at = pl.multiple_of(j * block, block)
            here = pl.ds(at, block)
            pair = jnp.concatenate([key_sum[here, :], value_sum[here, :]], axis=1).T
            gain_part, out = unwind(
                pair[:HD], raw_key_ref[:, here], cos_ref[:, here], sin_ref[:, here],
                gain_ref[:, 1:2],
            )
            both = jnp.concatenate([out, pair[HD:]], axis=0)
            joint_ref[here, wide:] = both.T.astype(jnp.bfloat16)
            return total + gain_part

        key_gain_sum = lax.fori_loop(
            0, steps, one_key, jnp.zeros(query_gain_sum.shape, jnp.float32)
        )
        both = jnp.concatenate([query_gain_sum[...], key_gain_sum], axis=0).T
        gain_grad_ref[...] = jnp.sum(both, axis=0, keepdims=True)


def attend_back(
    g, place, flipped, rows, context_flip, log_total, starts, dh, weight, raw, tables, head_gains
):
    slots, _, length = flipped.shape
    groups = slots // KINDS
    ratio = RATIO
    block = length // PIECES // HALVES
    wide = ratio * HD
    width = weight.shape[1]
    pieces = len(dh)
    flip_four = flipped.reshape(groups, KINDS, HD, length)
    row_four = rows.reshape(groups, KINDS, length, HD)
    raw_four = raw.reshape(groups, KINDS, HD, length)
    by_step = pl.BlockSpec((block, width), lambda i, f, l, p: (i, 0))
    whole = pl.BlockSpec((block, width), lambda i, f, l, p: (0, 0))
    outs = pl.pallas_call(
        lambda *refs: attend_back_kernel(pieces, *refs),
        grid_spec=pltpu.PrefetchScalarGridSpec(
            num_scalar_prefetch=3,
            grid=(length // block,),
            in_specs=[
                pl.BlockSpec((None, ratio, HD, block), lambda i, f, l, p: (g, 0, 0, i)),
                pl.BlockSpec((None, ratio, block, HD), lambda i, f, l, p: (g, 0, i, 0)),
                pl.BlockSpec((None, None, HD, length), lambda i, f, l, p: (g, ratio, 0, 0)),
                pl.BlockSpec((None, None, length, HD), lambda i, f, l, p: (g, ratio, 0, 0)),
                pl.BlockSpec((None, None, length, HD), lambda i, f, l, p: (g, ratio + 1, 0, 0)),
                pl.BlockSpec((wide, block), lambda i, f, l, p: (g, i)),
                pl.BlockSpec((None, ratio, 1, block), lambda i, f, l, p: (g, 0, 0, i)),
                pl.BlockSpec((1, block), lambda i, f, l, p: (0, i)),
                pl.BlockSpec((wide, width), lambda i, f, l, p: (g, 0)),
                pl.BlockSpec((None, ratio, HD, block), lambda i, f, l, p: (g, 0, 0, i)),
                pl.BlockSpec((None, None, HD, length), lambda i, f, l, p: (g, ratio, 0, 0)),
                pl.BlockSpec((HD // 2, length), lambda i, f, l, p: (0, 0)),
                pl.BlockSpec((HD // 2, length), lambda i, f, l, p: (0, 0)),
                pl.BlockSpec(head_gains.shape, lambda i, f, l, p: (0, 0)),
            ]
            + [whole if pieces > 1 else by_step] * pieces,
            out_specs=[
                pl.BlockSpec((length, wide + 2 * HD), lambda i, f, l, p: (0, 0)),
                pl.BlockSpec((1, 2 * HD), lambda i, f, l, p: (0, 0)),
            ]
            + [by_step] * (pieces > 1),
            scratch_shapes=[
                pltpu.VMEM((HD, ratio * block), jnp.float32),
                pltpu.VMEM((length, HD), jnp.float32),
                pltpu.VMEM((length, HD), jnp.float32),
                pltpu.VMEM((HD, block), jnp.float32),
            ],
        ),
        out_shape=[
            jax.ShapeDtypeStruct((length, wide + 2 * HD), jnp.bfloat16),
            jax.ShapeDtypeStruct((1, 2 * HD), jnp.float32),
        ]
        + [jax.ShapeDtypeStruct((length, width), jnp.bfloat16)] * (pieces > 1),
        compiler_params=params(),
        cost_estimate=cost(20 * length * length * 128, 12 * MIB),
        name="attend_back",
    )(
        starts[::block], starts[block - 1 :: block], place, flip_four, row_four, flip_four, row_four, row_four, context_flip,
        log_total, starts[None, :], weight, raw_four, raw_four, tables[0], tables[1],
        head_gains, *dh,
    )
    return outs


def spread_kernel(groups, place_ref, *refs):
    send_rows, keep_rows = refs[:groups], refs[groups : 2 * groups]
    weight_ref, send_out, keep_out = refs[2 * groups :]
    depth = weight_ref.shape[0] // groups
    for rows, out in ((send_rows, send_out), (keep_rows, keep_out)):
        joined = jnp.concatenate([row[...] for row in rows], axis=1)
        out[...] = dot_nn(joined, weight_ref[...]).astype(jnp.bfloat16)


def spread(place, rows, weight):
    groups = len(rows)
    length, depth = rows[0].shape
    width = weight.shape[1]
    block = length // PIECES
    out = jax.ShapeDtypeStruct((PIECES // 2, block, width), jnp.bfloat16)
    return pl.pallas_call(
        lambda *refs: spread_kernel(groups, *refs),
        grid_spec=pltpu.PrefetchScalarGridSpec(
            num_scalar_prefetch=1,
            grid=(PIECES // 2,),
            in_specs=[pl.BlockSpec((block, depth), lambda i, p: ((2 * i + 1) ^ p[0], 0))] * groups
            + [pl.BlockSpec((block, depth), lambda i, p: ((2 * i) ^ p[0], 0))] * groups
            + [pl.BlockSpec(weight.shape, lambda i, p: (0, 0))],
            out_specs=[pl.BlockSpec((None, block, width), lambda i, p: (i, 0, 0))] * 2,
        ),
        out_shape=[out, out],
        compiler_params=params(),
        cost_estimate=cost(2 * length * width * depth * groups, 6 * MIB),
        name="spread",
    )(place, *rows, *rows, weight)


def feed_kernel(*refs):
    xs, grads, joint_ref, down_ref = refs[:2], refs[2:4], refs[4], refs[5]
    x_ref, grad_ref, hidden_ref, low_ref, out_keep, out_send, back_keep, back_send = refs[-8:]
    hidden_width = down_ref.shape[0]
    block = xs[0].shape[0]
    for r in range(2):
        x_ref[r * block : (r + 1) * block, :] = xs[r][...]
        grad_ref[r * block : (r + 1) * block, :] = grads[r][...]
    both = dot_nn(x_ref[...], joint_ref[...])
    gate, up = (both[:, :hidden_width], both[:, hidden_width:])
    sigmoid = 1.0 / (1.0 + jnp.exp(-gate))
    swish = gate * sigmoid
    hidden = (swish * up).astype(jnp.bfloat16)
    hidden_ref[...] = hidden
    hidden_grad = dot_nt(grad_ref[...], down_ref[...])
    low_ref[:, :hidden_width] = (
        hidden_grad * up * sigmoid * (1.0 + gate * (1.0 - sigmoid))
    ).astype(jnp.bfloat16)
    low_ref[:, hidden_width:] = (hidden_grad * swish).astype(jnp.bfloat16)
    out = dot_nn(hidden, down_ref[...]).astype(jnp.bfloat16)
    out_keep[...] = out[:block]
    out_send[...] = out[block:]
    back = dot_nt(low_ref[...], joint_ref[...]).astype(jnp.bfloat16)
    back_keep[...] = back[:block]
    back_send[...] = back[block:]


def feed(call, half, earlier, normed, grads, joint_weight, down_weight):
    block, width = normed[0].shape
    hidden_width = down_weight.shape[0]
    length = block * PIECES * HALVES
    once = pl.Buffered(1)
    row = lambda columns: pl.BlockSpec((2 * block, columns), lambda i: (call, 0))
    whole = lambda value: pl.BlockSpec(value.shape, lambda i: (0, 0), pipeline_mode=once)
    pair = pl.BlockSpec((block, width), lambda i: (0, 0))
    full = lambda columns: jax.ShapeDtypeStruct((length, columns), jnp.bfloat16)
    outs = pl.pallas_call(
        feed_kernel,
        grid=(1,),
        in_specs=[pl.BlockSpec((block, width), lambda i: (0, 0), pipeline_mode=once)] * 2
        + [pl.BlockSpec((block, width), lambda i: (half, 0), pipeline_mode=once)] * 2
        + [whole(joint_weight), whole(down_weight)]
        + [pl.BlockSpec(memory_space=pl.ANY)] * len(earlier),
        out_specs=[row(width), row(width), row(hidden_width), row(2 * hidden_width)] + [pair] * 4,
        out_shape=[full(width), full(width), full(hidden_width), full(2 * hidden_width)]
        + [jax.ShapeDtypeStruct((block, width), jnp.bfloat16)] * 4,
        input_output_aliases={6 + k: k for k in range(len(earlier))},
        compiler_params=params(),
        cost_estimate=cost(3 * length * width * hidden_width, 16 * MIB),
        name="feed",
    )(*normed, *grads, joint_weight, down_weight, *earlier)
    return (outs[:4], outs[4:6], outs[6:8])


def norm_kernel(x_ref, keep_ref, near_ref, far_ref, gain_ref, middle_ref, normed_ref):
    f32 = jnp.float32
    middle = x_ref[...].astype(f32) + (
        keep_ref[...].astype(f32) + near_ref[...].astype(f32) + far_ref[...].astype(f32)
    )
    middle_ref[...] = middle
    normed_ref[...] = (middle * row_scale(middle) * gain_ref[...]).astype(jnp.bfloat16)


def first_of(value, rows, width):
    if value.ndim == 3:
        return pl.BlockSpec((None, rows, width), lambda i: (0, i, 0))
    return pl.BlockSpec((rows, width), lambda i: (i, 0))


def norm(half, tokens, keep, near, far, gain):
    length, width = far.shape
    steps = 2
    rows = length // steps
    flat = pl.BlockSpec((rows, width), lambda i: (i, 0))
    return pl.pallas_call(
        norm_kernel,
        grid=(steps,),
        in_specs=[
            pl.BlockSpec((rows, width), lambda i: (half * steps + i, 0)),
            first_of(keep, rows, width),
            first_of(near, rows, width),
            flat,
            pl.BlockSpec(gain.shape, lambda i: (0, 0)),
        ],
        out_specs=[flat, flat],
        out_shape=[
            jax.ShapeDtypeStruct((length, width), jnp.float32),
            jax.ShapeDtypeStruct((length, width), jnp.bfloat16),
        ],
        compiler_params=params(),
        cost_estimate=cost(0, 4 * MIB),
        name="norm",
    )(tokens, keep, near, far, gain)


def norm_back_of(value, skip, grad, gain):
    inverse = row_scale(value)
    scaled = grad * gain
    lean = jnp.mean(scaled * value, axis=-1, keepdims=True)
    total = skip + (inverse * scaled - value * (inverse**3 * lean))
    return total, jnp.sum(grad * value * inverse, axis=0, keepdims=True)


def norm_back_kernel(
    value_ref, skip_ref, keep_ref, near_ref, far_ref, gain_ref, low_ref, part_ref
):
    f32 = jnp.float32
    grad = keep_ref[...].astype(f32) + near_ref[...].astype(f32) + far_ref[...].astype(f32)
    total, part = norm_back_of(value_ref[...], skip_ref[...].astype(f32), grad, gain_ref[...])
    low_ref[...] = total.astype(jnp.bfloat16)

    @pl.when(pl.program_id(0) == 0)
    def _():
        part_ref[...] = jnp.zeros_like(part_ref)

    part_ref[...] += part


def norm_back(half, value, skip, keep, near, far, gain):
    length, width = far.shape
    steps = 2
    rows = length // steps
    flat = pl.BlockSpec((rows, width), lambda i: (i, 0))
    return pl.pallas_call(
        norm_back_kernel,
        grid=(steps,),
        in_specs=[
            flat,
            pl.BlockSpec((rows, width), lambda i: (half * steps + i, 0)),
            first_of(keep, rows, width),
            first_of(near, rows, width),
            flat,
            pl.BlockSpec(gain.shape, lambda i: (0, 0)),
        ],
        out_specs=[flat, pl.BlockSpec((1, width), lambda i: (0, 0))],
        out_shape=[
            jax.ShapeDtypeStruct((length, width), jnp.bfloat16),
            jax.ShapeDtypeStruct((1, width), jnp.float32),
        ],
        compiler_params=params(),
        cost_estimate=cost(0, 6 * MIB),
        name="norm_back",
    )(value, skip, keep, near, far, gain)


def row_kernel(counts, *refs):
    row_ref = refs[-1]
    parts, heads, squares = refs[: counts[0]], refs[counts[0] : counts[1]], refs[counts[1] : -1]
    width = parts[0].shape[1]
    total = lambda items: sum([item[...] for item in items[1:]], items[0][...])
    row_ref[:, :width] = jnp.zeros((1, width), jnp.float32)
    row_ref[:, width : 2 * width] = total(parts)
    row_ref[:, 2 * width : 2 * width + 2 * HD] = total(heads)
    lane = lax.broadcasted_iota(jnp.int32, (1, 2 * HD), 1)
    row_ref[:, 2 * width + 2 * HD :] = jnp.where(lane == 0, total(squares), 0.0)


def row_of(parts, heads, squares):
    counts = (len(parts), len(parts) + len(heads))
    return pl.pallas_call(
        lambda *refs: row_kernel(counts, *refs),
        out_shape=jax.ShapeDtypeStruct((1, 2 * parts[0].shape[1] + 4 * HD), jnp.float32),
        compiler_params=params(24),
        cost_estimate=cost(0, MIB),
        name="row",
    )(*parts, *heads, *squares)


def finish_kernel(
    x_ref, near_skip, far_skip, keep_ref, near_ref, far_ref, gain_ref, begin_ref, square_ref,
    input_grad_ref, row_ref,
):
    f32 = jnp.float32
    step = pl.program_id(0)
    width = x_ref.shape[1]
    grad = keep_ref[...].astype(f32) + near_ref[...].astype(f32) + far_ref[...].astype(f32)
    skip = jnp.where(step < pl.num_programs(0) // HALVES, near_skip[...], far_skip[...])
    total, part = norm_back_of(
        x_ref[...].astype(f32), skip.astype(f32), grad, gain_ref[...]
    )
    input_grad_ref[...] = total.astype(jnp.bfloat16)

    @pl.when(step == 0)
    def _():
        lane = lax.broadcasted_iota(jnp.int32, row_ref.shape, 1)
        last = jnp.where(lane == 2 * width + 2 * HD, square_ref[...], 0.0)
        row_ref[...] = begin_ref[...] + last

    row_ref[:, :width] += part


def finish(tokens, skips, keep, near, far, gain, row, square):
    length, width = far.shape
    each = 1
    rows = length // HALVES // each
    flat = pl.BlockSpec((rows, width), lambda i: (i, 0))
    whole = lambda value: pl.BlockSpec(value.shape, lambda i: (0, 0))
    return pl.pallas_call(
        finish_kernel,
        grid=(HALVES * each,),
        in_specs=[
            flat,
            pl.BlockSpec((rows, width), lambda i: (jnp.minimum(i, each - 1), 0)),
            pl.BlockSpec((rows, width), lambda i: (jnp.maximum(i - each, 0), 0)),
            first_of(keep, rows, width),
            first_of(near, rows, width),
            flat,
            whole(gain),
            whole(row),
            whole(square),
        ],
        out_specs=[flat, whole(row)],
        out_shape=[
            jax.ShapeDtypeStruct((length, width), jnp.bfloat16),
            jax.ShapeDtypeStruct(row.shape, jnp.float32),
        ],
        compiler_params=params(),
        cost_estimate=cost(0, 6 * MIB),
        name="finish",
    )(tokens, *skips, keep, near, far, gain, row, square)


def exchange(value, axis, bit):
    size = lax.axis_size(axis)
    return lax.ppermute(value, axis, [(i, i ^ bit) for i in range(size)])


def after(value, *others):
    return lax.optimization_barrier((value, *others))[0]


def power_of_two(count):
    return count & (count - 1) == 0


class ScatterSum:
    def __init__(self, grads, flipped, swapped=()):
        size = lax.axis_size("dp")
        rows = grads[0].shape[0] // size
        self.left = [1 << k for k in reversed(range(size.bit_length() - 1))]
        self.order = self.left[::-1]
        if swapped and len(self.order) > max(swapped):
            one, two = swapped
            self.order[one], self.order[two] = self.order[two], self.order[one]
        self.flipped = flipped
        self.sources = [grad.reshape(size, rows, grad.shape[1]) for grad in grads]
        self.columns = sum(grad.shape[1] for grad in grads)
        self.joined = True
        self.total = None


def advance_kernel(plans, here_ref, *refs):
    count = sum(plan[0] for plan in plans)
    ins, outs = refs[:count], refs[count:]
    squares = jnp.zeros((1, 1), jnp.float32)
    for sources, joined, stride, shift, flipped in plans:
        parts, ins = ins[:sources], ins[sources:]

        def value(at, parts=parts, joined=joined):
            if joined:
                return jnp.concatenate([part[at] for part in parts], axis=1)
            return parts[0][at].astype(jnp.float32) + parts[1][at].astype(jnp.float32)

        if stride is None:
            total = value(0).astype(jnp.float32)
            over = jnp.sum(total * total, axis=0, keepdims=True)
            squares += jnp.sum(over, axis=1, keepdims=True)
            at = 0
            for columns, turned in flipped:
                part = total[:, at : at + columns]
                outs[0][...] = part.T if turned else part
                at, outs = at + columns, outs[1:]
            continue
        sent, kept, outs = outs[0], outs[1], outs[2:]
        own = (here_ref[0] >> shift) & 1
        for k in range(sent.shape[0]):
            base = k // stride * 2 * stride + k % stride
            sent[k] = value(base + (1 - own) * stride).astype(sent.dtype)
            kept[k] = value(base + own * stride).astype(kept.dtype)
    outs[0][...] = squares


def advance(here, items, *gates):
    plans, ins, shapes = [], [], []
    for item in items:
        rows, columns = item.sources[0].shape[1], item.columns
        if item.order:
            bit = item.order[0]
            at = item.left.index(bit)
            stride = 1 << (len(item.left) - 1 - at)
            plans.append((len(item.sources), item.joined, stride, bit.bit_length() - 1, ()))
            half = (item.sources[0].shape[0] // 2, rows, columns)
            shapes += [jax.ShapeDtypeStruct(half, jnp.bfloat16)] * 2
        else:
            plans.append((len(item.sources), item.joined, None, 0, item.flipped))
            for part, turned in item.flipped:
                shape = (part, rows) if turned else (rows, part)
                shapes.append(jax.ShapeDtypeStruct(shape, jnp.float32))
        ins += item.sources
    shapes.append(jax.ShapeDtypeStruct((1, 1), jnp.float32))
    if gates:
        ins[-1] = after(ins[-1], *gates)
    vmem = pl.BlockSpec(memory_space=pltpu.VMEM)
    outs = list(pl.pallas_call(
        lambda *refs: advance_kernel(plans, *refs),
        in_specs=[pl.BlockSpec(memory_space=pltpu.SMEM)] + [vmem] * len(ins),
        out_specs=[vmem] * len(shapes),
        out_shape=shapes,
        compiler_params=params(24),
        cost_estimate=cost(0, 6 * MIB),
        name="advance",
    )(here, *ins))
    sent_all = []
    for item in items:
        if item.order:
            bit = item.order.pop(0)
            item.left.remove(bit)
            sent, kept = outs.pop(0), outs.pop(0)
            item.sources, item.joined = [kept, exchange(sent, "dp", bit)], False
            sent_all.append(sent)
        else:
            item.total = [outs.pop(0) for _ in item.flipped]
    return sent_all, outs[0]


def sum_all(value):
    for axis in ("tensor", "dp"):
        size = lax.axis_size(axis)
        if not power_of_two(size):
            value = lax.psum(value, axis)
            continue
        bit = 1
        while bit < size:
            if 2 * bit < size:
                one, two, three = [exchange(value, axis, bit * k) for k in (1, 2, 3)]
                value = (value + one) + (two + three)
                bit *= 4
            else:
                value = value + exchange(value, axis, bit)
                bit *= 2
    return value


def adam(master, mean, square, grad, factor, rate, decay):
    scaled = grad * factor
    mean_new = BETA_ONE * mean + (1.0 - BETA_ONE) * scaled
    square_new = BETA_TWO * square + (1.0 - BETA_TWO) * scaled * scaled
    mean_hat = mean_new / (1.0 - BETA_ONE**STEP)
    square_hat = square_new / (1.0 - BETA_TWO**STEP)
    new = master - rate * (mean_hat / (jnp.sqrt(square_hat) + ADAM_EPS) + decay * master)
    return (new, mean_new, square_new)


def adam_kernel(
    out_rate, entries, sum_ref, out_sum, early_ref, late_ref, gate_ref, up_ref, down_sum, *refs
):
    gain_sum = sum_ref[:, :entries]
    squares = sum_ref[:, entries : entries + 1]
    norm = jnp.sqrt(squares + jnp.sum(gain_sum * gain_sum, axis=1, keepdims=True))
    factor = CLIP_NORM / jnp.maximum(norm, CLIP_NORM)
    states = [refs[3 * k : 3 * k + 3] for k in range(4)]
    results = [refs[12 + 4 * k : 16 + 4 * k] for k in range(4)]
    refs[28][...] = norm

    def update(state, result, at, grad, rate):
        new, mean, square = adam(
            state[0][at], state[1][at], state[2][at], grad.astype(jnp.float32), factor, rate,
            DECAY,
        )
        result[0][at] = new
        result[1][at] = new.astype(jnp.bfloat16)
        result[2][at] = mean
        result[3][at] = square

    rows = slice(None)
    early = early_ref.shape[1]
    update(states[1], results[1], (rows, rows), out_sum[...], out_rate)
    update(states[0], results[0], (rows, slice(0, early)), early_ref[...], RATE_WEIGHT)
    update(states[0], results[0], (rows, slice(early, None)), late_ref[...], RATE_WEIGHT)
    update(states[2], results[2], (rows, 0, rows), gate_ref[...], RATE_WEIGHT)
    update(states[2], results[2], (rows, 1, rows), up_ref[...], RATE_WEIGHT)
    update(states[3], results[3], (rows, rows), down_sum[...], RATE_WEIGHT)


def adam_all(entries, summed, sums, states, out_rate):
    steps = max(1, states[0][0].shape[0] // 32)

    def block(array):
        rows = array.shape[0] // steps
        rest = array.shape[1:]
        return pl.BlockSpec((rows,) + rest, lambda i: (i,) + (0,) * len(rest))

    shapes = []
    for state in states:
        shapes += [
            jax.ShapeDtypeStruct(state[0].shape, dtype)
            for dtype in (jnp.float32, jnp.bfloat16, jnp.float32, jnp.float32)
        ]
    arrays = [*sums]
    for state in states:
        arrays += state
    small = lambda shape: pl.BlockSpec(shape, lambda i: (0, 0))
    return pl.pallas_call(
        lambda *refs: adam_kernel(out_rate, entries, *refs),
        grid=(steps,),
        in_specs=[small(summed.shape)] + [block(array) for array in arrays],
        out_specs=[block(shape) for shape in shapes] + [small((1, 1))],
        out_shape=shapes + [jax.ShapeDtypeStruct((1, 1), jnp.float32)],
        compiler_params=params(),
        cost_estimate=cost(0, 16 * MIB),
        name="adam",
    )(summed, *arrays)


def shards(
    tokens,
    segments,
    cotangent,
    qkv_weight,
    out_weight,
    gate_up_weight,
    down_weight,
    qkv_master,
    out_master,
    gate_up_master,
    down_master,
    qkv_mean,
    out_mean,
    gate_up_mean,
    down_mean,
    qkv_square,
    out_square,
    gate_up_square,
    down_square,
    gains,
    gains_mean,
    gains_square,
):
    width = tokens.shape[1]
    length = segments.shape[0]
    groups = qkv_weight.shape[1] // (KINDS * HD)
    hidden_width = down_weight.shape[0]
    block = length // PIECES // HALVES
    attn_gain = gains[None, :width]
    ffn_gain = gains[None, width : 2 * width]
    head_gains = jnp.stack([gains[2 * width : 2 * width + HD], gains[2 * width + HD :]], axis=1)
    place = lax.axis_index("tensor").astype(jnp.int32).reshape(1)
    here = lax.axis_index("dp").astype(jnp.int32).reshape(1)

    across = exchange(tokens, "tensor", ACROSS)
    beside = exchange(tokens, "tensor", CORE)
    starts = starts_of(segments)
    tables = rotary((jnp.arange(length, dtype=jnp.int32) - starts).astype(jnp.float32))
    weight_rows = qkv_weight.T
    inner = (attn_gain, weight_rows, head_gains, *tables)
    near_part = project(0, [], place, [tokens, beside], *inner)
    flat_weight = after(gate_up_weight, near_part[2]).reshape(width, 2 * hidden_width)
    across = after(across, near_part[2], flat_weight)
    corner = exchange(across, "tensor", CORE)
    normed_one, raw, flipped, rows = project(1, near_part, place, [across, corner], *inner)

    grad_across = exchange(after(cotangent, across), "tensor", ACROSS)
    grad_pieces = [
        cotangent,
        exchange(after(cotangent, across), "tensor", CORE),
        grad_across,
        exchange(grad_across, "tensor", CORE),
    ]

    def added(left, right):
        return (left.astype(jnp.float32) + right.astype(jnp.float32)).astype(jnp.bfloat16)

    def halfway(send, keep):
        near = exchange(send, "tensor", CORE)
        return (keep, near, added(keep[1], near[1]))

    def across_of(passed):
        keep, near, passed = passed
        return (keep, near, exchange(passed, "tensor", ACROSS))

    attended, send, keep = attend(0, [], place, flipped, rows, starts, out_weight)
    passed = halfway(after(send, grad_across), keep)
    shares = across_of(passed)
    flipped_late = after(flipped, passed[2])
    attended, send, keep = attend(1, attended, place, flipped_late, rows, starts, out_weight)
    context, context_flip, log_total = attended

    weights = (flat_weight, down_weight)
    middle, normed = norm(0, tokens, *shares, ffn_gain)
    middles = [middle]
    beside, across = exchange(normed, "tensor", CORE), exchange(normed, "tensor", ACROSS)
    passed = halfway(after(send, shares[2]), keep)
    shares = across_of(passed)
    full, out_near, back_near = feed(
        0, 0, [], [after(normed, passed[2]), beside], grad_pieces[:2], *weights
    )
    across = after(across, out_near[0])
    corner = exchange(across, "tensor", CORE)
    full, out_far, back_far = feed(1, 0, full, [across, corner], grad_pieces[2:], *weights)
    outs, backs = [(*out_near, *out_far)], [(*back_near, *back_far)]

    keep, near, far = shares
    middle, normed = norm(1, tokens, keep, near, after(far, out_far[0]), ffn_gain)
    middles.append(middle)
    beside, across = exchange(normed, "tensor", CORE), exchange(normed, "tensor", ACROSS)
    full, out_near, back_near = feed(2, 1, full, [normed, beside], grad_pieces[:2], *weights)

    def share_of(pieces, *gates):
        third = exchange(pieces[3], "tensor", CORE)
        third = after(third, *gates) if gates else third
        return (pieces[0], exchange(pieces[1], "tensor", CORE), added(pieces[2], third))

    passed = share_of(backs[0], out_near[0])
    sums = [across_of(passed)]
    across = after(across, out_near[0])
    corner = exchange(across, "tensor", CORE)
    across = after(across, passed[2])
    full, out_far, back_far = feed(3, 1, full, [across, corner], grad_pieces[2:], *weights)
    outs.append((*out_near, *out_far))
    backs.append((*back_near, *back_far))
    normed_two, grad_full, hidden, flat_low = full

    def dh_of(half, keep, near, far):
        low, part = norm_back(half, middles[half], cotangent, keep, near, far, ffn_gain)
        across = exchange(low, "tensor", ACROSS)
        pieces = [low, exchange(low, "tensor", CORE), across, exchange(across, "tensor", CORE)]
        return pieces, part

    keep, near, far = sums[0]
    first_dh = dh_of(0, keep, near, after(far, out_far[0]))
    passed = share_of(after(tuple(backs[1]), far))
    sums.append(across_of(passed))
    normed_two = after(normed_two, passed[2], first_dh[0][0])
    gate_grad = contract_rows(normed_two, flat_low[:, :hidden_width])
    gate = ScatterSum([gate_grad.astype(jnp.bfloat16)], [(hidden_width, False)], (1, 2))
    sent, square = advance(here, [gate])
    squares = [square]
    up_grad = contract_rows(after(normed_two, sent[0]), flat_low[:, hidden_width:])
    up = ScatterSum([up_grad.astype(jnp.bfloat16)], [(hidden_width, False)], (0, 1))
    sent, _ = advance(here, [up])
    out_sums = [share_of(after(tuple(out), passed[2])) for out in outs]
    keep, near, far = sums[1]
    second_dh = dh_of(1, keep, near, after(far, sent[0], first_dh[0][2]))
    pieces_dh, ffn_parts = zip(first_dh, second_dh)
    down_grad = contract_rows(after(grad_full, pieces_dh[1][0]), hidden).astype(jnp.bfloat16)
    down = ScatterSum([down_grad], [(hidden_width, True)], (1, 2))
    sent, _ = advance(here, [down])
    sent, _ = advance(here, [gate], sent[0])

    dh = [pieces_dh[half][r] for r in range(PIECES) for half in range(HALVES)]
    dh[0] = after(dh[0], *sent, *[item[2] for item in out_sums])
    out_fars = [
        exchange(after(item[2], pieces_dh[1][2]), "tensor", ACROSS) for item in out_sums
    ]

    joints, head_parts, mixed, early = [], [], [], []
    for g in range(groups):
        outs_back = attend_back(
            g, place, flipped, rows, context_flip, log_total, starts, dh, out_weight, raw, tables,
            head_gains,
        )
        joints.append(outs_back[0])
        head_parts.append(outs_back[1])
        if g == 0:
            dh_full = outs_back[2]
            early = ScatterSum(
                [
                    contract_rows(dh_full, context).astype(jnp.bfloat16),
                    contract_rows(normed_one, outs_back[0]).astype(jnp.bfloat16),
                ],
                [(context.shape[1], True), (joints[0].shape[1], False)],
            )
            sent, _ = advance(here, [gate, up, down, early], outs_back[1])
            dh = [after(dh_full, *sent, *out_fars)]
        else:
            dh = [dh_full]
    sent, square = advance(here, [gate, up, down, early], joints[-1])
    squares.append(square)
    joints[0] = after(joints[0], *sent)
    send, keep = spread(place, joints, weight_rows)
    late = [
        contract_rows(normed_one, after(joints[g], keep)).astype(jnp.bfloat16)
        for g in range(1, groups)
    ]
    near = exchange(send, "tensor", CORE)
    passed = (keep, near, added(keep[1], near[1]))
    keep, near, far = across_of(passed)
    late = ScatterSum(late, [(joints[0].shape[1] * (groups - 1), False)])
    advance(here, [late], passed[2])
    pending = [item for item in (gate, up, down, early, late) if item.total is None]
    while pending != [late]:
        _, square = advance(here, pending)
        squares.append(square)
        pending = [item for item in (gate, up, down, early, late) if item.total is None]

    results = []
    for half in range(HALVES):
        keep_out, near_out, _ = out_sums[half]
        total = keep_out.astype(jnp.float32) + near_out.astype(jnp.float32)
        results.append(middles[half] + (total + out_fars[half].astype(jnp.float32)))
    result = jnp.concatenate(results, axis=0).astype(jnp.bfloat16)

    ffn_parts = [after(ffn_parts[0], result), *ffn_parts[1:]]
    row = row_of(ffn_parts, head_parts, squares)
    gates = [row]
    while late.total is None:
        _, square = advance(here, [late], *gates)
        gates = []
    skips = [pieces[0] for pieces in pieces_dh]
    input_grad, row = finish(tokens, skips, keep, near, far, attn_gain, row, square)
    summed = sum_all(row)
    entries = gains.shape[0]
    out_fan = max(QH * HD * 16 // length, 16)
    out_rate = RATE_WEIGHT * (QH * HD / out_fan) ** 0.5
    updated = adam_all(
        entries, summed, [*early.total, *late.total, *gate.total, *up.total, *down.total],
        [
            (qkv_master, qkv_mean, qkv_square),
            (out_master, out_mean, out_square),
            (gate_up_master, gate_up_mean, gate_up_square),
            (down_master, down_mean, down_square),
        ],
        out_rate,
    )
    grad_norm = updated[16][0, 0]
    factor = CLIP_NORM / jnp.maximum(grad_norm, CLIP_NORM)
    gain_results = adam(
        gains, gains_mean, gains_square, summed[0, :entries], factor, RATE_GAIN, 0.0
    )
    return (result, input_grad, grad_norm, *updated[:16], *gain_results)


def solution(mesh):
    in_specs = (
        P(("dp", "tensor"), None),
        P("dp"),
        P(("dp", "tensor"), None),
        P(None, "tensor"),
        P("tensor", None),
        P(None, None, "tensor"),
        P("tensor", None),
        P("dp", "tensor"),
        P("tensor", "dp"),
        P("dp", None, "tensor"),
        P("tensor", "dp"),
        P("dp", "tensor"),
        P("tensor", "dp"),
        P("dp", None, "tensor"),
        P("tensor", "dp"),
        P("dp", "tensor"),
        P("tensor", "dp"),
        P("dp", None, "tensor"),
        P("tensor", "dp"),
        P(),
        P(),
        P(),
    )
    out_specs = (
        P(("dp", "tensor"), None),
        P(("dp", "tensor"), None),
        P(),
        P("dp", "tensor"),
        P("dp", "tensor"),
        P("dp", "tensor"),
        P("dp", "tensor"),
        P("tensor", "dp"),
        P("tensor", "dp"),
        P("tensor", "dp"),
        P("tensor", "dp"),
        P("dp", None, "tensor"),
        P("dp", None, "tensor"),
        P("dp", None, "tensor"),
        P("dp", None, "tensor"),
        P("tensor", "dp"),
        P("tensor", "dp"),
        P("tensor", "dp"),
        P("tensor", "dp"),
        P(),
        P(),
        P(),
    )
    return jax.shard_map(shards, mesh=mesh, in_specs=in_specs, out_specs=out_specs, check_vma=False)
```

```python
import jax
import jax.numpy as jnp
from jax import lax
from jax.experimental import pallas as pl
from jax.experimental.pallas import tpu as pltpu
from jax.sharding import PartitionSpec as P

QH = 16
KVH = 8
HD = 64
STEP = 5


NORM_EPS = 1e-06
ROPE_BASE = 1000000.0
CLIP_NORM = 1.0
BETA_ONE = 0.9
BETA_TWO = 0.95
ADAM_EPS = 1e-08
DECAY = 0.1
RATE_WEIGHT = 0.02
RATE_GAIN = 1.5
MASKED = -1e30

KINDS = QH // KVH + 2
RATIO = QH // KVH
PARTS = 1
PIECES = 4
HALVES = 2
CORE = 1
ACROSS = 2
MIB = 1024 * 1024


def params(limit=60):
    return pltpu.CompilerParams(vmem_limit_bytes=limit * MIB)


def cost(flops, size):
    return pl.CostEstimate(flops=flops // 8, bytes_accessed=size // 8, transcendentals=0)


def starts_of(seg):
    index = jnp.arange(seg.shape[0], dtype=jnp.int32)
    flag = (index == 0) | (seg != jnp.roll(seg, 1))
    return lax.cummax(jnp.where(flag, index, 0), axis=0)


def rotary(position):
    half = HD // 2
    freq = ROPE_BASE ** (-(jnp.arange(half, dtype=jnp.float32) * 2.0 / HD))
    angle = freq[:, None] * position[None, :]
    return (jnp.cos(angle), jnp.sin(angle))


def dot_nn(left, right):
    return lax.dot_general(
        left, right, (((1,), (0,)), ((), ())), preferred_element_type=jnp.float32
    )


def dot_nt(left, right):
    return lax.dot_general(
        left, right, (((1,), (1,)), ((), ())), preferred_element_type=jnp.float32
    )


def contract_rows(left, right):
    return lax.dot_general(
        left, right, (((0,), (0,)), ((), ())), preferred_element_type=jnp.float32
    )


def rotate(value, cosine, sine):
    half = value.shape[0] // 2
    first, second = (value[:half], value[half:])
    return jnp.concatenate(
        [first * cosine - second * sine, second * cosine + first * sine], axis=0
    )


def rotate_back(grad, cosine, sine):
    half = grad.shape[0] // 2
    first, second = (grad[:half], grad[half:])
    return jnp.concatenate(
        [first * cosine + second * sine, second * cosine - first * sine], axis=0
    )


def row_scale(value):
    return lax.rsqrt(jnp.mean(value * value, axis=-1, keepdims=True) + NORM_EPS)


def head_scale(value):
    return lax.rsqrt(jnp.mean(value * value, axis=0, keepdims=True) + NORM_EPS)


def project_kernel(place_ref, *refs):
    pieces = refs[:2]
    pre_ref, weight_ref, gain_ref, cos_ref, sin_ref = refs[2:7]
    normed_ref, raw_ref, flip_ref, row_ref = refs[-4:]
    step = pl.program_id(0)
    for r in range(2):

        @pl.when(step // PARTS == r)
        def _(r=r):
            value = pieces[r][...].astype(jnp.float32)
            normed_ref[...] = (value * row_scale(value) * pre_ref[...]).astype(jnp.bfloat16)

    joint = dot_nt(weight_ref[...], normed_ref[...])
    cosine, sine = cos_ref[...], sin_ref[...]
    for slot in range(raw_ref.shape[0]):
        kind = slot % KINDS
        raw = joint[slot * HD : (slot + 1) * HD]
        raw_ref[slot] = raw
        value = raw
        if kind < KINDS - 1:
            gain = gain_ref[:, 1:2] if kind == KINDS - 2 else gain_ref[:, 0:1]
            value = rotate(raw * head_scale(raw) * gain, cosine, sine)
        if kind < KINDS - 2:
            value = value * HD ** (-0.5)
        low = value.astype(jnp.bfloat16)
        flip_ref[slot] = low
        row_ref[slot] = low.T


def project(far, earlier, place, pieces, pre_gain, weight_rows, head_gains, cos_table, sin_table):
    rows, width = pieces[0].shape
    length = rows * PIECES
    block = rows // PARTS
    slots = weight_rows.shape[0] // HD
    at = lambda i, p: PARTS * ((i // PARTS + 2 * far) ^ p[0]) + i % PARTS

    def piece(r):
        return pl.BlockSpec(
            (block, width), lambda i, p: (jnp.clip(i - PARTS * r, 0, PARTS - 1), 0)
        )

    return pl.pallas_call(
        project_kernel,
        grid_spec=pltpu.PrefetchScalarGridSpec(
            num_scalar_prefetch=1,
            grid=(2 * PARTS,),
            in_specs=[piece(0), piece(1)]
            + [
                pl.BlockSpec(pre_gain.shape, lambda i, p: (0, 0)),
                pl.BlockSpec(weight_rows.shape, lambda i, p: (0, 0)),
                pl.BlockSpec(head_gains.shape, lambda i, p: (0, 0)),
                pl.BlockSpec((HD // 2, block), lambda i, p: (0, at(i, p))),
                pl.BlockSpec((HD // 2, block), lambda i, p: (0, at(i, p))),
            ]
            + [pl.BlockSpec(memory_space=pl.ANY)] * len(earlier),
            out_specs=[
                pl.BlockSpec((block, width), lambda i, p: (at(i, p), 0)),
                pl.BlockSpec((slots, HD, block), lambda i, p: (0, 0, at(i, p))),
                pl.BlockSpec((slots, HD, block), lambda i, p: (0, 0, at(i, p))),
                pl.BlockSpec((slots, block, HD), lambda i, p: (0, at(i, p), 0)),
            ],
        ),
        out_shape=[
            jax.ShapeDtypeStruct((length, width), jnp.bfloat16),
            jax.ShapeDtypeStruct((slots, HD, length), jnp.float32),
            jax.ShapeDtypeStruct((slots, HD, length), jnp.bfloat16),
            jax.ShapeDtypeStruct((slots, length, HD), jnp.bfloat16),
        ],
        input_output_aliases={8 + k: k for k in range(len(earlier))},
        compiler_params=params(),
        cost_estimate=cost(length * width * slots * HD, 8 * MIB),
        name="project",
    )(place, *pieces, pre_gain, weight_rows, head_gains, cos_table, sin_table, *earlier)


def mask_of(start_row, first_key, first_query, keys):
    queries = start_row.shape[1]
    key = first_key + lax.broadcasted_iota(jnp.int32, (keys, 1), 0)
    query = first_query + lax.broadcasted_iota(jnp.int32, (1, queries), 1)
    return (key >= start_row) & (key <= query)


def over_keys(one, first, last, at_query, block):
    begin = first // block
    whole = jnp.maximum(begin, jnp.minimum((last + block - 1) // block, at_query))
    pairs = (at_query - whole) // 2
    lax.fori_loop(begin, whole, lambda j, carry: one(True, j * block, block), None)
    lax.fori_loop(
        0, pairs, lambda k, carry: one(False, (whole + 2 * k) * block, 2 * block), None
    )
    lax.fori_loop(
        whole + 2 * pairs, at_query, lambda j, carry: one(False, j * block, block), None
    )
    one(True, at_query * block, block)


def attend_kernel(half, first_ref, last_ref, place_ref, *refs):
    query_ref, key_ref, value_ref, start_ref, weight_ref = refs[:5]
    context_ref, flip_ref, log_ref, send_ref, keep_ref, top_ref, total_ref, sum_ref = refs[-8:]
    groups, ratio = query_ref.shape[:2]
    block = start_ref.shape[1]
    step = pl.program_id(0)
    at_query = HALVES * (step ^ place_ref[0]) + half
    start_row = start_ref[...]
    queries = [
        jnp.concatenate([query_ref[g, h] for h in range(ratio)], axis=1) for g in range(groups)
    ]
    top_ref[...] = jnp.full_like(top_ref, MASKED)
    total_ref[...] = jnp.zeros_like(total_ref)
    sum_ref[...] = jnp.zeros_like(sum_ref)

    def one(masked, at, size):
        at = pl.multiple_of(at, block)
        if masked:
            mask = mask_of(start_row, at, at_query * block, size)
            mask = jnp.concatenate([mask] * ratio, axis=1)
        for g in range(groups):
            scores = dot_nn(key_ref[g, pl.ds(at, size), :], queries[g])
            if masked:
                scores = jnp.where(mask, scores, MASKED)
            top_old = top_ref[g]
            top = jnp.maximum(top_old, jnp.max(scores, axis=0, keepdims=True))
            expo = jnp.exp(scores - top)
            fade = jnp.exp(top_old - top)
            top_ref[g] = top
            total_ref[g] = total_ref[g] * fade + jnp.sum(expo, axis=0, keepdims=True)
            part = dot_nn(value_ref[g, :, pl.ds(at, size)], expo.astype(jnp.bfloat16))
            sum_ref[g] = sum_ref[g] * fade + part

    over_keys(one, first_ref[at_query], last_ref[at_query], at_query, block)
    wide = ratio * HD
    for g in range(groups):
        total = total_ref[g]
        output = sum_ref[g] / total
        both = jnp.concatenate(
            [output[:, h * block : (h + 1) * block] for h in range(ratio)], axis=0
        )
        flip_ref[g * wide : (g + 1) * wide, :] = both.astype(jnp.bfloat16)
        context_ref[:, g * wide : (g + 1) * wide] = both.T.astype(jnp.bfloat16)
        log_total = top_ref[g] + jnp.log(total)
        for h in range(ratio):
            log_ref[g, h] = log_total[:, h * block : (h + 1) * block]
    part = dot_nn(context_ref[...], weight_ref[...]).astype(jnp.bfloat16)

    @pl.when(step % 2 == 1)
    def _():
        send_ref[...] = part

    @pl.when(step % 2 == 0)
    def _():
        keep_ref[...] = part


def attend(half, earlier, place, flipped, rows, starts, weight):
    slots, _, length = flipped.shape
    groups = slots // KINDS
    block = length // PIECES // HALVES
    width = weight.shape[1]
    wide = groups * RATIO * HD
    at = lambda i, p: HALVES * (i ^ p[0]) + half
    flip_four = flipped.reshape(groups, KINDS, HD, length)
    row_four = rows.reshape(groups, KINDS, length, HD)
    out = jax.ShapeDtypeStruct((PIECES // 2, block, width), jnp.bfloat16)
    outs = pl.pallas_call(
        lambda *refs: attend_kernel(half, *refs),
        grid_spec=pltpu.PrefetchScalarGridSpec(
            num_scalar_prefetch=3,
            grid=(PIECES,),
            in_specs=[
                pl.BlockSpec((groups, RATIO, HD, block), lambda i, f, l, p: (0, 0, 0, at(i, p))),
                pl.BlockSpec((groups, None, length, HD), lambda i, f, l, p: (0, RATIO, 0, 0)),
                pl.BlockSpec((groups, None, HD, length), lambda i, f, l, p: (0, RATIO + 1, 0, 0)),
                pl.BlockSpec((1, block), lambda i, f, l, p: (0, at(i, p))),
                pl.BlockSpec(weight.shape, lambda i, f, l, p: (0, 0)),
            ]
            + [pl.BlockSpec(memory_space=pl.ANY)] * len(earlier),
            out_specs=[
                pl.BlockSpec((block, wide), lambda i, f, l, p: (at(i, p), 0)),
                pl.BlockSpec((wide, block), lambda i, f, l, p: (0, at(i, p))),
                pl.BlockSpec((groups, RATIO, 1, block), lambda i, f, l, p: (0, 0, 0, at(i, p))),
                pl.BlockSpec((None, block, width), lambda i, f, l, p: (i // 2, 0, 0)),
                pl.BlockSpec((None, block, width), lambda i, f, l, p: (i // 2, 0, 0)),
            ],
            scratch_shapes=[
                pltpu.VMEM((groups, 1, RATIO * block), jnp.float32),
                pltpu.VMEM((groups, 1, RATIO * block), jnp.float32),
                pltpu.VMEM((groups, HD, RATIO * block), jnp.float32),
            ],
        ),
        out_shape=[
            jax.ShapeDtypeStruct((length, wide), jnp.bfloat16),
            jax.ShapeDtypeStruct((wide, length), jnp.bfloat16),
            jax.ShapeDtypeStruct((groups, RATIO, 1, length), jnp.float32),
            out,
            out,
        ],
        input_output_aliases={8 + k: k for k in range(len(earlier))},
        compiler_params=params(),
        cost_estimate=cost(8 * groups * length * length * 64, 6 * MIB),
        name="attend",
    )(
        starts[::block], starts[block - 1 :: block], place, flip_four, row_four, flip_four,
        starts[None, :], weight, *earlier,
    )
    return (outs[:3], outs[3], outs[4])


def attend_back_kernel(pieces, first_ref, last_ref, place_ref, *refs):
    (query_ref, query_row_ref, key_ref, key_row_ref, value_row_ref, context_ref, log_ref,
     start_ref, weight_ref, raw_ref, raw_key_ref, cos_ref, sin_ref, gain_ref) = refs[:14]
    dh_pieces = refs[14 : 14 + pieces]
    if pieces > 1:
        joint_ref, gain_grad_ref, dh_ref = refs[14 + pieces : 17 + pieces]
    else:
        joint_ref, gain_grad_ref = refs[14 + pieces : 16 + pieces]
        dh_ref = dh_pieces[0]
    query_sum, key_sum, value_sum, query_gain_sum = refs[-4:]
    block = start_ref.shape[1]
    step = pl.program_id(0)
    steps = pl.num_programs(0)
    ratio = query_ref.shape[0]
    wide = ratio * HD

    @pl.when(step == 0)
    def _():
        key_sum[...] = jnp.zeros_like(key_sum)
        value_sum[...] = jnp.zeros_like(value_sum)
        query_gain_sum[...] = jnp.zeros_like(query_gain_sum)

    if pieces > 1:
        source = HALVES * ((step // HALVES) ^ place_ref[0]) + step % HALVES
        for r, piece in enumerate(dh_pieces):

            @pl.when(source == r)
            def _(piece=piece):
                dh_ref[...] = piece[...]

    query = jnp.concatenate([query_ref[h] for h in range(ratio)], axis=1)
    query_row = jnp.concatenate([query_row_ref[h] for h in range(ratio)], axis=0)
    start_row = start_ref[...]
    grad_wide = dot_nt(weight_ref[...], dh_ref[...]).astype(jnp.bfloat16)
    grad_float = grad_wide.astype(jnp.float32)
    products = grad_float * context_ref[...].astype(jnp.float32)
    delta = jnp.concatenate(
        [
            jnp.sum(products[h * HD : (h + 1) * HD], axis=0, keepdims=True)
            for h in range(ratio)
        ],
        axis=1,
    )
    grad = jnp.concatenate([grad_wide[h * HD : (h + 1) * HD] for h in range(ratio)], axis=1)
    turned = grad_float.T.astype(jnp.bfloat16)
    grad_row = jnp.concatenate([turned[:, h * HD : (h + 1) * HD] for h in range(ratio)], axis=0)
    log_total = jnp.concatenate([log_ref[h] for h in range(ratio)], axis=1)
    query_sum[...] = jnp.zeros_like(query_sum)

    def one(masked, at, size):
        at = pl.multiple_of(at, block)
        here = pl.ds(at, size)
        probs = jnp.exp(dot_nn(key_row_ref[here, :], query) - log_total)
        if masked:
            mask = mask_of(start_row, at, step * block, size)
            probs = jnp.where(jnp.concatenate([mask] * ratio, axis=1), probs, 0.0)
        prob_grad = dot_nn(value_row_ref[here, :], grad)
        score_grad = (probs * (prob_grad - delta)).astype(jnp.bfloat16)
        value_sum[here, :] += dot_nn(probs.astype(jnp.bfloat16), grad_row)
        key_sum[here, :] += dot_nn(score_grad, query_row)
        query_sum[...] += dot_nn(key_ref[:, here], score_grad)

    over_keys(one, first_ref[step], last_ref[step], step, block)

    def unwind(part, raw, cosine, sine, gain):
        inverse = head_scale(raw)
        back = rotate_back(part, cosine, sine)
        scaled = back * gain
        lean = jnp.mean(scaled * raw, axis=0, keepdims=True)
        return (back * raw * inverse, inverse * scaled - raw * inverse**3 * lean)

    at = pl.multiple_of(step * block, block)
    here = pl.ds(at, block)
    outs = []
    for h in range(ratio):
        part = query_sum[:, h * block : (h + 1) * block] * HD ** (-0.5)
        gain_part, out = unwind(
            part, raw_ref[h], cos_ref[:, here], sin_ref[:, here], gain_ref[:, 0:1]
        )
        query_gain_sum[...] += gain_part
        outs.append(out)
    joint_ref[here, :wide] = jnp.concatenate(outs, axis=0).T.astype(jnp.bfloat16)

    @pl.when(step == steps - 1)
    def _():
        def one_key(j, total):
            at = pl.multiple_of(j * block, block)
            here = pl.ds(at, block)
            pair = jnp.concatenate([key_sum[here, :], value_sum[here, :]], axis=1).T
            gain_part, out = unwind(
                pair[:HD], raw_key_ref[:, here], cos_ref[:, here], sin_ref[:, here],
                gain_ref[:, 1:2],
            )
            both = jnp.concatenate([out, pair[HD:]], axis=0)
            joint_ref[here, wide:] = both.T.astype(jnp.bfloat16)
            return total + gain_part

        key_gain_sum = lax.fori_loop(
            0, steps, one_key, jnp.zeros(query_gain_sum.shape, jnp.float32)
        )
        both = jnp.concatenate([query_gain_sum[...], key_gain_sum], axis=0).T
        gain_grad_ref[...] = jnp.sum(both, axis=0, keepdims=True)


def attend_back(
    g, place, flipped, rows, context_flip, log_total, starts, dh, weight, raw, tables, head_gains
):
    slots, _, length = flipped.shape
    groups = slots // KINDS
    ratio = RATIO
    block = length // PIECES // HALVES
    wide = ratio * HD
    width = weight.shape[1]
    pieces = len(dh)
    flip_four = flipped.reshape(groups, KINDS, HD, length)
    row_four = rows.reshape(groups, KINDS, length, HD)
    raw_four = raw.reshape(groups, KINDS, HD, length)
    by_step = pl.BlockSpec((block, width), lambda i, f, l, p: (i, 0))
    whole = pl.BlockSpec((block, width), lambda i, f, l, p: (0, 0))
    outs = pl.pallas_call(
        lambda *refs: attend_back_kernel(pieces, *refs),
        grid_spec=pltpu.PrefetchScalarGridSpec(
            num_scalar_prefetch=3,
            grid=(length // block,),
            in_specs=[
                pl.BlockSpec((None, ratio, HD, block), lambda i, f, l, p: (g, 0, 0, i)),
                pl.BlockSpec((None, ratio, block, HD), lambda i, f, l, p: (g, 0, i, 0)),
                pl.BlockSpec((None, None, HD, length), lambda i, f, l, p: (g, ratio, 0, 0)),
                pl.BlockSpec((None, None, length, HD), lambda i, f, l, p: (g, ratio, 0, 0)),
                pl.BlockSpec((None, None, length, HD), lambda i, f, l, p: (g, ratio + 1, 0, 0)),
                pl.BlockSpec((wide, block), lambda i, f, l, p: (g, i)),
                pl.BlockSpec((None, ratio, 1, block), lambda i, f, l, p: (g, 0, 0, i)),
                pl.BlockSpec((1, block), lambda i, f, l, p: (0, i)),
                pl.BlockSpec((wide, width), lambda i, f, l, p: (g, 0)),
                pl.BlockSpec((None, ratio, HD, block), lambda i, f, l, p: (g, 0, 0, i)),
                pl.BlockSpec((None, None, HD, length), lambda i, f, l, p: (g, ratio, 0, 0)),
                pl.BlockSpec((HD // 2, length), lambda i, f, l, p: (0, 0)),
                pl.BlockSpec((HD // 2, length), lambda i, f, l, p: (0, 0)),
                pl.BlockSpec(head_gains.shape, lambda i, f, l, p: (0, 0)),
            ]
            + [whole if pieces > 1 else by_step] * pieces,
            out_specs=[
                pl.BlockSpec((length, wide + 2 * HD), lambda i, f, l, p: (0, 0)),
                pl.BlockSpec((1, 2 * HD), lambda i, f, l, p: (0, 0)),
            ]
            + [by_step] * (pieces > 1),
            scratch_shapes=[
                pltpu.VMEM((HD, ratio * block), jnp.float32),
                pltpu.VMEM((length, HD), jnp.float32),
                pltpu.VMEM((length, HD), jnp.float32),
                pltpu.VMEM((HD, block), jnp.float32),
            ],
        ),
        out_shape=[
            jax.ShapeDtypeStruct((length, wide + 2 * HD), jnp.bfloat16),
            jax.ShapeDtypeStruct((1, 2 * HD), jnp.float32),
        ]
        + [jax.ShapeDtypeStruct((length, width), jnp.bfloat16)] * (pieces > 1),
        compiler_params=params(),
        cost_estimate=cost(20 * length * length * 128, 12 * MIB),
        name="attend_back",
    )(
        starts[::block], starts[block - 1 :: block], place, flip_four, row_four, flip_four, row_four, row_four, context_flip,
        log_total, starts[None, :], weight, raw_four, raw_four, tables[0], tables[1],
        head_gains, *dh,
    )
    return outs


def spread_kernel(groups, place_ref, *refs):
    send_rows, keep_rows = refs[:groups], refs[groups : 2 * groups]
    weight_ref, send_out, keep_out = refs[2 * groups :]
    depth = weight_ref.shape[0] // groups
    for rows, out in ((send_rows, send_out), (keep_rows, keep_out)):
        joined = jnp.concatenate([row[...] for row in rows], axis=1)
        out[...] = dot_nn(joined, weight_ref[...]).astype(jnp.bfloat16)


def spread(place, rows, weight):
    groups = len(rows)
    length, depth = rows[0].shape
    width = weight.shape[1]
    block = length // PIECES
    out = jax.ShapeDtypeStruct((PIECES // 2, block, width), jnp.bfloat16)
    return pl.pallas_call(
        lambda *refs: spread_kernel(groups, *refs),
        grid_spec=pltpu.PrefetchScalarGridSpec(
            num_scalar_prefetch=1,
            grid=(PIECES // 2,),
            in_specs=[pl.BlockSpec((block, depth), lambda i, p: ((2 * i + 1) ^ p[0], 0))] * groups
            + [pl.BlockSpec((block, depth), lambda i, p: ((2 * i) ^ p[0], 0))] * groups
            + [pl.BlockSpec(weight.shape, lambda i, p: (0, 0))],
            out_specs=[pl.BlockSpec((None, block, width), lambda i, p: (i, 0, 0))] * 2,
        ),
        out_shape=[out, out],
        compiler_params=params(),
        cost_estimate=cost(2 * length * width * depth * groups, 6 * MIB),
        name="spread",
    )(place, *rows, *rows, weight)


def feed_kernel(*refs):
    xs, grads, joint_ref, down_ref = refs[:2], refs[2:4], refs[4], refs[5]
    x_ref, grad_ref, hidden_ref, low_ref, out_keep, out_send, back_keep, back_send = refs[-8:]
    hidden_width = down_ref.shape[0]
    block = xs[0].shape[0]
    for r in range(2):
        x_ref[r * block : (r + 1) * block, :] = xs[r][...]
        grad_ref[r * block : (r + 1) * block, :] = grads[r][...]
    both = dot_nn(x_ref[...], joint_ref[...])
    gate, up = (both[:, :hidden_width], both[:, hidden_width:])
    sigmoid = 1.0 / (1.0 + jnp.exp(-gate))
    swish = gate * sigmoid
    hidden = (swish * up).astype(jnp.bfloat16)
    hidden_ref[...] = hidden
    hidden_grad = dot_nt(grad_ref[...], down_ref[...])
    low_ref[:, :hidden_width] = (
        hidden_grad * up * sigmoid * (1.0 + gate * (1.0 - sigmoid))
    ).astype(jnp.bfloat16)
    low_ref[:, hidden_width:] = (hidden_grad * swish).astype(jnp.bfloat16)
    out = dot_nn(hidden, down_ref[...]).astype(jnp.bfloat16)
    out_keep[...] = out[:block]
    out_send[...] = out[block:]
    back = dot_nt(low_ref[...], joint_ref[...]).astype(jnp.bfloat16)
    back_keep[...] = back[:block]
    back_send[...] = back[block:]


def feed(call, half, earlier, normed, grads, joint_weight, down_weight):
    block, width = normed[0].shape
    hidden_width = down_weight.shape[0]
    length = block * PIECES * HALVES
    once = pl.Buffered(1)
    row = lambda columns: pl.BlockSpec((2 * block, columns), lambda i: (call, 0))
    whole = lambda value: pl.BlockSpec(value.shape, lambda i: (0, 0), pipeline_mode=once)
    pair = pl.BlockSpec((block, width), lambda i: (0, 0))
    full = lambda columns: jax.ShapeDtypeStruct((length, columns), jnp.bfloat16)
    outs = pl.pallas_call(
        feed_kernel,
        grid=(1,),
        in_specs=[pl.BlockSpec((block, width), lambda i: (0, 0), pipeline_mode=once)] * 2
        + [pl.BlockSpec((block, width), lambda i: (half, 0), pipeline_mode=once)] * 2
        + [whole(joint_weight), whole(down_weight)]
        + [pl.BlockSpec(memory_space=pl.ANY)] * len(earlier),
        out_specs=[row(width), row(width), row(hidden_width), row(2 * hidden_width)] + [pair] * 4,
        out_shape=[full(width), full(width), full(hidden_width), full(2 * hidden_width)]
        + [jax.ShapeDtypeStruct((block, width), jnp.bfloat16)] * 4,
        input_output_aliases={6 + k: k for k in range(len(earlier))},
        compiler_params=params(),
        cost_estimate=cost(3 * length * width * hidden_width, 16 * MIB),
        name="feed",
    )(*normed, *grads, joint_weight, down_weight, *earlier)
    return (outs[:4], outs[4:6], outs[6:8])


def norm_kernel(x_ref, keep_ref, near_ref, far_ref, gain_ref, middle_ref, normed_ref):
    f32 = jnp.float32
    middle = x_ref[...].astype(f32) + (
        keep_ref[...].astype(f32) + near_ref[...].astype(f32) + far_ref[...].astype(f32)
    )
    middle_ref[...] = middle
    normed_ref[...] = (middle * row_scale(middle) * gain_ref[...]).astype(jnp.bfloat16)


def first_of(value, rows, width):
    if value.ndim == 3:
        return pl.BlockSpec((None, rows, width), lambda i: (0, i, 0))
    return pl.BlockSpec((rows, width), lambda i: (i, 0))


def norm(half, tokens, keep, near, far, gain):
    length, width = far.shape
    steps = 2
    rows = length // steps
    flat = pl.BlockSpec((rows, width), lambda i: (i, 0))
    return pl.pallas_call(
        norm_kernel,
        grid=(steps,),
        in_specs=[
            pl.BlockSpec((rows, width), lambda i: (half * steps + i, 0)),
            first_of(keep, rows, width),
            first_of(near, rows, width),
            flat,
            pl.BlockSpec(gain.shape, lambda i: (0, 0)),
        ],
        out_specs=[flat, flat],
        out_shape=[
            jax.ShapeDtypeStruct((length, width), jnp.float32),
            jax.ShapeDtypeStruct((length, width), jnp.bfloat16),
        ],
        compiler_params=params(),
        cost_estimate=cost(0, 4 * MIB),
        name="norm",
    )(tokens, keep, near, far, gain)


def norm_back_of(value, skip, grad, gain):
    inverse = row_scale(value)
    scaled = grad * gain
    lean = jnp.mean(scaled * value, axis=-1, keepdims=True)
    total = skip + (inverse * scaled - value * (inverse**3 * lean))
    return total, jnp.sum(grad * value * inverse, axis=0, keepdims=True)


def norm_back_kernel(
    value_ref, skip_ref, keep_ref, near_ref, far_ref, gain_ref, low_ref, part_ref
):
    f32 = jnp.float32
    grad = keep_ref[...].astype(f32) + near_ref[...].astype(f32) + far_ref[...].astype(f32)
    total, part = norm_back_of(value_ref[...], skip_ref[...].astype(f32), grad, gain_ref[...])
    low_ref[...] = total.astype(jnp.bfloat16)

    @pl.when(pl.program_id(0) == 0)
    def _():
        part_ref[...] = jnp.zeros_like(part_ref)

    part_ref[...] += part


def norm_back(half, value, skip, keep, near, far, gain):
    length, width = far.shape
    steps = 2
    rows = length // steps
    flat = pl.BlockSpec((rows, width), lambda i: (i, 0))
    return pl.pallas_call(
        norm_back_kernel,
        grid=(steps,),
        in_specs=[
            flat,
            pl.BlockSpec((rows, width), lambda i: (half * steps + i, 0)),
            first_of(keep, rows, width),
            first_of(near, rows, width),
            flat,
            pl.BlockSpec(gain.shape, lambda i: (0, 0)),
        ],
        out_specs=[flat, pl.BlockSpec((1, width), lambda i: (0, 0))],
        out_shape=[
            jax.ShapeDtypeStruct((length, width), jnp.bfloat16),
            jax.ShapeDtypeStruct((1, width), jnp.float32),
        ],
        compiler_params=params(),
        cost_estimate=cost(0, 6 * MIB),
        name="norm_back",
    )(value, skip, keep, near, far, gain)


def row_kernel(counts, *refs):
    row_ref = refs[-1]
    parts, heads, squares = refs[: counts[0]], refs[counts[0] : counts[1]], refs[counts[1] : -1]
    width = parts[0].shape[1]
    total = lambda items: sum([item[...] for item in items[1:]], items[0][...])
    row_ref[:, :width] = jnp.zeros((1, width), jnp.float32)
    row_ref[:, width : 2 * width] = total(parts)
    row_ref[:, 2 * width : 2 * width + 2 * HD] = total(heads)
    lane = lax.broadcasted_iota(jnp.int32, (1, 2 * HD), 1)
    row_ref[:, 2 * width + 2 * HD :] = jnp.where(lane == 0, total(squares), 0.0)


def row_of(parts, heads, squares):
    counts = (len(parts), len(parts) + len(heads))
    return pl.pallas_call(
        lambda *refs: row_kernel(counts, *refs),
        out_shape=jax.ShapeDtypeStruct((1, 2 * parts[0].shape[1] + 4 * HD), jnp.float32),
        compiler_params=params(24),
        cost_estimate=cost(0, MIB),
        name="row",
    )(*parts, *heads, *squares)


def finish_kernel(
    x_ref, near_skip, far_skip, keep_ref, near_ref, far_ref, gain_ref, begin_ref, square_ref,
    input_grad_ref, row_ref,
):
    f32 = jnp.float32
    step = pl.program_id(0)
    width = x_ref.shape[1]
    grad = keep_ref[...].astype(f32) + near_ref[...].astype(f32) + far_ref[...].astype(f32)
    skip = jnp.where(step < pl.num_programs(0) // HALVES, near_skip[...], far_skip[...])
    total, part = norm_back_of(
        x_ref[...].astype(f32), skip.astype(f32), grad, gain_ref[...]
    )
    input_grad_ref[...] = total.astype(jnp.bfloat16)

    @pl.when(step == 0)
    def _():
        lane = lax.broadcasted_iota(jnp.int32, row_ref.shape, 1)
        last = jnp.where(lane == 2 * width + 2 * HD, square_ref[...], 0.0)
        row_ref[...] = begin_ref[...] + last

    row_ref[:, :width] += part


def finish(tokens, skips, keep, near, far, gain, row, square):
    length, width = far.shape
    each = 1
    rows = length // HALVES // each
    flat = pl.BlockSpec((rows, width), lambda i: (i, 0))
    whole = lambda value: pl.BlockSpec(value.shape, lambda i: (0, 0))
    return pl.pallas_call(
        finish_kernel,
        grid=(HALVES * each,),
        in_specs=[
            flat,
            pl.BlockSpec((rows, width), lambda i: (jnp.minimum(i, each - 1), 0)),
            pl.BlockSpec((rows, width), lambda i: (jnp.maximum(i - each, 0), 0)),
            first_of(keep, rows, width),
            first_of(near, rows, width),
            flat,
            whole(gain),
            whole(row),
            whole(square),
        ],
        out_specs=[flat, whole(row)],
        out_shape=[
            jax.ShapeDtypeStruct((length, width), jnp.bfloat16),
            jax.ShapeDtypeStruct(row.shape, jnp.float32),
        ],
        compiler_params=params(),
        cost_estimate=cost(0, 6 * MIB),
        name="finish",
    )(tokens, *skips, keep, near, far, gain, row, square)


def exchange(value, axis, bit):
    size = lax.axis_size(axis)
    return lax.ppermute(value, axis, [(i, i ^ bit) for i in range(size)])


def after(value, *others):
    return lax.optimization_barrier((value, *others))[0]


def power_of_two(count):
    return count & (count - 1) == 0


class ScatterSum:
    def __init__(self, grads, flipped, swapped=()):
        size = lax.axis_size("dp")
        rows = grads[0].shape[0] // size
        self.left = [1 << k for k in reversed(range(size.bit_length() - 1))]
        self.order = self.left[::-1]
        if swapped and len(self.order) > max(swapped):
            one, two = swapped
            self.order[one], self.order[two] = self.order[two], self.order[one]
        self.flipped = flipped
        self.sources = [grad.reshape(size, rows, grad.shape[1]) for grad in grads]
        self.columns = sum(grad.shape[1] for grad in grads)
        self.joined = True
        self.total = None


def advance_kernel(plans, here_ref, *refs):
    count = sum(plan[0] for plan in plans)
    ins, outs = refs[:count], refs[count:]
    squares = jnp.zeros((1, 1), jnp.float32)
    for sources, joined, stride, shift, flipped in plans:
        parts, ins = ins[:sources], ins[sources:]

        def value(at, parts=parts, joined=joined):
            if joined:
                return jnp.concatenate([part[at] for part in parts], axis=1)
            return parts[0][at].astype(jnp.float32) + parts[1][at].astype(jnp.float32)

        if stride is None:
            total = value(0).astype(jnp.float32)
            over = jnp.sum(total * total, axis=0, keepdims=True)
            squares += jnp.sum(over, axis=1, keepdims=True)
            at = 0
            for columns, turned in flipped:
                part = total[:, at : at + columns]
                outs[0][...] = part.T if turned else part
                at, outs = at + columns, outs[1:]
            continue
        sent, kept, outs = outs[0], outs[1], outs[2:]
        own = (here_ref[0] >> shift) & 1
        for k in range(sent.shape[0]):
            base = k // stride * 2 * stride + k % stride
            sent[k] = value(base + (1 - own) * stride).astype(sent.dtype)
            kept[k] = value(base + own * stride).astype(kept.dtype)
    outs[0][...] = squares


def advance(here, items, *gates):
    plans, ins, shapes = [], [], []
    for item in items:
        rows, columns = item.sources[0].shape[1], item.columns
        if item.order:
            bit = item.order[0]
            at = item.left.index(bit)
            stride = 1 << (len(item.left) - 1 - at)
            plans.append((len(item.sources), item.joined, stride, bit.bit_length() - 1, ()))
            half = (item.sources[0].shape[0] // 2, rows, columns)
            shapes += [jax.ShapeDtypeStruct(half, jnp.bfloat16)] * 2
        else:
            plans.append((len(item.sources), item.joined, None, 0, item.flipped))
            for part, turned in item.flipped:
                shape = (part, rows) if turned else (rows, part)
                shapes.append(jax.ShapeDtypeStruct(shape, jnp.float32))
        ins += item.sources
    shapes.append(jax.ShapeDtypeStruct((1, 1), jnp.float32))
    if gates:
        ins[-1] = after(ins[-1], *gates)
    vmem = pl.BlockSpec(memory_space=pltpu.VMEM)
    outs = list(pl.pallas_call(
        lambda *refs: advance_kernel(plans, *refs),
        in_specs=[pl.BlockSpec(memory_space=pltpu.SMEM)] + [vmem] * len(ins),
        out_specs=[vmem] * len(shapes),
        out_shape=shapes,
        compiler_params=params(24),
        cost_estimate=cost(0, 6 * MIB),
        name="advance",
    )(here, *ins))
    sent_all = []
    for item in items:
        if item.order:
            bit = item.order.pop(0)
            item.left.remove(bit)
            sent, kept = outs.pop(0), outs.pop(0)
            item.sources, item.joined = [kept, exchange(sent, "dp", bit)], False
            sent_all.append(sent)
        else:
            item.total = [outs.pop(0) for _ in item.flipped]
    return sent_all, outs[0]


def sum_all(value):
    for axis in ("tensor", "dp"):
        size = lax.axis_size(axis)
        if not power_of_two(size):
            value = lax.psum(value, axis)
            continue
        bit = 1
        while bit < size:
            if 2 * bit < size:
                one, two, three = [exchange(value, axis, bit * k) for k in (1, 2, 3)]
                value = (value + one) + (two + three)
                bit *= 4
            else:
                value = value + exchange(value, axis, bit)
                bit *= 2
    return value


def adam(master, mean, square, grad, factor, rate, decay):
    scaled = grad * factor
    mean_new = BETA_ONE * mean + (1.0 - BETA_ONE) * scaled
    square_new = BETA_TWO * square + (1.0 - BETA_TWO) * scaled * scaled
    mean_hat = mean_new / (1.0 - BETA_ONE**STEP)
    square_hat = square_new / (1.0 - BETA_TWO**STEP)
    new = master - rate * (mean_hat / (jnp.sqrt(square_hat) + ADAM_EPS) + decay * master)
    return (new, mean_new, square_new)


def adam_kernel(
    out_rate, entries, sum_ref, out_sum, early_ref, late_ref, gate_ref, up_ref, down_sum, *refs
):
    gain_sum = sum_ref[:, :entries]
    squares = sum_ref[:, entries : entries + 1]
    norm = jnp.sqrt(squares + jnp.sum(gain_sum * gain_sum, axis=1, keepdims=True))
    factor = CLIP_NORM / jnp.maximum(norm, CLIP_NORM)
    states = [refs[3 * k : 3 * k + 3] for k in range(4)]
    results = [refs[12 + 4 * k : 16 + 4 * k] for k in range(4)]
    refs[28][...] = norm

    def update(state, result, at, grad, rate):
        new, mean, square = adam(
            state[0][at], state[1][at], state[2][at], grad.astype(jnp.float32), factor, rate,
            DECAY,
        )
        result[0][at] = new
        result[1][at] = new.astype(jnp.bfloat16)
        result[2][at] = mean
        result[3][at] = square

    rows = slice(None)
    early = early_ref.shape[1]
    update(states[1], results[1], (rows, rows), out_sum[...], out_rate)
    update(states[0], results[0], (rows, slice(0, early)), early_ref[...], RATE_WEIGHT)
    update(states[0], results[0], (rows, slice(early, None)), late_ref[...], RATE_WEIGHT)
    update(states[2], results[2], (rows, 0, rows), gate_ref[...], RATE_WEIGHT)
    update(states[2], results[2], (rows, 1, rows), up_ref[...], RATE_WEIGHT)
    update(states[3], results[3], (rows, rows), down_sum[...], RATE_WEIGHT)


def adam_all(entries, summed, sums, states, out_rate):
    steps = max(1, states[0][0].shape[0] // 32)

    def block(array):
        rows = array.shape[0] // steps
        rest = array.shape[1:]
        return pl.BlockSpec((rows,) + rest, lambda i: (i,) + (0,) * len(rest))

    shapes = []
    for state in states:
        shapes += [
            jax.ShapeDtypeStruct(state[0].shape, dtype)
            for dtype in (jnp.float32, jnp.bfloat16, jnp.float32, jnp.float32)
        ]
    arrays = [*sums]
    for state in states:
        arrays += state
    small = lambda shape: pl.BlockSpec(shape, lambda i: (0, 0))
    return pl.pallas_call(
        lambda *refs: adam_kernel(out_rate, entries, *refs),
        grid=(steps,),
        in_specs=[small(summed.shape)] + [block(array) for array in arrays],
        out_specs=[block(shape) for shape in shapes] + [small((1, 1))],
        out_shape=shapes + [jax.ShapeDtypeStruct((1, 1), jnp.float32)],
        compiler_params=params(),
        cost_estimate=cost(0, 16 * MIB),
        name="adam",
    )(summed, *arrays)


def shards(
    tokens,
    segments,
    cotangent,
    qkv_weight,
    out_weight,
    gate_up_weight,
    down_weight,
    qkv_master,
    out_master,
    gate_up_master,
    down_master,
    qkv_mean,
    out_mean,
    gate_up_mean,
    down_mean,
    qkv_square,
    out_square,
    gate_up_square,
    down_square,
    gains,
    gains_mean,
    gains_square,
):
    width = tokens.shape[1]
    length = segments.shape[0]
    groups = qkv_weight.shape[1] // (KINDS * HD)
    hidden_width = down_weight.shape[0]
    block = length // PIECES // HALVES
    attn_gain = gains[None, :width]
    ffn_gain = gains[None, width : 2 * width]
    head_gains = jnp.stack([gains[2 * width : 2 * width + HD], gains[2 * width + HD :]], axis=1)
    place = lax.axis_index("tensor").astype(jnp.int32).reshape(1)
    here = lax.axis_index("dp").astype(jnp.int32).reshape(1)

    across = exchange(tokens, "tensor", ACROSS)
    beside = exchange(tokens, "tensor", CORE)
    starts = starts_of(segments)
    tables = rotary((jnp.arange(length, dtype=jnp.int32) - starts).astype(jnp.float32))
    weight_rows = qkv_weight.T
    inner = (attn_gain, weight_rows, head_gains, *tables)
    near_part = project(0, [], place, [tokens, beside], *inner)
    flat_weight = after(gate_up_weight, near_part[2]).reshape(width, 2 * hidden_width)
    across = after(across, near_part[2], flat_weight)
    corner = exchange(across, "tensor", CORE)
    normed_one, raw, flipped, rows = project(1, near_part, place, [across, corner], *inner)

    grad_across = exchange(after(cotangent, across), "tensor", ACROSS)
    grad_pieces = [
        cotangent,
        exchange(after(cotangent, across), "tensor", CORE),
        grad_across,
        exchange(grad_across, "tensor", CORE),
    ]

    def added(left, right):
        return (left.astype(jnp.float32) + right.astype(jnp.float32)).astype(jnp.bfloat16)

    def halfway(send, keep):
        near = exchange(send, "tensor", CORE)
        return (keep, near, added(keep[1], near[1]))

    def across_of(passed):
        keep, near, passed = passed
        return (keep, near, exchange(passed, "tensor", ACROSS))

    attended, send, keep = attend(0, [], place, flipped, rows, starts, out_weight)
    passed = halfway(after(send, grad_across), keep)
    shares = across_of(passed)
    flipped_late = after(flipped, passed[2])
    attended, send, keep = attend(1, attended, place, flipped_late, rows, starts, out_weight)
    context, context_flip, log_total = attended

    weights = (flat_weight, down_weight)
    middle, normed = norm(0, tokens, *shares, ffn_gain)
    middles = [middle]
    beside, across = exchange(normed, "tensor", CORE), exchange(normed, "tensor", ACROSS)
    passed = halfway(after(send, shares[2]), keep)
    shares = across_of(passed)
    full, out_near, back_near = feed(
        0, 0, [], [after(normed, passed[2]), beside], grad_pieces[:2], *weights
    )
    across = after(across, out_near[0])
    corner = exchange(across, "tensor", CORE)
    full, out_far, back_far = feed(1, 0, full, [across, corner], grad_pieces[2:], *weights)
    outs, backs = [(*out_near, *out_far)], [(*back_near, *back_far)]

    keep, near, far = shares
    middle, normed = norm(1, tokens, keep, near, after(far, out_far[0]), ffn_gain)
    middles.append(middle)
    beside, across = exchange(normed, "tensor", CORE), exchange(normed, "tensor", ACROSS)
    full, out_near, back_near = feed(2, 1, full, [normed, beside], grad_pieces[:2], *weights)

    def share_of(pieces, *gates):
        third = exchange(pieces[3], "tensor", CORE)
        third = after(third, *gates) if gates else third
        return (pieces[0], exchange(pieces[1], "tensor", CORE), added(pieces[2], third))

    passed = share_of(backs[0], out_near[0])
    sums = [across_of(passed)]
    across = after(across, out_near[0])
    corner = exchange(across, "tensor", CORE)
    across = after(across, passed[2])
    full, out_far, back_far = feed(3, 1, full, [across, corner], grad_pieces[2:], *weights)
    outs.append((*out_near, *out_far))
    backs.append((*back_near, *back_far))
    normed_two, grad_full, hidden, flat_low = full

    def dh_of(half, keep, near, far):
        low, part = norm_back(half, middles[half], cotangent, keep, near, far, ffn_gain)
        across = exchange(low, "tensor", ACROSS)
        pieces = [low, exchange(low, "tensor", CORE), across, exchange(across, "tensor", CORE)]
        return pieces, part

    keep, near, far = sums[0]
    first_dh = dh_of(0, keep, near, after(far, out_far[0]))
    passed = share_of(after(tuple(backs[1]), far))
    sums.append(across_of(passed))
    normed_two = after(normed_two, passed[2], first_dh[0][0])
    gate_grad = contract_rows(normed_two, flat_low[:, :hidden_width])
    gate = ScatterSum([gate_grad.astype(jnp.bfloat16)], [(hidden_width, False)], (1, 2))
    sent, square = advance(here, [gate])
    squares = [square]
    up_grad = contract_rows(after(normed_two, sent[0]), flat_low[:, hidden_width:])
    up = ScatterSum([up_grad.astype(jnp.bfloat16)], [(hidden_width, False)], (0, 1))
    sent, _ = advance(here, [up])
    out_sums = [share_of(after(tuple(out), passed[2])) for out in outs]
    keep, near, far = sums[1]
    second_dh = dh_of(1, keep, near, after(far, sent[0], first_dh[0][2]))
    pieces_dh, ffn_parts = zip(first_dh, second_dh)
    down_grad = contract_rows(after(grad_full, pieces_dh[1][0]), hidden).astype(jnp.bfloat16)
    down = ScatterSum([down_grad], [(hidden_width, True)], (1, 2))
    sent, _ = advance(here, [down])
    sent, _ = advance(here, [gate], sent[0])

    dh = [pieces_dh[half][r] for r in range(PIECES) for half in range(HALVES)]
    dh[0] = after(dh[0], *sent, *[item[2] for item in out_sums])
    out_fars = [
        exchange(after(item[2], pieces_dh[1][2]), "tensor", ACROSS) for item in out_sums
    ]

    joints, head_parts, mixed, early = [], [], [], []
    for g in range(groups):
        outs_back = attend_back(
            g, place, flipped, rows, context_flip, log_total, starts, dh, out_weight, raw, tables,
            head_gains,
        )
        joints.append(outs_back[0])
        head_parts.append(outs_back[1])
        if g == 0:
            dh_full = outs_back[2]
            early = ScatterSum(
                [
                    contract_rows(dh_full, context).astype(jnp.bfloat16),
                    contract_rows(normed_one, outs_back[0]).astype(jnp.bfloat16),
                ],
                [(context.shape[1], True), (joints[0].shape[1], False)],
            )
            sent, _ = advance(here, [gate, up, down, early], outs_back[1])
            dh = [after(dh_full, *sent, *out_fars)]
        else:
            dh = [dh_full]
    late = [
        contract_rows(normed_one, joints[g]).astype(jnp.bfloat16) for g in range(1, groups)
    ]
    late = ScatterSum(late, [(joints[0].shape[1] * (groups - 1), False)])
    sent, square = advance(here, [gate, up, down, early, late])
    squares.append(square)
    joints[0] = after(joints[0], *sent)
    send, keep = spread(place, joints, weight_rows)
    near = exchange(send, "tensor", CORE)
    third = after(near, early.sources[1], late.sources[1])
    passed = (keep, near, added(keep[1], third[1]))
    keep, near, far = across_of(passed)
    pending = [early, late]
    gates = [passed[2]]
    while pending != [late]:
        _, square = advance(here, pending, *gates)
        gates = []
        squares.append(square)
        pending = [item for item in (gate, up, down, early, late) if item.total is None]

    results = []
    for half in range(HALVES):
        keep_out, near_out, _ = out_sums[half]
        total = keep_out.astype(jnp.float32) + near_out.astype(jnp.float32)
        results.append(middles[half] + (total + out_fars[half].astype(jnp.float32)))
    result = jnp.concatenate(results, axis=0).astype(jnp.bfloat16)

    ffn_parts = [after(ffn_parts[0], result), *ffn_parts[1:]]
    row = row_of(ffn_parts, head_parts, squares)
    gates = [row]
    while late.total is None:
        _, square = advance(here, [late], *gates)
        gates = []
    skips = [pieces[0] for pieces in pieces_dh]
    input_grad, row = finish(tokens, skips, keep, near, far, attn_gain, row, square)
    summed = sum_all(row)
    entries = gains.shape[0]
    out_fan = max(QH * HD * 16 // length, 16)
    out_rate = RATE_WEIGHT * (QH * HD / out_fan) ** 0.5
    updated = adam_all(
        entries, summed, [*early.total, *late.total, *gate.total, *up.total, *down.total],
        [
            (qkv_master, qkv_mean, qkv_square),
            (out_master, out_mean, out_square),
            (gate_up_master, gate_up_mean, gate_up_square),
            (down_master, down_mean, down_square),
        ],
        out_rate,
    )
    grad_norm = updated[16][0, 0]
    factor = CLIP_NORM / jnp.maximum(grad_norm, CLIP_NORM)
    gain_results = adam(
        gains, gains_mean, gains_square, summed[0, :entries], factor, RATE_GAIN, 0.0
    )
    return (result, input_grad, grad_norm, *updated[:16], *gain_results)


def solution(mesh):
    in_specs = (
        P(("dp", "tensor"), None),
        P("dp"),
        P(("dp", "tensor"), None),
        P(None, "tensor"),
        P("tensor", None),
        P(None, None, "tensor"),
        P("tensor", None),
        P("dp", "tensor"),
        P("tensor", "dp"),
        P("dp", None, "tensor"),
        P("tensor", "dp"),
        P("dp", "tensor"),
        P("tensor", "dp"),
        P("dp", None, "tensor"),
        P("tensor", "dp"),
        P("dp", "tensor"),
        P("tensor", "dp"),
        P("dp", None, "tensor"),
        P("tensor", "dp"),
        P(),
        P(),
        P(),
    )
    out_specs = (
        P(("dp", "tensor"), None),
        P(("dp", "tensor"), None),
        P(),
        P("dp", "tensor"),
        P("dp", "tensor"),
        P("dp", "tensor"),
        P("dp", "tensor"),
        P("tensor", "dp"),
        P("tensor", "dp"),
        P("tensor", "dp"),
        P("tensor", "dp"),
        P("dp", None, "tensor"),
        P("dp", None, "tensor"),
        P("dp", None, "tensor"),
        P("dp", None, "tensor"),
        P("tensor", "dp"),
        P("tensor", "dp"),
        P("tensor", "dp"),
        P("tensor", "dp"),
        P(),
        P(),
        P(),
    )
    return jax.shard_map(shards, mesh=mesh, in_specs=in_specs, out_specs=out_specs, check_vma=False)
```

```python
import jax
import jax.numpy as jnp
from jax import lax
from jax.experimental import pallas as pl
from jax.experimental.pallas import tpu as pltpu
from jax.sharding import PartitionSpec as P

QH = 16
KVH = 8
HD = 64
STEP = 5


NORM_EPS = 1e-06
ROPE_BASE = 1000000.0
CLIP_NORM = 1.0
BETA_ONE = 0.9
BETA_TWO = 0.95
ADAM_EPS = 1e-08
DECAY = 0.1
RATE_WEIGHT = 0.02
RATE_GAIN = 1.5
MASKED = -1e30

KINDS = QH // KVH + 2
RATIO = QH // KVH
PARTS = 1
PIECES = 4
HALVES = 2
CORE = 1
ACROSS = 2
MIB = 1024 * 1024


def params(limit=60):
    return pltpu.CompilerParams(vmem_limit_bytes=limit * MIB)


def cost(flops, size):
    return pl.CostEstimate(flops=flops // 8, bytes_accessed=size // 8, transcendentals=0)


def starts_of(seg):
    index = jnp.arange(seg.shape[0], dtype=jnp.int32)
    flag = (index == 0) | (seg != jnp.roll(seg, 1))
    return lax.cummax(jnp.where(flag, index, 0), axis=0)


def rotary(position):
    half = HD // 2
    freq = ROPE_BASE ** (-(jnp.arange(half, dtype=jnp.float32) * 2.0 / HD))
    angle = freq[:, None] * position[None, :]
    return (jnp.cos(angle), jnp.sin(angle))


def dot_nn(left, right):
    return lax.dot_general(
        left, right, (((1,), (0,)), ((), ())), preferred_element_type=jnp.float32
    )


def dot_nt(left, right):
    return lax.dot_general(
        left, right, (((1,), (1,)), ((), ())), preferred_element_type=jnp.float32
    )


def contract_rows(left, right):
    return lax.dot_general(
        left, right, (((0,), (0,)), ((), ())), preferred_element_type=jnp.float32
    )


def rotate(value, cosine, sine):
    half = value.shape[0] // 2
    first, second = (value[:half], value[half:])
    return jnp.concatenate(
        [first * cosine - second * sine, second * cosine + first * sine], axis=0
    )


def rotate_back(grad, cosine, sine):
    half = grad.shape[0] // 2
    first, second = (grad[:half], grad[half:])
    return jnp.concatenate(
        [first * cosine + second * sine, second * cosine - first * sine], axis=0
    )


def row_scale(value):
    return lax.rsqrt(jnp.mean(value * value, axis=-1, keepdims=True) + NORM_EPS)


def head_scale(value):
    return lax.rsqrt(jnp.mean(value * value, axis=0, keepdims=True) + NORM_EPS)


def project_kernel(place_ref, *refs):
    pieces = refs[:2]
    pre_ref, weight_ref, gain_ref, cos_ref, sin_ref = refs[2:7]
    normed_ref, raw_ref, flip_ref, row_ref = refs[-4:]
    step = pl.program_id(0)
    for r in range(2):

        @pl.when(step // PARTS == r)
        def _(r=r):
            value = pieces[r][...].astype(jnp.float32)
            normed_ref[...] = (value * row_scale(value) * pre_ref[...]).astype(jnp.bfloat16)

    joint = dot_nt(weight_ref[...], normed_ref[...])
    cosine, sine = cos_ref[...], sin_ref[...]
    for slot in range(raw_ref.shape[0]):
        kind = slot % KINDS
        raw = joint[slot * HD : (slot + 1) * HD]
        raw_ref[slot] = raw
        value = raw
        if kind < KINDS - 1:
            gain = gain_ref[:, 1:2] if kind == KINDS - 2 else gain_ref[:, 0:1]
            value = rotate(raw * head_scale(raw) * gain, cosine, sine)
        if kind < KINDS - 2:
            value = value * HD ** (-0.5)
        low = value.astype(jnp.bfloat16)
        flip_ref[slot] = low
        row_ref[slot] = low.T


def project(far, earlier, place, pieces, pre_gain, weight_rows, head_gains, cos_table, sin_table):
    rows, width = pieces[0].shape
    length = rows * PIECES
    block = rows // PARTS
    slots = weight_rows.shape[0] // HD
    at = lambda i, p: PARTS * ((i // PARTS + 2 * far) ^ p[0]) + i % PARTS

    def piece(r):
        return pl.BlockSpec(
            (block, width), lambda i, p: (jnp.clip(i - PARTS * r, 0, PARTS - 1), 0)
        )

    return pl.pallas_call(
        project_kernel,
        grid_spec=pltpu.PrefetchScalarGridSpec(
            num_scalar_prefetch=1,
            grid=(2 * PARTS,),
            in_specs=[piece(0), piece(1)]
            + [
                pl.BlockSpec(pre_gain.shape, lambda i, p: (0, 0)),
                pl.BlockSpec(weight_rows.shape, lambda i, p: (0, 0)),
                pl.BlockSpec(head_gains.shape, lambda i, p: (0, 0)),
                pl.BlockSpec((HD // 2, block), lambda i, p: (0, at(i, p))),
                pl.BlockSpec((HD // 2, block), lambda i, p: (0, at(i, p))),
            ]
            + [pl.BlockSpec(memory_space=pl.ANY)] * len(earlier),
            out_specs=[
                pl.BlockSpec((block, width), lambda i, p: (at(i, p), 0)),
                pl.BlockSpec((slots, HD, block), lambda i, p: (0, 0, at(i, p))),
                pl.BlockSpec((slots, HD, block), lambda i, p: (0, 0, at(i, p))),
                pl.BlockSpec((slots, block, HD), lambda i, p: (0, at(i, p), 0)),
            ],
        ),
        out_shape=[
            jax.ShapeDtypeStruct((length, width), jnp.bfloat16),
            jax.ShapeDtypeStruct((slots, HD, length), jnp.float32),
            jax.ShapeDtypeStruct((slots, HD, length), jnp.bfloat16),
            jax.ShapeDtypeStruct((slots, length, HD), jnp.bfloat16),
        ],
        input_output_aliases={8 + k: k for k in range(len(earlier))},
        compiler_params=params(),
        cost_estimate=cost(length * width * slots * HD, 8 * MIB),
        name="project",
    )(place, *pieces, pre_gain, weight_rows, head_gains, cos_table, sin_table, *earlier)


def mask_of(start_row, first_key, first_query, keys):
    queries = start_row.shape[1]
    key = first_key + lax.broadcasted_iota(jnp.int32, (keys, 1), 0)
    query = first_query + lax.broadcasted_iota(jnp.int32, (1, queries), 1)
    return (key >= start_row) & (key <= query)


def over_keys(one, first, last, at_query, block):
    begin = first // block
    whole = jnp.maximum(begin, jnp.minimum((last + block - 1) // block, at_query))
    pairs = (at_query - whole) // 2
    lax.fori_loop(begin, whole, lambda j, carry: one(True, j * block, block), None)
    lax.fori_loop(
        0, pairs, lambda k, carry: one(False, (whole + 2 * k) * block, 2 * block), None
    )
    lax.fori_loop(
        whole + 2 * pairs, at_query, lambda j, carry: one(False, j * block, block), None
    )
    one(True, at_query * block, block)


def attend_kernel(half, first_ref, last_ref, place_ref, *refs):
    query_ref, key_ref, value_ref, start_ref, weight_ref = refs[:5]
    context_ref, flip_ref, log_ref, send_ref, keep_ref, top_ref, total_ref, sum_ref = refs[-8:]
    groups, ratio = query_ref.shape[:2]
    block = start_ref.shape[1]
    step = pl.program_id(0)
    at_query = HALVES * (step ^ place_ref[0]) + half
    start_row = start_ref[...]
    queries = [
        jnp.concatenate([query_ref[g, h] for h in range(ratio)], axis=1) for g in range(groups)
    ]
    top_ref[...] = jnp.full_like(top_ref, MASKED)
    total_ref[...] = jnp.zeros_like(total_ref)
    sum_ref[...] = jnp.zeros_like(sum_ref)

    def one(masked, at, size):
        at = pl.multiple_of(at, block)
        if masked:
            mask = mask_of(start_row, at, at_query * block, size)
            mask = jnp.concatenate([mask] * ratio, axis=1)
        for g in range(groups):
            scores = dot_nn(key_ref[g, pl.ds(at, size), :], queries[g])
            if masked:
                scores = jnp.where(mask, scores, MASKED)
            top_old = top_ref[g]
            top = jnp.maximum(top_old, jnp.max(scores, axis=0, keepdims=True))
            expo = jnp.exp(scores - top)
            fade = jnp.exp(top_old - top)
            top_ref[g] = top
            total_ref[g] = total_ref[g] * fade + jnp.sum(expo, axis=0, keepdims=True)
            part = dot_nn(value_ref[g, :, pl.ds(at, size)], expo.astype(jnp.bfloat16))
            sum_ref[g] = sum_ref[g] * fade + part

    over_keys(one, first_ref[at_query], last_ref[at_query], at_query, block)
    wide = ratio * HD
    for g in range(groups):
        total = total_ref[g]
        output = sum_ref[g] / total
        both = jnp.concatenate(
            [output[:, h * block : (h + 1) * block] for h in range(ratio)], axis=0
        )
        flip_ref[g * wide : (g + 1) * wide, :] = both.astype(jnp.bfloat16)
        context_ref[:, g * wide : (g + 1) * wide] = both.T.astype(jnp.bfloat16)
        log_total = top_ref[g] + jnp.log(total)
        for h in range(ratio):
            log_ref[g, h] = log_total[:, h * block : (h + 1) * block]
    part = dot_nn(context_ref[...], weight_ref[...]).astype(jnp.bfloat16)

    @pl.when(step % 2 == 1)
    def _():
        send_ref[...] = part

    @pl.when(step % 2 == 0)
    def _():
        keep_ref[...] = part


def attend(half, earlier, place, flipped, rows, starts, weight):
    slots, _, length = flipped.shape
    groups = slots // KINDS
    block = length // PIECES // HALVES
    width = weight.shape[1]
    wide = groups * RATIO * HD
    at = lambda i, p: HALVES * (i ^ p[0]) + half
    flip_four = flipped.reshape(groups, KINDS, HD, length)
    row_four = rows.reshape(groups, KINDS, length, HD)
    out = jax.ShapeDtypeStruct((PIECES // 2, block, width), jnp.bfloat16)
    outs = pl.pallas_call(
        lambda *refs: attend_kernel(half, *refs),
        grid_spec=pltpu.PrefetchScalarGridSpec(
            num_scalar_prefetch=3,
            grid=(PIECES,),
            in_specs=[
                pl.BlockSpec((groups, RATIO, HD, block), lambda i, f, l, p: (0, 0, 0, at(i, p))),
                pl.BlockSpec((groups, None, length, HD), lambda i, f, l, p: (0, RATIO, 0, 0)),
                pl.BlockSpec((groups, None, HD, length), lambda i, f, l, p: (0, RATIO + 1, 0, 0)),
                pl.BlockSpec((1, block), lambda i, f, l, p: (0, at(i, p))),
                pl.BlockSpec(weight.shape, lambda i, f, l, p: (0, 0)),
            ]
            + [pl.BlockSpec(memory_space=pl.ANY)] * len(earlier),
            out_specs=[
                pl.BlockSpec((block, wide), lambda i, f, l, p: (at(i, p), 0)),
                pl.BlockSpec((wide, block), lambda i, f, l, p: (0, at(i, p))),
                pl.BlockSpec((groups, RATIO, 1, block), lambda i, f, l, p: (0, 0, 0, at(i, p))),
                pl.BlockSpec((None, block, width), lambda i, f, l, p: (i // 2, 0, 0)),
                pl.BlockSpec((None, block, width), lambda i, f, l, p: (i // 2, 0, 0)),
            ],
            scratch_shapes=[
                pltpu.VMEM((groups, 1, RATIO * block), jnp.float32),
                pltpu.VMEM((groups, 1, RATIO * block), jnp.float32),
                pltpu.VMEM((groups, HD, RATIO * block), jnp.float32),
            ],
        ),
        out_shape=[
            jax.ShapeDtypeStruct((length, wide), jnp.bfloat16),
            jax.ShapeDtypeStruct((wide, length), jnp.bfloat16),
            jax.ShapeDtypeStruct((groups, RATIO, 1, length), jnp.float32),
            out,
            out,
        ],
        input_output_aliases={8 + k: k for k in range(len(earlier))},
        compiler_params=params(),
        cost_estimate=cost(8 * groups * length * length * 64, 6 * MIB),
        name="attend",
    )(
        starts[::block], starts[block - 1 :: block], place, flip_four, row_four, flip_four,
        starts[None, :], weight, *earlier,
    )
    return (outs[:3], outs[3], outs[4])


def attend_back_kernel(pieces, first_ref, last_ref, place_ref, *refs):
    (query_ref, query_row_ref, key_ref, key_row_ref, value_row_ref, context_ref, log_ref,
     start_ref, weight_ref, raw_ref, raw_key_ref, cos_ref, sin_ref, gain_ref) = refs[:14]
    dh_pieces = refs[14 : 14 + pieces]
    if pieces > 1:
        joint_ref, gain_grad_ref, dh_ref = refs[14 + pieces : 17 + pieces]
    else:
        joint_ref, gain_grad_ref = refs[14 + pieces : 16 + pieces]
        dh_ref = dh_pieces[0]
    query_sum, key_sum, value_sum, query_gain_sum = refs[-4:]
    block = start_ref.shape[1]
    step = pl.program_id(0)
    steps = pl.num_programs(0)
    ratio = query_ref.shape[0]
    wide = ratio * HD

    @pl.when(step == 0)
    def _():
        key_sum[...] = jnp.zeros_like(key_sum)
        value_sum[...] = jnp.zeros_like(value_sum)
        query_gain_sum[...] = jnp.zeros_like(query_gain_sum)

    if pieces > 1:
        source = HALVES * ((step // HALVES) ^ place_ref[0]) + step % HALVES
        for r, piece in enumerate(dh_pieces):

            @pl.when(source == r)
            def _(piece=piece):
                dh_ref[...] = piece[...]

    query = jnp.concatenate([query_ref[h] for h in range(ratio)], axis=1)
    query_row = jnp.concatenate([query_row_ref[h] for h in range(ratio)], axis=0)
    start_row = start_ref[...]
    grad_wide = dot_nt(weight_ref[...], dh_ref[...]).astype(jnp.bfloat16)
    grad_float = grad_wide.astype(jnp.float32)
    products = grad_float * context_ref[...].astype(jnp.float32)
    delta = jnp.concatenate(
        [
            jnp.sum(products[h * HD : (h + 1) * HD], axis=0, keepdims=True)
            for h in range(ratio)
        ],
        axis=1,
    )
    grad = jnp.concatenate([grad_wide[h * HD : (h + 1) * HD] for h in range(ratio)], axis=1)
    turned = grad_float.T.astype(jnp.bfloat16)
    grad_row = jnp.concatenate([turned[:, h * HD : (h + 1) * HD] for h in range(ratio)], axis=0)
    log_total = jnp.concatenate([log_ref[h] for h in range(ratio)], axis=1)
    query_sum[...] = jnp.zeros_like(query_sum)

    def one(masked, at, size):
        at = pl.multiple_of(at, block)
        here = pl.ds(at, size)
        probs = jnp.exp(dot_nn(key_row_ref[here, :], query) - log_total)
        if masked:
            mask = mask_of(start_row, at, step * block, size)
            probs = jnp.where(jnp.concatenate([mask] * ratio, axis=1), probs, 0.0)
        prob_grad = dot_nn(value_row_ref[here, :], grad)
        score_grad = (probs * (prob_grad - delta)).astype(jnp.bfloat16)
        value_sum[here, :] += dot_nn(probs.astype(jnp.bfloat16), grad_row)
        key_sum[here, :] += dot_nn(score_grad, query_row)
        query_sum[...] += dot_nn(key_ref[:, here], score_grad)

    over_keys(one, first_ref[step], last_ref[step], step, block)

    def unwind(part, raw, cosine, sine, gain):
        inverse = head_scale(raw)
        back = rotate_back(part, cosine, sine)
        scaled = back * gain
        lean = jnp.mean(scaled * raw, axis=0, keepdims=True)
        return (back * raw * inverse, inverse * scaled - raw * inverse**3 * lean)

    at = pl.multiple_of(step * block, block)
    here = pl.ds(at, block)
    outs = []
    for h in range(ratio):
        part = query_sum[:, h * block : (h + 1) * block] * HD ** (-0.5)
        gain_part, out = unwind(
            part, raw_ref[h], cos_ref[:, here], sin_ref[:, here], gain_ref[:, 0:1]
        )
        query_gain_sum[...] += gain_part
        outs.append(out)
    joint_ref[here, :wide] = jnp.concatenate(outs, axis=0).T.astype(jnp.bfloat16)

    @pl.when(step == steps - 1)
    def _():
        def one_key(j, total):
            at = pl.multiple_of(j * block, block)
            here = pl.ds(at, block)
            pair = jnp.concatenate([key_sum[here, :], value_sum[here, :]], axis=1).T
            gain_part, out = unwind(
                pair[:HD], raw_key_ref[:, here], cos_ref[:, here], sin_ref[:, here],
                gain_ref[:, 1:2],
            )
            both = jnp.concatenate([out, pair[HD:]], axis=0)
            joint_ref[here, wide:] = both.T.astype(jnp.bfloat16)
            return total + gain_part

        key_gain_sum = lax.fori_loop(
            0, steps, one_key, jnp.zeros(query_gain_sum.shape, jnp.float32)
        )
        both = jnp.concatenate([query_gain_sum[...], key_gain_sum], axis=0).T
        gain_grad_ref[...] = jnp.sum(both, axis=0, keepdims=True)


def attend_back(
    g, place, flipped, rows, context_flip, log_total, starts, dh, weight, raw, tables, head_gains
):
    slots, _, length = flipped.shape
    groups = slots // KINDS
    ratio = RATIO
    block = length // PIECES // HALVES
    wide = ratio * HD
    width = weight.shape[1]
    pieces = len(dh)
    flip_four = flipped.reshape(groups, KINDS, HD, length)
    row_four = rows.reshape(groups, KINDS, length, HD)
    raw_four = raw.reshape(groups, KINDS, HD, length)
    by_step = pl.BlockSpec((block, width), lambda i, f, l, p: (i, 0))
    whole = pl.BlockSpec((block, width), lambda i, f, l, p: (0, 0))
    outs = pl.pallas_call(
        lambda *refs: attend_back_kernel(pieces, *refs),
        grid_spec=pltpu.PrefetchScalarGridSpec(
            num_scalar_prefetch=3,
            grid=(length // block,),
            in_specs=[
                pl.BlockSpec((None, ratio, HD, block), lambda i, f, l, p: (g, 0, 0, i)),
                pl.BlockSpec((None, ratio, block, HD), lambda i, f, l, p: (g, 0, i, 0)),
                pl.BlockSpec((None, None, HD, length), lambda i, f, l, p: (g, ratio, 0, 0)),
                pl.BlockSpec((None, None, length, HD), lambda i, f, l, p: (g, ratio, 0, 0)),
                pl.BlockSpec((None, None, length, HD), lambda i, f, l, p: (g, ratio + 1, 0, 0)),
                pl.BlockSpec((wide, block), lambda i, f, l, p: (g, i)),
                pl.BlockSpec((None, ratio, 1, block), lambda i, f, l, p: (g, 0, 0, i)),
                pl.BlockSpec((1, block), lambda i, f, l, p: (0, i)),
                pl.BlockSpec((wide, width), lambda i, f, l, p: (g, 0)),
                pl.BlockSpec((None, ratio, HD, block), lambda i, f, l, p: (g, 0, 0, i)),
                pl.BlockSpec((None, None, HD, length), lambda i, f, l, p: (g, ratio, 0, 0)),
                pl.BlockSpec((HD // 2, length), lambda i, f, l, p: (0, 0)),
                pl.BlockSpec((HD // 2, length), lambda i, f, l, p: (0, 0)),
                pl.BlockSpec(head_gains.shape, lambda i, f, l, p: (0, 0)),
            ]
            + [whole if pieces > 1 else by_step] * pieces,
            out_specs=[
                pl.BlockSpec((length, wide + 2 * HD), lambda i, f, l, p: (0, 0)),
                pl.BlockSpec((1, 2 * HD), lambda i, f, l, p: (0, 0)),
            ]
            + [by_step] * (pieces > 1),
            scratch_shapes=[
                pltpu.VMEM((HD, ratio * block), jnp.float32),
                pltpu.VMEM((length, HD), jnp.float32),
                pltpu.VMEM((length, HD), jnp.float32),
                pltpu.VMEM((HD, block), jnp.float32),
            ],
        ),
        out_shape=[
            jax.ShapeDtypeStruct((length, wide + 2 * HD), jnp.bfloat16),
            jax.ShapeDtypeStruct((1, 2 * HD), jnp.float32),
        ]
        + [jax.ShapeDtypeStruct((length, width), jnp.bfloat16)] * (pieces > 1),
        compiler_params=params(),
        cost_estimate=cost(20 * length * length * 128, 12 * MIB),
        name="attend_back",
    )(
        starts[::block], starts[block - 1 :: block], place, flip_four, row_four, flip_four, row_four, row_four, context_flip,
        log_total, starts[None, :], weight, raw_four, raw_four, tables[0], tables[1],
        head_gains, *dh,
    )
    return outs


def spread_kernel(groups, place_ref, *refs):
    send_rows, keep_rows = refs[:groups], refs[groups : 2 * groups]
    weight_ref, send_out, keep_out = refs[2 * groups :]
    depth = weight_ref.shape[0] // groups
    for rows, out in ((send_rows, send_out), (keep_rows, keep_out)):
        joined = jnp.concatenate([row[...] for row in rows], axis=1)
        out[...] = dot_nn(joined, weight_ref[...]).astype(jnp.bfloat16)


def spread(place, rows, weight):
    groups = len(rows)
    length, depth = rows[0].shape
    width = weight.shape[1]
    block = length // PIECES
    out = jax.ShapeDtypeStruct((PIECES // 2, block, width), jnp.bfloat16)
    return pl.pallas_call(
        lambda *refs: spread_kernel(groups, *refs),
        grid_spec=pltpu.PrefetchScalarGridSpec(
            num_scalar_prefetch=1,
            grid=(PIECES // 2,),
            in_specs=[pl.BlockSpec((block, depth), lambda i, p: ((2 * i + 1) ^ p[0], 0))] * groups
            + [pl.BlockSpec((block, depth), lambda i, p: ((2 * i) ^ p[0], 0))] * groups
            + [pl.BlockSpec(weight.shape, lambda i, p: (0, 0))],
            out_specs=[pl.BlockSpec((None, block, width), lambda i, p: (i, 0, 0))] * 2,
        ),
        out_shape=[out, out],
        compiler_params=params(),
        cost_estimate=cost(2 * length * width * depth * groups, 6 * MIB),
        name="spread",
    )(place, *rows, *rows, weight)


def feed_kernel(*refs):
    xs, grads, joint_ref, down_ref = refs[:2], refs[2:4], refs[4], refs[5]
    x_ref, grad_ref, hidden_ref, low_ref, out_keep, out_send, back_keep, back_send = refs[-8:]
    hidden_width = down_ref.shape[0]
    block = xs[0].shape[0]
    for r in range(2):
        x_ref[r * block : (r + 1) * block, :] = xs[r][...]
        grad_ref[r * block : (r + 1) * block, :] = grads[r][...]
    both = dot_nn(x_ref[...], joint_ref[...])
    gate, up = (both[:, :hidden_width], both[:, hidden_width:])
    sigmoid = 1.0 / (1.0 + jnp.exp(-gate))
    swish = gate * sigmoid
    hidden = (swish * up).astype(jnp.bfloat16)
    hidden_ref[...] = hidden
    hidden_grad = dot_nt(grad_ref[...], down_ref[...])
    low_ref[:, :hidden_width] = (
        hidden_grad * up * sigmoid * (1.0 + gate * (1.0 - sigmoid))
    ).astype(jnp.bfloat16)
    low_ref[:, hidden_width:] = (hidden_grad * swish).astype(jnp.bfloat16)
    out = dot_nn(hidden, down_ref[...]).astype(jnp.bfloat16)
    out_keep[...] = out[:block]
    out_send[...] = out[block:]
    back = dot_nt(low_ref[...], joint_ref[...]).astype(jnp.bfloat16)
    back_keep[...] = back[:block]
    back_send[...] = back[block:]


def feed(call, half, earlier, normed, grads, joint_weight, down_weight):
    block, width = normed[0].shape
    hidden_width = down_weight.shape[0]
    length = block * PIECES * HALVES
    once = pl.Buffered(1)
    row = lambda columns: pl.BlockSpec((2 * block, columns), lambda i: (call, 0))
    whole = lambda value: pl.BlockSpec(value.shape, lambda i: (0, 0), pipeline_mode=once)
    pair = pl.BlockSpec((block, width), lambda i: (0, 0))
    full = lambda columns: jax.ShapeDtypeStruct((length, columns), jnp.bfloat16)
    outs = pl.pallas_call(
        feed_kernel,
        grid=(1,),
        in_specs=[pl.BlockSpec((block, width), lambda i: (0, 0), pipeline_mode=once)] * 2
        + [pl.BlockSpec((block, width), lambda i: (half, 0), pipeline_mode=once)] * 2
        + [whole(joint_weight), whole(down_weight)]
        + [pl.BlockSpec(memory_space=pl.ANY)] * len(earlier),
        out_specs=[row(width), row(width), row(hidden_width), row(2 * hidden_width)] + [pair] * 4,
        out_shape=[full(width), full(width), full(hidden_width), full(2 * hidden_width)]
        + [jax.ShapeDtypeStruct((block, width), jnp.bfloat16)] * 4,
        input_output_aliases={6 + k: k for k in range(len(earlier))},
        compiler_params=params(),
        cost_estimate=cost(3 * length * width * hidden_width, 16 * MIB),
        name="feed",
    )(*normed, *grads, joint_weight, down_weight, *earlier)
    return (outs[:4], outs[4:6], outs[6:8])


def norm_kernel(x_ref, keep_ref, near_ref, far_ref, gain_ref, middle_ref, normed_ref):
    f32 = jnp.float32
    middle = x_ref[...].astype(f32) + (
        keep_ref[...].astype(f32) + near_ref[...].astype(f32) + far_ref[...].astype(f32)
    )
    middle_ref[...] = middle
    normed_ref[...] = (middle * row_scale(middle) * gain_ref[...]).astype(jnp.bfloat16)


def first_of(value, rows, width):
    if value.ndim == 3:
        return pl.BlockSpec((None, rows, width), lambda i: (0, i, 0))
    return pl.BlockSpec((rows, width), lambda i: (i, 0))


def norm(half, tokens, keep, near, far, gain):
    length, width = far.shape
    steps = 2
    rows = length // steps
    flat = pl.BlockSpec((rows, width), lambda i: (i, 0))
    return pl.pallas_call(
        norm_kernel,
        grid=(steps,),
        in_specs=[
            pl.BlockSpec((rows, width), lambda i: (half * steps + i, 0)),
            first_of(keep, rows, width),
            first_of(near, rows, width),
            flat,
            pl.BlockSpec(gain.shape, lambda i: (0, 0)),
        ],
        out_specs=[flat, flat],
        out_shape=[
            jax.ShapeDtypeStruct((length, width), jnp.float32),
            jax.ShapeDtypeStruct((length, width), jnp.bfloat16),
        ],
        compiler_params=params(),
        cost_estimate=cost(0, 4 * MIB),
        name="norm",
    )(tokens, keep, near, far, gain)


def norm_back_of(value, skip, grad, gain):
    inverse = row_scale(value)
    scaled = grad * gain
    lean = jnp.mean(scaled * value, axis=-1, keepdims=True)
    total = skip + (inverse * scaled - value * (inverse**3 * lean))
    return total, jnp.sum(grad * value * inverse, axis=0, keepdims=True)


def norm_back_kernel(
    value_ref, skip_ref, keep_ref, near_ref, far_ref, gain_ref, low_ref, part_ref
):
    f32 = jnp.float32
    grad = keep_ref[...].astype(f32) + near_ref[...].astype(f32) + far_ref[...].astype(f32)
    total, part = norm_back_of(value_ref[...], skip_ref[...].astype(f32), grad, gain_ref[...])
    low_ref[...] = total.astype(jnp.bfloat16)

    @pl.when(pl.program_id(0) == 0)
    def _():
        part_ref[...] = jnp.zeros_like(part_ref)

    part_ref[...] += part


def norm_back(half, value, skip, keep, near, far, gain):
    length, width = far.shape
    steps = 2
    rows = length // steps
    flat = pl.BlockSpec((rows, width), lambda i: (i, 0))
    return pl.pallas_call(
        norm_back_kernel,
        grid=(steps,),
        in_specs=[
            flat,
            pl.BlockSpec((rows, width), lambda i: (half * steps + i, 0)),
            first_of(keep, rows, width),
            first_of(near, rows, width),
            flat,
            pl.BlockSpec(gain.shape, lambda i: (0, 0)),
        ],
        out_specs=[flat, pl.BlockSpec((1, width), lambda i: (0, 0))],
        out_shape=[
            jax.ShapeDtypeStruct((length, width), jnp.bfloat16),
            jax.ShapeDtypeStruct((1, width), jnp.float32),
        ],
        compiler_params=params(),
        cost_estimate=cost(0, 6 * MIB),
        name="norm_back",
    )(value, skip, keep, near, far, gain)


def row_kernel(counts, *refs):
    row_ref = refs[-1]
    parts, heads, squares = refs[: counts[0]], refs[counts[0] : counts[1]], refs[counts[1] : -1]
    width = parts[0].shape[1]
    total = lambda items: sum([item[...] for item in items[1:]], items[0][...])
    row_ref[:, :width] = jnp.zeros((1, width), jnp.float32)
    row_ref[:, width : 2 * width] = total(parts)
    row_ref[:, 2 * width : 2 * width + 2 * HD] = total(heads)
    lane = lax.broadcasted_iota(jnp.int32, (1, 2 * HD), 1)
    row_ref[:, 2 * width + 2 * HD :] = jnp.where(lane == 0, total(squares), 0.0)


def row_of(parts, heads, squares):
    counts = (len(parts), len(parts) + len(heads))
    return pl.pallas_call(
        lambda *refs: row_kernel(counts, *refs),
        out_shape=jax.ShapeDtypeStruct((1, 2 * parts[0].shape[1] + 4 * HD), jnp.float32),
        compiler_params=params(24),
        cost_estimate=cost(0, MIB),
        name="row",
    )(*parts, *heads, *squares)


def finish_kernel(
    x_ref, near_skip, far_skip, keep_ref, near_ref, far_ref, gain_ref, begin_ref, square_ref,
    input_grad_ref, row_ref,
):
    f32 = jnp.float32
    step = pl.program_id(0)
    width = x_ref.shape[1]
    grad = keep_ref[...].astype(f32) + near_ref[...].astype(f32) + far_ref[...].astype(f32)
    skip = jnp.where(step < pl.num_programs(0) // HALVES, near_skip[...], far_skip[...])
    total, part = norm_back_of(
        x_ref[...].astype(f32), skip.astype(f32), grad, gain_ref[...]
    )
    input_grad_ref[...] = total.astype(jnp.bfloat16)

    @pl.when(step == 0)
    def _():
        lane = lax.broadcasted_iota(jnp.int32, row_ref.shape, 1)
        last = jnp.where(lane == 2 * width + 2 * HD, square_ref[...], 0.0)
        row_ref[...] = begin_ref[...] + last

    row_ref[:, :width] += part


def finish(tokens, skips, keep, near, far, gain, row, square):
    length, width = far.shape
    each = 1
    rows = length // HALVES // each
    flat = pl.BlockSpec((rows, width), lambda i: (i, 0))
    whole = lambda value: pl.BlockSpec(value.shape, lambda i: (0, 0))
    return pl.pallas_call(
        finish_kernel,
        grid=(HALVES * each,),
        in_specs=[
            flat,
            pl.BlockSpec((rows, width), lambda i: (jnp.minimum(i, each - 1), 0)),
            pl.BlockSpec((rows, width), lambda i: (jnp.maximum(i - each, 0), 0)),
            first_of(keep, rows, width),
            first_of(near, rows, width),
            flat,
            whole(gain),
            whole(row),
            whole(square),
        ],
        out_specs=[flat, whole(row)],
        out_shape=[
            jax.ShapeDtypeStruct((length, width), jnp.bfloat16),
            jax.ShapeDtypeStruct(row.shape, jnp.float32),
        ],
        compiler_params=params(),
        cost_estimate=cost(0, 6 * MIB),
        name="finish",
    )(tokens, *skips, keep, near, far, gain, row, square)


def exchange(value, axis, bit):
    size = lax.axis_size(axis)
    return lax.ppermute(value, axis, [(i, i ^ bit) for i in range(size)])


def after(value, *others):
    return lax.optimization_barrier((value, *others))[0]


def power_of_two(count):
    return count & (count - 1) == 0


class ScatterSum:
    def __init__(self, grads, flipped, swapped=()):
        size = lax.axis_size("dp")
        rows = grads[0].shape[0] // size
        self.left = [1 << k for k in reversed(range(size.bit_length() - 1))]
        self.order = self.left[::-1]
        if swapped and len(self.order) > max(swapped):
            one, two = swapped
            self.order[one], self.order[two] = self.order[two], self.order[one]
        self.flipped = flipped
        self.sources = [grad.reshape(size, rows, grad.shape[1]) for grad in grads]
        self.columns = sum(grad.shape[1] for grad in grads)
        self.joined = True
        self.total = None


def advance_kernel(plans, here_ref, *refs):
    count = sum(plan[0] for plan in plans)
    ins, outs = refs[:count], refs[count:]
    squares = jnp.zeros((1, 1), jnp.float32)
    for sources, joined, stride, shift, flipped in plans:
        parts, ins = ins[:sources], ins[sources:]

        def value(at, parts=parts, joined=joined):
            if joined:
                return jnp.concatenate([part[at] for part in parts], axis=1)
            return parts[0][at].astype(jnp.float32) + parts[1][at].astype(jnp.float32)

        if stride is None:
            total = value(0).astype(jnp.float32)
            over = jnp.sum(total * total, axis=0, keepdims=True)
            squares += jnp.sum(over, axis=1, keepdims=True)
            at = 0
            for columns, turned in flipped:
                part = total[:, at : at + columns]
                outs[0][...] = part.T if turned else part
                at, outs = at + columns, outs[1:]
            continue
        sent, kept, outs = outs[0], outs[1], outs[2:]
        own = (here_ref[0] >> shift) & 1
        for k in range(sent.shape[0]):
            base = k // stride * 2 * stride + k % stride
            sent[k] = value(base + (1 - own) * stride).astype(sent.dtype)
            kept[k] = value(base + own * stride).astype(kept.dtype)
    outs[0][...] = squares


def advance(here, items, *gates):
    plans, ins, shapes = [], [], []
    for item in items:
        rows, columns = item.sources[0].shape[1], item.columns
        if item.order:
            bit = item.order[0]
            at = item.left.index(bit)
            stride = 1 << (len(item.left) - 1 - at)
            plans.append((len(item.sources), item.joined, stride, bit.bit_length() - 1, ()))
            half = (item.sources[0].shape[0] // 2, rows, columns)
            shapes += [jax.ShapeDtypeStruct(half, jnp.bfloat16)] * 2
        else:
            plans.append((len(item.sources), item.joined, None, 0, item.flipped))
            for part, turned in item.flipped:
                shape = (part, rows) if turned else (rows, part)
                shapes.append(jax.ShapeDtypeStruct(shape, jnp.float32))
        ins += item.sources
    shapes.append(jax.ShapeDtypeStruct((1, 1), jnp.float32))
    if gates:
        ins[-1] = after(ins[-1], *gates)
    vmem = pl.BlockSpec(memory_space=pltpu.VMEM)
    outs = list(pl.pallas_call(
        lambda *refs: advance_kernel(plans, *refs),
        in_specs=[pl.BlockSpec(memory_space=pltpu.SMEM)] + [vmem] * len(ins),
        out_specs=[vmem] * len(shapes),
        out_shape=shapes,
        compiler_params=params(24),
        cost_estimate=cost(0, 6 * MIB),
        name="advance",
    )(here, *ins))
    sent_all = []
    for item in items:
        if item.order:
            bit = item.order.pop(0)
            item.left.remove(bit)
            sent, kept = outs.pop(0), outs.pop(0)
            item.sources, item.joined = [kept, exchange(sent, "dp", bit)], False
            sent_all.append(sent)
        else:
            item.total = [outs.pop(0) for _ in item.flipped]
    return sent_all, outs[0]


def sum_all(value):
    for axis in ("tensor", "dp"):
        size = lax.axis_size(axis)
        if not power_of_two(size):
            value = lax.psum(value, axis)
            continue
        bit = 1
        while bit < size:
            if 2 * bit < size:
                one, two, three = [exchange(value, axis, bit * k) for k in (1, 2, 3)]
                value = (value + one) + (two + three)
                bit *= 4
            else:
                value = value + exchange(value, axis, bit)
                bit *= 2
    return value


def adam(master, mean, square, grad, factor, rate, decay):
    scaled = grad * factor
    mean_new = BETA_ONE * mean + (1.0 - BETA_ONE) * scaled
    square_new = BETA_TWO * square + (1.0 - BETA_TWO) * scaled * scaled
    mean_hat = mean_new / (1.0 - BETA_ONE**STEP)
    square_hat = square_new / (1.0 - BETA_TWO**STEP)
    new = master - rate * (mean_hat / (jnp.sqrt(square_hat) + ADAM_EPS) + decay * master)
    return (new, mean_new, square_new)


def adam_kernel(
    out_rate, entries, sum_ref, out_sum, early_ref, late_ref, gate_ref, up_ref, down_sum, *refs
):
    gain_sum = sum_ref[:, :entries]
    squares = sum_ref[:, entries : entries + 1]
    norm = jnp.sqrt(squares + jnp.sum(gain_sum * gain_sum, axis=1, keepdims=True))
    factor = CLIP_NORM / jnp.maximum(norm, CLIP_NORM)
    states = [refs[3 * k : 3 * k + 3] for k in range(4)]
    results = [refs[12 + 4 * k : 16 + 4 * k] for k in range(4)]
    refs[28][...] = norm

    def update(state, result, at, grad, rate):
        new, mean, square = adam(
            state[0][at], state[1][at], state[2][at], grad.astype(jnp.float32), factor, rate,
            DECAY,
        )
        result[0][at] = new
        result[1][at] = new.astype(jnp.bfloat16)
        result[2][at] = mean
        result[3][at] = square

    rows = slice(None)
    early = early_ref.shape[1]
    update(states[1], results[1], (rows, rows), out_sum[...], out_rate)
    update(states[0], results[0], (rows, slice(0, early)), early_ref[...], RATE_WEIGHT)
    update(states[0], results[0], (rows, slice(early, None)), late_ref[...], RATE_WEIGHT)
    update(states[2], results[2], (rows, 0, rows), gate_ref[...], RATE_WEIGHT)
    update(states[2], results[2], (rows, 1, rows), up_ref[...], RATE_WEIGHT)
    update(states[3], results[3], (rows, rows), down_sum[...], RATE_WEIGHT)


def adam_all(entries, summed, sums, states, out_rate):
    steps = max(1, states[0][0].shape[0] // 32)

    def block(array):
        rows = array.shape[0] // steps
        rest = array.shape[1:]
        return pl.BlockSpec((rows,) + rest, lambda i: (i,) + (0,) * len(rest))

    shapes = []
    for state in states:
        shapes += [
            jax.ShapeDtypeStruct(state[0].shape, dtype)
            for dtype in (jnp.float32, jnp.bfloat16, jnp.float32, jnp.float32)
        ]
    arrays = [*sums]
    for state in states:
        arrays += state
    small = lambda shape: pl.BlockSpec(shape, lambda i: (0, 0))
    return pl.pallas_call(
        lambda *refs: adam_kernel(out_rate, entries, *refs),
        grid=(steps,),
        in_specs=[small(summed.shape)] + [block(array) for array in arrays],
        out_specs=[block(shape) for shape in shapes] + [small((1, 1))],
        out_shape=shapes + [jax.ShapeDtypeStruct((1, 1), jnp.float32)],
        compiler_params=params(),
        cost_estimate=cost(0, 16 * MIB),
        name="adam",
    )(summed, *arrays)


def shards(
    tokens,
    segments,
    cotangent,
    qkv_weight,
    out_weight,
    gate_up_weight,
    down_weight,
    qkv_master,
    out_master,
    gate_up_master,
    down_master,
    qkv_mean,
    out_mean,
    gate_up_mean,
    down_mean,
    qkv_square,
    out_square,
    gate_up_square,
    down_square,
    gains,
    gains_mean,
    gains_square,
):
    width = tokens.shape[1]
    length = segments.shape[0]
    groups = qkv_weight.shape[1] // (KINDS * HD)
    hidden_width = down_weight.shape[0]
    block = length // PIECES // HALVES
    attn_gain = gains[None, :width]
    ffn_gain = gains[None, width : 2 * width]
    head_gains = jnp.stack([gains[2 * width : 2 * width + HD], gains[2 * width + HD :]], axis=1)
    place = lax.axis_index("tensor").astype(jnp.int32).reshape(1)
    here = lax.axis_index("dp").astype(jnp.int32).reshape(1)

    across = exchange(tokens, "tensor", ACROSS)
    beside = exchange(tokens, "tensor", CORE)
    starts = starts_of(segments)
    tables = rotary((jnp.arange(length, dtype=jnp.int32) - starts).astype(jnp.float32))
    weight_rows = qkv_weight.T
    inner = (attn_gain, weight_rows, head_gains, *tables)
    near_part = project(0, [], place, [tokens, beside], *inner)
    flat_weight = after(gate_up_weight, near_part[2]).reshape(width, 2 * hidden_width)
    across = after(across, near_part[2], flat_weight)
    corner = exchange(across, "tensor", CORE)
    normed_one, raw, flipped, rows = project(1, near_part, place, [across, corner], *inner)

    grad_across = exchange(after(cotangent, across), "tensor", ACROSS)
    grad_pieces = [
        cotangent,
        exchange(after(cotangent, across), "tensor", CORE),
        grad_across,
        exchange(grad_across, "tensor", CORE),
    ]

    def added(left, right):
        return (left.astype(jnp.float32) + right.astype(jnp.float32)).astype(jnp.bfloat16)

    def halfway(send, keep):
        near = exchange(send, "tensor", CORE)
        return (keep, near, added(keep[1], near[1]))

    def across_of(passed):
        keep, near, passed = passed
        return (keep, near, exchange(passed, "tensor", ACROSS))

    attended, send, keep = attend(0, [], place, flipped, rows, starts, out_weight)
    passed = halfway(after(send, grad_across), keep)
    shares = across_of(passed)
    flipped_late = after(flipped, passed[2])
    attended, send, keep = attend(1, attended, place, flipped_late, rows, starts, out_weight)
    context, context_flip, log_total = attended

    weights = (flat_weight, down_weight)
    middle, normed = norm(0, tokens, *shares, ffn_gain)
    middles = [middle]
    beside, across = exchange(normed, "tensor", CORE), exchange(normed, "tensor", ACROSS)
    passed = halfway(after(send, shares[2]), keep)
    shares = across_of(passed)
    full, out_near, back_near = feed(
        0, 0, [], [after(normed, passed[2]), beside], grad_pieces[:2], *weights
    )
    across = after(across, out_near[0])
    corner = exchange(across, "tensor", CORE)
    full, out_far, back_far = feed(1, 0, full, [across, corner], grad_pieces[2:], *weights)
    outs, backs = [(*out_near, *out_far)], [(*back_near, *back_far)]

    keep, near, far = shares
    middle, normed = norm(1, tokens, keep, near, after(far, out_far[0]), ffn_gain)
    middles.append(middle)
    beside, across = exchange(normed, "tensor", CORE), exchange(normed, "tensor", ACROSS)
    full, out_near, back_near = feed(2, 1, full, [normed, beside], grad_pieces[:2], *weights)

    def share_of(pieces, *gates):
        third = exchange(pieces[3], "tensor", CORE)
        third = after(third, *gates) if gates else third
        return (pieces[0], exchange(pieces[1], "tensor", CORE), added(pieces[2], third))

    passed = share_of(backs[0], out_near[0])
    sums = [across_of(passed)]
    across = after(across, out_near[0])
    corner = exchange(across, "tensor", CORE)
    across = after(across, passed[2])
    full, out_far, back_far = feed(3, 1, full, [across, corner], grad_pieces[2:], *weights)
    outs.append((*out_near, *out_far))
    backs.append((*back_near, *back_far))
    normed_two, grad_full, hidden, flat_low = full

    def dh_of(half, keep, near, far):
        low, part = norm_back(half, middles[half], cotangent, keep, near, far, ffn_gain)
        across = exchange(low, "tensor", ACROSS)
        pieces = [low, exchange(low, "tensor", CORE), across, exchange(across, "tensor", CORE)]
        return pieces, part

    keep, near, far = sums[0]
    first_dh = dh_of(0, keep, near, after(far, out_far[0]))
    passed = share_of(after(tuple(backs[1]), far))
    sums.append(across_of(passed))
    normed_two = after(normed_two, passed[2], first_dh[0][0])
    gate_grad = contract_rows(normed_two, flat_low[:, :hidden_width])
    gate = ScatterSum([gate_grad.astype(jnp.bfloat16)], [(hidden_width, False)], (1, 2))
    sent, square = advance(here, [gate])
    squares = [square]
    up_grad = contract_rows(after(normed_two, sent[0]), flat_low[:, hidden_width:])
    up = ScatterSum([up_grad.astype(jnp.bfloat16)], [(hidden_width, False)], (0, 1))
    sent, _ = advance(here, [up])
    out_sums = [share_of(after(tuple(out), passed[2])) for out in outs]
    keep, near, far = sums[1]
    second_dh = dh_of(1, keep, near, after(far, sent[0], first_dh[0][2]))
    pieces_dh, ffn_parts = zip(first_dh, second_dh)
    down_grad = contract_rows(after(grad_full, pieces_dh[1][0]), hidden).astype(jnp.bfloat16)
    down = ScatterSum([down_grad], [(hidden_width, True)], (1, 2))
    sent, _ = advance(here, [down])
    sent, _ = advance(here, [gate], sent[0])

    dh = [pieces_dh[half][r] for r in range(PIECES) for half in range(HALVES)]
    dh[0] = after(dh[0], *sent, *[item[2] for item in out_sums])
    out_fars = [
        exchange(after(item[2], pieces_dh[1][2]), "tensor", ACROSS) for item in out_sums
    ]

    joints, head_parts, mixed, early = [], [], [], []
    for g in range(groups):
        outs_back = attend_back(
            g, place, flipped, rows, context_flip, log_total, starts, dh, out_weight, raw, tables,
            head_gains,
        )
        joints.append(outs_back[0])
        head_parts.append(outs_back[1])
        if g == 0:
            dh_full = outs_back[2]
            early = ScatterSum(
                [
                    contract_rows(dh_full, context).astype(jnp.bfloat16),
                    contract_rows(normed_one, outs_back[0]).astype(jnp.bfloat16),
                ],
                [(context.shape[1], True), (joints[0].shape[1], False)],
            )
            sent, _ = advance(here, [gate, up, down, early], outs_back[1])
            dh = [after(dh_full, *sent, *out_fars)]
        else:
            dh = [dh_full]
    late = [
        contract_rows(normed_one, joints[g]).astype(jnp.bfloat16) for g in range(1, groups)
    ]
    late = ScatterSum(late, [(joints[0].shape[1] * (groups - 1), False)])
    sent, square = advance(here, [gate, up, down, early, late])
    squares.append(square)
    joints[0] = after(joints[0], *sent)
    send, keep = spread(place, joints, weight_rows)
    near = exchange(send, "tensor", CORE)
    pending = [item for item in (gate, up, down, early, late) if item.total is None]
    third = after(near, *[item.sources[1] for item in pending])
    passed = (keep, near, added(keep[1], third[1]))
    keep, near, far = across_of(passed)
    gates = [passed[2]]
    while pending != [late]:
        _, square = advance(here, pending, *gates)
        gates = []
        squares.append(square)
        pending = [item for item in (gate, up, down, early, late) if item.total is None]

    results = []
    for half in range(HALVES):
        keep_out, near_out, _ = out_sums[half]
        total = keep_out.astype(jnp.float32) + near_out.astype(jnp.float32)
        results.append(middles[half] + (total + out_fars[half].astype(jnp.float32)))
    result = jnp.concatenate(results, axis=0).astype(jnp.bfloat16)

    ffn_parts = [after(ffn_parts[0], result), *ffn_parts[1:]]
    row = row_of(ffn_parts, head_parts, squares)
    gates = [row]
    while late.total is None:
        _, square = advance(here, [late], *gates)
        gates = []
    skips = [pieces[0] for pieces in pieces_dh]
    input_grad, row = finish(tokens, skips, keep, near, far, attn_gain, row, square)
    summed = sum_all(row)
    entries = gains.shape[0]
    out_fan = max(QH * HD * 16 // length, 16)
    out_rate = RATE_WEIGHT * (QH * HD / out_fan) ** 0.5
    updated = adam_all(
        entries, summed, [*early.total, *late.total, *gate.total, *up.total, *down.total],
        [
            (qkv_master, qkv_mean, qkv_square),
            (out_master, out_mean, out_square),
            (gate_up_master, gate_up_mean, gate_up_square),
            (down_master, down_mean, down_square),
        ],
        out_rate,
    )
    grad_norm = updated[16][0, 0]
    factor = CLIP_NORM / jnp.maximum(grad_norm, CLIP_NORM)
    gain_results = adam(
        gains, gains_mean, gains_square, summed[0, :entries], factor, RATE_GAIN, 0.0
    )
    return (result, input_grad, grad_norm, *updated[:16], *gain_results)


def solution(mesh):
    in_specs = (
        P(("dp", "tensor"), None),
        P("dp"),
        P(("dp", "tensor"), None),
        P(None, "tensor"),
        P("tensor", None),
        P(None, None, "tensor"),
        P("tensor", None),
        P("dp", "tensor"),
        P("tensor", "dp"),
        P("dp", None, "tensor"),
        P("tensor", "dp"),
        P("dp", "tensor"),
        P("tensor", "dp"),
        P("dp", None, "tensor"),
        P("tensor", "dp"),
        P("dp", "tensor"),
        P("tensor", "dp"),
        P("dp", None, "tensor"),
        P("tensor", "dp"),
        P(),
        P(),
        P(),
    )
    out_specs = (
        P(("dp", "tensor"), None),
        P(("dp", "tensor"), None),
        P(),
        P("dp", "tensor"),
        P("dp", "tensor"),
        P("dp", "tensor"),
        P("dp", "tensor"),
        P("tensor", "dp"),
        P("tensor", "dp"),
        P("tensor", "dp"),
        P("tensor", "dp"),
        P("dp", None, "tensor"),
        P("dp", None, "tensor"),
        P("dp", None, "tensor"),
        P("dp", None, "tensor"),
        P("tensor", "dp"),
        P("tensor", "dp"),
        P("tensor", "dp"),
        P("tensor", "dp"),
        P(),
        P(),
        P(),
    )
    return jax.shard_map(shards, mesh=mesh, in_specs=in_specs, out_specs=out_specs, check_vma=False)
```
